32 devices in a mesh: gx: 8 (over y, x, core), gy: 4 (over z).
Axes of the slice: x: 2, y: 2, z: 4, core: 2. Of those that a mesh axis runs over, the one named last changes fastest.
Arguments:
- populations: float32 [19, 32, 128, 256], P(None, 'gx', 'gy'), may hold values from 0.6 to 1.4
- relax_rates: float32 [19], replicated, may hold values from 0.8 to 1.9
- velocity: float32 [3, 16384], P(None, ('gx', 'gy')), may hold values from -0.2 to 0.2
- velocity_change: float32 [3, 16384], P(None, ('gx', 'gy')), may hold values from -0.16 to 0.16
- fractions: float32 [27, 16384], P(None, ('gx', 'gy')), may hold values from 0.05 to 0.5
- anchor: int32 [16384], P(('gx', 'gy')), may hold values from 8449 to 24318, as said below
- destination: int32 [16384], P(('gx', 'gy')), may hold values from 0 to 9, as said below
Outputs:
- advanced: float32 [19, 32, 128, 256], P(None, 'gx', 'gy')
The draws below stay inside these ranges and needn't reach their ends.
Inputs may be any that keep to these rules, and one draw needn't show every extreme that they name: `destination`: empty rows (9) carry no particle. Every brick sends exactly 4 particles to each of its 8 neighbouring bricks that lie inside the grid across the bed (gy index within 0 to 3; along gx the neighbours wrap around); the rest of the occupied rows stay (4); brick rows at gy index q hold 512 // 2^q occupied rows. Each anchor lies at least one cell inside its destination brick along x, y and z, so that the whole correlation cube lies in that brick.
All inputs are finite; a program needn't handle non-finite values.
Results may differ from the reference program's by a relative error of at most 0.0001.
Values sent between devices are 32-bit elements; how exact they have to be, the bound alone decides.
No kernel may reach another device: no remote copies, remote signals or barrier semaphores. Data moves between devices by JAX's collectives and lax.ppermute only.
A program may use at most 128 MiB of HBM per device.

```python
import math
import jax
import jax.numpy as jnp
import numpy as np
from jax import lax

CX = 4
CY = 32
CZ = 256
PSLOT = 512
CAP = 4
STEPS = 2
NX = 32
NY = 128
NZ = 256
BANDS = 4
PROWS = 16384
N_GX = 8
N_GY = 4


def draw_anchor(key, part):
    key_x, key_y, key_z = jax.random.split(key, 3)
    along_x = jax.random.randint(key_x, (PROWS,), 1, CX - 1)
    along_y = jax.random.randint(key_y, (PROWS,), 1, CY - 1)
    along_z = jax.random.randint(key_z, (PROWS,), 1, CZ - 1)
    return ((along_x * CY + along_y) * CZ + along_z).astype(jnp.int32)


def draw_destination(key, part):
    group_codes = jnp.array([0, 1, 2, 3, 5, 6, 7, 8], jnp.int32)
    position = jnp.arange(PSLOT, dtype=jnp.int32)

    def one_block(block_key, device):
        level = device % BANDS
        live_rows = jnp.right_shift(jnp.int32(PSLOT), level)
        group = jnp.minimum(position // CAP, 7)
        code_value = group_codes[group]
        across = code_value % 3 - 1
        valid = (position < 8 * CAP) & (level + across >= 0) & (level + across < BANDS)
        labels = jnp.where(valid, code_value, jnp.where(position < live_rows, 4, 9)).astype(jnp.int32)
        order = jax.random.permutation(block_key, PSLOT)
        return labels[order]
    block_count = PROWS // PSLOT
    block_keys = jax.random.split(key, block_count)
    blocks = jax.vmap(one_block)(block_keys, jnp.arange(block_count, dtype=jnp.int32))
    return blocks.reshape(-1).astype(jnp.int32)


def shard_levels(own_key, dims, shards, smallest, largest):
    def one(dim, shards_of):
        heights = jax.random.uniform(jax.random.fold_in(jax.random.fold_in(own_key, 6), dim), (shards_of,), jnp.float32, smallest / len(shards), largest / len(shards))
        return jnp.repeat(jnp.exp(heights), dims[dim] // shards_of).reshape((-1,) + (1,) * (len(dims) - dim - 1))

    factor_of = one(*shards[0])
    for cut in shards[1:]:
        factor_of = factor_of * one(*cut)
    return factor_of


def noise(key, extent, spread, limit, cuts=(), held_as=jnp.bfloat16):
    result = spread * jax.random.normal(key, extent, jnp.float32)
    if cuts:
        result = result * shard_levels(key, extent, cuts, -0.22, 0.18)
    return jnp.clip(result, -limit, limit).astype(held_as)


def setup_inputs(seed: int = 0) -> dict:
    key_list = jax.random.split(jax.random.key(seed), 8)
    return {
        "populations": jnp.clip(0.6 + 0.79999995 * jax.random.uniform(key_list[0], (19, NX, NY, NZ), jnp.float32) ** shard_levels(key_list[0], (19, NX, NY, NZ), ((1, 8), (2, 4)), -0.2, 0.2), 0.6, 1.4),
        "relax_rates": jnp.clip(jnp.exp(jax.random.uniform(key_list[1], (19,), jnp.float32, math.log(0.8), math.log(1.9))), 0.8, 1.9),
        "velocity": noise(key_list[2], (3, PROWS), 0.05, 0.2, ((1, 32),), jnp.float32),
        "velocity_change": noise(key_list[3], (3, PROWS), 0.04, 0.16, ((1, 32),), jnp.float32),
        "fractions": jnp.clip(0.05 + 0.45 * jax.random.uniform(key_list[4], (27, PROWS), jnp.float32) ** shard_levels(key_list[4], (27, PROWS), ((1, 32),), -0.2, 0.2), 0.05, 0.5),
        "anchor": draw_anchor(jax.random.fold_in(key_list[7], 71), 0),
        "destination": draw_destination(jax.random.fold_in(key_list[7], 71), 0),
    }


def lattice():
    vectors = [[0, 0, 0]]
    for axis_one in range(3):
        for orient in (1, -1):
            vector_one = [0, 0, 0]
            vector_one[axis_one] = orient
            vectors.append(vector_one)
    for axis_one, axis_two in ((0, 1), (0, 2), (1, 2)):
        for orient in (1, -1):
            for second in (1, -1):
                vector_one = [0, 0, 0]
                vector_one[axis_one] = orient
                vector_one[axis_two] = second
                vectors.append(vector_one)
    integral = np.array(vectors)
    speeds = integral * 1.0
    length = (speeds ** 2).sum(axis=1)
    weights = np.where(length == 0, 1.0 / 3.0, np.where(length == 1, 1.0 / 18.0, 1.0 / 36.0))
    opposite = np.array([vectors.index([0 - component for component in vector_one]) for vector_one in vectors])
    along_x, along_y, along_z = (speeds[:, 0], speeds[:, 1], speeds[:, 2])
    rows_list = [np.ones(19), along_x, along_y, along_z, length, 3 * along_x ** 2 - length, along_y ** 2 - along_z ** 2, along_x * along_y, along_y * along_z, along_x * along_z, along_x * length, along_y * length, along_z * length, along_x * (along_y ** 2 - along_z ** 2), along_y * (along_z ** 2 - along_x ** 2), along_z * (along_x ** 2 - along_y ** 2), length ** 2, (3 * along_x ** 2 - length) * length, (along_y ** 2 - along_z ** 2) * length]
    basis_rows = []
    for candidate in rows_list:
        for earlier in basis_rows:
            candidate = candidate - np.dot(candidate, earlier) * earlier
        basis_rows.append(candidate / np.sqrt(np.dot(candidate, candidate)))
    basis = np.array(basis_rows)
    return (speeds, weights, opposite, basis, integral)

def tables():
    speeds, weights, opposite, basis, integral = lattice()
    lattice_vel = jnp.asarray(speeds, jnp.float32)
    moment_rows = jnp.asarray(np.concatenate([weights[None, :], (weights[:, None] * speeds).T], axis=0), jnp.float32)
    to_moments = jnp.asarray(basis * weights[None, :], jnp.float32)
    from_moments = jnp.asarray(basis.T / weights[:, None], jnp.float32)
    return (lattice_vel, moment_rows, to_moments, from_moments, opposite, integral)

def equilibrium(density, flow, lattice_vel):
    projected = jnp.dot(lattice_vel, flow, precision=lax.Precision.HIGHEST)
    speed_sq = lax.optimization_barrier(jnp.sum(flow * flow, axis=0))
    return density[None, :] * (1.0 + 3.0 * projected + 4.5 * projected * projected - 1.5 * speed_sq[None, :])

def collide(states, solid_part, solid_flow, relax_rates, packed):
    lattice_vel, moment_rows, to_moments, from_moments, opposite = packed
    moments = jnp.dot(moment_rows, states, precision=lax.Precision.HIGHEST)
    density = moments[0]
    flow = moments[1:] / density[None, :]
    fluid_eq = equilibrium(density, flow, lattice_vel)
    solid_eq = equilibrium(density, solid_flow, lattice_vel)
    off_eq = states - fluid_eq
    projected = jnp.dot(to_moments, off_eq, precision=lax.Precision.HIGHEST)
    relaxed = jnp.dot(from_moments, relax_rates[:, None] * projected, precision=lax.Precision.HIGHEST)
    bounce = states[opposite] - fluid_eq[opposite] - (states - solid_eq)
    return states - (1.0 - solid_part)[None, :] * relaxed + solid_part[None, :] * bounce

def reference(populations, relax_rates, velocity, velocity_change, fractions, anchor, destination):
    lattice_vel, moment_rows, to_moments, from_moments, opposite, speeds = tables()
    packed = (lattice_vel, moment_rows, to_moments, from_moments, opposite)
    new_velocity = velocity + velocity_change
    owner = jnp.arange(PROWS, dtype=jnp.int32) // PSLOT
    owner_x = owner // N_GY
    owner_y = owner % N_GY
    target_x = (owner_x + destination // 3 - 1) % N_GX
    target_y = owner_y + destination % 3 - 1
    keep = (destination == 4) | (destination < 9) & (destination != 4)
    centre_x = target_x * CX + anchor // (CY * CZ)
    centre_y = target_y * CY + anchor // CZ % CY
    centre_z = anchor % CZ
    cube = jnp.arange(27, dtype=jnp.int32)[:, None]
    flat = ((centre_x[None, :] + cube // 9 - 1) * NY + centre_y[None, :] + cube // 3 % 3 - 1) * NZ + centre_z[None, :] + cube % 3 - 1
    cells = NX * NY * NZ
    flat = jnp.clip(flat, 0, cells - 1).reshape(-1)
    shares = jnp.where(keep[None, :], fractions, jnp.float32(0.0))
    solid_sum = jnp.zeros((cells,), jnp.float32).at[flat].add(shares.reshape(-1))
    momentum = jnp.zeros((3, cells), jnp.float32).at[:, flat].add((shares[None, :, :] * new_velocity[:, None, :]).reshape(3, -1))
    solid = jnp.minimum(solid_sum, 1.0)
    solid_velocity = momentum / (solid_sum + 1e-06)[None, :]
    solid_slabs = solid.reshape(NX, NY * NZ)
    velocity_slabs = jnp.moveaxis(solid_velocity.reshape(3, NX, NY * NZ), 1, 0)
    coord_y = jnp.arange(NY, dtype=jnp.int32)[None, :, None]
    states = populations
    for sweep_number in range(STEPS):
        slabs = jnp.moveaxis(states, 1, 0).reshape(NX, 19, NY * NZ)
        post = lax.map(lambda slab_args: collide(slab_args[0], slab_args[1], slab_args[2], relax_rates, packed), (slabs, solid_slabs, velocity_slabs))
        post = jnp.moveaxis(post.reshape(NX, 19, NY, NZ), 0, 1)
        read = []
        for number in range(19):
            shift_x, shift_y, shift_z = (int(speeds[number, 0]), int(speeds[number, 1]), int(speeds[number, 2]))
            pulled = jnp.roll(post[number], (shift_x, shift_y, shift_z), (0, 1, 2))
            if shift_y == 1:
                pulled = jnp.where(coord_y == 0, post[opposite[number]], pulled)
            elif shift_y == -1:
                pulled = jnp.where(coord_y == NY - 1, post[opposite[number]], pulled)
            read.append(pulled)
        states = jnp.stack(read, axis=0)
    return states
```

```python
import functools

import jax
import jax.numpy as jnp
import numpy as np
from jax import lax
from jax.experimental import pallas as pl
from jax.experimental.pallas import tpu as pltpu
from jax.sharding import PartitionSpec as P

CAP = 4
STEPS = 2
LANES = 8 * CAP
F32 = jnp.float32
BF16 = jnp.bfloat16
I32 = jnp.int32


def lattice():
    vectors = [[0, 0, 0]]
    for axis_one in range(3):
        for orient in (1, -1):
            vector_one = [0, 0, 0]
            vector_one[axis_one] = orient
            vectors.append(vector_one)
    for axis_one, axis_two in ((0, 1), (0, 2), (1, 2)):
        for orient in (1, -1):
            for second in (1, -1):
                vector_one = [0, 0, 0]
                vector_one[axis_one] = orient
                vector_one[axis_two] = second
                vectors.append(vector_one)
    integral = np.array(vectors)
    speeds = integral * 1.0
    length = (speeds**2).sum(axis=1)
    weights = np.where(length == 0, 1.0 / 3.0, np.where(length == 1, 1.0 / 18.0, 1.0 / 36.0))
    opposite = [vectors.index([0 - component for component in vector_one]) for vector_one in vectors]
    along_x, along_y, along_z = (speeds[:, 0], speeds[:, 1], speeds[:, 2])
    rows_list = [
        np.ones(19),
        along_x,
        along_y,
        along_z,
        length,
        3 * along_x**2 - length,
        along_y**2 - along_z**2,
        along_x * along_y,
        along_y * along_z,
        along_x * along_z,
        along_x * length,
        along_y * length,
        along_z * length,
        along_x * (along_y**2 - along_z**2),
        along_y * (along_z**2 - along_x**2),
        along_z * (along_x**2 - along_y**2),
        length**2,
        (3 * along_x**2 - length) * length,
        (along_y**2 - along_z**2) * length,
    ]
    basis_rows = []
    for candidate in rows_list:
        for earlier in basis_rows:
            candidate = candidate - np.dot(candidate, earlier) * earlier
        basis_rows.append(candidate / np.sqrt(np.dot(candidate, candidate)))
    return [tuple(v) for v in vectors], weights, opposite, np.array(basis_rows)


VEC, WEIGHTS, OPP, BASIS = lattice()
FORWARD = [i for i in range(19) if VEC[i][0] == 1]
BACKWARD = [i for i in range(19) if VEC[i][0] == -1]


def symmetric_blocks():
    def vec(entries):
        out = np.zeros(19)
        for index, value in entries.items():
            out[index] = value
        return out

    def plane(base):
        s_one, d_one = vec({base: 1, base + 3: 1}), vec({base: 1, base + 3: -1})
        s_two, d_two = vec({base + 1: 1, base + 2: 1}), vec({base + 1: 1, base + 2: -1})
        return s_one + s_two, s_one - s_two, d_one + d_two, d_one - d_two

    rest = vec({0: 1})
    s_x, s_y, s_z = vec({1: 1, 2: 1}), vec({3: 1, 4: 1}), vec({5: 1, 6: 1})
    d_x, d_y, d_z = vec({1: 1, 2: -1}), vec({3: 1, 4: -1}), vec({5: 1, 6: -1})
    xy, q_xy, x_xy, y_xy = plane(7)
    xz, q_xz, x_xz, z_xz = plane(11)
    yz, q_yz, y_yz, z_yz = plane(15)
    blocks = [
        [rest, s_x + s_y + s_z, xy + xz + yz],
        [2 * s_x - s_y - s_z, xy + xz - 2 * yz],
        [s_y - s_z, xy - xz],
        [q_xy],
        [q_xz],
        [q_yz],
        [d_x, x_xy, x_xz],
        [d_y, y_xy, y_yz],
        [d_z, z_xz, z_yz],
    ]
    scales = [[1, 1 / 6, 1 / 12], [1 / 12, 1 / 24], [1 / 4, 1 / 8]]
    scales += [[1 / 4]] * 3 + [[1 / 2, 1 / 4, 1 / 4]] * 3
    forward = np.array([row for block in blocks for row in block])
    back = np.linalg.inv(forward)
    left = forward @ np.diag(1.0 / WEIGHTS) @ BASIS.T
    right = BASIS @ np.diag(WEIGHTS) @ back
    table = []
    start = 0
    for block, scale in zip(blocks, scales):
        size = len(block)
        rows = []
        for a in range(size):
            row = []
            for b in range(size):
                per_rate = -scale[a] * left[start + a, :] * right[:, start + b]
                row.append([(k, float(v)) for k, v in enumerate(per_rate) if abs(v) > 1e-12])
            rows.append(row)
        table.append(rows)
        start += size
    return table


RELAX = symmetric_blocks()


def relax_blocks(rates):
    values = [rates[k] for k in range(19)]

    def entry(terms):
        total = None
        for k, factor in terms:
            part = values[k] * np.float32(factor)
            total = part if total is None else total + part
        return total

    return [[[entry(terms) for terms in row] for row in block] for block in RELAX]


def apply_block(block, values):
    out = []
    for row in block:
        total = None
        for factor, value in zip(row, values):
            part = factor * value
            total = part if total is None else total + part
        out.append(total)
    return out


def collide(h, solid, s_x, s_y, s_z, blocks):
    def plane(base):
        s_one, d_one = h[base] + h[base + 3], h[base] - h[base + 3]
        s_two, d_two = h[base + 1] + h[base + 2], h[base + 1] - h[base + 2]
        return s_one + s_two, s_one - s_two, d_one + d_two, d_one - d_two

    sum_x, dif_x = h[1] + h[2], h[1] - h[2]
    sum_y, dif_y = h[3] + h[4], h[3] - h[4]
    sum_z, dif_z = h[5] + h[6], h[5] - h[6]
    xy, q_xy, x_xy, y_xy = plane(7)
    xz, q_xz, x_xz, z_xz = plane(11)
    yz, q_yz, y_yz, z_yz = plane(15)
    axes = sum_x + sum_y + sum_z
    edges = xy + xz + yz
    density = h[0] * (1.0 / 3.0) + axes * (1.0 / 18.0) + edges * (1.0 / 36.0)
    m_x = dif_x * (1.0 / 18.0) + (x_xy + x_xz) * (1.0 / 36.0)
    m_y = dif_y * (1.0 / 18.0) + (y_xy + y_yz) * (1.0 / 36.0)
    m_z = dif_z * (1.0 / 18.0) + (z_xz + z_yz) * (1.0 / 36.0)
    inverse = 1.0 / density
    u_x, u_y, u_z = m_x * inverse, m_y * inverse, m_z * inverse
    e_xx, e_yy, e_zz = m_x * u_x, m_y * u_y, m_z * u_z
    e_xy, e_xz, e_yz = m_x * u_y, m_x * u_z, m_y * u_z
    energy = e_xx + e_yy + e_zz
    turn = e_yy - e_zz
    lean = 3.0 * e_xx - energy
    rest_off = h[0] - density + 1.5 * energy
    axes_off = axes - 6.0 * density
    edges_off = edges - 12.0 * density - 18.0 * energy
    a_one = 3.0 * sum_x - axes - 9.0 * lean
    b_one = edges - 3.0 * yz - 18.0 * lean
    a_two = sum_y - sum_z - 9.0 * turn
    b_two = xy - xz - 18.0 * turn
    q_xy = q_xy - 36.0 * e_xy
    q_xz = q_xz - 36.0 * e_xz
    q_yz = q_yz - 36.0 * e_yz

    r_rest, r_axes, r_edges = apply_block(blocks[0], [rest_off, axes_off, edges_off])
    r_a_one, r_b_one = apply_block(blocks[1], [a_one, b_one])
    r_a_two, r_b_two = apply_block(blocks[2], [a_two, b_two])
    fluid = 1.0 - solid
    mixed = solid * density
    w_x, w_y, w_z = solid * m_x, solid * m_y, solid * m_z
    n_x, n_y, n_z = mixed * s_x, mixed * s_y, mixed * s_z
    p_x = n_x * s_x - solid * e_xx
    p_y = n_y * s_y - solid * e_yy
    p_z = n_z * s_z - solid * e_zz
    total = 1.5 * (p_x + p_y + p_z)
    lean_s = 2.25 * p_x - 0.5 * total
    turn_s = 2.25 * (p_y - p_z)
    rest = fluid * r_rest - total
    axes = fluid * r_axes
    edges = fluid * r_edges + total
    a_one = fluid * r_a_one + lean_s
    b_one = fluid * r_b_one + lean_s
    a_two = fluid * r_a_two + turn_s
    b_two = fluid * r_b_two + turn_s
    q_xy = fluid * apply_block(blocks[3], [q_xy])[0] + 9.0 * (n_x * s_y - solid * e_xy)
    q_xz = fluid * apply_block(blocks[4], [q_xz])[0] + 9.0 * (n_x * s_z - solid * e_xz)
    q_yz = fluid * apply_block(blocks[5], [q_yz])[0] + 9.0 * (n_y * s_z - solid * e_yz)

    def odd(block, axis, one, two, m, n, w):
        six = 6.0 * m
        axis = axis - six
        twelve = six + six
        one = one - twelve
        two = two - twelve
        r_axis, r_one, r_two = apply_block(block, [axis, one, two])
        push = 3.0 * (n - w)
        half = 0.5 * solid
        return (
            fluid * r_axis - solid * axis + push,
            fluid * r_one - half * one + push,
            fluid * r_two - half * two + push,
        )

    d_x, x_xy, x_xz = odd(blocks[6], dif_x, x_xy, x_xz, m_x, n_x, w_x)
    d_y, y_xy, y_yz = odd(blocks[7], dif_y, y_xy, y_yz, m_y, n_y, w_y)
    d_z, z_xz, z_yz = odd(blocks[8], dif_z, z_xz, z_yz, m_z, n_z, w_z)
    out = [None] * 19
    out[0] = h[0] + rest
    even = axes + 2.0 * a_one
    out[1], out[2] = h[1] + (even + d_x), h[2] + (even - d_x)
    base = axes - a_one
    even = base + a_two
    out[3], out[4] = h[3] + (even + d_y), h[4] + (even - d_y)
    even = base - a_two
    out[5], out[6] = h[5] + (even + d_z), h[6] + (even - d_z)

    def spread(start, even, twist, one, two):
        same, cross = even + twist, even - twist
        plus, minus = one + two, one - two
        out[start] = h[start] + (same + plus)
        out[start + 3] = h[start + 3] + (same - plus)
        out[start + 1] = h[start + 1] + (cross + minus)
        out[start + 2] = h[start + 2] + (cross - minus)

    base = edges + b_one
    spread(7, base + b_two, q_xy, x_xy, y_xy)
    spread(11, base - b_two, q_xz, x_xz, z_xz)
    spread(15, edges - 2.0 * b_one, q_yz, y_yz, z_yz)
    return out


def iota(shape, dim):
    return lax.broadcasted_iota(I32, shape, dim)


def cells_of(anchor, size_y, size_z):
    plane = size_y * size_z
    a_x = lax.div(anchor, jnp.int32(plane))
    rest = anchor - a_x * plane
    a_y = lax.div(rest, jnp.int32(size_z))
    return a_x, a_y, rest - a_y * size_z


def halves(value):
    high = value.astype(BF16)
    return high, (value - high.astype(F32)).astype(BF16)


def dot_t(left, right):
    return lax.dot_general(left, right, (((1,), (1,)), ((), ())), preferred_element_type=F32)


def deposited(groups, shares, velocity, a_x, a_y, a_z, size_y, size_z):
    big = 8 * size_y
    centre = a_x * big + a_y
    lanes = centre.shape[1]
    totals = None
    rows_z = iota((size_z, lanes), 0)
    for off_z in range(3):
        weights = []
        for rows_x, rows_y in groups:
            away = rows_x * big + rows_y - centre
            weight = jnp.zeros(away.shape, F32)
            for off in range(9):
                move = (off // 3 - 1) * big + off % 3 - 1
                row = 3 * off + off_z
                weight = jnp.where(away == move, shares[row : row + 1, :], weight)
            weights.append([weight] + [weight * velocity[k : k + 1, :] for k in range(3)])
        rows = jnp.concatenate([w for block in weights for w in block], axis=0)
        high, low = halves(rows)
        hot = jnp.where(rows_z == a_z + (off_z - 1), 1.0, 0.0).astype(BF16)
        part = dot_t(high, hot) + dot_t(low, hot)
        totals = part if totals is None else totals + part
    return totals


def pack_kernel(velocity, change, fractions, anchor, destination, table, own, ahead, behind):
    rows = destination.shape[1]
    dest = destination[...]
    kinds = iota((16, rows), 0)
    hot = jnp.where(dest == kinds, 1.0, 0.0)
    order = jnp.where(iota((128, 128), 0) <= iota((128, 128), 1), 1.0, 0.0).astype(BF16)
    seen = jnp.zeros((16, 1), F32)
    ranks = []
    for start in range(0, rows, 128):
        counted = seen + lax.dot_general(
            hot[:, start : start + 128].astype(BF16),
            order,
            (((1,), (0,)), ((), ())),
            preferred_element_type=F32,
        )
        ranks.append(counted)
        seen = counted[:, 127:128]
    rank = jnp.concatenate(ranks, axis=1)
    kind = iota((16, 1), 0)
    begin = jnp.where(
        kind < 3,
        5 * CAP + CAP * kind,
        jnp.where(kind == 3, 0, jnp.where(kind == 5, CAP, 2 * CAP + CAP * (kind - 6))),
    ).astype(F32)
    leaving = (dest < 9) & (dest != 4)
    slot = jnp.sum(hot * (begin + rank - 1.0), axis=0, keepdims=True)
    slot = jnp.where(leaving, slot, -1.0).astype(I32)
    chosen = jnp.where(iota((128, rows), 0) == slot, 1.0, 0.0).astype(BF16)
    new_velocity = velocity[...] + change[...]
    payload = jnp.concatenate(
        [fractions[...], new_velocity, anchor[...].astype(F32), jnp.zeros((1, rows), F32)], axis=0
    )
    high = payload.astype(BF16)
    rest = payload - high.astype(F32)
    middle, low = halves(rest)
    packed = dot_t(high, chosen) + dot_t(middle, chosen) + dot_t(low, chosen)
    lane = iota((32, 128), 1)
    own[...] = jnp.where(lane < 2 * CAP, packed, 0.0)
    ahead[...] = jnp.where((lane >= 2 * CAP) & (lane < 5 * CAP), packed, 0.0)
    behind[...] = jnp.where(lane >= 5 * CAP, packed, 0.0)
    table[...] = jnp.where((iota((32, rows), 0) < 27) & (dest != 4), 0.0, payload)


def edge_kernel(size_x, size_y, size_z, populations, table, up, down):
    for i in range(19):
        for x in range(size_x):
            at = i * 2 * size_x + 2 * x
            down[at : at + 2, :] = populations[i, x, 0:2, :]
            up[at : at + 2, :] = populations[i, x, size_y - 2 : size_y, :]
    a_x, a_y, a_z = cells_of(table[30:31, :].astype(I32), size_y, size_z)
    rows = 2 * size_x
    index = iota((rows, 1), 0)
    rows_x, low = lax.div(index, jnp.int32(2)), lax.rem(index, jnp.int32(2))
    sums = deposited(
        [(rows_x, low), (rows_x, low + (size_y - 2))],
        table[0:27, :],
        table[27:30, :],
        a_x,
        a_y,
        a_z,
        size_y,
        size_z,
    )
    first = 19 * rows
    down[first : first + 4 * rows, :] = sums[: 4 * rows]
    up[first : first + 4 * rows, :] = sums[4 * rows :]


def stay_kernel(size_x, size_y, size_z, table, from_up, from_down, sums, outer):
    a_x, a_y, a_z = cells_of(table[30:31, :].astype(I32), size_y, size_z)
    index = iota((size_x * size_y, 1), 0)
    rows_x = lax.div(index, jnp.int32(size_y))
    totals = deposited(
        [(rows_x, index - rows_x * size_y)],
        table[0:27, :],
        table[27:30, :],
        a_x,
        a_y,
        a_z,
        size_y,
        size_z,
    )
    cells = size_x * size_y
    blank = jnp.zeros((8, size_z), F32)
    ones = jnp.ones((8, size_z), F32)
    for c in range(4):
        for x in range(size_x):
            at = c * cells + x * size_y
            sums[c, x, 0:size_y, :] = totals[at : at + size_y]
            sums[c, x, size_y : size_y + 8, :] = blank
            at = 19 * 2 * size_x + c * 2 * size_x + 2 * x
            sums[c, x, size_y : size_y + 2, :] = from_up[at : at + 2, :]
            sums[c, x, size_y + 6 : size_y + 8, :] = from_down[at : at + 2, :]
    for i in range(19):
        for x in range(size_x):
            at = i * 2 * size_x + 2 * x
            outer[i, x, :, :] = ones
            outer[i, x, 0:2, :] = from_up[at : at + 2, :]
            outer[i, x, 6:8, :] = from_down[at : at + 2, :]


def store_padded(target, i, x, tile, value, tiles):
    if tile == tiles:
        target[i, x, 0:8, :] = value
        target[i, x, 8 + 8 * tiles : 16 + 8 * tiles, :] = value
    else:
        target[i, x, 8 + 8 * tile : 16 + 8 * tile, :] = value
        if tile == 0:
            target[i, x, 16 + 8 * tiles : 24 + 8 * tiles, :] = value


def turned(value, shift, size_z):
    return value if shift == 0 else pltpu.roll(value, shift % size_z, 1)


def first_kernel(
    size_x, size_y, size_z, count, shifts, rates, sums, outer, populations, *refs
):
    columns = refs[: len(shifts)]
    post, solid, ahead, behind = refs[len(shifts) :]
    tiles = size_y // 8
    here = lax.axis_index("gy")
    per_group = 128 // LANES
    tables, offsets = [], []
    lane = iota((1, 128), 1)
    spot = lane % LANES
    group = spot // CAP
    across = jnp.where(
        (group == 0) | (group == 2) | (group == 5), -1, jnp.where((group == 3) | (group == 6), 0, 1)
    )
    for start in range(0, len(shifts), per_group):
        table = None
        offset = jnp.zeros((1, 128), I32)
        for k, shift in enumerate(shifts[start : start + per_group]):
            part = columns[start + k][...]
            part = part if k == 0 else pltpu.roll(part, k * LANES, 1)
            table = part if table is None else table + part
            source = lax.rem(here - shift + 2 * count, count)
            offset = jnp.where(lane // LANES == k, source - here, offset)
        tables.append(table)
        offsets.append((offset + across) * size_y)
    table = jnp.concatenate(tables, axis=1)
    offset = jnp.concatenate(offsets, axis=1)
    a_x, a_y, a_z = cells_of(table[30:31, :].astype(I32), size_y, size_z)
    wide = size_y + 8
    index = iota((size_x * wide, 1), 0)
    rows_x = lax.div(index, jnp.int32(wide))
    row = index - rows_x * wide
    rows_y = jnp.where(row < size_y + 2, row, jnp.where(row >= size_y + 6, row - wide, -3 * size_y))
    totals = deposited(
        [(rows_x, rows_y)], table[0:27, :], table[27:30, :], a_x, a_y + offset, a_z, size_y, size_z
    )
    blocks = relax_blocks(rates)
    cells = size_x * wide
    for x in range(size_x):
        for tile in range(tiles + 1):
            parts = []
            for c in range(4):
                at = c * cells + x * wide + 8 * tile
                parts.append(totals[at : at + 8] + sums[c, x, 8 * tile : 8 * tile + 8, :])
            scale = 1.0 / (parts[0] + 1e-06)
            share = jnp.minimum(parts[0], 1.0)
            flow = [parts[k] * scale for k in (1, 2, 3)]
            for c, value in enumerate([share] + flow):
                solid[c, x, 8 * tile : 8 * tile + 8, :] = value
            if tile == tiles:
                h = [outer[i, x, :, :] for i in range(19)]
            else:
                h = [populations[i, x, 8 * tile : 8 * tile + 8, :] for i in range(19)]
            out = collide(h, share, *flow, blocks)
            for i in range(19):
                store_padded(post, i, x, tile, out[i], tiles)
    faces(post, ahead, behind, size_x, size_z, tiles, tiles + 1)


def faces(post, ahead, behind, size_x, size_z, tiles, number):
    for target, numbers, x in ((ahead, FORWARD, size_x - 1), (behind, BACKWARD, 0)):
        for k, i in enumerate(numbers):
            _, c_y, c_z = VEC[i]
            for tile in range(number):
                at = 8 + 8 * tile - c_y
                target[k, 8 * tile : 8 * tile + 8, :] = turned(post[i, x, at : at + 8, :], c_z, size_z)


def streamed(post, from_behind, from_ahead, x, tile, size_x, size_y, size_z, at_low, at_high):
    tiles = size_y // 8
    out = []
    row = iota((8, size_z), 0)
    for i in range(19):
        c_x, c_y, c_z = VEC[i]
        if x - c_x < 0:
            value = from_behind[FORWARD.index(i), 8 * tile : 8 * tile + 8, :]
        elif x - c_x >= size_x:
            value = from_ahead[BACKWARD.index(i), 8 * tile : 8 * tile + 8, :]
        else:
            at = 8 + 8 * tile - c_y
            value = turned(post[i, x - c_x, at : at + 8, :], c_z, size_z)
        if c_y == 1 and tile == 0:
            back = post[OPP[i], x, 8:16, :]
            value = jnp.where((row == 0) & at_low, back, value)
        if c_y == -1 and tile == tiles - 1:
            back = post[OPP[i], x, 8 * tiles : 8 + 8 * tiles, :]
            value = jnp.where((row == 7) & at_high, back, value)
        out.append(value)
    return out


def second_kernel(
    size_x, size_y, size_z, count, rates, post, solid, from_behind, from_ahead, later, ahead, behind
):
    tiles = size_y // 8
    here = lax.axis_index("gy")
    at_low, at_high = here == 0, here == count - 1
    blocks = relax_blocks(rates)
    for x in range(size_x):
        for tile in range(tiles + 1):
            h = streamed(
                post, from_behind, from_ahead, x, tile, size_x, size_y, size_z, at_low, at_high
            )
            s = [solid[c, x, 8 * tile : 8 * tile + 8, :] for c in range(4)]
            out = collide(h, *s, blocks)
            for i in range(19):
                store_padded(later, i, x, tile, out[i], tiles)
    faces(later, ahead, behind, size_x, size_z, tiles, tiles)


def last_kernel(size_x, size_y, size_z, count, post, from_behind, from_ahead, advanced):
    here = lax.axis_index("gy")
    at_low, at_high = here == 0, here == count - 1
    for x in range(size_x):
        for tile in range(size_y // 8):
            h = streamed(
                post, from_behind, from_ahead, x, tile, size_x, size_y, size_z, at_low, at_high
            )
            for i in range(19):
                advanced[i, x, 8 * tile : 8 * tile + 8, :] = h[i]


def shape(*sizes):
    return jax.ShapeDtypeStruct(sizes, F32)


def call(kernel, out_shape, limit, in_specs=None):
    extra = {} if in_specs is None else {"in_specs": in_specs}
    return pl.pallas_call(
        kernel,
        out_shape=out_shape,
        compiler_params=pltpu.CompilerParams(vmem_limit_bytes=limit * 2**20),
        **extra,
    )


def around(value, axis, steps):
    count = lax.axis_size(axis)
    return lax.ppermute(value, axis, [(i, (i + steps) % count) for i in range(count)])


def local(populations, relax_rates, velocity, velocity_change, fractions, anchor, destination):
    _, size_x, size_y, size_z = populations.shape
    count = lax.axis_size("gy")
    rows = anchor.shape[0]
    sizes = (size_x, size_y, size_z)
    scalars = pl.BlockSpec(memory_space=pltpu.SMEM)
    blocks = pl.BlockSpec(memory_space=pltpu.VMEM)
    column_shape = shape(32, 128)
    table, own, ahead, behind = call(
        pack_kernel, (shape(32, rows), column_shape, column_shape, column_shape), 8
    )(velocity, velocity_change, fractions, anchor[None, :], destination[None, :])
    column = own + around(ahead, "gx", 1) + around(behind, "gx", -1)
    edge_rows = 23 * 2 * size_x
    up, down = call(
        functools.partial(edge_kernel, *sizes), (shape(edge_rows, size_z),) * 2, 8
    )(populations, table)
    from_down = around(up, "gy", 1)
    from_up = around(down, "gy", -1)
    shifts = [0]
    for shift in (1, -1, 2, -2):
        if all((shift - other) % count for other in shifts):
            shifts.append(shift)
    columns = [column] + [around(column, "gy", shift) for shift in shifts[1:]]
    sums, outer = call(
        functools.partial(stay_kernel, *sizes),
        (shape(4, size_x, size_y + 8, size_z), shape(19, size_x, 8, size_z)),
        16,
    )(table, from_up, from_down)
    padded = shape(19, size_x, size_y + 24, size_z)
    post, solid, ahead, behind = call(
        functools.partial(first_kernel, *sizes, count, shifts),
        (
            padded,
            shape(4, size_x, size_y + 8, size_z),
            shape(5, size_y + 8, size_z),
            shape(5, size_y + 8, size_z),
        ),
        24,
        [scalars] + [blocks] * (3 + len(shifts)),
    )(relax_rates, sums, outer, populations, *columns)
    from_behind, from_ahead = around(ahead, "gx", 1), around(behind, "gx", -1)
    later, ahead, behind = call(
        functools.partial(second_kernel, *sizes, count),
        (padded, shape(5, size_y, size_z), shape(5, size_y, size_z)),
        24,
        [scalars] + [blocks] * 4,
    )(relax_rates, post, solid, from_behind, from_ahead)
    from_behind, from_ahead = around(ahead, "gx", 1), around(behind, "gx", -1)
    return call(
        functools.partial(last_kernel, *sizes, count), shape(19, *sizes), 24, [blocks] * 3
    )(later, from_behind, from_ahead)


def solution(mesh):
    placed = (
        P(None, "gx", "gy", None),
        P(),
        P(None, ("gx", "gy")),
        P(None, ("gx", "gy")),
        P(None, ("gx", "gy")),
        P(("gx", "gy")),
        P(("gx", "gy")),
    )
    return jax.shard_map(
        local, mesh=mesh, in_specs=placed, out_specs=P(None, "gx", "gy", None), check_vma=False
    )
```

```python
import functools

import jax
import jax.numpy as jnp
import numpy as np
from jax import lax
from jax.experimental import pallas as pl
from jax.experimental.pallas import tpu as pltpu
from jax.sharding import PartitionSpec as P

CAP = 4
STEPS = 2
LANES = 8 * CAP
F32 = jnp.float32
BF16 = jnp.bfloat16
I32 = jnp.int32


def lattice():
    vectors = [[0, 0, 0]]
    for axis_one in range(3):
        for orient in (1, -1):
            vector_one = [0, 0, 0]
            vector_one[axis_one] = orient
            vectors.append(vector_one)
    for axis_one, axis_two in ((0, 1), (0, 2), (1, 2)):
        for orient in (1, -1):
            for second in (1, -1):
                vector_one = [0, 0, 0]
                vector_one[axis_one] = orient
                vector_one[axis_two] = second
                vectors.append(vector_one)
    integral = np.array(vectors)
    speeds = integral * 1.0
    length = (speeds**2).sum(axis=1)
    weights = np.where(length == 0, 1.0 / 3.0, np.where(length == 1, 1.0 / 18.0, 1.0 / 36.0))
    opposite = [vectors.index([0 - component for component in vector_one]) for vector_one in vectors]
    along_x, along_y, along_z = (speeds[:, 0], speeds[:, 1], speeds[:, 2])
    rows_list = [
        np.ones(19),
        along_x,
        along_y,
        along_z,
        length,
        3 * along_x**2 - length,
        along_y**2 - along_z**2,
        along_x * along_y,
        along_y * along_z,
        along_x * along_z,
        along_x * length,
        along_y * length,
        along_z * length,
        along_x * (along_y**2 - along_z**2),
        along_y * (along_z**2 - along_x**2),
        along_z * (along_x**2 - along_y**2),
        length**2,
        (3 * along_x**2 - length) * length,
        (along_y**2 - along_z**2) * length,
    ]
    basis_rows = []
    for candidate in rows_list:
        for earlier in basis_rows:
            candidate = candidate - np.dot(candidate, earlier) * earlier
        basis_rows.append(candidate / np.sqrt(np.dot(candidate, candidate)))
    return [tuple(v) for v in vectors], weights, opposite, np.array(basis_rows)


VEC, WEIGHTS, OPP, BASIS = lattice()
FORWARD = [i for i in range(19) if VEC[i][0] == 1]
BACKWARD = [i for i in range(19) if VEC[i][0] == -1]


def symmetric_blocks():
    def vec(entries):
        out = np.zeros(19)
        for index, value in entries.items():
            out[index] = value
        return out

    def plane(base):
        s_one, d_one = vec({base: 1, base + 3: 1}), vec({base: 1, base + 3: -1})
        s_two, d_two = vec({base + 1: 1, base + 2: 1}), vec({base + 1: 1, base + 2: -1})
        return s_one + s_two, s_one - s_two, d_one + d_two, d_one - d_two

    rest = vec({0: 1})
    s_x, s_y, s_z = vec({1: 1, 2: 1}), vec({3: 1, 4: 1}), vec({5: 1, 6: 1})
    d_x, d_y, d_z = vec({1: 1, 2: -1}), vec({3: 1, 4: -1}), vec({5: 1, 6: -1})
    xy, q_xy, x_xy, y_xy = plane(7)
    xz, q_xz, x_xz, z_xz = plane(11)
    yz, q_yz, y_yz, z_yz = plane(15)
    blocks = [
        [rest, s_x + s_y + s_z, xy + xz + yz],
        [2 * s_x - s_y - s_z, xy + xz - 2 * yz],
        [s_y - s_z, xy - xz],
        [q_xy],
        [q_xz],
        [q_yz],
        [d_x, x_xy, x_xz],
        [d_y, y_xy, y_yz],
        [d_z, z_xz, z_yz],
    ]
    scales = [[1, 1 / 6, 1 / 12], [1 / 12, 1 / 24], [1 / 4, 1 / 8]]
    scales += [[1 / 4]] * 3 + [[1 / 2, 1 / 4, 1 / 4]] * 3
    forward = np.array([row for block in blocks for row in block])
    back = np.linalg.inv(forward)
    left = forward @ np.diag(1.0 / WEIGHTS) @ BASIS.T
    right = BASIS @ np.diag(WEIGHTS) @ back
    table = []
    start = 0
    for block, scale in zip(blocks, scales):
        size = len(block)
        rows = []
        for a in range(size):
            row = []
            for b in range(size):
                per_rate = -scale[a] * left[start + a, :] * right[:, start + b]
                row.append([(k, float(v)) for k, v in enumerate(per_rate) if abs(v) > 1e-12])
            rows.append(row)
        table.append(rows)
        start += size
    return table


RELAX = symmetric_blocks()


def relax_rows(rates, target):
    values = [rates[k] for k in range(19)]
    at = 0
    for block in RELAX:
        for row in block:
            for terms in row:
                total = None
                for k, factor in terms:
                    part = values[k] * np.float32(factor)
                    total = part if total is None else total + part
                target[at] = jnp.full((8, 128), total, F32)
                at += 1


def relax_blocks(table):
    blocks, at = [], 0
    for block in RELAX:
        rows = []
        for row in block:
            rows.append([table[at + k] for k in range(len(row))])
            at += len(row)
        blocks.append(rows)
    return blocks


ENTRIES = sum(len(row) for block in RELAX for row in block)


def apply_block(block, values):
    out = []
    for row in block:
        total = None
        for factor, value in zip(row, values):
            part = factor * value
            total = part if total is None else total + part
        out.append(total)
    return out


def collide(h, solid, s_x, s_y, s_z, blocks):
    def plane(base):
        s_one, d_one = h[base] + h[base + 3], h[base] - h[base + 3]
        s_two, d_two = h[base + 1] + h[base + 2], h[base + 1] - h[base + 2]
        return s_one + s_two, s_one - s_two, d_one + d_two, d_one - d_two

    sum_x, dif_x = h[1] + h[2], h[1] - h[2]
    sum_y, dif_y = h[3] + h[4], h[3] - h[4]
    sum_z, dif_z = h[5] + h[6], h[5] - h[6]
    xy, q_xy, x_xy, y_xy = plane(7)
    xz, q_xz, x_xz, z_xz = plane(11)
    yz, q_yz, y_yz, z_yz = plane(15)
    axes = sum_x + sum_y + sum_z
    edges = xy + xz + yz
    density = h[0] * (1.0 / 3.0) + axes * (1.0 / 18.0) + edges * (1.0 / 36.0)
    m_x = dif_x * (1.0 / 18.0) + (x_xy + x_xz) * (1.0 / 36.0)
    m_y = dif_y * (1.0 / 18.0) + (y_xy + y_yz) * (1.0 / 36.0)
    m_z = dif_z * (1.0 / 18.0) + (z_xz + z_yz) * (1.0 / 36.0)
    inverse = 1.0 / density
    u_x, u_y, u_z = m_x * inverse, m_y * inverse, m_z * inverse
    e_xx, e_yy, e_zz = m_x * u_x, m_y * u_y, m_z * u_z
    e_xy, e_xz, e_yz = m_x * u_y, m_x * u_z, m_y * u_z
    energy = e_xx + e_yy + e_zz
    turn = e_yy - e_zz
    lean = 3.0 * e_xx - energy
    rest_off = h[0] - density + 1.5 * energy
    axes_off = axes - 6.0 * density
    edges_off = edges - 12.0 * density - 18.0 * energy
    a_one = 3.0 * sum_x - axes - 9.0 * lean
    b_one = edges - 3.0 * yz - 18.0 * lean
    a_two = sum_y - sum_z - 9.0 * turn
    b_two = xy - xz - 18.0 * turn
    q_xy = q_xy - 36.0 * e_xy
    q_xz = q_xz - 36.0 * e_xz
    q_yz = q_yz - 36.0 * e_yz

    r_rest, r_axes, r_edges = apply_block(blocks[0], [rest_off, axes_off, edges_off])
    r_a_one, r_b_one = apply_block(blocks[1], [a_one, b_one])
    r_a_two, r_b_two = apply_block(blocks[2], [a_two, b_two])
    fluid = 1.0 - solid
    mixed = solid * density
    w_x, w_y, w_z = solid * m_x, solid * m_y, solid * m_z
    n_x, n_y, n_z = mixed * s_x, mixed * s_y, mixed * s_z
    p_x = n_x * s_x - solid * e_xx
    p_y = n_y * s_y - solid * e_yy
    p_z = n_z * s_z - solid * e_zz
    total = 1.5 * (p_x + p_y + p_z)
    lean_s = 2.25 * p_x - 0.5 * total
    turn_s = 2.25 * (p_y - p_z)
    rest = fluid * r_rest - total
    axes = fluid * r_axes
    edges = fluid * r_edges + total
    a_one = fluid * r_a_one + lean_s
    b_one = fluid * r_b_one + lean_s
    a_two = fluid * r_a_two + turn_s
    b_two = fluid * r_b_two + turn_s
    q_xy = fluid * apply_block(blocks[3], [q_xy])[0] + 9.0 * (n_x * s_y - solid * e_xy)
    q_xz = fluid * apply_block(blocks[4], [q_xz])[0] + 9.0 * (n_x * s_z - solid * e_xz)
    q_yz = fluid * apply_block(blocks[5], [q_yz])[0] + 9.0 * (n_y * s_z - solid * e_yz)

    def odd(block, axis, one, two, m, n, w):
        six = 6.0 * m
        axis = axis - six
        twelve = six + six
        one = one - twelve
        two = two - twelve
        r_axis, r_one, r_two = apply_block(block, [axis, one, two])
        push = 3.0 * (n - w)
        half = 0.5 * solid
        return (
            fluid * r_axis - solid * axis + push,
            fluid * r_one - half * one + push,
            fluid * r_two - half * two + push,
        )

    d_x, x_xy, x_xz = odd(blocks[6], dif_x, x_xy, x_xz, m_x, n_x, w_x)
    d_y, y_xy, y_yz = odd(blocks[7], dif_y, y_xy, y_yz, m_y, n_y, w_y)
    d_z, z_xz, z_yz = odd(blocks[8], dif_z, z_xz, z_yz, m_z, n_z, w_z)
    out = [None] * 19
    out[0] = h[0] + rest
    even = axes + 2.0 * a_one
    out[1], out[2] = h[1] + (even + d_x), h[2] + (even - d_x)
    base = axes - a_one
    even = base + a_two
    out[3], out[4] = h[3] + (even + d_y), h[4] + (even - d_y)
    even = base - a_two
    out[5], out[6] = h[5] + (even + d_z), h[6] + (even - d_z)

    def spread(start, even, twist, one, two):
        same, cross = even + twist, even - twist
        plus, minus = one + two, one - two
        out[start] = h[start] + (same + plus)
        out[start + 3] = h[start + 3] + (same - plus)
        out[start + 1] = h[start + 1] + (cross + minus)
        out[start + 2] = h[start + 2] + (cross - minus)

    base = edges + b_one
    spread(7, base + b_two, q_xy, x_xy, y_xy)
    spread(11, base - b_two, q_xz, x_xz, z_xz)
    spread(15, edges - 2.0 * b_one, q_yz, y_yz, z_yz)
    return out


def iota(shape, dim):
    return lax.broadcasted_iota(I32, shape, dim)


def cells_of(anchor, size_y, size_z):
    plane = size_y * size_z
    a_x = lax.div(anchor, jnp.int32(plane))
    rest = anchor - a_x * plane
    a_y = lax.div(rest, jnp.int32(size_z))
    return a_x, a_y, rest - a_y * size_z


def halves(value):
    high = value.astype(BF16)
    return high, (value - high.astype(F32)).astype(BF16)


def dot_t(left, right):
    return lax.dot_general(left, right, (((1,), (1,)), ((), ())), preferred_element_type=F32)


def deposited(groups, shares, velocity, a_x, a_y, a_z, size_z, big):
    centre = a_x * big + a_y
    lanes = centre.shape[1]
    totals = None
    rows_z = iota((size_z, lanes), 0)
    for off_z in range(3):
        weights = []
        for rows_x, rows_y in groups:
            away = rows_x * big + rows_y - centre
            weight = jnp.zeros(away.shape, F32)
            for off in range(9):
                move = (off // 3 - 1) * big + off % 3 - 1
                row = 3 * off + off_z
                weight = jnp.where(away == move, shares[row : row + 1, :], weight)
            weights.append([weight] + [weight * velocity[k : k + 1, :] for k in range(3)])
        rows = jnp.concatenate([w for block in weights for w in block], axis=0)
        high, low = halves(rows)
        hot = jnp.where(rows_z == a_z + (off_z - 1), 1.0, 0.0).astype(BF16)
        part = dot_t(high, hot) + dot_t(low, hot)
        totals = part if totals is None else totals + part
    return totals


def pack_kernel(
    velocity_in,
    change_in,
    fractions_in,
    anchor_in,
    destination_in,
    table,
    own,
    ahead,
    behind,
    velocity,
    change,
    fractions,
    anchor,
    destination,
    done,
):
    pairs = (
        (destination_in, destination),
        (velocity_in, velocity),
        (change_in, change),
        (fractions_in, fractions),
        (anchor_in, anchor),
    )
    copies = [pltpu.make_async_copy(a, b, done.at[k]) for k, (a, b) in enumerate(pairs)]
    for copy in copies:
        copy.start()
    rows = destination.shape[1]
    order = jnp.where(iota((128, 128), 0) <= iota((128, 128), 1), 1.0, 0.0).astype(BF16)
    for copy in copies:
        copy.wait()
    dest = destination[...]
    kinds = iota((16, rows), 0)
    hot = jnp.where(dest == kinds, 1.0, 0.0)
    seen = jnp.zeros((16, 1), F32)
    ranks = []
    for start in range(0, rows, 128):
        counted = seen + lax.dot_general(
            hot[:, start : start + 128].astype(BF16),
            order,
            (((1,), (0,)), ((), ())),
            preferred_element_type=F32,
        )
        ranks.append(counted)
        seen = counted[:, 127:128]
    rank = jnp.concatenate(ranks, axis=1)
    kind = iota((16, 1), 0)
    begin = jnp.where(
        kind < 3,
        5 * CAP + CAP * kind,
        jnp.where(kind == 3, 0, jnp.where(kind == 5, CAP, 2 * CAP + CAP * (kind - 6))),
    ).astype(F32)
    leaving = (dest < 9) & (dest != 4)
    slot = jnp.sum(hot * (begin + rank - 1.0), axis=0, keepdims=True)
    slot = jnp.where(leaving, slot, -1.0).astype(I32)
    chosen = jnp.where(iota((128, rows), 0) == slot, 1.0, 0.0).astype(BF16)
    new_velocity = velocity[...] + change[...]
    payload = jnp.concatenate(
        [fractions[...], new_velocity, anchor[...].astype(F32), jnp.zeros((1, rows), F32)], axis=0
    )
    high = payload.astype(BF16)
    middle, low = halves(payload - high.astype(F32))
    packed = dot_t(high, chosen) + dot_t(middle, chosen) + dot_t(low, chosen)
    lane = iota((32, 128), 1)
    own[...] = jnp.where(lane < 2 * CAP, packed, 0.0)
    ahead[...] = jnp.where((lane >= 2 * CAP) & (lane < 5 * CAP), packed, 0.0)
    behind[...] = jnp.where(lane >= 5 * CAP, packed, 0.0)
    table[...] = jnp.where((iota((32, rows), 0) < 27) & (dest != 4), 0.0, payload)


def edge_kernel(size_x, size_y, size_z, populations, table, one, two):
    a_x, a_y, a_z = cells_of(table[30:31, :].astype(I32), size_y, size_z)
    rows = 2 * size_x
    index = iota((rows, 1), 0)
    rows_x, low = lax.div(index, jnp.int32(2)), lax.rem(index, jnp.int32(2))
    sums = deposited(
        [(rows_x, low), (rows_x, low + (size_y - 2))],
        table[0:27, :],
        table[27:30, :],
        a_x,
        a_y,
        a_z,
        size_z,
        8 * size_y,
    )
    first = 19 * rows

    def write(down, up):
        for i in range(19):
            for x in range(size_x):
                at = i * rows + 2 * x
                down[at : at + 2, :] = populations[i, x, 0:2, :]
                up[at : at + 2, :] = populations[i, x, size_y - 2 : size_y, :]
        down[first : first + 4 * rows, :] = sums[: 4 * rows]
        up[first : first + 4 * rows, :] = sums[4 * rows :]

    even = lax.rem(lax.axis_index("gy"), 2) == 0

    @pl.when(even)
    def _():
        write(two, one)

    @pl.when(jnp.logical_not(even))
    def _():
        write(one, two)


def merge_kernel(first, fold, own, from_behind, from_ahead, one_in, two_in, column, one, two):
    del one_in, two_in
    merged = own[...] + from_behind[...] + from_ahead[...]
    column[...] = merged
    deep = 32 // fold
    for k in range(fold):
        for target in (one, two):
            target[first : first + deep, 128 * k : 128 * k + 128] = merged[deep * k : deep * k + deep]


def stay_kernel(size_x, size_y, size_z, rates, table, sums, entries):
    relax_rows(rates, entries)
    a_x, a_y, a_z = cells_of(table[30:31, :].astype(I32), size_y, size_z)
    index = iota((size_x * size_y, 1), 0)
    rows_x = lax.div(index, jnp.int32(size_y))
    totals = deposited(
        [(rows_x, index - rows_x * size_y)],
        table[0:27, :],
        table[27:30, :],
        a_x,
        a_y,
        a_z,
        size_z,
        8 * size_y,
    )
    cells = size_x * size_y
    for c in range(4):
        for x in range(size_x):
            at = c * cells + x * size_y
            sums[c, x, :, :] = totals[at : at + size_y]


def outer_kernel(size_x, size_z, one, two, sums, outer):
    blank = jnp.zeros((8, size_z), F32)
    ones = jnp.ones((8, size_z), F32)
    rows = 2 * size_x

    def write(above, below):
        for c in range(4):
            for x in range(size_x):
                at = (19 + c) * rows + 2 * x
                sums[c, x, :, :] = blank
                sums[c, x, 0:2, :] = above[at : at + 2, :]
                sums[c, x, 6:8, :] = below[at : at + 2, :]
        for i in range(19):
            for x in range(size_x):
                at = i * rows + 2 * x
                outer[i, x, :, :] = ones
                outer[i, x, 0:2, :] = above[at : at + 2, :]
                outer[i, x, 6:8, :] = below[at : at + 2, :]

    even = lax.rem(lax.axis_index("gy"), 2) == 0

    @pl.when(even)
    def _():
        write(one, two)

    @pl.when(jnp.logical_not(even))
    def _():
        write(two, one)


def pair_source(here, parity, count):
    other = jnp.where(lax.rem(here, 2) == parity, here + 1, here - 1)
    return jnp.where((other >= 0) & (other < count), other, here + 2 * count)


def arrivals(size_y, size_z, count, shifts, first, column, one, two, rest):
    here = lax.axis_index("gy")
    fold = size_z // 128
    deep = 32 // fold

    def unfolded(message):
        return jnp.concatenate(
            [message[first : first + deep, 128 * k : 128 * k + 128] for k in range(fold)], axis=0
        )

    parts = [column[...], unfolded(one), unfolded(two)] + [r[...] for r in rest]
    sources = [here, pair_source(here, 0, count), pair_source(here, 1, count)]
    sources += [lax.rem(here - shift + 2 * count, count) for shift in shifts]
    lane = iota((1, 128), 1)
    spot = lax.rem(lane, jnp.int32(LANES))
    group = lax.div(spot, jnp.int32(CAP))
    across = jnp.where(
        (group == 0) | (group == 2) | (group == 5), -1, jnp.where((group == 3) | (group == 6), 0, 1)
    )
    per_group = 128 // LANES
    tables, offsets = [], []
    for start in range(0, len(parts), per_group):
        table = None
        offset = jnp.full((1, 128), 2 * count, I32)
        for k, part in enumerate(parts[start : start + per_group]):
            part = part if k == 0 else pltpu.roll(part, k * LANES, 1)
            table = part if table is None else table + part
            offset = jnp.where(lax.div(lane, jnp.int32(LANES)) == k, sources[start + k] - here, offset)
        tables.append(table)
        offsets.append((offset + across) * size_y)
    table = jnp.concatenate(tables, axis=1)
    a_x, a_y, a_z = cells_of(table[30:31, :].astype(I32), size_y, size_z)
    return table, a_x, a_y + jnp.concatenate(offsets, axis=1), a_z


def store_padded(target, i, x, tile, part, value, tiles):
    lanes = slice(128 * part, 128 * part + 128)
    if tile == tiles:
        target[i, x, 0:8, lanes] = value
        target[i, x, 8 + 8 * tiles : 16 + 8 * tiles, lanes] = value
    else:
        target[i, x, 8 + 8 * tile : 16 + 8 * tile, lanes] = value
        if tile == 0:
            target[i, x, 16 + 8 * tiles : 24 + 8 * tiles, lanes] = value


def turned(value, shift, size_z):
    return value if shift == 0 else pltpu.roll(value, shift % size_z, 1)


def first_kernel(
    size_x, size_y, size_z, count, shifts, first, planes, entries, sums, outer_sums, outer,
    populations, column, one, two, *refs
):
    rest, (post, solid), faces_out = refs[: len(shifts)], refs[len(shifts) : len(shifts) + 2], refs[len(shifts) + 2 :]
    tiles = size_y // 8
    table, a_x, a_y, a_z = arrivals(size_y, size_z, count, shifts, first, column, one, two, rest)
    wide = size_y + 8
    index = iota((len(planes) * wide, 1), 0)
    number = lax.div(index, jnp.int32(wide))
    row = index - number * wide
    rows_x = number + planes[0] if len(planes) == planes[-1] - planes[0] + 1 else number * (size_x - 1)
    rows_y = jnp.where(row < size_y + 2, row, jnp.where(row >= size_y + 6, row - wide, -3 * size_y))
    big = 4 * size_y * (count + 2)
    totals = deposited(
        [(rows_x, rows_y)], table[0:27, :], table[27:30, :], a_x, a_y, a_z, size_z, big
    )
    blocks = relax_blocks(entries)
    cells = len(planes) * wide
    for p, x in enumerate(planes):
        for tile in range(tiles + 1):
            rows = slice(8 * tile, 8 * tile + 8)
            for part in range(size_z // 128):
                lanes = slice(128 * part, 128 * part + 128)
                parts = []
                for c in range(4):
                    at = c * cells + p * wide + 8 * tile
                    staying = outer_sums[c, x, :, lanes] if tile == tiles else sums[c, x, rows, lanes]
                    parts.append(totals[at : at + 8, lanes] + staying)
                scale = 1.0 / (parts[0] + 1e-06)
                share = jnp.minimum(parts[0], 1.0)
                flow = [parts[k] * scale for k in (1, 2, 3)]
                for c, value in enumerate([share] + flow):
                    solid[c, p, rows, lanes] = value
                if tile == tiles:
                    h = [outer[i, x, :, lanes] for i in range(19)]
                else:
                    h = [populations[i, x, rows, lanes] for i in range(19)]
                out = collide(h, share, *flow, blocks)
                for i in range(19):
                    store_padded(post, i, p, tile, part, out[i], tiles)
    if faces_out:
        faces(post, *faces_out, size_y, size_z, True)


def faces(post, ahead, behind, size_y, size_z, outer):
    tiles = size_y // 8
    for target, numbers, p in ((ahead, FORWARD, 1), (behind, BACKWARD, 0)):
        for k, i in enumerate(numbers):
            _, c_y, c_z = VEC[i]
            for tile in range(tiles):
                at = 8 + 8 * tile - c_y
                to = k * size_y + 8 * tile
                target[to : to + 8, :] = turned(post[i, p, at : at + 8, :], c_z, size_z)
            if outer:
                at = 8 + size_y - c_y
                value = turned(post[i, p, at : at + 8, :], c_z, size_z)
                to = 5 * size_y + 2 * k
                target[to : to + 1, :] = value[0:1]
                target[to + 1 : to + 2, :] = value[7:8]


def streamed(ends, middle, message_behind, message_ahead, i, x, tile, size_x, size_y, size_z, walls):
    tiles = size_y // 8
    row = iota((8, size_z), 0)
    c_x, c_y, c_z = VEC[i]

    def plane(x):
        if x == 0:
            return ends, 0
        if x == size_x - 1:
            return ends, 1
        return middle, x - 1

    from_x = x - c_x
    if 0 <= from_x < size_x:
        source, p = plane(from_x)
        at = 8 + 8 * tile - c_y
        value = turned(source[i, p, at : at + 8, :], c_z, size_z)
    else:
        message, numbers = (message_behind, FORWARD) if from_x < 0 else (message_ahead, BACKWARD)
        k = numbers.index(i)
        if tile < tiles:
            at = k * size_y + 8 * tile
            value = message[at : at + 8, :]
        else:
            at = 5 * size_y + 2 * k
            value = jnp.where(row < 4, message[at : at + 1, :], message[at + 1 : at + 2, :])
    source, p = plane(x)
    if c_y == 1 and tile == 0:
        value = jnp.where((row == 0) & walls[0], source[OPP[i], p, 8:16, :], value)
    if c_y == -1 and tile == tiles - 1:
        back = source[OPP[i], p, size_y : 8 + size_y, :]
        value = jnp.where((row == 7) & walls[1], back, value)
    return value


def walls_of(count):
    here = lax.axis_index("gy")
    return here == 0, here == count - 1


def second_kernel(size_x, size_y, size_z, count, planes, entries, ends, middle, solid, *refs):
    refs = list(refs)
    message_behind, message_ahead = (refs.pop(0), refs.pop(0)) if planes[0] == 0 else (None, None)
    later, faces_out = refs[0], refs[1:]
    tiles = size_y // 8
    walls = walls_of(count)
    blocks = relax_blocks(entries)
    for p, x in enumerate(planes):
        for tile in range(tiles + 1):
            rows = slice(8 * tile, 8 * tile + 8)
            h = [
                streamed(
                    ends, middle, message_behind, message_ahead, i, x, tile, size_x, size_y, size_z, walls
                )
                for i in range(19)
            ]
            for part in range(size_z // 128):
                lanes = slice(128 * part, 128 * part + 128)
                s = [solid[c, p, rows, lanes] for c in range(4)]
                out = collide([v[:, lanes] for v in h], *s, blocks)
                for i in range(19):
                    store_padded(later, i, p, tile, part, out[i], tiles)
    if faces_out:
        faces(later, *faces_out, size_y, size_z, False)


def last_kernel(size_x, size_y, size_z, count, ends, middle, advanced, held, done):
    walls = walls_of(count)
    copies = []
    for i in range(19):
        for x in range(size_x):
            if not 0 <= x - VEC[i][0] < size_x:
                continue
            for tile in range(size_y // 8):
                held[i, x, 8 * tile : 8 * tile + 8, :] = streamed(
                    ends, middle, None, None, i, x, tile, size_x, size_y, size_z, walls
                )
        low, high = max(0, VEC[i][0]), size_x + min(0, VEC[i][0])
        copy = pltpu.make_async_copy(
            held.at[i, low:high], advanced.at[i, low:high], done.at[i]
        )
        copy.start()
        copies.append(copy)
    for copy in copies:
        copy.wait()


def enter_kernel(
    size_x, size_y, size_z, count, ends, message_behind, message_ahead, given, advanced, held, done
):
    del given
    walls = walls_of(count)
    copies = []
    for x, numbers in ((0, FORWARD), (size_x - 1, BACKWARD)):
        for i in numbers:
            k = len(copies)
            for tile in range(size_y // 8):
                held[k, 8 * tile : 8 * tile + 8, :] = streamed(
                    ends, None, message_behind, message_ahead, i, x, tile, size_x, size_y, size_z, walls
                )
            copy = pltpu.make_async_copy(held.at[k], advanced.at[i, x], done.at[k])
            copy.start()
            copies.append(copy)
    for copy in copies:
        copy.wait()


def shape(*sizes):
    return jax.ShapeDtypeStruct(sizes, F32)


VMEM = pl.BlockSpec(memory_space=pltpu.VMEM)
SMEM = pl.BlockSpec(memory_space=pltpu.SMEM)
HBM = pl.BlockSpec(memory_space=pltpu.HBM)


def call(kernel, out_shape, limit, in_specs, out_specs=None, scratch=(), aliases=None):
    return pl.pallas_call(
        kernel,
        out_shape=out_shape,
        in_specs=in_specs,
        out_specs=jax.tree.map(lambda _: VMEM, out_shape) if out_specs is None else out_specs,
        scratch_shapes=scratch,
        input_output_aliases={} if aliases is None else aliases,
        compiler_params=pltpu.CompilerParams(vmem_limit_bytes=limit * 2**20),
    )


def around(value, axis, steps):
    count = lax.axis_size(axis)
    return lax.ppermute(value, axis, [(i, (i + steps) % count) for i in range(count)])


def paired(value, axis, parity):
    count = lax.axis_size(axis)
    pairs = []
    for i in range(count):
        other = i + 1 if i % 2 == parity else i - 1
        pairs.append((i, other if 0 <= other < count else i))
    return lax.ppermute(value, axis, pairs)


def local(populations, relax_rates, velocity, velocity_change, fractions, anchor, destination):
    _, size_x, size_y, size_z = populations.shape
    count = lax.axis_size("gy")
    rows = anchor.shape[0]
    sizes = (size_x, size_y, size_z)
    part = functools.partial
    migrants = shape(32, 128)
    table, own, ahead, behind = call(
        pack_kernel,
        (shape(32, rows), migrants, migrants, migrants),
        8,
        [HBM] * 5,
        scratch=[
            pltpu.VMEM((3, rows), F32),
            pltpu.VMEM((3, rows), F32),
            pltpu.VMEM((27, rows), F32),
            pltpu.VMEM((1, rows), I32),
            pltpu.VMEM((1, rows), I32),
            pltpu.SemaphoreType.DMA((5,)),
        ],
    )(velocity, velocity_change, fractions, anchor[None, :], destination[None, :])
    from_behind, from_ahead = around(ahead, "gx", 1), around(behind, "gx", -1)
    first = 23 * 2 * size_x
    fold = size_z // 128
    message = shape(first + 32 // fold, size_z)
    one, two = call(part(edge_kernel, *sizes), (message, message), 8, [VMEM] * 2)(populations, table)
    column, one, two = call(
        part(merge_kernel, first, fold),
        (migrants, message, message),
        8,
        [VMEM] * 5,
        aliases={3: 1, 4: 2},
    )(own, from_behind, from_ahead, one, two)
    shifts = []
    for shift in (2, -2):
        if shift % count > 1 and all((shift - other) % count for other in shifts):
            shifts.append(shift)
    rest = [around(column, "gy", shift) for shift in shifts]
    one, two = paired(one, "gy", 0), paired(two, "gy", 1)
    sums, entries = call(
        part(stay_kernel, *sizes), (shape(4, *sizes), shape(ENTRIES, 8, 128)), 16, [SMEM, VMEM]
    )(relax_rates, table)
    outer_sums, outer = call(
        part(outer_kernel, size_x, size_z),
        (shape(4, size_x, 8, size_z), shape(19, size_x, 8, size_z)),
        8,
        [VMEM] * 2,
    )(one, two)

    def padded(planes):
        return shape(19, planes, size_y + 24, size_z)

    def solids(planes):
        return shape(4, planes, size_y + 8, size_z)

    outside, inside = (0, size_x - 1), tuple(range(1, size_x - 1))
    known = (entries, sums, outer_sums, outer, populations, column, one, two, *rest)
    wide_face = shape((5 * size_y + 10 + 7) // 8 * 8, size_z)
    face = shape(5 * size_y, size_z)
    ends, solid_ends, ahead, behind = call(
        part(first_kernel, *sizes, count, shifts, first, outside),
        (padded(2), solids(2), wide_face, wide_face),
        16,
        [VMEM] * len(known),
    )(*known)
    from_behind, from_ahead = around(ahead, "gx", 1), around(behind, "gx", -1)
    middle, solid_middle = call(
        part(first_kernel, *sizes, count, shifts, first, inside),
        (padded(len(inside)), solids(len(inside))),
        16,
        [VMEM] * len(known),
    )(*known)
    later_middle = call(
        part(second_kernel, *sizes, count, inside), padded(len(inside)), 16, [VMEM] * 4
    )(entries, ends, middle, solid_middle)
    later_ends, ahead, behind = call(
        part(second_kernel, *sizes, count, outside), (padded(2), face, face), 16, [VMEM] * 6
    )(entries, ends, middle, solid_ends, from_behind, from_ahead)
    from_behind, from_ahead = around(ahead, "gx", 1), around(behind, "gx", -1)
    advanced = call(
        part(last_kernel, *sizes, count),
        shape(19, *sizes),
        16,
        [VMEM] * 2,
        HBM,
        [pltpu.VMEM((19, *sizes), F32), pltpu.SemaphoreType.DMA((19,))],
    )(later_ends, later_middle)
    return call(
        part(enter_kernel, *sizes, count),
        shape(19, *sizes),
        16,
        [VMEM] * 3 + [HBM],
        HBM,
        [pltpu.VMEM((10, size_y, size_z), F32), pltpu.SemaphoreType.DMA((10,))],
        {3: 0},
    )(later_ends, from_behind, from_ahead, advanced)


def solution(mesh):
    placed = (
        P(None, "gx", "gy", None),
        P(),
        P(None, ("gx", "gy")),
        P(None, ("gx", "gy")),
        P(None, ("gx", "gy")),
        P(("gx", "gy")),
        P(("gx", "gy")),
    )
    return jax.shard_map(
        local, mesh=mesh, in_specs=placed, out_specs=P(None, "gx", "gy", None), check_vma=False
    )
```

```python
import functools

import jax
import jax.numpy as jnp
import numpy as np
from jax import lax
from jax.experimental import pallas as pl
from jax.experimental.pallas import tpu as pltpu
from jax.sharding import PartitionSpec as P

CAP = 4
STEPS = 2
LANES = 8 * CAP
F32 = jnp.float32
BF16 = jnp.bfloat16
I32 = jnp.int32


def lattice():
    vectors = [[0, 0, 0]]
    for axis_one in range(3):
        for orient in (1, -1):
            vector_one = [0, 0, 0]
            vector_one[axis_one] = orient
            vectors.append(vector_one)
    for axis_one, axis_two in ((0, 1), (0, 2), (1, 2)):
        for orient in (1, -1):
            for second in (1, -1):
                vector_one = [0, 0, 0]
                vector_one[axis_one] = orient
                vector_one[axis_two] = second
                vectors.append(vector_one)
    integral = np.array(vectors)
    speeds = integral * 1.0
    length = (speeds**2).sum(axis=1)
    weights = np.where(length == 0, 1.0 / 3.0, np.where(length == 1, 1.0 / 18.0, 1.0 / 36.0))
    opposite = [vectors.index([0 - component for component in vector_one]) for vector_one in vectors]
    along_x, along_y, along_z = (speeds[:, 0], speeds[:, 1], speeds[:, 2])
    rows_list = [
        np.ones(19),
        along_x,
        along_y,
        along_z,
        length,
        3 * along_x**2 - length,
        along_y**2 - along_z**2,
        along_x * along_y,
        along_y * along_z,
        along_x * along_z,
        along_x * length,
        along_y * length,
        along_z * length,
        along_x * (along_y**2 - along_z**2),
        along_y * (along_z**2 - along_x**2),
        along_z * (along_x**2 - along_y**2),
        length**2,
        (3 * along_x**2 - length) * length,
        (along_y**2 - along_z**2) * length,
    ]
    basis_rows = []
    for candidate in rows_list:
        for earlier in basis_rows:
            candidate = candidate - np.dot(candidate, earlier) * earlier
        basis_rows.append(candidate / np.sqrt(np.dot(candidate, candidate)))
    return [tuple(v) for v in vectors], weights, opposite, np.array(basis_rows)


VEC, WEIGHTS, OPP, BASIS = lattice()
FORWARD = [i for i in range(19) if VEC[i][0] == 1]
BACKWARD = [i for i in range(19) if VEC[i][0] == -1]


def symmetric_blocks():
    def vec(entries):
        out = np.zeros(19)
        for index, value in entries.items():
            out[index] = value
        return out

    def plane(base):
        s_one, d_one = vec({base: 1, base + 3: 1}), vec({base: 1, base + 3: -1})
        s_two, d_two = vec({base + 1: 1, base + 2: 1}), vec({base + 1: 1, base + 2: -1})
        return s_one + s_two, s_one - s_two, d_one + d_two, d_one - d_two

    rest = vec({0: 1})
    s_x, s_y, s_z = vec({1: 1, 2: 1}), vec({3: 1, 4: 1}), vec({5: 1, 6: 1})
    d_x, d_y, d_z = vec({1: 1, 2: -1}), vec({3: 1, 4: -1}), vec({5: 1, 6: -1})
    xy, q_xy, x_xy, y_xy = plane(7)
    xz, q_xz, x_xz, z_xz = plane(11)
    yz, q_yz, y_yz, z_yz = plane(15)
    blocks = [
        [rest, s_x + s_y + s_z, xy + xz + yz],
        [2 * s_x - s_y - s_z, xy + xz - 2 * yz],
        [s_y - s_z, xy - xz],
        [q_xy],
        [q_xz],
        [q_yz],
        [d_x, x_xy, x_xz],
        [d_y, y_xy, y_yz],
        [d_z, z_xz, z_yz],
    ]
    scales = [[1, 1 / 6, 1 / 12], [1 / 12, 1 / 24], [1 / 4, 1 / 8]]
    scales += [[1 / 4]] * 3 + [[1 / 2, 1 / 4, 1 / 4]] * 3
    forward = np.array([row for block in blocks for row in block])
    back = np.linalg.inv(forward)
    left = forward @ np.diag(1.0 / WEIGHTS) @ BASIS.T
    right = BASIS @ np.diag(WEIGHTS) @ back
    table = []
    start = 0
    for block, scale in zip(blocks, scales):
        size = len(block)
        rows = []
        for a in range(size):
            row = []
            for b in range(size):
                per_rate = -scale[a] * left[start + a, :] * right[:, start + b]
                row.append([(k, float(v)) for k, v in enumerate(per_rate) if abs(v) > 1e-12])
            rows.append(row)
        table.append(rows)
        start += size
    return table


RELAX = symmetric_blocks()


def relax_rows(rates, target):
    values = [rates[k] for k in range(19)]
    at = 0
    for block in RELAX:
        for row in block:
            for terms in row:
                total = None
                for k, factor in terms:
                    part = values[k] * np.float32(factor)
                    total = part if total is None else total + part
                target[at] = jnp.full((8, 128), total, F32)
                at += 1


def relax_blocks(table):
    blocks, at = [], 0
    for block in RELAX:
        rows = []
        for row in block:
            rows.append([table[at + k] for k in range(len(row))])
            at += len(row)
        blocks.append(rows)
    return blocks


ENTRIES = sum(len(row) for block in RELAX for row in block)


def apply_block(block, values):
    out = []
    for row in block:
        total = None
        for factor, value in zip(row, values):
            part = factor * value
            total = part if total is None else total + part
        out.append(total)
    return out


def collide(h, solid, s_x, s_y, s_z, blocks):
    def plane(base):
        s_one, d_one = h[base] + h[base + 3], h[base] - h[base + 3]
        s_two, d_two = h[base + 1] + h[base + 2], h[base + 1] - h[base + 2]
        return s_one + s_two, s_one - s_two, d_one + d_two, d_one - d_two

    sum_x, dif_x = h[1] + h[2], h[1] - h[2]
    sum_y, dif_y = h[3] + h[4], h[3] - h[4]
    sum_z, dif_z = h[5] + h[6], h[5] - h[6]
    xy, q_xy, x_xy, y_xy = plane(7)
    xz, q_xz, x_xz, z_xz = plane(11)
    yz, q_yz, y_yz, z_yz = plane(15)
    axes = sum_x + sum_y + sum_z
    edges = xy + xz + yz
    density = h[0] * (1.0 / 3.0) + axes * (1.0 / 18.0) + edges * (1.0 / 36.0)
    m_x = dif_x * (1.0 / 18.0) + (x_xy + x_xz) * (1.0 / 36.0)
    m_y = dif_y * (1.0 / 18.0) + (y_xy + y_yz) * (1.0 / 36.0)
    m_z = dif_z * (1.0 / 18.0) + (z_xz + z_yz) * (1.0 / 36.0)
    inverse = 1.0 / density
    u_x, u_y, u_z = m_x * inverse, m_y * inverse, m_z * inverse
    e_xx, e_yy, e_zz = m_x * u_x, m_y * u_y, m_z * u_z
    e_xy, e_xz, e_yz = m_x * u_y, m_x * u_z, m_y * u_z
    energy = e_xx + e_yy + e_zz
    turn = e_yy - e_zz
    lean = 3.0 * e_xx - energy
    rest_off = h[0] - density + 1.5 * energy
    axes_off = axes - 6.0 * density
    edges_off = edges - 12.0 * density - 18.0 * energy
    a_one = 3.0 * sum_x - axes - 9.0 * lean
    b_one = edges - 3.0 * yz - 18.0 * lean
    a_two = sum_y - sum_z - 9.0 * turn
    b_two = xy - xz - 18.0 * turn
    q_xy = q_xy - 36.0 * e_xy
    q_xz = q_xz - 36.0 * e_xz
    q_yz = q_yz - 36.0 * e_yz

    r_rest, r_axes, r_edges = apply_block(blocks[0], [rest_off, axes_off, edges_off])
    r_a_one, r_b_one = apply_block(blocks[1], [a_one, b_one])
    r_a_two, r_b_two = apply_block(blocks[2], [a_two, b_two])
    fluid = 1.0 - solid
    mixed = solid * density
    w_x, w_y, w_z = solid * m_x, solid * m_y, solid * m_z
    n_x, n_y, n_z = mixed * s_x, mixed * s_y, mixed * s_z
    p_x = n_x * s_x - solid * e_xx
    p_y = n_y * s_y - solid * e_yy
    p_z = n_z * s_z - solid * e_zz
    total = 1.5 * (p_x + p_y + p_z)
    lean_s = 2.25 * p_x - 0.5 * total
    turn_s = 2.25 * (p_y - p_z)
    rest = fluid * r_rest - total
    axes = fluid * r_axes
    edges = fluid * r_edges + total
    a_one = fluid * r_a_one + lean_s
    b_one = fluid * r_b_one + lean_s
    a_two = fluid * r_a_two + turn_s
    b_two = fluid * r_b_two + turn_s
    q_xy = fluid * apply_block(blocks[3], [q_xy])[0] + 9.0 * (n_x * s_y - solid * e_xy)
    q_xz = fluid * apply_block(blocks[4], [q_xz])[0] + 9.0 * (n_x * s_z - solid * e_xz)
    q_yz = fluid * apply_block(blocks[5], [q_yz])[0] + 9.0 * (n_y * s_z - solid * e_yz)

    def odd(block, axis, one, two, m, n, w):
        six = 6.0 * m
        axis = axis - six
        twelve = six + six
        one = one - twelve
        two = two - twelve
        r_axis, r_one, r_two = apply_block(block, [axis, one, two])
        push = 3.0 * (n - w)
        half = 0.5 * solid
        return (
            fluid * r_axis - solid * axis + push,
            fluid * r_one - half * one + push,
            fluid * r_two - half * two + push,
        )

    d_x, x_xy, x_xz = odd(blocks[6], dif_x, x_xy, x_xz, m_x, n_x, w_x)
    d_y, y_xy, y_yz = odd(blocks[7], dif_y, y_xy, y_yz, m_y, n_y, w_y)
    d_z, z_xz, z_yz = odd(blocks[8], dif_z, z_xz, z_yz, m_z, n_z, w_z)
    out = [None] * 19
    out[0] = h[0] + rest
    even = axes + 2.0 * a_one
    out[1], out[2] = h[1] + (even + d_x), h[2] + (even - d_x)
    base = axes - a_one
    even = base + a_two
    out[3], out[4] = h[3] + (even + d_y), h[4] + (even - d_y)
    even = base - a_two
    out[5], out[6] = h[5] + (even + d_z), h[6] + (even - d_z)

    def spread(start, even, twist, one, two):
        same, cross = even + twist, even - twist
        plus, minus = one + two, one - two
        out[start] = h[start] + (same + plus)
        out[start + 3] = h[start + 3] + (same - plus)
        out[start + 1] = h[start + 1] + (cross + minus)
        out[start + 2] = h[start + 2] + (cross - minus)

    base = edges + b_one
    spread(7, base + b_two, q_xy, x_xy, y_xy)
    spread(11, base - b_two, q_xz, x_xz, z_xz)
    spread(15, edges - 2.0 * b_one, q_yz, y_yz, z_yz)
    return out


def iota(shape, dim):
    return lax.broadcasted_iota(I32, shape, dim)


def cells_of(anchor, size_y, size_z):
    plane = size_y * size_z
    a_x = lax.div(anchor, jnp.int32(plane))
    rest = anchor - a_x * plane
    a_y = lax.div(rest, jnp.int32(size_z))
    return a_x, a_y, rest - a_y * size_z


def halves(value):
    high = value.astype(BF16)
    return high, (value - high.astype(F32)).astype(BF16)


def dot_t(left, right):
    return lax.dot_general(left, right, (((1,), (1,)), ((), ())), preferred_element_type=F32)


def deposited(groups, shares, velocity, a_x, a_y, a_z, size_z, big):
    centre = a_x * big + a_y
    lanes = centre.shape[1]
    totals = None
    rows_z = iota((size_z, lanes), 0)
    for off_z in range(3):
        weights = []
        for rows_x, rows_y in groups:
            away = rows_x * big + rows_y - centre
            weight = jnp.zeros(away.shape, F32)
            for off in range(9):
                move = (off // 3 - 1) * big + off % 3 - 1
                row = 3 * off + off_z
                weight = jnp.where(away == move, shares[row : row + 1, :], weight)
            weights.append([weight] + [weight * velocity[k : k + 1, :] for k in range(3)])
        rows = jnp.concatenate([w for block in weights for w in block], axis=0)
        high, low = halves(rows)
        hot = jnp.where(rows_z == a_z + (off_z - 1), 1.0, 0.0).astype(BF16)
        part = dot_t(high, hot) + dot_t(low, hot)
        totals = part if totals is None else totals + part
    return totals


def pack_kernel(
    velocity_in,
    change_in,
    fractions_in,
    anchor_in,
    destination_in,
    table,
    own,
    ahead,
    behind,
    velocity,
    change,
    fractions,
    anchor,
    destination,
    done,
):
    pairs = (
        (destination_in, destination),
        (velocity_in, velocity),
        (change_in, change),
        (fractions_in, fractions),
        (anchor_in, anchor),
    )
    copies = [pltpu.make_async_copy(a, b, done.at[k]) for k, (a, b) in enumerate(pairs)]
    for copy in copies:
        copy.start()
    rows = destination.shape[1]
    order = jnp.where(iota((128, 128), 0) <= iota((128, 128), 1), 1.0, 0.0).astype(BF16)
    for copy in copies:
        copy.wait()
    dest = destination[...]
    kinds = iota((16, rows), 0)
    hot = jnp.where(dest == kinds, 1.0, 0.0)
    seen = jnp.zeros((16, 1), F32)
    ranks = []
    for start in range(0, rows, 128):
        counted = seen + lax.dot_general(
            hot[:, start : start + 128].astype(BF16),
            order,
            (((1,), (0,)), ((), ())),
            preferred_element_type=F32,
        )
        ranks.append(counted)
        seen = counted[:, 127:128]
    rank = jnp.concatenate(ranks, axis=1)
    kind = iota((16, 1), 0)
    begin = jnp.where(
        kind < 3,
        5 * CAP + CAP * kind,
        jnp.where(kind == 3, 0, jnp.where(kind == 5, CAP, 2 * CAP + CAP * (kind - 6))),
    ).astype(F32)
    leaving = (dest < 9) & (dest != 4)
    slot = jnp.sum(hot * (begin + rank - 1.0), axis=0, keepdims=True)
    slot = jnp.where(leaving, slot, -1.0).astype(I32)
    chosen = jnp.where(iota((128, rows), 0) == slot, 1.0, 0.0).astype(BF16)
    new_velocity = velocity[...] + change[...]
    payload = jnp.concatenate(
        [fractions[...], new_velocity, anchor[...].astype(F32), jnp.zeros((1, rows), F32)], axis=0
    )
    high = payload.astype(BF16)
    middle, low = halves(payload - high.astype(F32))
    packed = dot_t(high, chosen) + dot_t(middle, chosen) + dot_t(low, chosen)
    lane = iota((32, 128), 1)
    own[...] = jnp.where(lane < 2 * CAP, packed, 0.0)
    ahead[...] = jnp.where((lane >= 2 * CAP) & (lane < 5 * CAP), packed, 0.0)
    behind[...] = jnp.where(lane >= 5 * CAP, packed, 0.0)
    table[...] = jnp.where((iota((32, rows), 0) < 27) & (dest != 4), 0.0, payload)


def edge_kernel(size_x, size_y, size_z, populations, table, one, two, bottom, top, done):
    copies = (
        pltpu.make_async_copy(populations.at[:, :, 0:8, :], bottom, done.at[0]),
        pltpu.make_async_copy(populations.at[:, :, size_y - 8 : size_y, :], top, done.at[1]),
    )
    for copy in copies:
        copy.start()
    a_x, a_y, a_z = cells_of(table[30:31, :].astype(I32), size_y, size_z)
    rows = 2 * size_x
    index = iota((rows, 1), 0)
    rows_x, low = lax.div(index, jnp.int32(2)), lax.rem(index, jnp.int32(2))
    sums = deposited(
        [(rows_x, low), (rows_x, low + (size_y - 2))],
        table[0:27, :],
        table[27:30, :],
        a_x,
        a_y,
        a_z,
        size_z,
        8 * size_y,
    )
    first = 19 * rows
    for copy in copies:
        copy.wait()

    def write(down, up):
        for i in range(19):
            for x in range(size_x):
                at = i * rows + 2 * x
                down[at : at + 2, :] = bottom[i, x, 0:2, :]
                up[at : at + 2, :] = top[i, x, 6:8, :]
        down[first : first + 4 * rows, :] = sums[: 4 * rows]
        up[first : first + 4 * rows, :] = sums[4 * rows :]

    even = lax.rem(lax.axis_index("gy"), 2) == 0

    @pl.when(even)
    def _():
        write(two, one)

    @pl.when(jnp.logical_not(even))
    def _():
        write(one, two)


def merge_kernel(first, fold, own, from_behind, from_ahead, one_in, two_in, column, one, two):
    del one_in, two_in
    merged = own[...] + from_behind[...] + from_ahead[...]
    column[...] = merged
    deep = 32 // fold
    for k in range(fold):
        for target in (one, two):
            target[first : first + deep, 128 * k : 128 * k + 128] = merged[deep * k : deep * k + deep]


def stay_kernel(size_x, size_y, size_z, rates, table, sums, entries):
    relax_rows(rates, entries)
    a_x, a_y, a_z = cells_of(table[30:31, :].astype(I32), size_y, size_z)
    index = iota((size_x * size_y, 1), 0)
    rows_x = lax.div(index, jnp.int32(size_y))
    totals = deposited(
        [(rows_x, index - rows_x * size_y)],
        table[0:27, :],
        table[27:30, :],
        a_x,
        a_y,
        a_z,
        size_z,
        8 * size_y,
    )
    cells = size_x * size_y
    for c in range(4):
        for x in range(size_x):
            at = c * cells + x * size_y
            sums[c, x, :, :] = totals[at : at + size_y]


def outer_kernel(size_x, size_y, size_z, count, shifts, column, one, two, *refs):
    rest, (sums, outer, migrants) = refs[: len(shifts)], refs[len(shifts) :]
    arrivals(size_x, size_y, size_z, count, shifts, column, one, two, rest, migrants)
    blank = jnp.zeros((8, size_z), F32)
    ones = jnp.ones((8, size_z), F32)
    rows = 2 * size_x

    def write(above, below):
        for c in range(4):
            for x in range(size_x):
                at = (19 + c) * rows + 2 * x
                sums[c, x, :, :] = blank
                sums[c, x, 0:2, :] = above[at : at + 2, :]
                sums[c, x, 6:8, :] = below[at : at + 2, :]
        for i in range(19):
            for x in range(size_x):
                at = i * rows + 2 * x
                outer[i, x, :, :] = ones
                outer[i, x, 0:2, :] = above[at : at + 2, :]
                outer[i, x, 6:8, :] = below[at : at + 2, :]

    even = lax.rem(lax.axis_index("gy"), 2) == 0

    @pl.when(even)
    def _():
        write(one, two)

    @pl.when(jnp.logical_not(even))
    def _():
        write(two, one)


def pair_source(here, parity, count):
    other = jnp.where(lax.rem(here, 2) == parity, here + 1, here - 1)
    return jnp.where((other >= 0) & (other < count), other, here + 2 * count)


def arrivals(size_x, size_y, size_z, count, shifts, column, one, two, rest, migrants):
    first = 23 * 2 * size_x
    here = lax.axis_index("gy")
    fold = size_z // 128
    deep = 32 // fold

    def unfolded(message):
        return jnp.concatenate(
            [message[first : first + deep, 128 * k : 128 * k + 128] for k in range(fold)], axis=0
        )

    parts = [column[...], unfolded(one), unfolded(two)] + [r[...] for r in rest]
    sources = [here, pair_source(here, 0, count), pair_source(here, 1, count)]
    sources += [lax.rem(here - shift + 2 * count, count) for shift in shifts]
    lane = iota((1, 128), 1)
    spot = lax.rem(lane, jnp.int32(LANES))
    group = lax.div(spot, jnp.int32(CAP))
    across = jnp.where(
        (group == 0) | (group == 2) | (group == 5), -1, jnp.where((group == 3) | (group == 6), 0, 1)
    )
    per_group = 128 // LANES
    tables, offsets = [], []
    for start in range(0, len(parts), per_group):
        table = None
        offset = jnp.full((1, 128), 2 * count, I32)
        for k, part in enumerate(parts[start : start + per_group]):
            part = part if k == 0 else pltpu.roll(part, k * LANES, 1)
            table = part if table is None else table + part
            offset = jnp.where(lax.div(lane, jnp.int32(LANES)) == k, sources[start + k] - here, offset)
        tables.append(table)
        offsets.append((offset + across) * size_y)
    table = jnp.concatenate(tables, axis=1)
    a_x, a_y, a_z = cells_of(table[30:31, :].astype(I32), size_y, size_z)
    migrants[0:32, :] = table
    migrants[32:33, :] = a_x.astype(F32)
    migrants[33:34, :] = (a_y + jnp.concatenate(offsets, axis=1)).astype(F32)
    migrants[34:35, :] = a_z.astype(F32)


def store_padded(target, i, x, tile, part, value, tiles):
    lanes = slice(128 * part, 128 * part + 128)
    if tile == tiles:
        target[i, x, 0:8, lanes] = value
        target[i, x, 8 + 8 * tiles : 16 + 8 * tiles, lanes] = value
    else:
        target[i, x, 8 + 8 * tile : 16 + 8 * tile, lanes] = value
        if tile == 0:
            target[i, x, 16 + 8 * tiles : 24 + 8 * tiles, lanes] = value


def turned(value, shift, size_z):
    return value if shift == 0 else pltpu.roll(value, shift % size_z, 1)


def first_kernel(
    size_x, size_y, size_z, count, planes, entries, sums, outer_sums, outer, populations, migrants,
    post, solid, *faces_out
):
    tiles = size_y // 8
    a_x, a_y, a_z = (migrants[k : k + 1, :].astype(I32) for k in (32, 33, 34))
    wide = size_y + 8
    index = iota((len(planes) * wide, 1), 0)
    number = lax.div(index, jnp.int32(wide))
    row = index - number * wide
    rows_x = number + planes[0] if len(planes) == planes[-1] - planes[0] + 1 else number * (size_x - 1)
    rows_y = jnp.where(row < size_y + 2, row, jnp.where(row >= size_y + 6, row - wide, -3 * size_y))
    big = 4 * size_y * (count + 2)
    totals = deposited(
        [(rows_x, rows_y)], migrants[0:27, :], migrants[27:30, :], a_x, a_y, a_z, size_z, big
    )
    blocks = relax_blocks(entries)
    cells = len(planes) * wide
    for p, x in enumerate(planes):
        for tile in range(tiles + 1):
            rows = slice(8 * tile, 8 * tile + 8)
            for part in range(size_z // 128):
                lanes = slice(128 * part, 128 * part + 128)
                parts = []
                for c in range(4):
                    at = c * cells + p * wide + 8 * tile
                    staying = outer_sums[c, x, :, lanes] if tile == tiles else sums[c, x, rows, lanes]
                    parts.append(totals[at : at + 8, lanes] + staying)
                scale = 1.0 / (parts[0] + 1e-06)
                share = jnp.minimum(parts[0], 1.0)
                flow = [parts[k] * scale for k in (1, 2, 3)]
                for c, value in enumerate([share] + flow):
                    solid[c, p, rows, lanes] = value
                if tile == tiles:
                    h = [outer[i, x, :, lanes] for i in range(19)]
                else:
                    h = [populations[i, x, rows, lanes] for i in range(19)]
                out = collide(h, share, *flow, blocks)
                for i in range(19):
                    store_padded(post, i, p, tile, part, out[i], tiles)
    if faces_out:
        faces(post, *faces_out, size_y, size_z, True)


def faces(post, ahead, behind, size_y, size_z, outer):
    tiles = size_y // 8
    for target, numbers, p in ((ahead, FORWARD, 1), (behind, BACKWARD, 0)):
        for k, i in enumerate(numbers):
            _, c_y, c_z = VEC[i]
            for tile in range(tiles):
                at = 8 + 8 * tile - c_y
                to = k * size_y + 8 * tile
                target[to : to + 8, :] = turned(post[i, p, at : at + 8, :], c_z, size_z)
            if outer:
                at = 8 + size_y - c_y
                value = turned(post[i, p, at : at + 8, :], c_z, size_z)
                to = 5 * size_y + 2 * k
                target[to : to + 1, :] = value[0:1]
                target[to + 1 : to + 2, :] = value[7:8]


def streamed(ends, middle, message_behind, message_ahead, i, x, tile, size_x, size_y, size_z, walls):
    tiles = size_y // 8
    row = iota((8, size_z), 0)
    c_x, c_y, c_z = VEC[i]

    def plane(x):
        if x == 0:
            return ends, 0
        if x == size_x - 1:
            return ends, 1
        return middle, x - 1

    from_x = x - c_x
    if 0 <= from_x < size_x:
        source, p = plane(from_x)
        at = 8 + 8 * tile - c_y
        value = turned(source[i, p, at : at + 8, :], c_z, size_z)
    else:
        message, numbers = (message_behind, FORWARD) if from_x < 0 else (message_ahead, BACKWARD)
        k = numbers.index(i)
        if tile < tiles:
            at = k * size_y + 8 * tile
            value = message[at : at + 8, :]
        else:
            at = 5 * size_y + 2 * k
            value = jnp.where(row < 4, message[at : at + 1, :], message[at + 1 : at + 2, :])
    source, p = plane(x)
    if c_y == 1 and tile == 0:
        value = jnp.where((row == 0) & walls[0], source[OPP[i], p, 8:16, :], value)
    if c_y == -1 and tile == tiles - 1:
        back = source[OPP[i], p, size_y : 8 + size_y, :]
        value = jnp.where((row == 7) & walls[1], back, value)
    return value


def walls_of(count):
    here = lax.axis_index("gy")
    return here == 0, here == count - 1


def second_kernel(size_x, size_y, size_z, count, planes, entries, ends, middle, solid, *refs):
    refs = list(refs)
    message_behind, message_ahead = (refs.pop(0), refs.pop(0)) if planes[0] == 0 else (None, None)
    later, faces_out = refs[0], refs[1:]
    tiles = size_y // 8
    walls = walls_of(count)
    blocks = relax_blocks(entries)
    for p, x in enumerate(planes):
        for tile in range(tiles + 1):
            rows = slice(8 * tile, 8 * tile + 8)
            h = [
                streamed(
                    ends, middle, message_behind, message_ahead, i, x, tile, size_x, size_y, size_z, walls
                )
                for i in range(19)
            ]
            for part in range(size_z // 128):
                lanes = slice(128 * part, 128 * part + 128)
                s = [solid[c, p, rows, lanes] for c in range(4)]
                out = collide([v[:, lanes] for v in h], *s, blocks)
                for i in range(19):
                    store_padded(later, i, p, tile, part, out[i], tiles)
    if faces_out:
        faces(later, *faces_out, size_y, size_z, False)


def last_kernel(size_x, size_y, size_z, count, ends, middle, advanced, held, done):
    walls = walls_of(count)
    copies = []
    for i in range(19):
        for x in range(size_x):
            if not 0 <= x - VEC[i][0] < size_x:
                continue
            for tile in range(size_y // 8):
                held[i, x, 8 * tile : 8 * tile + 8, :] = streamed(
                    ends, middle, None, None, i, x, tile, size_x, size_y, size_z, walls
                )
        low, high = max(0, VEC[i][0]), size_x + min(0, VEC[i][0])
        copy = pltpu.make_async_copy(
            held.at[i, low:high], advanced.at[i, low:high], done.at[i]
        )
        copy.start()
        copies.append(copy)
    for copy in copies:
        copy.wait()


def enter_kernel(
    size_x, size_y, size_z, count, ends, message_behind, message_ahead, given, advanced, held, done
):
    del given
    walls = walls_of(count)
    copies = []
    for x, numbers in ((0, FORWARD), (size_x - 1, BACKWARD)):
        for i in numbers:
            k = len(copies)
            for tile in range(size_y // 8):
                held[k, 8 * tile : 8 * tile + 8, :] = streamed(
                    ends, None, message_behind, message_ahead, i, x, tile, size_x, size_y, size_z, walls
                )
            copy = pltpu.make_async_copy(held.at[k], advanced.at[i, x], done.at[k])
            copy.start()
            copies.append(copy)
    for copy in copies:
        copy.wait()


def shape(*sizes):
    return jax.ShapeDtypeStruct(sizes, F32)


VMEM = pl.BlockSpec(memory_space=pltpu.VMEM)
SMEM = pl.BlockSpec(memory_space=pltpu.SMEM)
HBM = pl.BlockSpec(memory_space=pltpu.HBM)


def call(kernel, out_shape, limit, in_specs, out_specs=None, scratch=(), aliases=None):
    return pl.pallas_call(
        kernel,
        out_shape=out_shape,
        in_specs=in_specs,
        out_specs=jax.tree.map(lambda _: VMEM, out_shape) if out_specs is None else out_specs,
        scratch_shapes=scratch,
        input_output_aliases={} if aliases is None else aliases,
        compiler_params=pltpu.CompilerParams(vmem_limit_bytes=limit * 2**20),
    )


def in_hbm(value):
    return pltpu.with_memory_space_constraint(value, pltpu.HBM)


def around(value, axis, steps):
    count = lax.axis_size(axis)
    return lax.ppermute(value, axis, [(i, (i + steps) % count) for i in range(count)])


def paired(value, axis, parity):
    count = lax.axis_size(axis)
    pairs = []
    for i in range(count):
        other = i + 1 if i % 2 == parity else i - 1
        pairs.append((i, other if 0 <= other < count else i))
    return lax.ppermute(value, axis, pairs)


def local(populations, relax_rates, velocity, velocity_change, fractions, anchor, destination):
    _, size_x, size_y, size_z = populations.shape
    count = lax.axis_size("gy")
    rows = anchor.shape[0]
    sizes = (size_x, size_y, size_z)
    part = functools.partial
    packed = shape(32, 128)
    table, own, ahead, behind = call(
        pack_kernel,
        (shape(32, rows), packed, packed, packed),
        8,
        [HBM] * 5,
        scratch=[
            pltpu.VMEM((3, rows), F32),
            pltpu.VMEM((3, rows), F32),
            pltpu.VMEM((27, rows), F32),
            pltpu.VMEM((1, rows), I32),
            pltpu.VMEM((1, rows), I32),
            pltpu.SemaphoreType.DMA((5,)),
        ],
    )(*map(in_hbm, (velocity, velocity_change, fractions, anchor[None, :], destination[None, :])))
    from_behind, from_ahead = around(ahead, "gx", 1), around(behind, "gx", -1)
    first = 23 * 2 * size_x
    fold = size_z // 128
    message = shape(first + 32 // fold, size_z)
    one, two = call(
        part(edge_kernel, *sizes),
        (message, message),
        8,
        [HBM, VMEM],
        scratch=[pltpu.VMEM((19, size_x, 8, size_z), F32)] * 2 + [pltpu.SemaphoreType.DMA((2,))],
    )(in_hbm(populations), table)
    column, one, two = call(
        part(merge_kernel, first, fold),
        (packed, message, message),
        8,
        [VMEM] * 5,
        aliases={3: 1, 4: 2},
    )(own, from_behind, from_ahead, one, two)
    shifts = []
    for shift in (2, -2):
        if shift % count > 1 and all((shift - other) % count for other in shifts):
            shifts.append(shift)
    rest = [around(column, "gy", shift) for shift in shifts]
    one, two = paired(one, "gy", 0), paired(two, "gy", 1)
    sums, entries = call(
        part(stay_kernel, *sizes), (shape(4, *sizes), shape(ENTRIES, 8, 128)), 16, [SMEM, VMEM]
    )(relax_rates, table)
    width = -(-(3 + len(shifts)) * LANES // 128) * 128
    outer_sums, outer, migrants = call(
        part(outer_kernel, *sizes, count, shifts),
        (shape(4, size_x, 8, size_z), shape(19, size_x, 8, size_z), shape(40, width)),
        8,
        [VMEM] * (3 + len(shifts)),
    )(column, one, two, *rest)

    def padded(planes):
        return shape(19, planes, size_y + 24, size_z)

    def solids(planes):
        return shape(4, planes, size_y + 8, size_z)

    outside, inside = (0, size_x - 1), tuple(range(1, size_x - 1))
    known = (entries, sums, outer_sums, outer, populations, migrants)
    wide_face = shape((5 * size_y + 10 + 7) // 8 * 8, size_z)
    face = shape(5 * size_y, size_z)
    ends, solid_ends, ahead, behind = call(
        part(first_kernel, *sizes, count, outside),
        (padded(2), solids(2), wide_face, wide_face),
        16,
        [VMEM] * len(known),
    )(*known)
    from_behind, from_ahead = around(ahead, "gx", 1), around(behind, "gx", -1)
    middle, solid_middle = call(
        part(first_kernel, *sizes, count, inside),
        (padded(len(inside)), solids(len(inside))),
        16,
        [VMEM] * len(known),
    )(*known)
    later_middle = call(
        part(second_kernel, *sizes, count, inside), padded(len(inside)), 16, [VMEM] * 4
    )(entries, ends, middle, solid_middle)
    later_ends, ahead, behind = call(
        part(second_kernel, *sizes, count, outside), (padded(2), face, face), 16, [VMEM] * 6
    )(entries, ends, middle, solid_ends, from_behind, from_ahead)
    from_behind, from_ahead = around(ahead, "gx", 1), around(behind, "gx", -1)
    advanced = call(
        part(last_kernel, *sizes, count),
        shape(19, *sizes),
        16,
        [VMEM] * 2,
        HBM,
        [pltpu.VMEM((19, *sizes), F32), pltpu.SemaphoreType.DMA((19,))],
    )(later_ends, later_middle)
    return call(
        part(enter_kernel, *sizes, count),
        shape(19, *sizes),
        16,
        [VMEM] * 3 + [HBM],
        HBM,
        [pltpu.VMEM((10, size_y, size_z), F32), pltpu.SemaphoreType.DMA((10,))],
        {3: 0},
    )(later_ends, from_behind, from_ahead, advanced)


def solution(mesh):
    placed = (
        P(None, "gx", "gy", None),
        P(),
        P(None, ("gx", "gy")),
        P(None, ("gx", "gy")),
        P(None, ("gx", "gy")),
        P(("gx", "gy")),
        P(("gx", "gy")),
    )
    return jax.shard_map(
        local, mesh=mesh, in_specs=placed, out_specs=P(None, "gx", "gy", None), check_vma=False
    )
```

```python
import functools

import jax
import jax.numpy as jnp
import numpy as np
from jax import lax
from jax.experimental import pallas as pl
from jax.experimental.pallas import tpu as pltpu
from jax.sharding import PartitionSpec as P

CAP = 4
STEPS = 2
LANES = 8 * CAP
F32 = jnp.float32
BF16 = jnp.bfloat16
I32 = jnp.int32


def lattice():
    vectors = [[0, 0, 0]]
    for axis_one in range(3):
        for orient in (1, -1):
            vector_one = [0, 0, 0]
            vector_one[axis_one] = orient
            vectors.append(vector_one)
    for axis_one, axis_two in ((0, 1), (0, 2), (1, 2)):
        for orient in (1, -1):
            for second in (1, -1):
                vector_one = [0, 0, 0]
                vector_one[axis_one] = orient
                vector_one[axis_two] = second
                vectors.append(vector_one)
    integral = np.array(vectors)
    speeds = integral * 1.0
    length = (speeds**2).sum(axis=1)
    weights = np.where(length == 0, 1.0 / 3.0, np.where(length == 1, 1.0 / 18.0, 1.0 / 36.0))
    opposite = [vectors.index([0 - component for component in vector_one]) for vector_one in vectors]
    along_x, along_y, along_z = (speeds[:, 0], speeds[:, 1], speeds[:, 2])
    rows_list = [
        np.ones(19),
        along_x,
        along_y,
        along_z,
        length,
        3 * along_x**2 - length,
        along_y**2 - along_z**2,
        along_x * along_y,
        along_y * along_z,
        along_x * along_z,
        along_x * length,
        along_y * length,
        along_z * length,
        along_x * (along_y**2 - along_z**2),
        along_y * (along_z**2 - along_x**2),
        along_z * (along_x**2 - along_y**2),
        length**2,
        (3 * along_x**2 - length) * length,
        (along_y**2 - along_z**2) * length,
    ]
    basis_rows = []
    for candidate in rows_list:
        for earlier in basis_rows:
            candidate = candidate - np.dot(candidate, earlier) * earlier
        basis_rows.append(candidate / np.sqrt(np.dot(candidate, candidate)))
    return [tuple(v) for v in vectors], weights, opposite, np.array(basis_rows)


VEC, WEIGHTS, OPP, BASIS = lattice()
FORWARD = [i for i in range(19) if VEC[i][0] == 1]
BACKWARD = [i for i in range(19) if VEC[i][0] == -1]
DOWNWARD = [i for i in range(19) if VEC[i][1] == -1]
UPWARD = [OPP[i] for i in DOWNWARD]


def symmetric_blocks():
    def vec(entries):
        out = np.zeros(19)
        for index, value in entries.items():
            out[index] = value
        return out

    def plane(base):
        s_one, d_one = vec({base: 1, base + 3: 1}), vec({base: 1, base + 3: -1})
        s_two, d_two = vec({base + 1: 1, base + 2: 1}), vec({base + 1: 1, base + 2: -1})
        return s_one + s_two, s_one - s_two, d_one + d_two, d_one - d_two

    rest = vec({0: 1})
    s_x, s_y, s_z = vec({1: 1, 2: 1}), vec({3: 1, 4: 1}), vec({5: 1, 6: 1})
    d_x, d_y, d_z = vec({1: 1, 2: -1}), vec({3: 1, 4: -1}), vec({5: 1, 6: -1})
    xy, q_xy, x_xy, y_xy = plane(7)
    xz, q_xz, x_xz, z_xz = plane(11)
    yz, q_yz, y_yz, z_yz = plane(15)
    blocks = [
        [rest, s_x + s_y + s_z, xy + xz + yz],
        [2 * s_x - s_y - s_z, xy + xz - 2 * yz],
        [s_y - s_z, xy - xz],
        [q_xy],
        [q_xz],
        [q_yz],
        [d_x, x_xy, x_xz],
        [d_y, y_xy, y_yz],
        [d_z, z_xz, z_yz],
    ]
    scales = [[1, 1 / 6, 1 / 12], [1 / 12, 1 / 24], [1 / 4, 1 / 8]]
    scales += [[1 / 4]] * 3 + [[1 / 2, 1 / 4, 1 / 4]] * 3
    forward = np.array([row for block in blocks for row in block])
    back = np.linalg.inv(forward)
    left = forward @ np.diag(1.0 / WEIGHTS) @ BASIS.T
    right = BASIS @ np.diag(WEIGHTS) @ back
    table = []
    start = 0
    for block, scale in zip(blocks, scales):
        size = len(block)
        rows = []
        for a in range(size):
            row = []
            for b in range(size):
                per_rate = -scale[a] * left[start + a, :] * right[:, start + b]
                row.append([(k, float(v)) for k, v in enumerate(per_rate) if abs(v) > 1e-12])
            rows.append(row)
        table.append(rows)
        start += size
    return table


RELAX = symmetric_blocks()


def relax_rows(rates, target):
    values = [rates[k] for k in range(19)]
    at = 0
    for block in RELAX:
        for row in block:
            for terms in row:
                total = None
                for k, factor in terms:
                    part = values[k] * np.float32(factor)
                    total = part if total is None else total + part
                target[at] = jnp.full((8, 128), total, F32)
                at += 1


def relax_blocks(table, lanes=128):
    blocks, at = [], 0
    for block in RELAX:
        rows = []
        for row in block:
            rows.append(
                [jnp.concatenate([table[at + k]] * (lanes // 128), axis=1) for k in range(len(row))]
            )
            at += len(row)
        blocks.append(rows)
    return blocks


ENTRIES = sum(len(row) for block in RELAX for row in block)


def apply_block(block, values):
    out = []
    for row in block:
        total = None
        for factor, value in zip(row, values):
            part = factor * value
            total = part if total is None else total + part
        out.append(total)
    return out


def collide(h, solid, s_x, s_y, s_z, blocks):
    def plane(base):
        s_one, d_one = h[base] + h[base + 3], h[base] - h[base + 3]
        s_two, d_two = h[base + 1] + h[base + 2], h[base + 1] - h[base + 2]
        return s_one + s_two, s_one - s_two, d_one + d_two, d_one - d_two

    sum_x, dif_x = h[1] + h[2], h[1] - h[2]
    sum_y, dif_y = h[3] + h[4], h[3] - h[4]
    sum_z, dif_z = h[5] + h[6], h[5] - h[6]
    xy, q_xy, x_xy, y_xy = plane(7)
    xz, q_xz, x_xz, z_xz = plane(11)
    yz, q_yz, y_yz, z_yz = plane(15)
    axes = sum_x + sum_y + sum_z
    edges = xy + xz + yz
    density = h[0] * (1.0 / 3.0) + axes * (1.0 / 18.0) + edges * (1.0 / 36.0)
    m_x = dif_x * (1.0 / 18.0) + (x_xy + x_xz) * (1.0 / 36.0)
    m_y = dif_y * (1.0 / 18.0) + (y_xy + y_yz) * (1.0 / 36.0)
    m_z = dif_z * (1.0 / 18.0) + (z_xz + z_yz) * (1.0 / 36.0)
    inverse = 1.0 / density
    u_x, u_y, u_z = m_x * inverse, m_y * inverse, m_z * inverse
    e_xx, e_yy, e_zz = m_x * u_x, m_y * u_y, m_z * u_z
    e_xy, e_xz, e_yz = m_x * u_y, m_x * u_z, m_y * u_z
    energy = e_xx + e_yy + e_zz
    turn = e_yy - e_zz
    lean = 3.0 * e_xx - energy
    rest_off = h[0] - density + 1.5 * energy
    axes_off = axes - 6.0 * density
    edges_off = edges - 12.0 * density - 18.0 * energy
    a_one = 3.0 * sum_x - axes - 9.0 * lean
    b_one = edges - 3.0 * yz - 18.0 * lean
    a_two = sum_y - sum_z - 9.0 * turn
    b_two = xy - xz - 18.0 * turn
    q_xy = q_xy - 36.0 * e_xy
    q_xz = q_xz - 36.0 * e_xz
    q_yz = q_yz - 36.0 * e_yz

    r_rest, r_axes, r_edges = apply_block(blocks[0], [rest_off, axes_off, edges_off])
    r_a_one, r_b_one = apply_block(blocks[1], [a_one, b_one])
    r_a_two, r_b_two = apply_block(blocks[2], [a_two, b_two])
    fluid = 1.0 - solid
    mixed = solid * density
    w_x, w_y, w_z = solid * m_x, solid * m_y, solid * m_z
    n_x, n_y, n_z = mixed * s_x, mixed * s_y, mixed * s_z
    p_x = n_x * s_x - solid * e_xx
    p_y = n_y * s_y - solid * e_yy
    p_z = n_z * s_z - solid * e_zz
    total = 1.5 * (p_x + p_y + p_z)
    lean_s = 2.25 * p_x - 0.5 * total
    turn_s = 2.25 * (p_y - p_z)
    rest = fluid * r_rest - total
    axes = fluid * r_axes
    edges = fluid * r_edges + total
    a_one = fluid * r_a_one + lean_s
    b_one = fluid * r_b_one + lean_s
    a_two = fluid * r_a_two + turn_s
    b_two = fluid * r_b_two + turn_s
    q_xy = fluid * apply_block(blocks[3], [q_xy])[0] + 9.0 * (n_x * s_y - solid * e_xy)
    q_xz = fluid * apply_block(blocks[4], [q_xz])[0] + 9.0 * (n_x * s_z - solid * e_xz)
    q_yz = fluid * apply_block(blocks[5], [q_yz])[0] + 9.0 * (n_y * s_z - solid * e_yz)

    def odd(block, axis, one, two, m, n, w):
        six = 6.0 * m
        axis = axis - six
        twelve = six + six
        one = one - twelve
        two = two - twelve
        r_axis, r_one, r_two = apply_block(block, [axis, one, two])
        push = 3.0 * (n - w)
        half = 0.5 * solid
        return (
            fluid * r_axis - solid * axis + push,
            fluid * r_one - half * one + push,
            fluid * r_two - half * two + push,
        )

    d_x, x_xy, x_xz = odd(blocks[6], dif_x, x_xy, x_xz, m_x, n_x, w_x)
    d_y, y_xy, y_yz = odd(blocks[7], dif_y, y_xy, y_yz, m_y, n_y, w_y)
    d_z, z_xz, z_yz = odd(blocks[8], dif_z, z_xz, z_yz, m_z, n_z, w_z)
    out = [None] * 19
    out[0] = h[0] + rest
    even = axes + 2.0 * a_one
    out[1], out[2] = h[1] + (even + d_x), h[2] + (even - d_x)
    base = axes - a_one
    even = base + a_two
    out[3], out[4] = h[3] + (even + d_y), h[4] + (even - d_y)
    even = base - a_two
    out[5], out[6] = h[5] + (even + d_z), h[6] + (even - d_z)

    def spread(start, even, twist, one, two):
        same, cross = even + twist, even - twist
        plus, minus = one + two, one - two
        out[start] = h[start] + (same + plus)
        out[start + 3] = h[start + 3] + (same - plus)
        out[start + 1] = h[start + 1] + (cross + minus)
        out[start + 2] = h[start + 2] + (cross - minus)

    base = edges + b_one
    spread(7, base + b_two, q_xy, x_xy, y_xy)
    spread(11, base - b_two, q_xz, x_xz, z_xz)
    spread(15, edges - 2.0 * b_one, q_yz, y_yz, z_yz)
    return out


def equilibrium(density, flow, numbers):
    v_x, v_y, v_z = flow
    rest = 1.0 - 1.5 * (v_x * v_x + v_y * v_y + v_z * v_z)
    out = {}
    for i in numbers:
        if i in out:
            continue
        along = None
        for sign, v in zip(VEC[i], flow):
            if sign:
                part = v if sign == 1 else -v
                along = part if along is None else along + part
        if along is None:
            out[i] = rest
        else:
            along = 3.0 * along
            even = rest + 0.5 * along * along
            out[i], out[OPP[i]] = even + along, even - along
    return out


def fluid_parts(h, blocks, numbers):
    zero = jnp.zeros_like(h[0])
    relaxed = collide(h, zero, zero, zero, zero, blocks)
    density, flow = zero, [zero, zero, zero]
    for i in range(19):
        part = np.float32(WEIGHTS[i]) * h[i]
        density = density + part
        for k in range(3):
            if VEC[i][k]:
                flow[k] = flow[k] + part if VEC[i][k] == 1 else flow[k] - part
    inverse = 1.0 / density
    still = equilibrium(density, [f * inverse for f in flow], numbers)
    bounced = [h[OPP[i]] - density * still[OPP[i]] for i in numbers]
    return [relaxed[i] for i in numbers], bounced, density


def blended(relaxed, bounced, density, share, still):
    return relaxed + share * ((bounced + density * still) - relaxed)


def iota(shape, dim):
    return lax.broadcasted_iota(I32, shape, dim)


def cells_of(anchor, size_y, size_z):
    plane = size_y * size_z
    a_x = lax.div(anchor, jnp.int32(plane))
    rest = anchor - a_x * plane
    a_y = lax.div(rest, jnp.int32(size_z))
    return a_x, a_y, rest - a_y * size_z


def halves(value):
    high = value.astype(BF16)
    return high, (value - high.astype(F32)).astype(BF16)


def dot_t(left, right):
    return lax.dot_general(left, right, (((1,), (1,)), ((), ())), preferred_element_type=F32)


def deposited(groups, shares, velocity, a_x, a_y, a_z, size_z, big):
    centre = a_x * big + a_y
    lanes = centre.shape[1]
    totals = None
    rows_z = iota((size_z, lanes), 0)
    for off_z in range(3):
        weights = []
        for rows_x, rows_y in groups:
            away = rows_x * big + rows_y - centre
            weight = jnp.zeros(away.shape, F32)
            for off in range(9):
                move = (off // 3 - 1) * big + off % 3 - 1
                row = 3 * off + off_z
                weight = jnp.where(away == move, shares[row : row + 1, :], weight)
            weights.append([weight] + [weight * velocity[k : k + 1, :] for k in range(3)])
        rows = jnp.concatenate([w for block in weights for w in block], axis=0)
        high, low = halves(rows)
        hot = jnp.where(rows_z == a_z + (off_z - 1), 1.0, 0.0).astype(BF16)
        part = dot_t(high, hot) + dot_t(low, hot)
        totals = part if totals is None else totals + part
    return totals


def even_x():
    return lax.rem(lax.axis_index("gx"), 2) == 0


def pack_kernel(
    velocity_in,
    change_in,
    fractions_in,
    anchor_in,
    destination_in,
    populations,
    table,
    own,
    near,
    far,
    bottom,
    top,
    velocity,
    change,
    fractions,
    anchor,
    destination,
    done,
):
    pairs = (
        (destination_in, destination),
        (velocity_in, velocity),
        (change_in, change),
        (fractions_in, fractions),
        (anchor_in, anchor),
        (populations.at[:, :, 0:8, :], bottom),
        (populations.at[:, :, populations.shape[2] - 8 :, :], top),
    )
    copies = [pltpu.make_async_copy(a, b, done.at[k]) for k, (a, b) in enumerate(pairs)]
    for copy in copies:
        copy.start()
    rows = destination.shape[1]
    order = jnp.where(iota((128, 128), 0) <= iota((128, 128), 1), 1.0, 0.0).astype(BF16)
    for copy in copies[:5]:
        copy.wait()
    dest = destination[...]
    kinds = iota((16, rows), 0)
    hot = jnp.where(dest == kinds, 1.0, 0.0)
    seen = jnp.zeros((16, 1), F32)
    ranks = []
    for start in range(0, rows, 128):
        counted = seen + lax.dot_general(
            hot[:, start : start + 128].astype(BF16),
            order,
            (((1,), (0,)), ((), ())),
            preferred_element_type=F32,
        )
        ranks.append(counted)
        seen = counted[:, 127:128]
    rank = jnp.concatenate(ranks, axis=1)
    kind = iota((16, 1), 0)
    begin = jnp.where(
        kind < 3,
        5 * CAP + CAP * kind,
        jnp.where(kind == 3, 0, jnp.where(kind == 5, CAP, 2 * CAP + CAP * (kind - 6))),
    ).astype(F32)
    leaving = (dest < 9) & (dest != 4)
    slot = jnp.sum(hot * (begin + rank - 1.0), axis=0, keepdims=True)
    slot = jnp.where(leaving, slot, -1.0).astype(I32)
    chosen = jnp.where(iota((128, rows), 0) == slot, 1.0, 0.0).astype(BF16)
    new_velocity = velocity[...] + change[...]
    payload = jnp.concatenate(
        [fractions[...], new_velocity, anchor[...].astype(F32), jnp.zeros((1, rows), F32)], axis=0
    )
    high = payload.astype(BF16)
    middle, low = halves(payload - high.astype(F32))
    packed = dot_t(high, chosen) + dot_t(middle, chosen) + dot_t(low, chosen)
    lane = iota((32, 128), 1)
    own[...] = jnp.where(lane < 2 * CAP, packed, 0.0)
    ahead = jnp.where((lane >= 2 * CAP) & (lane < 5 * CAP), packed, 0.0)
    behind = jnp.where(lane >= 5 * CAP, packed, 0.0)
    even = even_x()
    near[...] = jnp.where(even, ahead, behind)
    far[...] = jnp.where(even, behind, ahead)
    table[...] = jnp.where((iota((32, rows), 0) < 27) & (dest != 4), 0.0, payload)
    for copy in copies[5:]:
        copy.wait()


def edge_rows(size_x):
    starts = [0]
    for rows in (19 * size_x, 4 * 2 * size_x, 11 * size_x):
        starts.append(starts[-1] + rows)
    return starts


def edge_kernel(size_x, size_y, size_z, bottom, top, table, entries, one, two, held):
    a_x, a_y, a_z = cells_of(table[30:31, :].astype(I32), size_y, size_z)
    rows = 2 * size_x
    index = iota((rows, 1), 0)
    rows_x, low = lax.div(index, jnp.int32(2)), lax.rem(index, jnp.int32(2))
    sums = deposited(
        [(rows_x, low), (rows_x, low + (size_y - 2))],
        table[0:27, :],
        table[27:30, :],
        a_x,
        a_y,
        a_z,
        size_z,
        8 * size_y,
    )
    _, at_sums, at_second, _ = edge_rows(size_x)
    for i in range(19):
        for x in range(size_x):
            held[i, x : x + 1, :] = bottom[i, x, 1:2, :]
            held[i, size_x + x : size_x + x + 1, :] = top[i, x, 6:7, :]
    second = fluid_parts([held[i] for i in range(19)], relax_blocks(entries, size_z), DOWNWARD + UPWARD)
    relaxed, bounced, density = second

    def write(down, up):
        for i in range(19):
            for x in range(size_x):
                at = i * size_x + x
                down[at : at + 1, :] = bottom[i, x, 0:1, :]
                up[at : at + 1, :] = top[i, x, 7:8, :]
        down[at_sums : at_sums + 4 * rows, :] = sums[: 4 * rows]
        up[at_sums : at_sums + 4 * rows, :] = sums[4 * rows :]
        for target, own, at_row in ((down, 0, 0), (up, 5, size_x)):
            parts = relaxed[own : own + 5] + bounced[own : own + 5] + [density]
            for k, value in enumerate(parts):
                at = at_second + k * size_x
                target[at : at + size_x, :] = value[at_row : at_row + size_x]

    even = lax.rem(lax.axis_index("gy"), 2) == 0

    @pl.when(even)
    def _():
        write(two, one)

    @pl.when(jnp.logical_not(even))
    def _():
        write(one, two)


def folded(table):
    return sum(
        table[8 * k : 8 * k + 8] if k == 0 else pltpu.roll(table[8 * k : 8 * k + 8], LANES * k, 1)
        for k in range(4)
    )


def merge_kernel(first, fold, own, far, near, one_in, two_in, column, one, two):
    del one_in, two_in
    merged = folded(own[...] + near[...] + far[...])
    column[...] = merged
    deep = 8 // fold
    for k in range(fold):
        for target in (one, two):
            target[first : first + deep, 128 * k : 128 * k + 128] = merged[deep * k : deep * k + deep]


def relax_kernel(rates, entries):
    relax_rows(rates, entries)


def fluid_kernel(size_x, size_y, size_z, entries, populations, relaxed, bounced, density):
    blocks = relax_blocks(entries)
    for p, x in enumerate((0, size_x - 1)):
        for tile in range(size_y // 8):
            rows = slice(8 * tile, 8 * tile + 8)
            for part in range(size_z // 128):
                lanes = slice(128 * part, 128 * part + 128)
                f, b, d = fluid_parts([populations[i, x, rows, lanes] for i in range(19)], blocks, range(19))
                for i in range(19):
                    relaxed[i, p, rows, lanes] = f[i]
                    bounced[i, p, rows, lanes] = b[i]
                density[p, rows, lanes] = d


def stay_kernel(size_x, size_y, size_z, table, sums):
    a_x, a_y, a_z = cells_of(table[30:31, :].astype(I32), size_y, size_z)
    index = iota((size_x * size_y, 1), 0)
    rows_x = lax.div(index, jnp.int32(size_y))
    totals = deposited(
        [(rows_x, index - rows_x * size_y)],
        table[0:27, :],
        table[27:30, :],
        a_x,
        a_y,
        a_z,
        size_z,
        8 * size_y,
    )
    cells = size_x * size_y
    for c in range(4):
        for x in range(size_x):
            at = c * cells + x * size_y
            sums[c, x, :, :] = totals[at : at + size_y]


def outer_kernel(size_x, size_y, size_z, count, shifts, column, *refs):
    rest, (two, one, sums, outer, second, migrants) = refs[: len(shifts)], refs[len(shifts) :]
    arrivals(size_x, size_y, size_z, count, shifts, column, one, two, rest, migrants)
    blank = jnp.zeros((8, size_z), F32)
    ones = jnp.ones((8, size_z), F32)
    _, at_sums, at_second, _ = edge_rows(size_x)

    def write(above, below):
        for c in range(4):
            for x in range(size_x):
                at = at_sums + c * 2 * size_x + 2 * x
                sums[c, x, :, :] = blank
                sums[c, x, 0:2, :] = above[at : at + 2, :]
                sums[c, x, 6:8, :] = below[at : at + 2, :]
        for i in range(19):
            for x in range(size_x):
                at = i * size_x + x
                outer[i, x, :, :] = ones
                outer[i, x, 0:1, :] = above[at : at + 1, :]
                outer[i, x, 7:8, :] = below[at : at + 1, :]
        for k in range(11):
            for x in range(size_x):
                at = at_second + k * size_x + x
                second[k, x, :, :] = ones
                second[k, x, 1:2, :] = above[at : at + 1, :]
                second[k, x, 6:7, :] = below[at : at + 1, :]

    even = lax.rem(lax.axis_index("gy"), 2) == 0

    @pl.when(even)
    def _():
        write(one, two)

    @pl.when(jnp.logical_not(even))
    def _():
        write(two, one)


def pair_source(here, parity, count):
    other = jnp.where(lax.rem(here, 2) == parity, here + 1, here - 1)
    return jnp.where((other >= 0) & (other < count), other, here + 2 * count)


def arrivals(size_x, size_y, size_z, count, shifts, column, one, two, rest, migrants):
    first = edge_rows(size_x)[-1]
    here = lax.axis_index("gy")
    fold = size_z // 128
    deep = 8 // fold

    def gathered(message):
        return jnp.concatenate(
            [message[first : first + deep, 128 * k : 128 * k + 128] for k in range(fold)], axis=0
        )

    parts = [column[...], gathered(one), gathered(two)] + [r[...] for r in rest]
    sources = [here, pair_source(here, 0, count), pair_source(here, 1, count)]
    sources += [lax.rem(here - shift + 2 * count, count) for shift in shifts]
    lane = iota((1, 128), 1)
    spot = lax.rem(lane, jnp.int32(LANES))
    group = lax.div(spot, jnp.int32(CAP))
    across = jnp.where(
        (group == 0) | (group == 2) | (group == 5), -1, jnp.where((group == 3) | (group == 6), 0, 1)
    )
    per_group = 128 // LANES
    tables, offsets = [], []
    for start in range(0, len(parts), per_group):
        blocks = [jnp.zeros((8, 128), F32)] * 4
        offset = jnp.full((1, 128), 2 * count, I32)
        for k, part in enumerate(parts[start : start + per_group]):
            place = lax.div(lane, jnp.int32(LANES)) == k
            for q in range(4):
                turn = LANES * (k - q) % 128
                blocks[q] = jnp.where(place, part if turn == 0 else pltpu.roll(part, turn, 1), blocks[q])
            offset = jnp.where(lax.div(lane, jnp.int32(LANES)) == k, sources[start + k] - here, offset)
        tables.append(jnp.concatenate(blocks, axis=0))
        offsets.append((offset + across) * size_y)
    table = jnp.concatenate(tables, axis=1)
    a_x, a_y, a_z = cells_of(table[30:31, :].astype(I32), size_y, size_z)
    migrants[0:32, :] = table
    migrants[32:33, :] = a_x.astype(F32)
    migrants[33:34, :] = (a_y + jnp.concatenate(offsets, axis=1)).astype(F32)
    migrants[34:35, :] = a_z.astype(F32)


def store_padded(target, i, x, tile, part, value, tiles):
    lanes = slice(128 * part, 128 * part + 128)
    if tile == tiles:
        target[i, x, 0:8, lanes] = value
        target[i, x, 8 + 8 * tiles : 16 + 8 * tiles, lanes] = value
    else:
        target[i, x, 8 + 8 * tile : 16 + 8 * tile, lanes] = value
        if tile == 0:
            target[i, x, 16 + 8 * tiles : 24 + 8 * tiles, lanes] = value


def turned(value, shift, size_z):
    return value if shift == 0 else pltpu.roll(value, shift % size_z, 1)


def first_kernel(
    size_x, size_y, size_z, count, planes, entries, sums, outer_sums, outer, second, migrants, *refs
):
    prepared = planes[0] == 0
    given, (post, solid, *faces_out) = (refs[:3], refs[3:]) if prepared else (refs[:1], refs[1:])
    tiles = size_y // 8
    a_x, a_y, a_z = (migrants[k : k + 1, :].astype(I32) for k in (32, 33, 34))
    wide = size_y + 8
    index = iota((len(planes) * wide, 1), 0)
    number = lax.div(index, jnp.int32(wide))
    row = index - number * wide
    rows_x = number + planes[0] if len(planes) == planes[-1] - planes[0] + 1 else number * (size_x - 1)
    rows_y = jnp.where(row < size_y + 2, row, jnp.where(row >= size_y + 6, row - wide, -3 * size_y))
    big = 4 * size_y * (count + 2)
    totals = deposited(
        [(rows_x, rows_y)], migrants[0:27, :], migrants[27:30, :], a_x, a_y, a_z, size_z, big
    )
    blocks = relax_blocks(entries)
    cells = len(planes) * wide
    for p, x in enumerate(planes):
        for tile in range(tiles + 1):
            rows = slice(8 * tile, 8 * tile + 8)
            for part in range(size_z // 128):
                lanes = slice(128 * part, 128 * part + 128)
                parts = []
                for c in range(4):
                    at = c * cells + p * wide + 8 * tile
                    staying = outer_sums[c, x, :, lanes] if tile == tiles else sums[c, x, rows, lanes]
                    parts.append(totals[at : at + 8, lanes] + staying)
                scale = 1.0 / (parts[0] + 1e-06)
                share = jnp.minimum(parts[0], 1.0)
                flow = [parts[k] * scale for k in (1, 2, 3)]
                for c, value in enumerate([share] + flow):
                    solid[c, p, rows, lanes] = value
                if tile == tiles:
                    h = [outer[i, x, :, lanes] for i in range(19)]
                    out = collide(h, share, *flow, blocks)
                    line = iota((8, 128), 0)
                    away = jnp.where(line < 4, 1.0, -1.0)
                    still = equilibrium(None, [away * v for v in flow], DOWNWARD)
                    density = second[10, x, :, lanes]
                    for k, (i, j) in enumerate(zip(DOWNWARD, UPWARD)):
                        parts = (second[k, x, :, lanes], second[5 + k, x, :, lanes], density)
                        value = blended(*parts, share, still[i])
                        out[i] = jnp.where(line == 1, value, out[i])
                        out[j] = jnp.where(line == 6, value, out[j])
                elif prepared:
                    relaxed, bounced, dense = given
                    still = equilibrium(None, flow, range(19))
                    density = dense[p, rows, lanes]
                    out = [
                        blended(relaxed[i, p, rows, lanes], bounced[i, p, rows, lanes], density, share, still[i])
                        for i in range(19)
                    ]
                else:
                    h = [given[0][i, x, rows, lanes] for i in range(19)]
                    out = collide(h, share, *flow, blocks)
                for i in range(19):
                    store_padded(post, i, p, tile, part, out[i], tiles)
    if faces_out:
        send_faces(post, *faces_out, size_y, size_z, True)


def send_faces(post, near, far, size_y, size_z, outer):
    even = even_x()

    @pl.when(even)
    def _():
        faces(post, near, far, size_y, size_z, outer)

    @pl.when(jnp.logical_not(even))
    def _():
        faces(post, far, near, size_y, size_z, outer)


def faces(post, ahead, behind, size_y, size_z, outer):
    tiles = size_y // 8
    for target, numbers, p in ((ahead, FORWARD, 1), (behind, BACKWARD, 0)):
        for k, i in enumerate(numbers):
            _, c_y, c_z = VEC[i]
            for tile in range(tiles):
                at = 8 + 8 * tile - c_y
                to = k * size_y + 8 * tile
                target[to : to + 8, :] = turned(post[i, p, at : at + 8, :], c_z, size_z)
            if outer:
                at = 8 + size_y - c_y
                value = turned(post[i, p, at : at + 8, :], c_z, size_z)
                to = 5 * size_y + 2 * k
                target[to : to + 1, :] = value[0:1]
                target[to + 1 : to + 2, :] = value[7:8]


def streamed(ends, middle, messages, i, x, tile, size_x, size_y, size_z, walls):
    tiles = size_y // 8
    row = iota((8, size_z), 0)
    c_x, c_y, c_z = VEC[i]

    def plane(x):
        if x == 0:
            return ends, 0
        if x == size_x - 1:
            return ends, 1
        return middle, x - 1

    from_x = x - c_x
    if 0 <= from_x < size_x:
        source, p = plane(from_x)
        at = 8 + 8 * tile - c_y
        value = turned(source[i, p, at : at + 8, :], c_z, size_z)
    else:
        near, far, even = messages
        from_near, numbers = (jnp.logical_not(even), FORWARD) if from_x < 0 else (even, BACKWARD)
        k = numbers.index(i)

        def received(at, rows):
            return jnp.where(from_near, near[at : at + rows, :], far[at : at + rows, :])

        if tile < tiles:
            value = received(k * size_y + 8 * tile, 8)
        else:
            at = 5 * size_y + 2 * k
            value = jnp.where(row < 4, received(at, 1), received(at + 1, 1))
    source, p = plane(x)
    if c_y == 1 and tile == 0:
        value = jnp.where((row == 0) & walls[0], source[OPP[i], p, 8:16, :], value)
    if c_y == -1 and tile == tiles - 1:
        back = source[OPP[i], p, size_y : 8 + size_y, :]
        value = jnp.where((row == 7) & walls[1], back, value)
    return value


def walls_of(count):
    here = lax.axis_index("gy")
    return here == 0, here == count - 1


def second_kernel(size_x, size_y, size_z, count, planes, entries, ends, middle, solid, *refs):
    refs = list(refs)
    messages = (refs.pop(1), refs.pop(0), even_x()) if planes[0] == 0 else None
    later, faces_out = refs[0], refs[1:]
    tiles = size_y // 8
    walls = walls_of(count)
    blocks = relax_blocks(entries)
    for p, x in enumerate(planes):
        for tile in range(tiles + 1):
            rows = slice(8 * tile, 8 * tile + 8)
            h = [
                streamed(
                    ends, middle, messages, i, x, tile, size_x, size_y, size_z, walls
                )
                for i in range(19)
            ]
            for part in range(size_z // 128):
                lanes = slice(128 * part, 128 * part + 128)
                s = [solid[c, p, rows, lanes] for c in range(4)]
                out = collide([v[:, lanes] for v in h], *s, blocks)
                for i in range(19):
                    store_padded(later, i, p, tile, part, out[i], tiles)
    if faces_out:
        send_faces(later, *faces_out, size_y, size_z, False)


def last_kernel(size_x, size_y, size_z, count, ends, middle, advanced, held, done):
    walls = walls_of(count)
    copies = []
    for i in range(19):
        for x in range(size_x):
            if not 0 <= x - VEC[i][0] < size_x:
                continue
            for tile in range(size_y // 8):
                held[i, x, 8 * tile : 8 * tile + 8, :] = streamed(
                    ends, middle, None, i, x, tile, size_x, size_y, size_z, walls
                )
        low, high = max(0, VEC[i][0]), size_x + min(0, VEC[i][0])
        copy = pltpu.make_async_copy(
            held.at[i, low:high], advanced.at[i, low:high], done.at[i]
        )
        copy.start()
        copies.append(copy)
    for copy in copies:
        copy.wait()


def enter_kernel(
    size_x, size_y, size_z, count, ends, far, near, given, advanced, held, done
):
    del given
    messages = (near, far, even_x())
    walls = walls_of(count)
    copies = []
    for x, numbers in ((0, FORWARD), (size_x - 1, BACKWARD)):
        for i in numbers:
            k = len(copies)
            for tile in range(size_y // 8):
                held[k, 8 * tile : 8 * tile + 8, :] = streamed(
                    ends, None, messages, i, x, tile, size_x, size_y, size_z, walls
                )
            copy = pltpu.make_async_copy(held.at[k], advanced.at[i, x], done.at[k])
            copy.start()
            copies.append(copy)
    for copy in copies:
        copy.wait()


def shape(*sizes):
    return jax.ShapeDtypeStruct(sizes, F32)


VMEM = pl.BlockSpec(memory_space=pltpu.VMEM)
SMEM = pl.BlockSpec(memory_space=pltpu.SMEM)
HBM = pl.BlockSpec(memory_space=pltpu.HBM)


def call(kernel, out_shape, limit, in_specs, out_specs=None, scratch=(), aliases=None):
    return pl.pallas_call(
        kernel,
        out_shape=out_shape,
        in_specs=in_specs,
        out_specs=jax.tree.map(lambda _: VMEM, out_shape) if out_specs is None else out_specs,
        scratch_shapes=scratch,
        input_output_aliases={} if aliases is None else aliases,
        compiler_params=pltpu.CompilerParams(vmem_limit_bytes=limit * 2**20),
    )


def in_hbm(value):
    return pltpu.with_memory_space_constraint(value, pltpu.HBM)


def around(value, axis, steps):
    count = lax.axis_size(axis)
    return lax.ppermute(value, axis, [(i, (i + steps) % count) for i in range(count)])


def paired(value, axis, parity, wrap=False):
    count = lax.axis_size(axis)
    if wrap and count % 2:
        raise ValueError("odd ring")
    pairs = []
    for i in range(count):
        other = i + 1 if i % 2 == parity else i - 1
        other = other % count if wrap else other
        pairs.append((i, other if 0 <= other < count else i))
    return lax.ppermute(value, axis, pairs)


def exchanged(near, far):
    far = paired(far, "gx", 1, True)
    return paired(near, "gx", 0, True), far


def local(populations, relax_rates, velocity, velocity_change, fractions, anchor, destination):
    _, size_x, size_y, size_z = populations.shape
    count = lax.axis_size("gy")
    rows = anchor.shape[0]
    sizes = (size_x, size_y, size_z)
    part = functools.partial
    packed = shape(32, 128)
    band = shape(19, size_x, 8, size_z)
    table, own, near, far, bottom, top = call(
        pack_kernel,
        (shape(32, rows), packed, packed, packed, band, band),
        8,
        [HBM] * 6,
        scratch=[
            pltpu.VMEM((3, rows), F32),
            pltpu.VMEM((3, rows), F32),
            pltpu.VMEM((27, rows), F32),
            pltpu.VMEM((1, rows), I32),
            pltpu.VMEM((1, rows), I32),
            pltpu.SemaphoreType.DMA((7,)),
        ],
    )(*map(in_hbm, (velocity, velocity_change, fractions, anchor[None, :], destination[None, :], populations)))
    near, far = exchanged(near, far)
    first = edge_rows(size_x)[-1]
    fold = size_z // 128
    message = shape(-(-(first + 8 // fold) // 8) * 8, size_z)
    entries = call(relax_kernel, shape(ENTRIES, 8, 128), 8, [SMEM])(relax_rates)
    one, two = call(
        part(edge_kernel, *sizes),
        (message, message),
        8,
        [VMEM] * 4,
        scratch=[pltpu.VMEM((19, 2 * size_x, size_z), F32)],
    )(bottom, top, table, entries)
    column, one, two = call(
        part(merge_kernel, first, fold),
        (shape(8, 128), message, message),
        8,
        [VMEM] * 5,
        aliases={3: 1, 4: 2},
    )(own, far, near, one, two)
    shifts = []
    for shift in (2, -2):
        if shift % count > 1 and all((shift - other) % count for other in shifts):
            shifts.append(shift)
    rest = [around(column, "gy", shift) for shift in shifts]
    one, two = paired(one, "gy", 0), paired(two, "gy", 1)
    sums = call(part(stay_kernel, *sizes), shape(4, *sizes), 16, [VMEM])(table)
    plane_pair = shape(19, 2, size_y, size_z)
    parts = call(
        part(fluid_kernel, *sizes), (plane_pair, plane_pair, shape(2, size_y, size_z)), 16, [VMEM] * 2
    )(entries, populations)
    width = -(-(3 + len(shifts)) * LANES // 128) * 128
    outer_sums, outer, second, migrants = call(
        part(outer_kernel, *sizes, count, shifts),
        (
            shape(4, size_x, 8, size_z),
            shape(19, size_x, 8, size_z),
            shape(11, size_x, 8, size_z),
            shape(40, width),
        ),
        8,
        [VMEM] * (3 + len(shifts)),
    )(column, *rest, two, one)

    def padded(planes):
        return shape(19, planes, size_y + 24, size_z)

    def solids(planes):
        return shape(4, planes, size_y + 8, size_z)

    outside, inside = (0, size_x - 1), tuple(range(1, size_x - 1))
    known = (entries, sums, outer_sums, outer, second, migrants)
    wide_face = shape((5 * size_y + 10 + 7) // 8 * 8, size_z)
    face = shape(5 * size_y, size_z)
    ends, solid_ends, near, far = call(
        part(first_kernel, *sizes, count, outside),
        (padded(2), solids(2), wide_face, wide_face),
        16,
        [VMEM] * (len(known) + 3),
    )(*known, *parts)
    near, far = exchanged(near, far)
    middle, solid_middle = call(
        part(first_kernel, *sizes, count, inside),
        (padded(len(inside)), solids(len(inside))),
        16,
        [VMEM] * (len(known) + 1),
    )(*known, populations)
    later_middle = call(
        part(second_kernel, *sizes, count, inside), padded(len(inside)), 16, [VMEM] * 4
    )(entries, ends, middle, solid_middle)
    later_ends, near, far = call(
        part(second_kernel, *sizes, count, outside), (padded(2), face, face), 16, [VMEM] * 6
    )(entries, ends, middle, solid_ends, far, near)
    near, far = exchanged(near, far)
    advanced = call(
        part(last_kernel, *sizes, count),
        shape(19, *sizes),
        16,
        [VMEM] * 2,
        HBM,
        [pltpu.VMEM((19, *sizes), F32), pltpu.SemaphoreType.DMA((19,))],
    )(later_ends, later_middle)
    return call(
        part(enter_kernel, *sizes, count),
        shape(19, *sizes),
        16,
        [VMEM] * 3 + [HBM],
        HBM,
        [pltpu.VMEM((10, size_y, size_z), F32), pltpu.SemaphoreType.DMA((10,))],
        {3: 0},
    )(later_ends, far, near, advanced)


def solution(mesh):
    placed = (
        P(None, "gx", "gy", None),
        P(),
        P(None, ("gx", "gy")),
        P(None, ("gx", "gy")),
        P(None, ("gx", "gy")),
        P(("gx", "gy")),
        P(("gx", "gy")),
    )
    return jax.shard_map(
        local, mesh=mesh, in_specs=placed, out_specs=P(None, "gx", "gy", None), check_vma=False
    )
```

```python
import functools

import jax
import jax.numpy as jnp
import numpy as np
from jax import lax
from jax.experimental import pallas as pl
from jax.experimental.pallas import tpu as pltpu
from jax.sharding import PartitionSpec as P

CAP = 4
STEPS = 2
LANES = 8 * CAP
F32 = jnp.float32
BF16 = jnp.bfloat16
I32 = jnp.int32


def lattice():
    vectors = [[0, 0, 0]]
    for axis_one in range(3):
        for orient in (1, -1):
            vector_one = [0, 0, 0]
            vector_one[axis_one] = orient
            vectors.append(vector_one)
    for axis_one, axis_two in ((0, 1), (0, 2), (1, 2)):
        for orient in (1, -1):
            for second in (1, -1):
                vector_one = [0, 0, 0]
                vector_one[axis_one] = orient
                vector_one[axis_two] = second
                vectors.append(vector_one)
    integral = np.array(vectors)
    speeds = integral * 1.0
    length = (speeds**2).sum(axis=1)
    weights = np.where(length == 0, 1.0 / 3.0, np.where(length == 1, 1.0 / 18.0, 1.0 / 36.0))
    opposite = [vectors.index([0 - component for component in vector_one]) for vector_one in vectors]
    along_x, along_y, along_z = (speeds[:, 0], speeds[:, 1], speeds[:, 2])
    rows_list = [
        np.ones(19),
        along_x,
        along_y,
        along_z,
        length,
        3 * along_x**2 - length,
        along_y**2 - along_z**2,
        along_x * along_y,
        along_y * along_z,
        along_x * along_z,
        along_x * length,
        along_y * length,
        along_z * length,
        along_x * (along_y**2 - along_z**2),
        along_y * (along_z**2 - along_x**2),
        along_z * (along_x**2 - along_y**2),
        length**2,
        (3 * along_x**2 - length) * length,
        (along_y**2 - along_z**2) * length,
    ]
    basis_rows = []
    for candidate in rows_list:
        for earlier in basis_rows:
            candidate = candidate - np.dot(candidate, earlier) * earlier
        basis_rows.append(candidate / np.sqrt(np.dot(candidate, candidate)))
    return [tuple(v) for v in vectors], weights, opposite, np.array(basis_rows)


VEC, WEIGHTS, OPP, BASIS = lattice()
FORWARD = [i for i in range(19) if VEC[i][0] == 1]
BACKWARD = [i for i in range(19) if VEC[i][0] == -1]
DOWNWARD = [i for i in range(19) if VEC[i][1] == -1]
UPWARD = [OPP[i] for i in DOWNWARD]


def symmetric_blocks():
    def vec(entries):
        out = np.zeros(19)
        for index, value in entries.items():
            out[index] = value
        return out

    def plane(base):
        s_one, d_one = vec({base: 1, base + 3: 1}), vec({base: 1, base + 3: -1})
        s_two, d_two = vec({base + 1: 1, base + 2: 1}), vec({base + 1: 1, base + 2: -1})
        return s_one + s_two, s_one - s_two, d_one + d_two, d_one - d_two

    rest = vec({0: 1})
    s_x, s_y, s_z = vec({1: 1, 2: 1}), vec({3: 1, 4: 1}), vec({5: 1, 6: 1})
    d_x, d_y, d_z = vec({1: 1, 2: -1}), vec({3: 1, 4: -1}), vec({5: 1, 6: -1})
    xy, q_xy, x_xy, y_xy = plane(7)
    xz, q_xz, x_xz, z_xz = plane(11)
    yz, q_yz, y_yz, z_yz = plane(15)
    blocks = [
        [rest, s_x + s_y + s_z, xy + xz + yz],
        [2 * s_x - s_y - s_z, xy + xz - 2 * yz],
        [s_y - s_z, xy - xz],
        [q_xy],
        [q_xz],
        [q_yz],
        [d_x, x_xy, x_xz],
        [d_y, y_xy, y_yz],
        [d_z, z_xz, z_yz],
    ]
    scales = [[1, 1 / 6, 1 / 12], [1 / 12, 1 / 24], [1 / 4, 1 / 8]]
    scales += [[1 / 4]] * 3 + [[1 / 2, 1 / 4, 1 / 4]] * 3
    forward = np.array([row for block in blocks for row in block])
    back = np.linalg.inv(forward)
    left = forward @ np.diag(1.0 / WEIGHTS) @ BASIS.T
    right = BASIS @ np.diag(WEIGHTS) @ back
    table = []
    start = 0
    for block, scale in zip(blocks, scales):
        size = len(block)
        rows = []
        for a in range(size):
            row = []
            for b in range(size):
                per_rate = -scale[a] * left[start + a, :] * right[:, start + b]
                row.append([(k, float(v)) for k, v in enumerate(per_rate) if abs(v) > 1e-12])
            rows.append(row)
        table.append(rows)
        start += size
    return table


RELAX = symmetric_blocks()


def relax_rows(rates, target):
    values = [rates[k] for k in range(19)]
    at = 0
    for block in RELAX:
        for row in block:
            for terms in row:
                total = None
                for k, factor in terms:
                    part = values[k] * np.float32(factor)
                    total = part if total is None else total + part
                target[at] = jnp.full((8, 128), total, F32)
                at += 1


def relax_blocks(table, lanes=128):
    blocks, at = [], 0
    for block in RELAX:
        rows = []
        for row in block:
            rows.append(
                [jnp.concatenate([table[at + k]] * (lanes // 128), axis=1) for k in range(len(row))]
            )
            at += len(row)
        blocks.append(rows)
    return blocks


ENTRIES = sum(len(row) for block in RELAX for row in block)


def apply_block(block, values):
    out = []
    for row in block:
        total = None
        for factor, value in zip(row, values):
            part = factor * value
            total = part if total is None else total + part
        out.append(total)
    return out


def collide(h, solid, s_x, s_y, s_z, blocks):
    def plane(base):
        s_one, d_one = h[base] + h[base + 3], h[base] - h[base + 3]
        s_two, d_two = h[base + 1] + h[base + 2], h[base + 1] - h[base + 2]
        return s_one + s_two, s_one - s_two, d_one + d_two, d_one - d_two

    sum_x, dif_x = h[1] + h[2], h[1] - h[2]
    sum_y, dif_y = h[3] + h[4], h[3] - h[4]
    sum_z, dif_z = h[5] + h[6], h[5] - h[6]
    xy, q_xy, x_xy, y_xy = plane(7)
    xz, q_xz, x_xz, z_xz = plane(11)
    yz, q_yz, y_yz, z_yz = plane(15)
    axes = sum_x + sum_y + sum_z
    edges = xy + xz + yz
    density = h[0] * (1.0 / 3.0) + axes * (1.0 / 18.0) + edges * (1.0 / 36.0)
    m_x = dif_x * (1.0 / 18.0) + (x_xy + x_xz) * (1.0 / 36.0)
    m_y = dif_y * (1.0 / 18.0) + (y_xy + y_yz) * (1.0 / 36.0)
    m_z = dif_z * (1.0 / 18.0) + (z_xz + z_yz) * (1.0 / 36.0)
    inverse = 1.0 / density
    u_x, u_y, u_z = m_x * inverse, m_y * inverse, m_z * inverse
    e_xx, e_yy, e_zz = m_x * u_x, m_y * u_y, m_z * u_z
    e_xy, e_xz, e_yz = m_x * u_y, m_x * u_z, m_y * u_z
    energy = e_xx + e_yy + e_zz
    turn = e_yy - e_zz
    lean = 3.0 * e_xx - energy
    rest_off = h[0] - density + 1.5 * energy
    axes_off = axes - 6.0 * density
    edges_off = edges - 12.0 * density - 18.0 * energy
    a_one = 3.0 * sum_x - axes - 9.0 * lean
    b_one = edges - 3.0 * yz - 18.0 * lean
    a_two = sum_y - sum_z - 9.0 * turn
    b_two = xy - xz - 18.0 * turn
    q_xy = q_xy - 36.0 * e_xy
    q_xz = q_xz - 36.0 * e_xz
    q_yz = q_yz - 36.0 * e_yz

    r_rest, r_axes, r_edges = apply_block(blocks[0], [rest_off, axes_off, edges_off])
    r_a_one, r_b_one = apply_block(blocks[1], [a_one, b_one])
    r_a_two, r_b_two = apply_block(blocks[2], [a_two, b_two])
    fluid = 1.0 - solid
    mixed = solid * density
    w_x, w_y, w_z = solid * m_x, solid * m_y, solid * m_z
    n_x, n_y, n_z = mixed * s_x, mixed * s_y, mixed * s_z
    p_x = n_x * s_x - solid * e_xx
    p_y = n_y * s_y - solid * e_yy
    p_z = n_z * s_z - solid * e_zz
    total = 1.5 * (p_x + p_y + p_z)
    lean_s = 2.25 * p_x - 0.5 * total
    turn_s = 2.25 * (p_y - p_z)
    rest = fluid * r_rest - total
    axes = fluid * r_axes
    edges = fluid * r_edges + total
    a_one = fluid * r_a_one + lean_s
    b_one = fluid * r_b_one + lean_s
    a_two = fluid * r_a_two + turn_s
    b_two = fluid * r_b_two + turn_s
    q_xy = fluid * apply_block(blocks[3], [q_xy])[0] + 9.0 * (n_x * s_y - solid * e_xy)
    q_xz = fluid * apply_block(blocks[4], [q_xz])[0] + 9.0 * (n_x * s_z - solid * e_xz)
    q_yz = fluid * apply_block(blocks[5], [q_yz])[0] + 9.0 * (n_y * s_z - solid * e_yz)

    def odd(block, axis, one, two, m, n, w):
        six = 6.0 * m
        axis = axis - six
        twelve = six + six
        one = one - twelve
        two = two - twelve
        r_axis, r_one, r_two = apply_block(block, [axis, one, two])
        push = 3.0 * (n - w)
        half = 0.5 * solid
        return (
            fluid * r_axis - solid * axis + push,
            fluid * r_one - half * one + push,
            fluid * r_two - half * two + push,
        )

    d_x, x_xy, x_xz = odd(blocks[6], dif_x, x_xy, x_xz, m_x, n_x, w_x)
    d_y, y_xy, y_yz = odd(blocks[7], dif_y, y_xy, y_yz, m_y, n_y, w_y)
    d_z, z_xz, z_yz = odd(blocks[8], dif_z, z_xz, z_yz, m_z, n_z, w_z)
    out = [None] * 19
    out[0] = h[0] + rest
    even = axes + 2.0 * a_one
    out[1], out[2] = h[1] + (even + d_x), h[2] + (even - d_x)
    base = axes - a_one
    even = base + a_two
    out[3], out[4] = h[3] + (even + d_y), h[4] + (even - d_y)
    even = base - a_two
    out[5], out[6] = h[5] + (even + d_z), h[6] + (even - d_z)

    def spread(start, even, twist, one, two):
        same, cross = even + twist, even - twist
        plus, minus = one + two, one - two
        out[start] = h[start] + (same + plus)
        out[start + 3] = h[start + 3] + (same - plus)
        out[start + 1] = h[start + 1] + (cross + minus)
        out[start + 2] = h[start + 2] + (cross - minus)

    base = edges + b_one
    spread(7, base + b_two, q_xy, x_xy, y_xy)
    spread(11, base - b_two, q_xz, x_xz, z_xz)
    spread(15, edges - 2.0 * b_one, q_yz, y_yz, z_yz)
    return out


def equilibrium(density, flow, numbers):
    v_x, v_y, v_z = flow
    rest = 1.0 - 1.5 * (v_x * v_x + v_y * v_y + v_z * v_z)
    out = {}
    for i in numbers:
        if i in out:
            continue
        along = None
        for sign, v in zip(VEC[i], flow):
            if sign:
                part = v if sign == 1 else -v
                along = part if along is None else along + part
        if along is None:
            out[i] = rest
        else:
            along = 3.0 * along
            even = rest + 0.5 * along * along
            out[i], out[OPP[i]] = even + along, even - along
    return out


def fluid_parts(h, blocks, numbers):
    zero = jnp.zeros_like(h[0])
    relaxed = collide(h, zero, zero, zero, zero, blocks)
    density, flow = zero, [zero, zero, zero]
    for i in range(19):
        part = np.float32(WEIGHTS[i]) * h[i]
        density = density + part
        for k in range(3):
            if VEC[i][k]:
                flow[k] = flow[k] + part if VEC[i][k] == 1 else flow[k] - part
    inverse = 1.0 / density
    still = equilibrium(density, [f * inverse for f in flow], numbers)
    bounced = [h[OPP[i]] - density * still[OPP[i]] for i in numbers]
    return [relaxed[i] for i in numbers], bounced, density


def blended(relaxed, bounced, density, share, still):
    return relaxed + share * ((bounced + density * still) - relaxed)


def iota(shape, dim):
    return lax.broadcasted_iota(I32, shape, dim)


def cells_of(anchor, size_y, size_z):
    plane = size_y * size_z
    a_x = lax.div(anchor, jnp.int32(plane))
    rest = anchor - a_x * plane
    a_y = lax.div(rest, jnp.int32(size_z))
    return a_x, a_y, rest - a_y * size_z


def halves(value):
    high = value.astype(BF16)
    return high, (value - high.astype(F32)).astype(BF16)


def dot_t(left, right):
    return lax.dot_general(left, right, (((1,), (1,)), ((), ())), preferred_element_type=F32)


def deposited(groups, shares, velocity, a_x, a_y, a_z, size_z, big):
    centre = a_x * big + a_y
    lanes = centre.shape[1]
    totals = None
    rows_z = iota((size_z, lanes), 0)
    for off_z in range(3):
        weights = []
        for rows_x, rows_y in groups:
            away = rows_x * big + rows_y - centre
            weight = jnp.zeros(away.shape, F32)
            for off in range(9):
                move = (off // 3 - 1) * big + off % 3 - 1
                row = 3 * off + off_z
                weight = jnp.where(away == move, shares[row : row + 1, :], weight)
            weights.append([weight] + [weight * velocity[k : k + 1, :] for k in range(3)])
        rows = jnp.concatenate([w for block in weights for w in block], axis=0)
        high, low = halves(rows)
        hot = jnp.where(rows_z == a_z + (off_z - 1), 1.0, 0.0).astype(BF16)
        part = dot_t(high, hot) + dot_t(low, hot)
        totals = part if totals is None else totals + part
    return totals


def even_x():
    return lax.rem(lax.axis_index("gx"), 2) == 0


def pack_kernel(
    velocity_in,
    change_in,
    fractions_in,
    anchor_in,
    destination_in,
    populations,
    table,
    own,
    near,
    far,
    bottom,
    top,
    velocity,
    change,
    fractions,
    anchor,
    destination,
    done,
):
    pairs = (
        (destination_in, destination),
        (velocity_in, velocity),
        (change_in, change),
        (fractions_in, fractions),
        (anchor_in, anchor),
        (populations.at[:, :, 0:8, :], bottom),
        (populations.at[:, :, populations.shape[2] - 8 :, :], top),
    )
    copies = [pltpu.make_async_copy(a, b, done.at[k]) for k, (a, b) in enumerate(pairs)]
    for copy in copies:
        copy.start()
    rows = destination.shape[1]
    order = jnp.where(iota((128, 128), 0) <= iota((128, 128), 1), 1.0, 0.0).astype(BF16)
    for copy in copies[:5]:
        copy.wait()
    dest = destination[...]
    kinds = iota((16, rows), 0)
    hot = jnp.where(dest == kinds, 1.0, 0.0)
    seen = jnp.zeros((16, 1), F32)
    ranks = []
    for start in range(0, rows, 128):
        counted = seen + lax.dot_general(
            hot[:, start : start + 128].astype(BF16),
            order,
            (((1,), (0,)), ((), ())),
            preferred_element_type=F32,
        )
        ranks.append(counted)
        seen = counted[:, 127:128]
    rank = jnp.concatenate(ranks, axis=1)
    kind = iota((16, 1), 0)
    begin = jnp.where(
        kind < 3,
        5 * CAP + CAP * kind,
        jnp.where(kind == 3, 0, jnp.where(kind == 5, CAP, 2 * CAP + CAP * (kind - 6))),
    ).astype(F32)
    leaving = (dest < 9) & (dest != 4)
    slot = jnp.sum(hot * (begin + rank - 1.0), axis=0, keepdims=True)
    slot = jnp.where(leaving, slot, -1.0).astype(I32)
    chosen = jnp.where(iota((128, rows), 0) == slot, 1.0, 0.0).astype(BF16)
    new_velocity = velocity[...] + change[...]
    payload = jnp.concatenate(
        [fractions[...], new_velocity, anchor[...].astype(F32), jnp.zeros((1, rows), F32)], axis=0
    )
    high = payload.astype(BF16)
    middle, low = halves(payload - high.astype(F32))
    packed = dot_t(high, chosen) + dot_t(middle, chosen) + dot_t(low, chosen)
    packed = folded(packed)
    lane = lax.rem(iota((8, 128), 1), jnp.int32(LANES))
    own[...] = jnp.where(lane < 2 * CAP, packed, 0.0)
    ahead = jnp.where((lane >= 2 * CAP) & (lane < 5 * CAP), packed, 0.0)
    behind = jnp.where(lane >= 5 * CAP, packed, 0.0)
    even = even_x()
    near[...] = jnp.where(even, ahead, behind)
    far[...] = jnp.where(even, behind, ahead)
    table[...] = jnp.where((iota((32, rows), 0) < 27) & (dest != 4), 0.0, payload)
    for copy in copies[5:]:
        copy.wait()


def edge_rows(size_x):
    starts = [0]
    for rows in (19 * size_x, 4 * 2 * size_x, 11 * size_x):
        starts.append(starts[-1] + rows)
    return starts


def edge_kernel(size_x, size_y, size_z, bottom, top, table, entries, one, two, held):
    a_x, a_y, a_z = cells_of(table[30:31, :].astype(I32), size_y, size_z)
    rows = 2 * size_x
    index = iota((rows, 1), 0)
    rows_x, low = lax.div(index, jnp.int32(2)), lax.rem(index, jnp.int32(2))
    sums = deposited(
        [(rows_x, low), (rows_x, low + (size_y - 2))],
        table[0:27, :],
        table[27:30, :],
        a_x,
        a_y,
        a_z,
        size_z,
        8 * size_y,
    )
    _, at_sums, at_second, _ = edge_rows(size_x)
    for i in range(19):
        for x in range(size_x):
            held[i, x : x + 1, :] = bottom[i, x, 1:2, :]
            held[i, size_x + x : size_x + x + 1, :] = top[i, x, 6:7, :]
    second = fluid_parts([held[i] for i in range(19)], relax_blocks(entries, size_z), DOWNWARD + UPWARD)
    relaxed, bounced, density = second

    def write(down, up):
        for i in range(19):
            for x in range(size_x):
                at = i * size_x + x
                down[at : at + 1, :] = bottom[i, x, 0:1, :]
                up[at : at + 1, :] = top[i, x, 7:8, :]
        down[at_sums : at_sums + 4 * rows, :] = sums[: 4 * rows]
        up[at_sums : at_sums + 4 * rows, :] = sums[4 * rows :]
        for target, own, at_row in ((down, 0, 0), (up, 5, size_x)):
            parts = relaxed[own : own + 5] + bounced[own : own + 5] + [density]
            for k, value in enumerate(parts):
                at = at_second + k * size_x
                target[at : at + size_x, :] = value[at_row : at_row + size_x]

    even = lax.rem(lax.axis_index("gy"), 2) == 0

    @pl.when(even)
    def _():
        write(two, one)

    @pl.when(jnp.logical_not(even))
    def _():
        write(one, two)


def folded(table):
    return sum(
        table[8 * k : 8 * k + 8] if k == 0 else pltpu.roll(table[8 * k : 8 * k + 8], LANES * k, 1)
        for k in range(4)
    )


def merge_kernel(first, fold, own, far, near, one_in, two_in, column, one, two):
    del one_in, two_in
    merged = own[...] + near[...] + far[...]
    column[...] = merged
    deep = 8 // fold
    for k in range(fold):
        for target in (one, two):
            target[first : first + deep, 128 * k : 128 * k + 128] = merged[deep * k : deep * k + deep]


def relax_kernel(rates, entries):
    relax_rows(rates, entries)


def fluid_kernel(size_x, size_y, size_z, entries, populations, relaxed, bounced, density):
    blocks = relax_blocks(entries)
    for p, x in enumerate((0, size_x - 1)):
        for tile in range(size_y // 8):
            rows = slice(8 * tile, 8 * tile + 8)
            for part in range(size_z // 128):
                lanes = slice(128 * part, 128 * part + 128)
                f, b, d = fluid_parts([populations[i, x, rows, lanes] for i in range(19)], blocks, range(19))
                for i in range(19):
                    relaxed[i, p, rows, lanes] = f[i]
                    bounced[i, p, rows, lanes] = b[i]
                density[p, rows, lanes] = d


def stay_kernel(size_x, size_y, size_z, table, sums):
    a_x, a_y, a_z = cells_of(table[30:31, :].astype(I32), size_y, size_z)
    index = iota((size_x * size_y, 1), 0)
    rows_x = lax.div(index, jnp.int32(size_y))
    totals = deposited(
        [(rows_x, index - rows_x * size_y)],
        table[0:27, :],
        table[27:30, :],
        a_x,
        a_y,
        a_z,
        size_z,
        8 * size_y,
    )
    cells = size_x * size_y
    for c in range(4):
        for x in range(size_x):
            at = c * cells + x * size_y
            sums[c, x, :, :] = totals[at : at + size_y]


def outer_kernel(size_x, size_y, size_z, count, shifts, column, *refs):
    rest, (two, one, sums, outer, second, migrants) = refs[: len(shifts)], refs[len(shifts) :]
    arrivals(size_x, size_y, size_z, count, shifts, column, one, two, rest, migrants)
    blank = jnp.zeros((8, size_z), F32)
    ones = jnp.ones((8, size_z), F32)
    _, at_sums, at_second, _ = edge_rows(size_x)

    def write(above, below):
        for c in range(4):
            for x in range(size_x):
                at = at_sums + c * 2 * size_x + 2 * x
                sums[c, x, :, :] = blank
                sums[c, x, 0:2, :] = above[at : at + 2, :]
                sums[c, x, 6:8, :] = below[at : at + 2, :]
        for i in range(19):
            for x in range(size_x):
                at = i * size_x + x
                outer[i, x, :, :] = ones
                outer[i, x, 0:1, :] = above[at : at + 1, :]
                outer[i, x, 7:8, :] = below[at : at + 1, :]
        for k in range(11):
            for x in range(size_x):
                at = at_second + k * size_x + x
                second[k, x, :, :] = ones
                second[k, x, 1:2, :] = above[at : at + 1, :]
                second[k, x, 6:7, :] = below[at : at + 1, :]

    even = lax.rem(lax.axis_index("gy"), 2) == 0

    @pl.when(even)
    def _():
        write(one, two)

    @pl.when(jnp.logical_not(even))
    def _():
        write(two, one)


def pair_source(here, parity, count):
    other = jnp.where(lax.rem(here, 2) == parity, here + 1, here - 1)
    return jnp.where((other >= 0) & (other < count), other, here + 2 * count)


def arrivals(size_x, size_y, size_z, count, shifts, column, one, two, rest, migrants):
    first = edge_rows(size_x)[-1]
    here = lax.axis_index("gy")
    fold = size_z // 128
    deep = 8 // fold

    def gathered(message):
        return jnp.concatenate(
            [message[first : first + deep, 128 * k : 128 * k + 128] for k in range(fold)], axis=0
        )

    parts = [column[...], gathered(one), gathered(two)] + [r[...] for r in rest]
    sources = [here, pair_source(here, 0, count), pair_source(here, 1, count)]
    sources += [lax.rem(here - shift + 2 * count, count) for shift in shifts]
    lane = iota((1, 128), 1)
    spot = lax.rem(lane, jnp.int32(LANES))
    group = lax.div(spot, jnp.int32(CAP))
    across = jnp.where(
        (group == 0) | (group == 2) | (group == 5), -1, jnp.where((group == 3) | (group == 6), 0, 1)
    )
    per_group = 128 // LANES
    tables, offsets = [], []
    for start in range(0, len(parts), per_group):
        blocks = [jnp.zeros((8, 128), F32)] * 4
        offset = jnp.full((1, 128), 2 * count, I32)
        for k, part in enumerate(parts[start : start + per_group]):
            place = lax.div(lane, jnp.int32(LANES)) == k
            for q in range(4):
                turn = LANES * (k - q) % 128
                blocks[q] = jnp.where(place, part if turn == 0 else pltpu.roll(part, turn, 1), blocks[q])
            offset = jnp.where(lax.div(lane, jnp.int32(LANES)) == k, sources[start + k] - here, offset)
        tables.append(jnp.concatenate(blocks, axis=0))
        offsets.append((offset + across) * size_y)
    table = jnp.concatenate(tables, axis=1)
    a_x, a_y, a_z = cells_of(table[30:31, :].astype(I32), size_y, size_z)
    migrants[0:32, :] = table
    migrants[32:33, :] = a_x.astype(F32)
    migrants[33:34, :] = (a_y + jnp.concatenate(offsets, axis=1)).astype(F32)
    migrants[34:35, :] = a_z.astype(F32)


def store_padded(target, i, x, tile, part, value, tiles):
    lanes = slice(128 * part, 128 * part + 128)
    if tile == tiles:
        target[i, x, 0:8, lanes] = value
        target[i, x, 8 + 8 * tiles : 16 + 8 * tiles, lanes] = value
    else:
        target[i, x, 8 + 8 * tile : 16 + 8 * tile, lanes] = value
        if tile == 0:
            target[i, x, 16 + 8 * tiles : 24 + 8 * tiles, lanes] = value


def turned(value, shift, size_z):
    return value if shift == 0 else pltpu.roll(value, shift % size_z, 1)


def solids(size_x, size_y, size_z, planes, sums, outer_sums, migrants, solid):
    a_x, a_y, a_z = (migrants[k : k + 1, :].astype(I32) for k in (32, 33, 34))
    wide = size_y + 8
    index = iota((len(planes) * wide, 1), 0)
    number = lax.div(index, jnp.int32(wide))
    row = index - number * wide
    rows_x = number + planes[0] if len(planes) == planes[-1] - planes[0] + 1 else number * (size_x - 1)
    rows_y = jnp.where(row < size_y + 2, row, jnp.where(row >= size_y + 6, row - wide, -3 * size_y))
    big = 4 * size_y * (lax.axis_size("gy") + 2)
    totals = deposited(
        [(rows_x, rows_y)], migrants[0:27, :], migrants[27:30, :], a_x, a_y, a_z, size_z, big
    )
    cells = len(planes) * wide
    for p, x in enumerate(planes):
        parts = []
        for c in range(4):
            at = c * cells + p * wide
            solid_sum = jnp.concatenate([sums[c, x, :, :], outer_sums[c, x, :, :]], axis=0)
            parts.append(totals[at : at + wide] + solid_sum)
        scale = 1.0 / (parts[0] + 1e-06)
        solid[0, p, :, :] = jnp.minimum(parts[0], 1.0)
        for c in (1, 2, 3):
            solid[c, p, :, :] = parts[c] * scale


def outer_collision(solid, outer, second, blocks, p, x, lanes, rows):
    share, *flow = (solid[c, p, rows, lanes] for c in range(4))
    out = collide([outer[i, x, :, lanes] for i in range(19)], share, *flow, blocks)
    line = iota((8, 128), 0)
    away = jnp.where(line < 4, 1.0, -1.0)
    still = equilibrium(None, [away * v for v in flow], DOWNWARD)
    density = second[10, x, :, lanes]
    for k, (i, j) in enumerate(zip(DOWNWARD, UPWARD)):
        value = blended(second[k, x, :, lanes], second[5 + k, x, :, lanes], density, share, still[i])
        out[i] = jnp.where(line == 1, value, out[i])
        out[j] = jnp.where(line == 6, value, out[j])
    return out


def prepared_collision(solid, relaxed, bounced, dense, p, rows, lanes, numbers):
    share, *flow = (solid[c, p, rows, lanes] for c in range(4))
    still = equilibrium(None, flow, numbers)
    density = dense[p, rows, lanes]
    return {
        i: blended(relaxed[i, p, rows, lanes], bounced[i, p, rows, lanes], density, share, still[i])
        for i in numbers
    }


def tile_parts(size_y, size_z):
    for tile in range(size_y // 8 + 1):
        for part in range(size_z // 128):
            yield tile, slice(8 * tile, 8 * tile + 8), part, slice(128 * part, 128 * part + 128)


def leaving_kernel(
    size_x, size_y, size_z, entries, sums, outer_sums, outer, second, migrants, relaxed, bounced, dense,
    solid, near, far, leaving
):
    tiles = size_y // 8
    planes = (0, size_x - 1)
    solids(size_x, size_y, size_z, planes, sums, outer_sums, migrants, solid)
    blocks = relax_blocks(entries)
    for p, x in enumerate(planes):
        numbers = FORWARD if p else BACKWARD
        for tile, rows, part, lanes in tile_parts(size_y, size_z):
            if tile == tiles:
                out = outer_collision(solid, outer, second, blocks, p, x, lanes, rows)
            else:
                out = prepared_collision(solid, relaxed, bounced, dense, p, rows, lanes, numbers)
            for k, i in enumerate(numbers):
                store_padded(leaving, k, p, tile, part, out[i], tiles)
    send_faces(leaving, near, far, size_y, size_z, True)


def ends_kernel(
    size_x, size_y, size_z, entries, outer, second, relaxed, bounced, dense, solid, post
):
    tiles = size_y // 8
    blocks = relax_blocks(entries)
    for p, x in enumerate((0, size_x - 1)):
        for tile, rows, part, lanes in tile_parts(size_y, size_z):
            if tile == tiles:
                out = outer_collision(solid, outer, second, blocks, p, x, lanes, rows)
            else:
                out = prepared_collision(solid, relaxed, bounced, dense, p, rows, lanes, range(19))
            for i in range(19):
                store_padded(post, i, p, tile, part, out[i], tiles)


def middle_kernel(
    size_x, size_y, size_z, planes, entries, sums, outer_sums, outer, second, migrants, populations,
    post, solid
):
    tiles = size_y // 8
    solids(size_x, size_y, size_z, planes, sums, outer_sums, migrants, solid)
    blocks = relax_blocks(entries)
    for p, x in enumerate(planes):
        for tile, rows, part, lanes in tile_parts(size_y, size_z):
            if tile == tiles:
                out = outer_collision(solid, outer, second, blocks, p, x, lanes, rows)
            else:
                share, *flow = (solid[c, p, rows, lanes] for c in range(4))
                h = [populations[i, x, rows, lanes] for i in range(19)]
                out = collide(h, share, *flow, blocks)
            for i in range(19):
                store_padded(post, i, p, tile, part, out[i], tiles)


def send_faces(post, near, far, size_y, size_z, outer):
    even = even_x()

    @pl.when(even)
    def _():
        faces(post, near, far, size_y, size_z, outer)

    @pl.when(jnp.logical_not(even))
    def _():
        faces(post, far, near, size_y, size_z, outer)


def faces(post, ahead, behind, size_y, size_z, outer):
    tiles = size_y // 8
    for target, numbers, p in ((ahead, FORWARD, 1), (behind, BACKWARD, 0)):
        for k, i in enumerate(numbers):
            _, c_y, c_z = VEC[i]
            for tile in range(tiles):
                at = 8 + 8 * tile - c_y
                to = k * size_y + 8 * tile
                target[to : to + 8, :] = turned(post[k, p, at : at + 8, :], c_z, size_z)
            if outer:
                at = 8 + size_y - c_y
                value = turned(post[k, p, at : at + 8, :], c_z, size_z)
                to = 5 * size_y + 2 * k
                target[to : to + 1, :] = value[0:1]
                target[to + 1 : to + 2, :] = value[7:8]


def streamed(ends, middle, messages, i, x, tile, size_x, size_y, size_z, walls):
    tiles = size_y // 8
    row = iota((8, size_z), 0)
    c_x, c_y, c_z = VEC[i]

    def plane(x):
        if x == 0:
            return ends, 0
        if x == size_x - 1:
            return ends, 1
        return middle, x - 1

    from_x = x - c_x
    if 0 <= from_x < size_x:
        source, p = plane(from_x)
        at = 8 + 8 * tile - c_y
        value = turned(source[i, p, at : at + 8, :], c_z, size_z)
    else:
        near, far, even = messages
        from_near, numbers = (jnp.logical_not(even), FORWARD) if from_x < 0 else (even, BACKWARD)
        k = numbers.index(i)

        def received(at, rows):
            return jnp.where(from_near, near[at : at + rows, :], far[at : at + rows, :])

        if tile < tiles:
            value = received(k * size_y + 8 * tile, 8)
        else:
            at = 5 * size_y + 2 * k
            value = jnp.where(row < 4, received(at, 1), received(at + 1, 1))
    source, p = plane(x)
    if c_y == 1 and tile == 0:
        value = jnp.where((row == 0) & walls[0], source[OPP[i], p, 8:16, :], value)
    if c_y == -1 and tile == tiles - 1:
        back = source[OPP[i], p, size_y : 8 + size_y, :]
        value = jnp.where((row == 7) & walls[1], back, value)
    return value


def walls_of(count):
    here = lax.axis_index("gy")
    return here == 0, here == count - 1


def second_kernel(size_x, size_y, size_z, count, planes, entries, ends, middle, solid, *refs):
    refs = list(refs)
    outside = planes[0] == 0
    messages = (refs.pop(1), refs.pop(0), even_x()) if outside else None
    leaving = len(refs) > 1
    if leaving:
        del refs[0]
    tiles = size_y // 8
    walls = walls_of(count)
    blocks = relax_blocks(entries)
    for p, x in enumerate(planes):
        numbers = (FORWARD if p else BACKWARD) if leaving else range(19)
        for tile in range(tiles + 1):
            rows = slice(8 * tile, 8 * tile + 8)
            h = [
                streamed(ends, middle, messages, i, x, tile, size_x, size_y, size_z, walls)
                for i in range(19)
            ]
            for part in range(size_z // 128):
                lanes = slice(128 * part, 128 * part + 128)
                s = [solid[c, p, rows, lanes] for c in range(4)]
                out = collide([v[:, lanes] for v in h], *s, blocks)
                for k, i in enumerate(numbers):
                    store_padded(refs[-1], k, p, tile, part, out[i], tiles)
    if leaving:
        send_faces(refs[-1], refs[0], refs[1], size_y, size_z, False)


def last_kernel(size_x, size_y, size_z, count, ends, middle, advanced, held, done):
    walls = walls_of(count)
    copies = []
    for i in range(19):
        for x in range(size_x):
            if not 0 <= x - VEC[i][0] < size_x:
                continue
            for tile in range(size_y // 8):
                held[i, x, 8 * tile : 8 * tile + 8, :] = streamed(
                    ends, middle, None, i, x, tile, size_x, size_y, size_z, walls
                )
        low, high = max(0, VEC[i][0]), size_x + min(0, VEC[i][0])
        copy = pltpu.make_async_copy(
            held.at[i, low:high], advanced.at[i, low:high], done.at[i]
        )
        copy.start()
        copies.append(copy)
    for copy in copies:
        copy.wait()


def enter_kernel(
    size_x, size_y, size_z, count, ends, far, near, given, advanced, held, done
):
    del given
    messages = (near, far, even_x())
    walls = walls_of(count)
    copies = []
    for x, numbers in ((0, FORWARD), (size_x - 1, BACKWARD)):
        for i in numbers:
            k = len(copies)
            for tile in range(size_y // 8):
                held[k, 8 * tile : 8 * tile + 8, :] = streamed(
                    ends, None, messages, i, x, tile, size_x, size_y, size_z, walls
                )
            copy = pltpu.make_async_copy(held.at[k], advanced.at[i, x], done.at[k])
            copy.start()
            copies.append(copy)
    for copy in copies:
        copy.wait()


def shape(*sizes):
    return jax.ShapeDtypeStruct(sizes, F32)


VMEM = pl.BlockSpec(memory_space=pltpu.VMEM)
SMEM = pl.BlockSpec(memory_space=pltpu.SMEM)
HBM = pl.BlockSpec(memory_space=pltpu.HBM)


def call(kernel, out_shape, limit, in_specs, out_specs=None, scratch=(), aliases=None):
    return pl.pallas_call(
        kernel,
        out_shape=out_shape,
        in_specs=in_specs,
        out_specs=jax.tree.map(lambda _: VMEM, out_shape) if out_specs is None else out_specs,
        scratch_shapes=scratch,
        input_output_aliases={} if aliases is None else aliases,
        compiler_params=pltpu.CompilerParams(vmem_limit_bytes=limit * 2**20),
    )


def in_hbm(value):
    return pltpu.with_memory_space_constraint(value, pltpu.HBM)


def around(value, axis, steps):
    count = lax.axis_size(axis)
    return lax.ppermute(value, axis, [(i, (i + steps) % count) for i in range(count)])


def paired(value, axis, parity, wrap=False):
    count = lax.axis_size(axis)
    if wrap and count % 2:
        raise ValueError("odd ring")
    pairs = []
    for i in range(count):
        other = i + 1 if i % 2 == parity else i - 1
        other = other % count if wrap else other
        pairs.append((i, other if 0 <= other < count else i))
    return lax.ppermute(value, axis, pairs)


def exchanged(near, far):
    far = paired(far, "gx", 1, True)
    return paired(near, "gx", 0, True), far


def local(populations, relax_rates, velocity, velocity_change, fractions, anchor, destination):
    _, size_x, size_y, size_z = populations.shape
    count = lax.axis_size("gy")
    rows = anchor.shape[0]
    sizes = (size_x, size_y, size_z)
    part = functools.partial
    packed = shape(8, 128)
    band = shape(19, size_x, 8, size_z)
    table, own, near, far, bottom, top = call(
        pack_kernel,
        (shape(32, rows), packed, packed, packed, band, band),
        8,
        [HBM] * 6,
        scratch=[
            pltpu.VMEM((3, rows), F32),
            pltpu.VMEM((3, rows), F32),
            pltpu.VMEM((27, rows), F32),
            pltpu.VMEM((1, rows), I32),
            pltpu.VMEM((1, rows), I32),
            pltpu.SemaphoreType.DMA((7,)),
        ],
    )(*map(in_hbm, (velocity, velocity_change, fractions, anchor[None, :], destination[None, :], populations)))
    near, far = exchanged(near, far)
    first = edge_rows(size_x)[-1]
    fold = size_z // 128
    message = shape(-(-(first + 8 // fold) // 8) * 8, size_z)
    entries = call(relax_kernel, shape(ENTRIES, 8, 128), 8, [SMEM])(relax_rates)
    one, two = call(
        part(edge_kernel, *sizes),
        (message, message),
        8,
        [VMEM] * 4,
        scratch=[pltpu.VMEM((19, 2 * size_x, size_z), F32)],
    )(bottom, top, table, entries)
    column, one, two = call(
        part(merge_kernel, first, fold),
        (shape(8, 128), message, message),
        8,
        [VMEM] * 5,
        aliases={3: 1, 4: 2},
    )(own, far, near, one, two)
    shifts = []
    for shift in (2, -2):
        if shift % count > 1 and all((shift - other) % count for other in shifts):
            shifts.append(shift)
    rest = [around(column, "gy", shift) for shift in shifts]
    one, two = paired(one, "gy", 0), paired(two, "gy", 1)
    sums = call(part(stay_kernel, *sizes), shape(4, *sizes), 16, [VMEM])(table)
    plane_pair = shape(19, 2, size_y, size_z)
    parts = call(
        part(fluid_kernel, *sizes), (plane_pair, plane_pair, shape(2, size_y, size_z)), 16, [VMEM] * 2
    )(entries, populations)
    width = -(-(3 + len(shifts)) * LANES // 128) * 128
    outer_sums, outer, second, migrants = call(
        part(outer_kernel, *sizes, count, shifts),
        (
            shape(4, size_x, 8, size_z),
            shape(19, size_x, 8, size_z),
            shape(11, size_x, 8, size_z),
            shape(40, width),
        ),
        8,
        [VMEM] * (3 + len(shifts)),
    )(column, *rest, two, one)

    def padded(planes):
        return shape(19, planes, size_y + 24, size_z)

    def solid_shape(planes):
        return shape(4, planes, size_y + 8, size_z)

    outside, inside = (0, size_x - 1), tuple(range(1, size_x - 1))
    sent = pltpu.VMEM((5, 2, size_y + 24, size_z), F32)
    wide_face = shape((5 * size_y + 10 + 7) // 8 * 8, size_z)
    face = shape(5 * size_y, size_z)
    known = (entries, sums, outer_sums, outer, second, migrants)
    solid_ends, near, far = call(
        part(leaving_kernel, *sizes), (solid_shape(2), wide_face, wide_face), 16, [VMEM] * 9, scratch=[sent]
    )(*known, *parts)
    near, far = exchanged(near, far)
    middle, solid_middle = call(
        part(middle_kernel, *sizes, inside),
        (padded(len(inside)), solid_shape(len(inside))),
        16,
        [VMEM] * 7,
    )(*known, populations)
    ends = call(part(ends_kernel, *sizes), padded(2), 16, [VMEM] * 7)(
        entries, outer, second, *parts, solid_ends
    )
    later_middle = call(
        part(second_kernel, *sizes, count, inside), padded(len(inside)), 16, [VMEM] * 4
    )(entries, ends, middle, solid_middle)
    given = (entries, ends, middle, solid_ends, far, near)
    near, far = call(
        part(second_kernel, *sizes, count, outside),
        (face, face),
        16,
        [VMEM] * 6 + [pl.BlockSpec(memory_space=pl.ANY)],
        scratch=[sent],
    )(*given, later_middle)
    later_ends = call(part(second_kernel, *sizes, count, outside), padded(2), 16, [VMEM] * 6)(*given)
    near, far = exchanged(near, far)
    advanced = call(
        part(last_kernel, *sizes, count),
        shape(19, *sizes),
        16,
        [VMEM] * 2,
        HBM,
        [pltpu.VMEM((19, *sizes), F32), pltpu.SemaphoreType.DMA((19,))],
    )(later_ends, later_middle)
    return call(
        part(enter_kernel, *sizes, count),
        shape(19, *sizes),
        16,
        [VMEM] * 3 + [HBM],
        HBM,
        [pltpu.VMEM((10, size_y, size_z), F32), pltpu.SemaphoreType.DMA((10,))],
        {3: 0},
    )(later_ends, far, near, advanced)


def solution(mesh):
    placed = (
        P(None, "gx", "gy", None),
        P(),
        P(None, ("gx", "gy")),
        P(None, ("gx", "gy")),
        P(None, ("gx", "gy")),
        P(("gx", "gy")),
        P(("gx", "gy")),
    )
    return jax.shard_map(
        local, mesh=mesh, in_specs=placed, out_specs=P(None, "gx", "gy", None), check_vma=False
    )
```

```python
import functools

import jax
import jax.numpy as jnp
import numpy as np
from jax import lax
from jax.experimental import pallas as pl
from jax.experimental.pallas import tpu as pltpu
from jax.sharding import PartitionSpec as P

CAP = 4
STEPS = 2
LANES = 8 * CAP
F32 = jnp.float32
BF16 = jnp.bfloat16
I32 = jnp.int32


def lattice():
    vectors = [[0, 0, 0]]
    for axis_one in range(3):
        for orient in (1, -1):
            vector_one = [0, 0, 0]
            vector_one[axis_one] = orient
            vectors.append(vector_one)
    for axis_one, axis_two in ((0, 1), (0, 2), (1, 2)):
        for orient in (1, -1):
            for second in (1, -1):
                vector_one = [0, 0, 0]
                vector_one[axis_one] = orient
                vector_one[axis_two] = second
                vectors.append(vector_one)
    integral = np.array(vectors)
    speeds = integral * 1.0
    length = (speeds**2).sum(axis=1)
    weights = np.where(length == 0, 1.0 / 3.0, np.where(length == 1, 1.0 / 18.0, 1.0 / 36.0))
    opposite = [vectors.index([0 - component for component in vector_one]) for vector_one in vectors]
    along_x, along_y, along_z = (speeds[:, 0], speeds[:, 1], speeds[:, 2])
    rows_list = [
        np.ones(19),
        along_x,
        along_y,
        along_z,
        length,
        3 * along_x**2 - length,
        along_y**2 - along_z**2,
        along_x * along_y,
        along_y * along_z,
        along_x * along_z,
        along_x * length,
        along_y * length,
        along_z * length,
        along_x * (along_y**2 - along_z**2),
        along_y * (along_z**2 - along_x**2),
        along_z * (along_x**2 - along_y**2),
        length**2,
        (3 * along_x**2 - length) * length,
        (along_y**2 - along_z**2) * length,
    ]
    basis_rows = []
    for candidate in rows_list:
        for earlier in basis_rows:
            candidate = candidate - np.dot(candidate, earlier) * earlier
        basis_rows.append(candidate / np.sqrt(np.dot(candidate, candidate)))
    return [tuple(v) for v in vectors], weights, opposite, np.array(basis_rows)


VEC, WEIGHTS, OPP, BASIS = lattice()
FORWARD = [i for i in range(19) if VEC[i][0] == 1]
BACKWARD = [i for i in range(19) if VEC[i][0] == -1]
DOWNWARD = [i for i in range(19) if VEC[i][1] == -1]
UPWARD = [OPP[i] for i in DOWNWARD]


def symmetric_blocks():
    def vec(entries):
        out = np.zeros(19)
        for index, value in entries.items():
            out[index] = value
        return out

    def plane(base):
        s_one, d_one = vec({base: 1, base + 3: 1}), vec({base: 1, base + 3: -1})
        s_two, d_two = vec({base + 1: 1, base + 2: 1}), vec({base + 1: 1, base + 2: -1})
        return s_one + s_two, s_one - s_two, d_one + d_two, d_one - d_two

    rest = vec({0: 1})
    s_x, s_y, s_z = vec({1: 1, 2: 1}), vec({3: 1, 4: 1}), vec({5: 1, 6: 1})
    d_x, d_y, d_z = vec({1: 1, 2: -1}), vec({3: 1, 4: -1}), vec({5: 1, 6: -1})
    xy, q_xy, x_xy, y_xy = plane(7)
    xz, q_xz, x_xz, z_xz = plane(11)
    yz, q_yz, y_yz, z_yz = plane(15)
    blocks = [
        [rest, s_x + s_y + s_z, xy + xz + yz],
        [2 * s_x - s_y - s_z, xy + xz - 2 * yz],
        [s_y - s_z, xy - xz],
        [q_xy],
        [q_xz],
        [q_yz],
        [d_x, x_xy, x_xz],
        [d_y, y_xy, y_yz],
        [d_z, z_xz, z_yz],
    ]
    scales = [[1, 1 / 6, 1 / 12], [1 / 12, 1 / 24], [1 / 4, 1 / 8]]
    scales += [[1 / 4]] * 3 + [[1 / 2, 1 / 4, 1 / 4]] * 3
    forward = np.array([row for block in blocks for row in block])
    back = np.linalg.inv(forward)
    left = forward @ np.diag(1.0 / WEIGHTS) @ BASIS.T
    right = BASIS @ np.diag(WEIGHTS) @ back
    table = []
    start = 0
    for block, scale in zip(blocks, scales):
        size = len(block)
        rows = []
        for a in range(size):
            row = []
            for b in range(size):
                per_rate = -scale[a] * left[start + a, :] * right[:, start + b]
                row.append([(k, float(v)) for k, v in enumerate(per_rate) if abs(v) > 1e-12])
            rows.append(row)
        table.append(rows)
        start += size
    return table


RELAX = symmetric_blocks()


def relax_rows(rates, target):
    values = [rates[k] for k in range(19)]
    at = 0
    for block in RELAX:
        for row in block:
            for terms in row:
                total = None
                for k, factor in terms:
                    part = values[k] * np.float32(factor)
                    total = part if total is None else total + part
                target[at] = jnp.full((8, 128), total, F32)
                at += 1


def relax_blocks(table, lanes=128):
    blocks, at = [], 0
    for block in RELAX:
        rows = []
        for row in block:
            rows.append(
                [jnp.concatenate([table[at + k]] * (lanes // 128), axis=1) for k in range(len(row))]
            )
            at += len(row)
        blocks.append(rows)
    return blocks


ENTRIES = sum(len(row) for block in RELAX for row in block)


def apply_block(block, values):
    out = []
    for row in block:
        total = None
        for factor, value in zip(row, values):
            part = factor * value
            total = part if total is None else total + part
        out.append(total)
    return out


def collide(h, solid, s_x, s_y, s_z, blocks):
    def plane(base):
        s_one, d_one = h[base] + h[base + 3], h[base] - h[base + 3]
        s_two, d_two = h[base + 1] + h[base + 2], h[base + 1] - h[base + 2]
        return s_one + s_two, s_one - s_two, d_one + d_two, d_one - d_two

    sum_x, dif_x = h[1] + h[2], h[1] - h[2]
    sum_y, dif_y = h[3] + h[4], h[3] - h[4]
    sum_z, dif_z = h[5] + h[6], h[5] - h[6]
    xy, q_xy, x_xy, y_xy = plane(7)
    xz, q_xz, x_xz, z_xz = plane(11)
    yz, q_yz, y_yz, z_yz = plane(15)
    axes = sum_x + sum_y + sum_z
    edges = xy + xz + yz
    density = h[0] * (1.0 / 3.0) + axes * (1.0 / 18.0) + edges * (1.0 / 36.0)
    m_x = dif_x * (1.0 / 18.0) + (x_xy + x_xz) * (1.0 / 36.0)
    m_y = dif_y * (1.0 / 18.0) + (y_xy + y_yz) * (1.0 / 36.0)
    m_z = dif_z * (1.0 / 18.0) + (z_xz + z_yz) * (1.0 / 36.0)
    inverse = 1.0 / density
    u_x, u_y, u_z = m_x * inverse, m_y * inverse, m_z * inverse
    e_xx, e_yy, e_zz = m_x * u_x, m_y * u_y, m_z * u_z
    e_xy, e_xz, e_yz = m_x * u_y, m_x * u_z, m_y * u_z
    energy = e_xx + e_yy + e_zz
    turn = e_yy - e_zz
    lean = 3.0 * e_xx - energy
    rest_off = h[0] - density + 1.5 * energy
    axes_off = axes - 6.0 * density
    edges_off = edges - 12.0 * density - 18.0 * energy
    a_one = 3.0 * sum_x - axes - 9.0 * lean
    b_one = edges - 3.0 * yz - 18.0 * lean
    a_two = sum_y - sum_z - 9.0 * turn
    b_two = xy - xz - 18.0 * turn
    q_xy = q_xy - 36.0 * e_xy
    q_xz = q_xz - 36.0 * e_xz
    q_yz = q_yz - 36.0 * e_yz

    r_rest, r_axes, r_edges = apply_block(blocks[0], [rest_off, axes_off, edges_off])
    r_a_one, r_b_one = apply_block(blocks[1], [a_one, b_one])
    r_a_two, r_b_two = apply_block(blocks[2], [a_two, b_two])
    fluid = 1.0 - solid
    mixed = solid * density
    w_x, w_y, w_z = solid * m_x, solid * m_y, solid * m_z
    n_x, n_y, n_z = mixed * s_x, mixed * s_y, mixed * s_z
    p_x = n_x * s_x - solid * e_xx
    p_y = n_y * s_y - solid * e_yy
    p_z = n_z * s_z - solid * e_zz
    total = 1.5 * (p_x + p_y + p_z)
    lean_s = 2.25 * p_x - 0.5 * total
    turn_s = 2.25 * (p_y - p_z)
    rest = fluid * r_rest - total
    axes = fluid * r_axes
    edges = fluid * r_edges + total
    a_one = fluid * r_a_one + lean_s
    b_one = fluid * r_b_one + lean_s
    a_two = fluid * r_a_two + turn_s
    b_two = fluid * r_b_two + turn_s
    q_xy = fluid * apply_block(blocks[3], [q_xy])[0] + 9.0 * (n_x * s_y - solid * e_xy)
    q_xz = fluid * apply_block(blocks[4], [q_xz])[0] + 9.0 * (n_x * s_z - solid * e_xz)
    q_yz = fluid * apply_block(blocks[5], [q_yz])[0] + 9.0 * (n_y * s_z - solid * e_yz)

    def odd(block, axis, one, two, m, n, w):
        six = 6.0 * m
        axis = axis - six
        twelve = six + six
        one = one - twelve
        two = two - twelve
        r_axis, r_one, r_two = apply_block(block, [axis, one, two])
        push = 3.0 * (n - w)
        half = 0.5 * solid
        return (
            fluid * r_axis - solid * axis + push,
            fluid * r_one - half * one + push,
            fluid * r_two - half * two + push,
        )

    d_x, x_xy, x_xz = odd(blocks[6], dif_x, x_xy, x_xz, m_x, n_x, w_x)
    d_y, y_xy, y_yz = odd(blocks[7], dif_y, y_xy, y_yz, m_y, n_y, w_y)
    d_z, z_xz, z_yz = odd(blocks[8], dif_z, z_xz, z_yz, m_z, n_z, w_z)
    out = [None] * 19
    out[0] = h[0] + rest
    even = axes + 2.0 * a_one
    out[1], out[2] = h[1] + (even + d_x), h[2] + (even - d_x)
    base = axes - a_one
    even = base + a_two
    out[3], out[4] = h[3] + (even + d_y), h[4] + (even - d_y)
    even = base - a_two
    out[5], out[6] = h[5] + (even + d_z), h[6] + (even - d_z)

    def spread(start, even, twist, one, two):
        same, cross = even + twist, even - twist
        plus, minus = one + two, one - two
        out[start] = h[start] + (same + plus)
        out[start + 3] = h[start + 3] + (same - plus)
        out[start + 1] = h[start + 1] + (cross + minus)
        out[start + 2] = h[start + 2] + (cross - minus)

    base = edges + b_one
    spread(7, base + b_two, q_xy, x_xy, y_xy)
    spread(11, base - b_two, q_xz, x_xz, z_xz)
    spread(15, edges - 2.0 * b_one, q_yz, y_yz, z_yz)
    return out


def equilibrium(density, flow, numbers):
    v_x, v_y, v_z = flow
    rest = 1.0 - 1.5 * (v_x * v_x + v_y * v_y + v_z * v_z)
    out = {}
    for i in numbers:
        if i in out:
            continue
        along = None
        for sign, v in zip(VEC[i], flow):
            if sign:
                part = v if sign == 1 else -v
                along = part if along is None else along + part
        if along is None:
            out[i] = rest
        else:
            along = 3.0 * along
            even = rest + 0.5 * along * along
            out[i], out[OPP[i]] = even + along, even - along
    return out


def fluid_parts(h, blocks, numbers):
    zero = jnp.zeros_like(h[0])
    relaxed = collide(h, zero, zero, zero, zero, blocks)
    density, flow = zero, [zero, zero, zero]
    for i in range(19):
        part = np.float32(WEIGHTS[i]) * h[i]
        density = density + part
        for k in range(3):
            if VEC[i][k]:
                flow[k] = flow[k] + part if VEC[i][k] == 1 else flow[k] - part
    inverse = 1.0 / density
    still = equilibrium(density, [f * inverse for f in flow], numbers)
    bounced = [h[OPP[i]] - density * still[OPP[i]] for i in numbers]
    return [relaxed[i] for i in numbers], bounced, density


def blended(relaxed, bounced, density, share, still):
    return relaxed + share * ((bounced + density * still) - relaxed)


def iota(shape, dim):
    return lax.broadcasted_iota(I32, shape, dim)


def cells_of(anchor, size_y, size_z):
    plane = size_y * size_z
    a_x = lax.div(anchor, jnp.int32(plane))
    rest = anchor - a_x * plane
    a_y = lax.div(rest, jnp.int32(size_z))
    return a_x, a_y, rest - a_y * size_z


def halves(value):
    high = value.astype(BF16)
    return high, (value - high.astype(F32)).astype(BF16)


def dot_t(left, right):
    return lax.dot_general(left, right, (((1,), (1,)), ((), ())), preferred_element_type=F32)


def deposited(groups, shares, velocity, a_x, a_y, a_z, size_z, big):
    centre = a_x * big + a_y
    lanes = centre.shape[1]
    totals = None
    rows_z = iota((size_z, lanes), 0)
    for off_z in range(3):
        weights = []
        for rows_x, rows_y in groups:
            away = rows_x * big + rows_y - centre
            weight = jnp.zeros(away.shape, F32)
            for off in range(9):
                move = (off // 3 - 1) * big + off % 3 - 1
                row = 3 * off + off_z
                weight = jnp.where(away == move, shares[row : row + 1, :], weight)
            weights.append([weight] + [weight * velocity[k : k + 1, :] for k in range(3)])
        rows = jnp.concatenate([w for block in weights for w in block], axis=0)
        high, low = halves(rows)
        hot = jnp.where(rows_z == a_z + (off_z - 1), 1.0, 0.0).astype(BF16)
        part = dot_t(high, hot) + dot_t(low, hot)
        totals = part if totals is None else totals + part
    return totals


def even_x():
    return lax.rem(lax.axis_index("gx"), 2) == 0


def pack_kernel(
    velocity_in,
    change_in,
    fractions_in,
    anchor_in,
    destination_in,
    populations,
    table,
    own,
    near,
    far,
    bottom,
    top,
    velocity,
    change,
    fractions,
    anchor,
    destination,
    done,
):
    pairs = (
        (destination_in, destination),
        (velocity_in, velocity),
        (change_in, change),
        (fractions_in, fractions),
        (anchor_in, anchor),
        (populations.at[:, :, 0:8, :], bottom),
        (populations.at[:, :, populations.shape[2] - 8 :, :], top),
    )
    copies = [pltpu.make_async_copy(a, b, done.at[k]) for k, (a, b) in enumerate(pairs)]
    for copy in copies:
        copy.start()
    rows = destination.shape[1]
    order = jnp.where(iota((128, 128), 0) <= iota((128, 128), 1), 1.0, 0.0).astype(BF16)
    for copy in copies[:5]:
        copy.wait()
    dest = destination[...]
    kinds = iota((16, rows), 0)
    hot = jnp.where(dest == kinds, 1.0, 0.0)
    seen = jnp.zeros((16, 1), F32)
    ranks = []
    for start in range(0, rows, 128):
        counted = seen + lax.dot_general(
            hot[:, start : start + 128].astype(BF16),
            order,
            (((1,), (0,)), ((), ())),
            preferred_element_type=F32,
        )
        ranks.append(counted)
        seen = counted[:, 127:128]
    rank = jnp.concatenate(ranks, axis=1)
    kind = iota((16, 1), 0)
    begin = jnp.where(
        kind < 3,
        5 * CAP + CAP * kind,
        jnp.where(kind == 3, 0, jnp.where(kind == 5, CAP, 2 * CAP + CAP * (kind - 6))),
    ).astype(F32)
    leaving = (dest < 9) & (dest != 4)
    slot = jnp.sum(hot * (begin + rank - 1.0), axis=0, keepdims=True)
    slot = jnp.where(leaving, slot, -1.0).astype(I32)
    chosen = jnp.where(iota((128, rows), 0) == slot, 1.0, 0.0).astype(BF16)
    new_velocity = velocity[...] + change[...]
    payload = jnp.concatenate(
        [fractions[...], new_velocity, anchor[...].astype(F32), jnp.zeros((1, rows), F32)], axis=0
    )
    high = payload.astype(BF16)
    middle, low = halves(payload - high.astype(F32))
    packed = dot_t(high, chosen) + dot_t(middle, chosen) + dot_t(low, chosen)
    packed = folded(packed)
    lane = lax.rem(iota((8, 128), 1), jnp.int32(LANES))
    own[...] = jnp.where(lane < 2 * CAP, packed, 0.0)
    ahead = jnp.where((lane >= 2 * CAP) & (lane < 5 * CAP), packed, 0.0)
    behind = jnp.where(lane >= 5 * CAP, packed, 0.0)
    even = even_x()
    near[...] = jnp.where(even, ahead, behind)
    far[...] = jnp.where(even, behind, ahead)
    table[...] = jnp.where((iota((32, rows), 0) < 27) & (dest != 4), 0.0, payload)
    for copy in copies[5:]:
        copy.wait()


def edge_rows(size_x):
    starts = [0]
    for rows in (19 * size_x, 4 * 2 * size_x, 11 * size_x):
        starts.append(starts[-1] + rows)
    return starts


def edge_kernel(size_x, size_y, size_z, bottom, top, table, entries, one, two, held):
    a_x, a_y, a_z = cells_of(table[30:31, :].astype(I32), size_y, size_z)
    rows = 2 * size_x
    index = iota((rows, 1), 0)
    rows_x, low = lax.div(index, jnp.int32(2)), lax.rem(index, jnp.int32(2))
    sums = deposited(
        [(rows_x, low), (rows_x, low + (size_y - 2))],
        table[0:27, :],
        table[27:30, :],
        a_x,
        a_y,
        a_z,
        size_z,
        8 * size_y,
    )
    _, at_sums, at_second, _ = edge_rows(size_x)
    for i in range(19):
        for x in range(size_x):
            held[i, x : x + 1, :] = bottom[i, x, 1:2, :]
            held[i, size_x + x : size_x + x + 1, :] = top[i, x, 6:7, :]
    second = fluid_parts([held[i] for i in range(19)], relax_blocks(entries, size_z), DOWNWARD + UPWARD)
    relaxed, bounced, density = second

    def write(down, up):
        for i in range(19):
            for x in range(size_x):
                at = i * size_x + x
                down[at : at + 1, :] = bottom[i, x, 0:1, :]
                up[at : at + 1, :] = top[i, x, 7:8, :]
        down[at_sums : at_sums + 4 * rows, :] = sums[: 4 * rows]
        up[at_sums : at_sums + 4 * rows, :] = sums[4 * rows :]
        for target, own, at_row in ((down, 0, 0), (up, 5, size_x)):
            parts = relaxed[own : own + 5] + bounced[own : own + 5] + [density]
            for k, value in enumerate(parts):
                at = at_second + k * size_x
                target[at : at + size_x, :] = value[at_row : at_row + size_x]

    even = lax.rem(lax.axis_index("gy"), 2) == 0

    @pl.when(even)
    def _():
        write(two, one)

    @pl.when(jnp.logical_not(even))
    def _():
        write(one, two)


def folded(table):
    return sum(
        table[8 * k : 8 * k + 8] if k == 0 else pltpu.roll(table[8 * k : 8 * k + 8], LANES * k, 1)
        for k in range(4)
    )


def merge_kernel(first, fold, own, far, near, one_in, two_in, column, one, two):
    del one_in, two_in
    merged = own[...] + near[...] + far[...]
    column[...] = merged
    deep = 8 // fold
    for k in range(fold):
        for target in (one, two):
            target[first : first + deep, 128 * k : 128 * k + 128] = merged[deep * k : deep * k + deep]


def relax_kernel(rates, entries):
    relax_rows(rates, entries)


def fluid_kernel(size_x, size_y, size_z, entries, populations, relaxed, bounced, density):
    blocks = relax_blocks(entries)
    for p, x in enumerate((0, size_x - 1)):
        for tile in range(size_y // 8):
            rows = slice(8 * tile, 8 * tile + 8)
            for part in range(size_z // 128):
                lanes = slice(128 * part, 128 * part + 128)
                f, b, d = fluid_parts([populations[i, x, rows, lanes] for i in range(19)], blocks, range(19))
                for i in range(19):
                    relaxed[i, p, rows, lanes] = f[i]
                    bounced[i, p, rows, lanes] = b[i]
                density[p, rows, lanes] = d


def stay_kernel(size_x, size_y, size_z, table, sums):
    a_x, a_y, a_z = cells_of(table[30:31, :].astype(I32), size_y, size_z)
    index = iota((size_x * size_y, 1), 0)
    rows_x = lax.div(index, jnp.int32(size_y))
    totals = deposited(
        [(rows_x, index - rows_x * size_y)],
        table[0:27, :],
        table[27:30, :],
        a_x,
        a_y,
        a_z,
        size_z,
        8 * size_y,
    )
    cells = size_x * size_y
    for c in range(4):
        for x in range(size_x):
            at = c * cells + x * size_y
            sums[c, x, :, :] = totals[at : at + size_y]


def outer_kernel(size_x, size_y, size_z, count, shifts, planes, *refs):
    if planes[0] == 0:
        column, *rest = refs[: 1 + len(shifts)]
        two, one, sums, outer, second, migrants = refs[1 + len(shifts) :]
        arrivals(size_x, size_y, size_z, count, shifts, column, one, two, rest, migrants)
    else:
        two, one, sums, outer, second = refs
    blank = jnp.zeros((8, size_z), F32)
    ones = jnp.ones((8, size_z), F32)
    _, at_sums, at_second, _ = edge_rows(size_x)

    def write(above, below):
        for p, x in enumerate(planes):
            for c in range(4):
                at = at_sums + c * 2 * size_x + 2 * x
                sums[c, p, :, :] = blank
                sums[c, p, 0:2, :] = above[at : at + 2, :]
                sums[c, p, 6:8, :] = below[at : at + 2, :]
            for i in range(19):
                at = i * size_x + x
                outer[i, p, :, :] = ones
                outer[i, p, 0:1, :] = above[at : at + 1, :]
                outer[i, p, 7:8, :] = below[at : at + 1, :]
            for k in range(11):
                at = at_second + k * size_x + x
                second[k, p, :, :] = ones
                second[k, p, 1:2, :] = above[at : at + 1, :]
                second[k, p, 6:7, :] = below[at : at + 1, :]

    even = lax.rem(lax.axis_index("gy"), 2) == 0

    @pl.when(even)
    def _():
        write(one, two)

    @pl.when(jnp.logical_not(even))
    def _():
        write(two, one)


def pair_source(here, parity, count):
    other = jnp.where(lax.rem(here, 2) == parity, here + 1, here - 1)
    return jnp.where((other >= 0) & (other < count), other, here + 2 * count)


def arrivals(size_x, size_y, size_z, count, shifts, column, one, two, rest, migrants):
    first = edge_rows(size_x)[-1]
    here = lax.axis_index("gy")
    fold = size_z // 128
    deep = 8 // fold

    def gathered(message):
        return jnp.concatenate(
            [message[first : first + deep, 128 * k : 128 * k + 128] for k in range(fold)], axis=0
        )

    parts = [column[...], gathered(one), gathered(two)] + [r[...] for r in rest]
    sources = [here, pair_source(here, 0, count), pair_source(here, 1, count)]
    sources += [lax.rem(here - shift + 2 * count, count) for shift in shifts]
    lane = iota((1, 128), 1)
    spot = lax.rem(lane, jnp.int32(LANES))
    group = lax.div(spot, jnp.int32(CAP))
    across = jnp.where(
        (group == 0) | (group == 2) | (group == 5), -1, jnp.where((group == 3) | (group == 6), 0, 1)
    )
    per_group = 128 // LANES
    tables, offsets = [], []
    for start in range(0, len(parts), per_group):
        blocks = [jnp.zeros((8, 128), F32)] * 4
        offset = jnp.full((1, 128), 2 * count, I32)
        for k, part in enumerate(parts[start : start + per_group]):
            place = lax.div(lane, jnp.int32(LANES)) == k
            for q in range(4):
                turn = LANES * (k - q) % 128
                blocks[q] = jnp.where(place, part if turn == 0 else pltpu.roll(part, turn, 1), blocks[q])
            offset = jnp.where(lax.div(lane, jnp.int32(LANES)) == k, sources[start + k] - here, offset)
        tables.append(jnp.concatenate(blocks, axis=0))
        offsets.append((offset + across) * size_y)
    table = jnp.concatenate(tables, axis=1)
    a_x, a_y, a_z = cells_of(table[30:31, :].astype(I32), size_y, size_z)
    migrants[0:32, :] = table
    migrants[32:33, :] = a_x.astype(F32)
    migrants[33:34, :] = (a_y + jnp.concatenate(offsets, axis=1)).astype(F32)
    migrants[34:35, :] = a_z.astype(F32)


def store_padded(target, i, x, tile, part, value, tiles):
    lanes = slice(128 * part, 128 * part + 128)
    if tile == tiles:
        target[i, x, 0:8, lanes] = value
        target[i, x, 8 + 8 * tiles : 16 + 8 * tiles, lanes] = value
    else:
        target[i, x, 8 + 8 * tile : 16 + 8 * tile, lanes] = value
        if tile == 0:
            target[i, x, 16 + 8 * tiles : 24 + 8 * tiles, lanes] = value


def turned(value, shift, size_z):
    return value if shift == 0 else pltpu.roll(value, shift % size_z, 1)


def solids(size_x, size_y, size_z, planes, first, sums, outer_sums, migrants, solid):
    a_x, a_y, a_z = (migrants[k : k + 1, :].astype(I32) for k in (32, 33, 34))
    wide = size_y + 8
    index = iota((len(planes) * wide, 1), 0)
    number = lax.div(index, jnp.int32(wide))
    row = index - number * wide
    rows_y = jnp.where(row < size_y + 2, row, jnp.where(row >= size_y + 6, row - wide, -3 * size_y))
    big = 4 * size_y * (lax.axis_size("gy") + 2)
    totals = deposited(
        [(number + planes[0], rows_y)], migrants[0:27, :], migrants[27:30, :], a_x, a_y, a_z, size_z, big
    )
    cells = len(planes) * wide
    for p, x in enumerate(planes):
        parts = []
        for c in range(4):
            at = c * cells + p * wide
            solid_sum = jnp.concatenate([sums[c, x, :, :], outer_sums[c, first + p, :, :]], axis=0)
            parts.append(totals[at : at + wide] + solid_sum)
        scale = 1.0 / (parts[0] + 1e-06)
        solid[0, p, :, :] = jnp.minimum(parts[0], 1.0)
        for c in (1, 2, 3):
            solid[c, p, :, :] = parts[c] * scale


def outer_collision(solid, outer, second, blocks, p, lanes):
    share, *flow = solid
    out = collide([outer[i, p, :, lanes] for i in range(19)], share, *flow, blocks)
    line = iota((8, 128), 0)
    away = jnp.where(line < 4, 1.0, -1.0)
    still = equilibrium(None, [away * v for v in flow], DOWNWARD)
    density = second[10, p, :, lanes]
    for k, (i, j) in enumerate(zip(DOWNWARD, UPWARD)):
        value = blended(second[k, p, :, lanes], second[5 + k, p, :, lanes], density, share, still[i])
        out[i] = jnp.where(line == 1, value, out[i])
        out[j] = jnp.where(line == 6, value, out[j])
    return out


def prepared_collision(solid, relaxed, bounced, dense, p, rows, lanes, numbers):
    share, *flow = solid
    still = equilibrium(None, flow, numbers)
    density = dense[p, rows, lanes]
    return {
        i: blended(relaxed[i, p, rows, lanes], bounced[i, p, rows, lanes], density, share, still[i])
        for i in numbers
    }


def tile_parts(size_y, size_z):
    for tile in range(size_y // 8 + 1):
        for part in range(size_z // 128):
            yield tile, slice(8 * tile, 8 * tile + 8), part, slice(128 * part, 128 * part + 128)


def by_plane(work, far):
    even = even_x()

    @pl.when(even if far else jnp.logical_not(even))
    def _():
        work(0, BACKWARD)

    @pl.when(jnp.logical_not(even) if far else even)
    def _():
        work(1, FORWARD)


def leaving_kernel(
    size_x, size_y, size_z, far, entries, sums, outer_sums, outer, second, migrants, relaxed, bounced,
    dense, *refs
):
    solid, message, leaving = refs[-3:]
    tiles = size_y // 8

    def work(place, numbers):
        plane = place * (size_x - 1)
        solids(size_x, size_y, size_z, (plane,), place, sums, outer_sums, migrants, solid)
        blocks = relax_blocks(entries)
        for tile, rows, part, lanes in tile_parts(size_y, size_z):
            s = [solid[c, 0, rows, lanes] for c in range(4)]
            if tile == tiles:
                out = outer_collision(s, outer, second, blocks, place, lanes)
            else:
                out = prepared_collision(s, relaxed, bounced, dense, place, rows, lanes, numbers)
            for k, i in enumerate(numbers):
                store_padded(leaving, k, 0, tile, part, out[i], tiles)
        write_face(leaving, message, numbers, size_y, size_z, True)

    by_plane(work, far)


def plane_solid(far, near, place, rows, lanes):
    in_far = even_x() if place == 0 else jnp.logical_not(even_x())
    return [jnp.where(in_far, far[c, 0, rows, lanes], near[c, 0, rows, lanes]) for c in range(4)]


def ends_kernel(
    size_x, size_y, size_z, entries, outer, second, relaxed, bounced, dense, solid_far, solid_near, post
):
    tiles = size_y // 8
    blocks = relax_blocks(entries)
    for p in range(2):
        for tile, rows, part, lanes in tile_parts(size_y, size_z):
            s = plane_solid(solid_far, solid_near, p, rows, lanes)
            if tile == tiles:
                out = outer_collision(s, outer, second, blocks, p, lanes)
            else:
                out = prepared_collision(s, relaxed, bounced, dense, p, rows, lanes, range(19))
            for i in range(19):
                store_padded(post, i, p, tile, part, out[i], tiles)


def middle_kernel(
    size_x, size_y, size_z, planes, entries, sums, outer_sums, outer, second, migrants, populations,
    post, solid
):
    tiles = size_y // 8
    solids(size_x, size_y, size_z, planes, 0, sums, outer_sums, migrants, solid)
    blocks = relax_blocks(entries)
    for p, x in enumerate(planes):
        for tile, rows, part, lanes in tile_parts(size_y, size_z):
            share, *flow = (solid[c, p, rows, lanes] for c in range(4))
            if tile == tiles:
                out = outer_collision((share, *flow), outer, second, blocks, p, lanes)
            else:
                h = [populations[i, x, rows, lanes] for i in range(19)]
                out = collide(h, share, *flow, blocks)
            for i in range(19):
                store_padded(post, i, p, tile, part, out[i], tiles)


def write_face(post, message, numbers, size_y, size_z, outer):
    tiles = size_y // 8
    for k, i in enumerate(numbers):
        _, c_y, c_z = VEC[i]
        for tile in range(tiles):
            at = 8 + 8 * tile - c_y
            to = k * size_y + 8 * tile
            message[to : to + 8, :] = turned(post[k, 0, at : at + 8, :], c_z, size_z)
        if outer:
            at = 8 + size_y - c_y
            value = turned(post[k, 0, at : at + 8, :], c_z, size_z)
            to = 5 * size_y + 2 * k
            message[to : to + 1, :] = value[0:1]
            message[to + 1 : to + 2, :] = value[7:8]


def streamed(ends, middle, messages, i, x, tile, size_x, size_y, size_z, walls):
    tiles = size_y // 8
    row = iota((8, size_z), 0)
    c_x, c_y, c_z = VEC[i]

    def plane(x):
        if x == 0:
            return ends, 0
        if x == size_x - 1:
            return ends, 1
        return middle, x - 1

    from_x = x - c_x
    if 0 <= from_x < size_x:
        source, p = plane(from_x)
        at = 8 + 8 * tile - c_y
        value = turned(source[i, p, at : at + 8, :], c_z, size_z)
    else:
        numbers = FORWARD if from_x < 0 else BACKWARD
        k = numbers.index(i)

        def received(at, rows):
            if len(messages) == 1:
                return messages[0][at : at + rows, :]
            near, far = messages
            from_near = jnp.logical_not(even_x()) if from_x < 0 else even_x()
            return jnp.where(from_near, near[at : at + rows, :], far[at : at + rows, :])

        if tile < tiles:
            value = received(k * size_y + 8 * tile, 8)
        else:
            at = 5 * size_y + 2 * k
            value = jnp.where(row < 4, received(at, 1), received(at + 1, 1))
    source, p = plane(x)
    if c_y == 1 and tile == 0:
        value = jnp.where((row == 0) & walls[0], source[OPP[i], p, 8:16, :], value)
    if c_y == -1 and tile == tiles - 1:
        back = source[OPP[i], p, size_y : 8 + size_y, :]
        value = jnp.where((row == 7) & walls[1], back, value)
    return value


def walls_of(count):
    here = lax.axis_index("gy")
    return here == 0, here == count - 1


def second_kernel(size_x, size_y, size_z, count, entries, ends, middle, solid, later):
    walls = walls_of(count)
    blocks = relax_blocks(entries)
    for p in range(size_x - 2):
        for tile in range(size_y // 8 + 1):
            rows = slice(8 * tile, 8 * tile + 8)
            h = [
                streamed(ends, middle, None, i, p + 1, tile, size_x, size_y, size_z, walls)
                for i in range(19)
            ]
            for part in range(size_z // 128):
                lanes = slice(128 * part, 128 * part + 128)
                s = [solid[c, p, rows, lanes] for c in range(4)]
                out = collide([v[:, lanes] for v in h], *s, blocks)
                for i in range(19):
                    store_padded(later, i, p, tile, part, out[i], size_y // 8)


def second_ends(
    size_x, size_y, size_z, count, entries, ends, middle, solid, messages, place, numbers, later, p
):
    walls = walls_of(count)
    blocks = relax_blocks(entries)
    x = place * (size_x - 1)
    for tile in range(size_y // 8 + 1):
        rows = slice(8 * tile, 8 * tile + 8)
        h = [
            streamed(ends, middle, messages, i, x, tile, size_x, size_y, size_z, walls) for i in range(19)
        ]
        for part in range(size_z // 128):
            lanes = slice(128 * part, 128 * part + 128)
            s = solid(rows, lanes)
            out = collide([v[:, lanes] for v in h], *s, blocks)
            for k, i in enumerate(numbers):
                store_padded(later, k, p, tile, part, out[i], size_y // 8)


def second_leaving_kernel(size_x, size_y, size_z, count, far, entries, ends, middle, solid, received, *refs):
    message, leaving = refs[-2:]

    def work(place, numbers):
        second_ends(
            size_x,
            size_y,
            size_z,
            count,
            entries,
            ends,
            middle,
            lambda rows, lanes: [solid[c, 0, rows, lanes] for c in range(4)],
            (received,),
            place,
            numbers,
            leaving,
            0,
        )
        write_face(leaving, message, numbers, size_y, size_z, False)

    by_plane(work, far)


def second_ends_kernel(
    size_x, size_y, size_z, count, entries, ends, middle, solid_far, solid_near, far, near, later
):
    for place in range(2):
        second_ends(
            size_x,
            size_y,
            size_z,
            count,
            entries,
            ends,
            middle,
            lambda rows, lanes: plane_solid(solid_far, solid_near, place, rows, lanes),
            (near, far),
            place,
            range(19),
            later,
            place,
        )


def last_kernel(size_x, size_y, size_z, count, ends, middle, advanced, held, done):
    walls = walls_of(count)
    copies = []
    for i in range(19):
        for x in range(size_x):
            if not 0 <= x - VEC[i][0] < size_x:
                continue
            for tile in range(size_y // 8):
                held[i, x, 8 * tile : 8 * tile + 8, :] = streamed(
                    ends, middle, None, i, x, tile, size_x, size_y, size_z, walls
                )
        low, high = max(0, VEC[i][0]), size_x + min(0, VEC[i][0])
        copy = pltpu.make_async_copy(
            held.at[i, low:high], advanced.at[i, low:high], done.at[i]
        )
        copy.start()
        copies.append(copy)
    for copy in copies:
        copy.wait()


def entering(size_x, size_y, size_z, count, ends, received, place, k, target):
    numbers = BACKWARD if place else FORWARD
    walls = walls_of(count)
    for tile in range(size_y // 8):
        target[k, 8 * tile : 8 * tile + 8, :] = streamed(
            ends, None, (received,), numbers[k], place * (size_x - 1), tile, size_x, size_y, size_z, walls
        )


def far_kernel(size_x, size_y, size_z, count, ends, received, held):
    def work(place, numbers):
        del numbers
        for k in range(5):
            entering(size_x, size_y, size_z, count, ends, received, place, k, held)

    by_plane(work, True)


def enter_kernel(size_x, size_y, size_z, count, ends, received, far, given, advanced, near, done):
    del given

    def write(place, held, base):
        numbers = BACKWARD if place else FORWARD
        for k, i in enumerate(numbers):
            copy = pltpu.make_async_copy(held.at[k], advanced.at[i, place * (size_x - 1)], done.at[base + k])
            copy.start()

    def work(place, numbers):
        del numbers
        write(1 - place, far, 0)
        for k in range(5):
            entering(size_x, size_y, size_z, count, ends, received, place, k, near)
        write(place, near, 5)

    by_plane(work, False)
    for k in range(5):
        pltpu.make_async_copy(far.at[k], advanced.at[FORWARD[k], 0], done.at[k]).wait()
        pltpu.make_async_copy(near.at[k], advanced.at[FORWARD[k], 0], done.at[5 + k]).wait()


def shape(*sizes):
    return jax.ShapeDtypeStruct(sizes, F32)


VMEM = pl.BlockSpec(memory_space=pltpu.VMEM)
SMEM = pl.BlockSpec(memory_space=pltpu.SMEM)
HBM = pl.BlockSpec(memory_space=pltpu.HBM)


def call(kernel, out_shape, limit, in_specs, out_specs=None, scratch=(), aliases=None):
    return pl.pallas_call(
        kernel,
        out_shape=out_shape,
        in_specs=in_specs,
        out_specs=jax.tree.map(lambda _: VMEM, out_shape) if out_specs is None else out_specs,
        scratch_shapes=scratch,
        input_output_aliases={} if aliases is None else aliases,
        compiler_params=pltpu.CompilerParams(vmem_limit_bytes=limit * 2**20),
    )


def in_hbm(value):
    return pltpu.with_memory_space_constraint(value, pltpu.HBM)


def around(value, axis, steps):
    count = lax.axis_size(axis)
    return lax.ppermute(value, axis, [(i, (i + steps) % count) for i in range(count)])


def paired(value, axis, parity, wrap=False):
    count = lax.axis_size(axis)
    if wrap and count % 2:
        raise ValueError("odd ring")
    pairs = []
    for i in range(count):
        other = i + 1 if i % 2 == parity else i - 1
        other = other % count if wrap else other
        pairs.append((i, other if 0 <= other < count else i))
    return lax.ppermute(value, axis, pairs)


def exchanged(near, far):
    far = paired(far, "gx", 1, True)
    return paired(near, "gx", 0, True), far


def local(populations, relax_rates, velocity, velocity_change, fractions, anchor, destination):
    _, size_x, size_y, size_z = populations.shape
    count = lax.axis_size("gy")
    rows = anchor.shape[0]
    sizes = (size_x, size_y, size_z)
    part = functools.partial
    packed = shape(8, 128)
    band = shape(19, size_x, 8, size_z)
    table, own, near, far, bottom, top = call(
        pack_kernel,
        (shape(32, rows), packed, packed, packed, band, band),
        8,
        [HBM] * 6,
        scratch=[
            pltpu.VMEM((3, rows), F32),
            pltpu.VMEM((3, rows), F32),
            pltpu.VMEM((27, rows), F32),
            pltpu.VMEM((1, rows), I32),
            pltpu.VMEM((1, rows), I32),
            pltpu.SemaphoreType.DMA((7,)),
        ],
    )(*map(in_hbm, (velocity, velocity_change, fractions, anchor[None, :], destination[None, :], populations)))
    near, far = exchanged(near, far)
    first = edge_rows(size_x)[-1]
    fold = size_z // 128
    message = shape(-(-(first + 8 // fold) // 8) * 8, size_z)
    entries = call(relax_kernel, shape(ENTRIES, 8, 128), 8, [SMEM])(relax_rates)
    one, two = call(
        part(edge_kernel, *sizes),
        (message, message),
        8,
        [VMEM] * 4,
        scratch=[pltpu.VMEM((19, 2 * size_x, size_z), F32)],
    )(bottom, top, table, entries)
    column, one, two = call(
        part(merge_kernel, first, fold),
        (shape(8, 128), message, message),
        8,
        [VMEM] * 5,
        aliases={3: 1, 4: 2},
    )(own, far, near, one, two)
    shifts = []
    for shift in (2, -2):
        if shift % count > 1 and all((shift - other) % count for other in shifts):
            shifts.append(shift)
    rest = [around(column, "gy", shift) for shift in shifts]
    one, two = paired(one, "gy", 0), paired(two, "gy", 1)
    sums = call(part(stay_kernel, *sizes), shape(4, *sizes), 16, [VMEM])(table)
    plane_pair = shape(19, 2, size_y, size_z)
    parts = call(
        part(fluid_kernel, *sizes), (plane_pair, plane_pair, shape(2, size_y, size_z)), 16, [VMEM] * 2
    )(entries, populations)
    width = -(-(3 + len(shifts)) * LANES // 128) * 128
    outside, inside = (0, size_x - 1), tuple(range(1, size_x - 1))

    def outer_shapes(planes):
        return tuple(shape(k, len(planes), 8, size_z) for k in (4, 19, 11))

    outer_sums, outer, second, migrants = call(
        part(outer_kernel, *sizes, count, shifts, outside),
        outer_shapes(outside) + (shape(40, width),),
        8,
        [VMEM] * (3 + len(shifts)),
    )(column, *rest, two, one)

    def padded(planes):
        return shape(19, planes, size_y + 24, size_z)

    def solid_shape(planes):
        return shape(4, planes, size_y + 8, size_z)

    unused = pl.BlockSpec(memory_space=pl.ANY)
    sent = pltpu.VMEM((5, 1, size_y + 24, size_z), F32)
    wide_face = shape((5 * size_y + 10 + 7) // 8 * 8, size_z)
    face = shape(5 * size_y, size_z)

    def leaving(far, *given):
        return call(
            part(leaving_kernel, *sizes, far),
            (solid_shape(1), wide_face),
            16,
            [VMEM] * 9 + [unused] * (len(given) - 9),
            scratch=[sent],
        )(*given)

    known = (entries, sums, outer_sums, outer, second, migrants, *parts)
    solid_far, far = leaving(True, *known)
    solid_near, near = leaving(False, *known, solid_far)
    near, far = exchanged(near, far)
    inner = call(part(outer_kernel, *sizes, count, shifts, inside), outer_shapes(inside), 8, [VMEM] * 2)(
        two, one
    )
    middle, solid_middle = call(
        part(middle_kernel, *sizes, inside),
        (padded(len(inside)), solid_shape(len(inside))),
        16,
        [VMEM] * 7,
    )(entries, sums, *inner, migrants, populations)
    ends = call(part(ends_kernel, *sizes), padded(2), 16, [VMEM] * 8)(
        entries, outer, second, *parts, solid_far, solid_near
    )
    later_middle = call(part(second_kernel, *sizes, count), padded(len(inside)), 16, [VMEM] * 4)(
        entries, ends, middle, solid_middle
    )

    def second_leaving(far, *given):
        return call(
            part(second_leaving_kernel, *sizes, count, far),
            face,
            16,
            [VMEM] * 5 + [unused] * (len(given) - 5),
            scratch=[sent],
        )(*given)

    received = (far, near)
    far = second_leaving(True, entries, ends, middle, solid_far, far, later_middle)
    near = second_leaving(False, entries, ends, middle, solid_near, near, far)
    near, far = exchanged(near, far)
    later_ends = call(part(second_ends_kernel, *sizes, count), padded(2), 16, [VMEM] * 7)(
        entries, ends, middle, solid_far, solid_near, *received
    )
    advanced = call(
        part(last_kernel, *sizes, count),
        shape(19, *sizes),
        16,
        [VMEM] * 2,
        HBM,
        [pltpu.VMEM((19, *sizes), F32), pltpu.SemaphoreType.DMA((19,))],
    )(later_ends, later_middle)
    slabs = (5, size_y, size_z)
    far = call(part(far_kernel, *sizes, count), shape(*slabs), 16, [VMEM] * 2)(later_ends, far)
    return call(
        part(enter_kernel, *sizes, count),
        shape(19, *sizes),
        16,
        [VMEM] * 3 + [HBM],
        HBM,
        [pltpu.VMEM(slabs, F32), pltpu.SemaphoreType.DMA((10,))],
        {3: 0},
    )(later_ends, near, far, advanced)


def solution(mesh):
    placed = (
        P(None, "gx", "gy", None),
        P(),
        P(None, ("gx", "gy")),
        P(None, ("gx", "gy")),
        P(None, ("gx", "gy")),
        P(("gx", "gy")),
        P(("gx", "gy")),
    )
    return jax.shard_map(
        local, mesh=mesh, in_specs=placed, out_specs=P(None, "gx", "gy", None), check_vma=False
    )
```

```python
import functools

import jax
import jax.numpy as jnp
import numpy as np
from jax import lax
from jax.experimental import pallas as pl
from jax.experimental.pallas import tpu as pltpu
from jax.sharding import PartitionSpec as P

CAP = 4
STEPS = 2
LANES = 8 * CAP
F32 = jnp.float32
BF16 = jnp.bfloat16
I32 = jnp.int32


def lattice():
    vectors = [[0, 0, 0]]
    for axis_one in range(3):
        for orient in (1, -1):
            vector_one = [0, 0, 0]
            vector_one[axis_one] = orient
            vectors.append(vector_one)
    for axis_one, axis_two in ((0, 1), (0, 2), (1, 2)):
        for orient in (1, -1):
            for second in (1, -1):
                vector_one = [0, 0, 0]
                vector_one[axis_one] = orient
                vector_one[axis_two] = second
                vectors.append(vector_one)
    integral = np.array(vectors)
    speeds = integral * 1.0
    length = (speeds**2).sum(axis=1)
    weights = np.where(length == 0, 1.0 / 3.0, np.where(length == 1, 1.0 / 18.0, 1.0 / 36.0))
    opposite = [vectors.index([0 - component for component in vector_one]) for vector_one in vectors]
    along_x, along_y, along_z = (speeds[:, 0], speeds[:, 1], speeds[:, 2])
    rows_list = [
        np.ones(19),
        along_x,
        along_y,
        along_z,
        length,
        3 * along_x**2 - length,
        along_y**2 - along_z**2,
        along_x * along_y,
        along_y * along_z,
        along_x * along_z,
        along_x * length,
        along_y * length,
        along_z * length,
        along_x * (along_y**2 - along_z**2),
        along_y * (along_z**2 - along_x**2),
        along_z * (along_x**2 - along_y**2),
        length**2,
        (3 * along_x**2 - length) * length,
        (along_y**2 - along_z**2) * length,
    ]
    basis_rows = []
    for candidate in rows_list:
        for earlier in basis_rows:
            candidate = candidate - np.dot(candidate, earlier) * earlier
        basis_rows.append(candidate / np.sqrt(np.dot(candidate, candidate)))
    return [tuple(v) for v in vectors], weights, opposite, np.array(basis_rows)


VEC, WEIGHTS, OPP, BASIS = lattice()
FORWARD = [i for i in range(19) if VEC[i][0] == 1]
BACKWARD = [i for i in range(19) if VEC[i][0] == -1]
DOWNWARD = [i for i in range(19) if VEC[i][1] == -1]
UPWARD = [OPP[i] for i in DOWNWARD]


def symmetric_blocks():
    def vec(entries):
        out = np.zeros(19)
        for index, value in entries.items():
            out[index] = value
        return out

    def plane(base):
        s_one, d_one = vec({base: 1, base + 3: 1}), vec({base: 1, base + 3: -1})
        s_two, d_two = vec({base + 1: 1, base + 2: 1}), vec({base + 1: 1, base + 2: -1})
        return s_one + s_two, s_one - s_two, d_one + d_two, d_one - d_two

    rest = vec({0: 1})
    s_x, s_y, s_z = vec({1: 1, 2: 1}), vec({3: 1, 4: 1}), vec({5: 1, 6: 1})
    d_x, d_y, d_z = vec({1: 1, 2: -1}), vec({3: 1, 4: -1}), vec({5: 1, 6: -1})
    xy, q_xy, x_xy, y_xy = plane(7)
    xz, q_xz, x_xz, z_xz = plane(11)
    yz, q_yz, y_yz, z_yz = plane(15)
    blocks = [
        [rest, s_x + s_y + s_z, xy + xz + yz],
        [2 * s_x - s_y - s_z, xy + xz - 2 * yz],
        [s_y - s_z, xy - xz],
        [q_xy],
        [q_xz],
        [q_yz],
        [d_x, x_xy, x_xz],
        [d_y, y_xy, y_yz],
        [d_z, z_xz, z_yz],
    ]
    scales = [[1, 1 / 6, 1 / 12], [1 / 12, 1 / 24], [1 / 4, 1 / 8]]
    scales += [[1 / 4]] * 3 + [[1 / 2, 1 / 4, 1 / 4]] * 3
    forward = np.array([row for block in blocks for row in block])
    back = np.linalg.inv(forward)
    left = forward @ np.diag(1.0 / WEIGHTS) @ BASIS.T
    right = BASIS @ np.diag(WEIGHTS) @ back
    table = []
    start = 0
    for block, scale in zip(blocks, scales):
        size = len(block)
        rows = []
        for a in range(size):
            row = []
            for b in range(size):
                per_rate = -scale[a] * left[start + a, :] * right[:, start + b]
                row.append([(k, float(v)) for k, v in enumerate(per_rate) if abs(v) > 1e-12])
            rows.append(row)
        table.append(rows)
        start += size
    return table


RELAX = symmetric_blocks()


def relax_rows(rates, target):
    values = [rates[k] for k in range(19)]
    at = 0
    for block in RELAX:
        for row in block:
            for terms in row:
                total = None
                for k, factor in terms:
                    part = values[k] * np.float32(factor)
                    total = part if total is None else total + part
                target[at] = jnp.full((8, 128), total, F32)
                at += 1


def relax_blocks(table, lanes=128):
    blocks, at = [], 0
    for block in RELAX:
        rows = []
        for row in block:
            rows.append(
                [jnp.concatenate([table[at + k]] * (lanes // 128), axis=1) for k in range(len(row))]
            )
            at += len(row)
        blocks.append(rows)
    return blocks


ENTRIES = sum(len(row) for block in RELAX for row in block)


def apply_block(block, values):
    out = []
    for row in block:
        total = None
        for factor, value in zip(row, values):
            part = factor * value
            total = part if total is None else total + part
        out.append(total)
    return out


def collide(h, solid, s_x, s_y, s_z, blocks):
    def plane(base):
        s_one, d_one = h[base] + h[base + 3], h[base] - h[base + 3]
        s_two, d_two = h[base + 1] + h[base + 2], h[base + 1] - h[base + 2]
        return s_one + s_two, s_one - s_two, d_one + d_two, d_one - d_two

    sum_x, dif_x = h[1] + h[2], h[1] - h[2]
    sum_y, dif_y = h[3] + h[4], h[3] - h[4]
    sum_z, dif_z = h[5] + h[6], h[5] - h[6]
    xy, q_xy, x_xy, y_xy = plane(7)
    xz, q_xz, x_xz, z_xz = plane(11)
    yz, q_yz, y_yz, z_yz = plane(15)
    axes = sum_x + sum_y + sum_z
    edges = xy + xz + yz
    density = h[0] * (1.0 / 3.0) + axes * (1.0 / 18.0) + edges * (1.0 / 36.0)
    m_x = dif_x * (1.0 / 18.0) + (x_xy + x_xz) * (1.0 / 36.0)
    m_y = dif_y * (1.0 / 18.0) + (y_xy + y_yz) * (1.0 / 36.0)
    m_z = dif_z * (1.0 / 18.0) + (z_xz + z_yz) * (1.0 / 36.0)
    inverse = 1.0 / density
    u_x, u_y, u_z = m_x * inverse, m_y * inverse, m_z * inverse
    e_xx, e_yy, e_zz = m_x * u_x, m_y * u_y, m_z * u_z
    e_xy, e_xz, e_yz = m_x * u_y, m_x * u_z, m_y * u_z
    energy = e_xx + e_yy + e_zz
    turn = e_yy - e_zz
    lean = 3.0 * e_xx - energy
    rest_off = h[0] - density + 1.5 * energy
    axes_off = axes - 6.0 * density
    edges_off = edges - 12.0 * density - 18.0 * energy
    a_one = 3.0 * sum_x - axes - 9.0 * lean
    b_one = edges - 3.0 * yz - 18.0 * lean
    a_two = sum_y - sum_z - 9.0 * turn
    b_two = xy - xz - 18.0 * turn
    q_xy = q_xy - 36.0 * e_xy
    q_xz = q_xz - 36.0 * e_xz
    q_yz = q_yz - 36.0 * e_yz

    r_rest, r_axes, r_edges = apply_block(blocks[0], [rest_off, axes_off, edges_off])
    r_a_one, r_b_one = apply_block(blocks[1], [a_one, b_one])
    r_a_two, r_b_two = apply_block(blocks[2], [a_two, b_two])
    fluid = 1.0 - solid
    mixed = solid * density
    w_x, w_y, w_z = solid * m_x, solid * m_y, solid * m_z
    n_x, n_y, n_z = mixed * s_x, mixed * s_y, mixed * s_z
    p_x = n_x * s_x - solid * e_xx
    p_y = n_y * s_y - solid * e_yy
    p_z = n_z * s_z - solid * e_zz
    total = 1.5 * (p_x + p_y + p_z)
    lean_s = 2.25 * p_x - 0.5 * total
    turn_s = 2.25 * (p_y - p_z)
    rest = fluid * r_rest - total
    axes = fluid * r_axes
    edges = fluid * r_edges + total
    a_one = fluid * r_a_one + lean_s
    b_one = fluid * r_b_one + lean_s
    a_two = fluid * r_a_two + turn_s
    b_two = fluid * r_b_two + turn_s
    q_xy = fluid * apply_block(blocks[3], [q_xy])[0] + 9.0 * (n_x * s_y - solid * e_xy)
    q_xz = fluid * apply_block(blocks[4], [q_xz])[0] + 9.0 * (n_x * s_z - solid * e_xz)
    q_yz = fluid * apply_block(blocks[5], [q_yz])[0] + 9.0 * (n_y * s_z - solid * e_yz)

    def odd(block, axis, one, two, m, n, w):
        six = 6.0 * m
        axis = axis - six
        twelve = six + six
        one = one - twelve
        two = two - twelve
        r_axis, r_one, r_two = apply_block(block, [axis, one, two])
        push = 3.0 * (n - w)
        half = 0.5 * solid
        return (
            fluid * r_axis - solid * axis + push,
            fluid * r_one - half * one + push,
            fluid * r_two - half * two + push,
        )

    d_x, x_xy, x_xz = odd(blocks[6], dif_x, x_xy, x_xz, m_x, n_x, w_x)
    d_y, y_xy, y_yz = odd(blocks[7], dif_y, y_xy, y_yz, m_y, n_y, w_y)
    d_z, z_xz, z_yz = odd(blocks[8], dif_z, z_xz, z_yz, m_z, n_z, w_z)
    out = [None] * 19
    out[0] = h[0] + rest
    even = axes + 2.0 * a_one
    out[1], out[2] = h[1] + (even + d_x), h[2] + (even - d_x)
    base = axes - a_one
    even = base + a_two
    out[3], out[4] = h[3] + (even + d_y), h[4] + (even - d_y)
    even = base - a_two
    out[5], out[6] = h[5] + (even + d_z), h[6] + (even - d_z)

    def spread(start, even, twist, one, two):
        same, cross = even + twist, even - twist
        plus, minus = one + two, one - two
        out[start] = h[start] + (same + plus)
        out[start + 3] = h[start + 3] + (same - plus)
        out[start + 1] = h[start + 1] + (cross + minus)
        out[start + 2] = h[start + 2] + (cross - minus)

    base = edges + b_one
    spread(7, base + b_two, q_xy, x_xy, y_xy)
    spread(11, base - b_two, q_xz, x_xz, z_xz)
    spread(15, edges - 2.0 * b_one, q_yz, y_yz, z_yz)
    return out


def equilibrium(density, flow, numbers):
    v_x, v_y, v_z = flow
    rest = 1.0 - 1.5 * (v_x * v_x + v_y * v_y + v_z * v_z)
    out = {}
    for i in numbers:
        if i in out:
            continue
        along = None
        for sign, v in zip(VEC[i], flow):
            if sign:
                part = v if sign == 1 else -v
                along = part if along is None else along + part
        if along is None:
            out[i] = rest
        else:
            along = 3.0 * along
            even = rest + 0.5 * along * along
            out[i], out[OPP[i]] = even + along, even - along
    return out


def fluid_parts(h, blocks, numbers):
    zero = jnp.zeros_like(h[0])
    relaxed = collide(h, zero, zero, zero, zero, blocks)
    density, flow = zero, [zero, zero, zero]
    for i in range(19):
        part = np.float32(WEIGHTS[i]) * h[i]
        density = density + part
        for k in range(3):
            if VEC[i][k]:
                flow[k] = flow[k] + part if VEC[i][k] == 1 else flow[k] - part
    inverse = 1.0 / density
    still = equilibrium(density, [f * inverse for f in flow], numbers)
    bounced = [h[OPP[i]] - density * still[OPP[i]] for i in numbers]
    return [relaxed[i] for i in numbers], bounced, density


def blended(relaxed, bounced, density, share, still):
    return relaxed + share * ((bounced + density * still) - relaxed)


def iota(shape, dim):
    return lax.broadcasted_iota(I32, shape, dim)


def cells_of(anchor, size_y, size_z):
    plane = size_y * size_z
    a_x = lax.div(anchor, jnp.int32(plane))
    rest = anchor - a_x * plane
    a_y = lax.div(rest, jnp.int32(size_z))
    return a_x, a_y, rest - a_y * size_z


def halves(value):
    high = value.astype(BF16)
    return high, (value - high.astype(F32)).astype(BF16)


def dot_t(left, right):
    return lax.dot_general(left, right, (((1,), (1,)), ((), ())), preferred_element_type=F32)


def deposited(groups, shares, velocity, a_x, a_y, a_z, size_z, big):
    centre = a_x * big + a_y
    lanes = centre.shape[1]
    totals = None
    rows_z = iota((size_z, lanes), 0)
    for off_z in range(3):
        weights = []
        for rows_x, rows_y in groups:
            away = rows_x * big + rows_y - centre
            weight = jnp.zeros(away.shape, F32)
            for off in range(9):
                move = (off // 3 - 1) * big + off % 3 - 1
                row = 3 * off + off_z
                weight = jnp.where(away == move, shares[row : row + 1, :], weight)
            weights.append([weight] + [weight * velocity[k : k + 1, :] for k in range(3)])
        rows = jnp.concatenate([w for block in weights for w in block], axis=0)
        high, low = halves(rows)
        hot = jnp.where(rows_z == a_z + (off_z - 1), 1.0, 0.0).astype(BF16)
        part = dot_t(high, hot) + dot_t(low, hot)
        totals = part if totals is None else totals + part
    return totals


def even_x():
    return lax.rem(lax.axis_index("gx"), 2) == 0


def pack_kernel(
    velocity_in,
    change_in,
    fractions_in,
    anchor_in,
    destination_in,
    populations,
    table,
    own,
    near,
    far,
    bottom,
    top,
    velocity,
    change,
    fractions,
    anchor,
    destination,
    done,
):
    pairs = (
        (destination_in, destination),
        (velocity_in, velocity),
        (change_in, change),
        (fractions_in, fractions),
        (anchor_in, anchor),
        (populations.at[:, :, 0:8, :], bottom),
        (populations.at[:, :, populations.shape[2] - 8 :, :], top),
    )
    copies = [pltpu.make_async_copy(a, b, done.at[k]) for k, (a, b) in enumerate(pairs)]
    for copy in copies:
        copy.start()
    rows = destination.shape[1]
    order = jnp.where(iota((128, 128), 0) <= iota((128, 128), 1), 1.0, 0.0).astype(BF16)
    for copy in copies[:5]:
        copy.wait()
    dest = destination[...]
    kinds = iota((16, rows), 0)
    hot = jnp.where(dest == kinds, 1.0, 0.0)
    seen = jnp.zeros((16, 1), F32)
    ranks = []
    for start in range(0, rows, 128):
        counted = seen + lax.dot_general(
            hot[:, start : start + 128].astype(BF16),
            order,
            (((1,), (0,)), ((), ())),
            preferred_element_type=F32,
        )
        ranks.append(counted)
        seen = counted[:, 127:128]
    rank = jnp.concatenate(ranks, axis=1)
    kind = iota((16, 1), 0)
    begin = jnp.where(
        kind < 3,
        5 * CAP + CAP * kind,
        jnp.where(kind == 3, 0, jnp.where(kind == 5, CAP, 2 * CAP + CAP * (kind - 6))),
    ).astype(F32)
    leaving = (dest < 9) & (dest != 4)
    slot = jnp.sum(hot * (begin + rank - 1.0), axis=0, keepdims=True)
    slot = jnp.where(leaving, slot, -1.0).astype(I32)
    chosen = jnp.where(iota((128, rows), 0) == slot, 1.0, 0.0).astype(BF16)
    new_velocity = velocity[...] + change[...]
    payload = jnp.concatenate(
        [fractions[...], new_velocity, anchor[...].astype(F32), jnp.zeros((1, rows), F32)], axis=0
    )
    high = payload.astype(BF16)
    middle, low = halves(payload - high.astype(F32))
    packed = dot_t(high, chosen) + dot_t(middle, chosen) + dot_t(low, chosen)
    packed = folded(packed)
    lane = lax.rem(iota((8, 128), 1), jnp.int32(LANES))
    own[...] = jnp.where(lane < 2 * CAP, packed, 0.0)
    ahead = jnp.where((lane >= 2 * CAP) & (lane < 5 * CAP), packed, 0.0)
    behind = jnp.where(lane >= 5 * CAP, packed, 0.0)
    even = even_x()
    near[...] = jnp.where(even, ahead, behind)
    far[...] = jnp.where(even, behind, ahead)
    table[...] = jnp.where((iota((32, rows), 0) < 27) & (dest != 4), 0.0, payload)
    for copy in copies[5:]:
        copy.wait()


def edge_rows(size_x):
    starts = [0]
    for rows in (19 * size_x, 4 * 2 * size_x, 11 * size_x):
        starts.append(starts[-1] + rows)
    return starts


def edge_kernel(size_x, size_y, size_z, bottom, top, table, entries, one, two, held):
    a_x, a_y, a_z = cells_of(table[30:31, :].astype(I32), size_y, size_z)
    rows = 2 * size_x
    index = iota((rows, 1), 0)
    rows_x, low = lax.div(index, jnp.int32(2)), lax.rem(index, jnp.int32(2))
    sums = deposited(
        [(rows_x, low), (rows_x, low + (size_y - 2))],
        table[0:27, :],
        table[27:30, :],
        a_x,
        a_y,
        a_z,
        size_z,
        8 * size_y,
    )
    _, at_sums, at_second, _ = edge_rows(size_x)
    for i in range(19):
        for x in range(size_x):
            held[i, x : x + 1, :] = bottom[i, x, 1:2, :]
            held[i, size_x + x : size_x + x + 1, :] = top[i, x, 6:7, :]
    second = fluid_parts([held[i] for i in range(19)], relax_blocks(entries, size_z), DOWNWARD + UPWARD)
    relaxed, bounced, density = second

    def write(down, up):
        for i in range(19):
            for x in range(size_x):
                at = i * size_x + x
                down[at : at + 1, :] = bottom[i, x, 0:1, :]
                up[at : at + 1, :] = top[i, x, 7:8, :]
        down[at_sums : at_sums + 4 * rows, :] = sums[: 4 * rows]
        up[at_sums : at_sums + 4 * rows, :] = sums[4 * rows :]
        for target, own, at_row in ((down, 0, 0), (up, 5, size_x)):
            parts = relaxed[own : own + 5] + bounced[own : own + 5] + [density]
            for k, value in enumerate(parts):
                at = at_second + k * size_x
                target[at : at + size_x, :] = value[at_row : at_row + size_x]

    even = lax.rem(lax.axis_index("gy"), 2) == 0

    @pl.when(even)
    def _():
        write(two, one)

    @pl.when(jnp.logical_not(even))
    def _():
        write(one, two)


def folded(table):
    return sum(
        table[8 * k : 8 * k + 8] if k == 0 else pltpu.roll(table[8 * k : 8 * k + 8], LANES * k, 1)
        for k in range(4)
    )


def merge_kernel(first, fold, own, far, near, one_in, column, one):
    del one_in
    merged = own[...] + near[...] + far[...]
    column[...] = merged
    deep = 8 // fold
    for k in range(fold):
        one[first : first + deep, 128 * k : 128 * k + 128] = merged[deep * k : deep * k + deep]


def relax_kernel(rates, entries):
    relax_rows(rates, entries)


def fluid_kernel(size_x, size_y, size_z, entries, populations, relaxed, bounced, density):
    blocks = relax_blocks(entries)
    for p, x in enumerate((0, size_x - 1)):
        for tile in range(size_y // 8):
            rows = slice(8 * tile, 8 * tile + 8)
            for part in range(size_z // 128):
                lanes = slice(128 * part, 128 * part + 128)
                f, b, d = fluid_parts([populations[i, x, rows, lanes] for i in range(19)], blocks, range(19))
                for i in range(19):
                    relaxed[i, p, rows, lanes] = f[i]
                    bounced[i, p, rows, lanes] = b[i]
                density[p, rows, lanes] = d


def stay_kernel(size_x, size_y, size_z, table, after, sums):
    del after
    a_x, a_y, a_z = cells_of(table[30:31, :].astype(I32), size_y, size_z)
    index = iota((size_x * size_y, 1), 0)
    rows_x = lax.div(index, jnp.int32(size_y))
    totals = deposited(
        [(rows_x, index - rows_x * size_y)],
        table[0:27, :],
        table[27:30, :],
        a_x,
        a_y,
        a_z,
        size_z,
        8 * size_y,
    )
    cells = size_x * size_y
    for c in range(4):
        for x in range(size_x):
            at = c * cells + x * size_y
            sums[c, x, :, :] = totals[at : at + size_y]


def outer_kernel(size_x, size_y, size_z, count, shifts, planes, *refs):
    if planes[0] == 0:
        column, one, column_two, *rest = refs[: 3 + len(shifts)]
        two, sums, outer, second, migrants = refs[3 + len(shifts) :]
        arrivals(size_x, size_y, size_z, count, shifts, column, one, column_two, rest, migrants)
    else:
        two, one, sums, outer, second = refs
    blank = jnp.zeros((8, size_z), F32)
    ones = jnp.ones((8, size_z), F32)
    _, at_sums, at_second, _ = edge_rows(size_x)

    def write(above, below):
        for p, x in enumerate(planes):
            for c in range(4):
                at = at_sums + c * 2 * size_x + 2 * x
                sums[c, p, :, :] = blank
                sums[c, p, 0:2, :] = above[at : at + 2, :]
                sums[c, p, 6:8, :] = below[at : at + 2, :]
            for i in range(19):
                at = i * size_x + x
                outer[i, p, :, :] = ones
                outer[i, p, 0:1, :] = above[at : at + 1, :]
                outer[i, p, 7:8, :] = below[at : at + 1, :]
            for k in range(11):
                at = at_second + k * size_x + x
                second[k, p, :, :] = ones
                second[k, p, 1:2, :] = above[at : at + 1, :]
                second[k, p, 6:7, :] = below[at : at + 1, :]

    even = lax.rem(lax.axis_index("gy"), 2) == 0

    @pl.when(even)
    def _():
        write(one, two)

    @pl.when(jnp.logical_not(even))
    def _():
        write(two, one)


def pair_source(here, parity, count):
    other = jnp.where(lax.rem(here, 2) == parity, here + 1, here - 1)
    return jnp.where((other >= 0) & (other < count), other, here + 2 * count)


def arrivals(size_x, size_y, size_z, count, shifts, column, one, two, rest, migrants):
    first = edge_rows(size_x)[-1]
    here = lax.axis_index("gy")
    fold = size_z // 128
    deep = 8 // fold

    def gathered(message):
        return jnp.concatenate(
            [message[first : first + deep, 128 * k : 128 * k + 128] for k in range(fold)], axis=0
        )

    parts = [column[...], gathered(one), two[...]] + [r[...] for r in rest]
    sources = [here, pair_source(here, 0, count), pair_source(here, 1, count)]
    sources += [lax.rem(here - shift + 2 * count, count) for shift in shifts]
    lane = iota((1, 128), 1)
    spot = lax.rem(lane, jnp.int32(LANES))
    group = lax.div(spot, jnp.int32(CAP))
    across = jnp.where(
        (group == 0) | (group == 2) | (group == 5), -1, jnp.where((group == 3) | (group == 6), 0, 1)
    )
    per_group = 128 // LANES
    tables, offsets = [], []
    for start in range(0, len(parts), per_group):
        blocks = [jnp.zeros((8, 128), F32)] * 4
        offset = jnp.full((1, 128), 2 * count, I32)
        for k, part in enumerate(parts[start : start + per_group]):
            place = lax.div(lane, jnp.int32(LANES)) == k
            for q in range(4):
                turn = LANES * (k - q) % 128
                blocks[q] = jnp.where(place, part if turn == 0 else pltpu.roll(part, turn, 1), blocks[q])
            offset = jnp.where(lax.div(lane, jnp.int32(LANES)) == k, sources[start + k] - here, offset)
        tables.append(jnp.concatenate(blocks, axis=0))
        offsets.append((offset + across) * size_y)
    table = jnp.concatenate(tables, axis=1)
    a_x, a_y, a_z = cells_of(table[30:31, :].astype(I32), size_y, size_z)
    migrants[0:32, :] = table
    migrants[32:33, :] = a_x.astype(F32)
    migrants[33:34, :] = (a_y + jnp.concatenate(offsets, axis=1)).astype(F32)
    migrants[34:35, :] = a_z.astype(F32)


def store_padded(target, i, x, tile, part, value, tiles):
    lanes = slice(128 * part, 128 * part + 128)
    if tile == tiles:
        target[i, x, 0:8, lanes] = value
        target[i, x, 8 + 8 * tiles : 16 + 8 * tiles, lanes] = value
    else:
        target[i, x, 8 + 8 * tile : 16 + 8 * tile, lanes] = value
        if tile == 0:
            target[i, x, 16 + 8 * tiles : 24 + 8 * tiles, lanes] = value


def turned(value, shift, size_z):
    return value if shift == 0 else pltpu.roll(value, shift % size_z, 1)


def solids(size_x, size_y, size_z, planes, first, sums, outer_sums, migrants, solid):
    a_x, a_y, a_z = (migrants[k : k + 1, :].astype(I32) for k in (32, 33, 34))
    wide = size_y + 8
    index = iota((len(planes) * wide, 1), 0)
    number = lax.div(index, jnp.int32(wide))
    row = index - number * wide
    rows_y = jnp.where(row < size_y + 2, row, jnp.where(row >= size_y + 6, row - wide, -3 * size_y))
    big = 4 * size_y * (lax.axis_size("gy") + 2)
    totals = deposited(
        [(number + planes[0], rows_y)], migrants[0:27, :], migrants[27:30, :], a_x, a_y, a_z, size_z, big
    )
    cells = len(planes) * wide
    for p, x in enumerate(planes):
        parts = []
        for c in range(4):
            at = c * cells + p * wide
            solid_sum = jnp.concatenate([sums[c, x, :, :], outer_sums[c, first + p, :, :]], axis=0)
            parts.append(totals[at : at + wide] + solid_sum)
        scale = 1.0 / (parts[0] + 1e-06)
        solid[0, p, :, :] = jnp.minimum(parts[0], 1.0)
        for c in (1, 2, 3):
            solid[c, p, :, :] = parts[c] * scale


def outer_collision(solid, outer, second, blocks, p, lanes):
    share, *flow = solid
    out = collide([outer[i, p, :, lanes] for i in range(19)], share, *flow, blocks)
    line = iota((8, 128), 0)
    away = jnp.where(line < 4, 1.0, -1.0)
    still = equilibrium(None, [away * v for v in flow], DOWNWARD)
    density = second[10, p, :, lanes]
    for k, (i, j) in enumerate(zip(DOWNWARD, UPWARD)):
        value = blended(second[k, p, :, lanes], second[5 + k, p, :, lanes], density, share, still[i])
        out[i] = jnp.where(line == 1, value, out[i])
        out[j] = jnp.where(line == 6, value, out[j])
    return out


def prepared_collision(solid, relaxed, bounced, dense, p, rows, lanes, numbers):
    share, *flow = solid
    still = equilibrium(None, flow, numbers)
    density = dense[p, rows, lanes]
    return {
        i: blended(relaxed[i, p, rows, lanes], bounced[i, p, rows, lanes], density, share, still[i])
        for i in numbers
    }


def tile_parts(size_y, size_z):
    for tile in range(size_y // 8 + 1):
        for part in range(size_z // 128):
            yield tile, slice(8 * tile, 8 * tile + 8), part, slice(128 * part, 128 * part + 128)


def by_plane(work, far):
    even = even_x()

    @pl.when(even if far else jnp.logical_not(even))
    def _():
        work(0, BACKWARD)

    @pl.when(jnp.logical_not(even) if far else even)
    def _():
        work(1, FORWARD)


def leaving_kernel(
    size_x, size_y, size_z, far, entries, sums, outer_sums, outer, second, migrants, relaxed, bounced,
    dense, *refs
):
    solid, message, leaving = refs[-3:]
    tiles = size_y // 8

    def work(place, numbers):
        plane = place * (size_x - 1)
        solids(size_x, size_y, size_z, (plane,), place, sums, outer_sums, migrants, solid)
        blocks = relax_blocks(entries)
        for tile, rows, part, lanes in tile_parts(size_y, size_z):
            s = [solid[c, 0, rows, lanes] for c in range(4)]
            if tile == tiles:
                out = outer_collision(s, outer, second, blocks, place, lanes)
            else:
                out = prepared_collision(s, relaxed, bounced, dense, place, rows, lanes, numbers)
            for k, i in enumerate(numbers):
                store_padded(leaving, k, 0, tile, part, out[i], tiles)
        write_face(leaving, message, numbers, size_y, size_z, True)

    by_plane(work, far)


def plane_solid(far, near, place, rows, lanes):
    in_far = even_x() if place == 0 else jnp.logical_not(even_x())
    return [jnp.where(in_far, far[c, 0, rows, lanes], near[c, 0, rows, lanes]) for c in range(4)]


def ends_kernel(
    size_x, size_y, size_z, entries, outer, second, relaxed, bounced, dense, solid_far, solid_near, post
):
    tiles = size_y // 8
    blocks = relax_blocks(entries)
    for p in range(2):
        for tile, rows, part, lanes in tile_parts(size_y, size_z):
            s = plane_solid(solid_far, solid_near, p, rows, lanes)
            if tile == tiles:
                out = outer_collision(s, outer, second, blocks, p, lanes)
            else:
                out = prepared_collision(s, relaxed, bounced, dense, p, rows, lanes, range(19))
            for i in range(19):
                store_padded(post, i, p, tile, part, out[i], tiles)


def middle_kernel(
    size_x, size_y, size_z, planes, entries, sums, outer_sums, outer, second, migrants, populations,
    post, solid
):
    tiles = size_y // 8
    solids(size_x, size_y, size_z, planes, 0, sums, outer_sums, migrants, solid)
    blocks = relax_blocks(entries)
    for p, x in enumerate(planes):
        for tile, rows, part, lanes in tile_parts(size_y, size_z):
            share, *flow = (solid[c, p, rows, lanes] for c in range(4))
            if tile == tiles:
                out = outer_collision((share, *flow), outer, second, blocks, p, lanes)
            else:
                h = [populations[i, x, rows, lanes] for i in range(19)]
                out = collide(h, share, *flow, blocks)
            for i in range(19):
                store_padded(post, i, p, tile, part, out[i], tiles)


def write_face(post, message, numbers, size_y, size_z, outer):
    tiles = size_y // 8
    for k, i in enumerate(numbers):
        _, c_y, c_z = VEC[i]
        for tile in range(tiles):
            at = 8 + 8 * tile - c_y
            to = k * size_y + 8 * tile
            message[to : to + 8, :] = turned(post[k, 0, at : at + 8, :], c_z, size_z)
        if outer:
            at = 8 + size_y - c_y
            value = turned(post[k, 0, at : at + 8, :], c_z, size_z)
            to = 5 * size_y + 2 * k
            message[to : to + 1, :] = value[0:1]
            message[to + 1 : to + 2, :] = value[7:8]


def streamed(ends, middle, messages, i, x, tile, size_x, size_y, size_z, walls):
    tiles = size_y // 8
    row = iota((8, size_z), 0)
    c_x, c_y, c_z = VEC[i]

    def plane(x):
        if x == 0:
            return ends, 0
        if x == size_x - 1:
            return ends, 1
        return middle, x - 1

    from_x = x - c_x
    if 0 <= from_x < size_x:
        source, p = plane(from_x)
        at = 8 + 8 * tile - c_y
        value = turned(source[i, p, at : at + 8, :], c_z, size_z)
    else:
        numbers = FORWARD if from_x < 0 else BACKWARD
        k = numbers.index(i)

        def received(at, rows):
            if len(messages) == 1:
                return messages[0][at : at + rows, :]
            near, far = messages
            from_near = jnp.logical_not(even_x()) if from_x < 0 else even_x()
            return jnp.where(from_near, near[at : at + rows, :], far[at : at + rows, :])

        if tile < tiles:
            value = received(k * size_y + 8 * tile, 8)
        else:
            at = 5 * size_y + 2 * k
            value = jnp.where(row < 4, received(at, 1), received(at + 1, 1))
    source, p = plane(x)
    if c_y == 1 and tile == 0:
        value = jnp.where((row == 0) & walls[0], source[OPP[i], p, 8:16, :], value)
    if c_y == -1 and tile == tiles - 1:
        back = source[OPP[i], p, size_y : 8 + size_y, :]
        value = jnp.where((row == 7) & walls[1], back, value)
    return value


def walls_of(count):
    here = lax.axis_index("gy")
    return here == 0, here == count - 1


def second_kernel(size_x, size_y, size_z, count, entries, ends, middle, solid, later):
    walls = walls_of(count)
    blocks = relax_blocks(entries)
    for p in range(size_x - 2):
        for tile in range(size_y // 8 + 1):
            rows = slice(8 * tile, 8 * tile + 8)
            h = [
                streamed(ends, middle, None, i, p + 1, tile, size_x, size_y, size_z, walls)
                for i in range(19)
            ]
            for part in range(size_z // 128):
                lanes = slice(128 * part, 128 * part + 128)
                s = [solid[c, p, rows, lanes] for c in range(4)]
                out = collide([v[:, lanes] for v in h], *s, blocks)
                for i in range(19):
                    store_padded(later, i, p, tile, part, out[i], size_y // 8)


def second_ends(
    size_x, size_y, size_z, count, entries, ends, middle, solid, messages, place, numbers, later, p
):
    walls = walls_of(count)
    blocks = relax_blocks(entries)
    x = place * (size_x - 1)
    for tile in range(size_y // 8 + 1):
        rows = slice(8 * tile, 8 * tile + 8)
        h = [
            streamed(ends, middle, messages, i, x, tile, size_x, size_y, size_z, walls) for i in range(19)
        ]
        for part in range(size_z // 128):
            lanes = slice(128 * part, 128 * part + 128)
            s = solid(rows, lanes)
            out = collide([v[:, lanes] for v in h], *s, blocks)
            for k, i in enumerate(numbers):
                store_padded(later, k, p, tile, part, out[i], size_y // 8)


def second_leaving_kernel(size_x, size_y, size_z, count, far, entries, ends, middle, solid, received, *refs):
    message, leaving = refs[-2:]

    def work(place, numbers):
        second_ends(
            size_x,
            size_y,
            size_z,
            count,
            entries,
            ends,
            middle,
            lambda rows, lanes: [solid[c, 0, rows, lanes] for c in range(4)],
            (received,),
            place,
            numbers,
            leaving,
            0,
        )
        write_face(leaving, message, numbers, size_y, size_z, False)

    by_plane(work, far)


def second_ends_kernel(
    size_x, size_y, size_z, count, entries, ends, middle, solid_far, solid_near, far, near, later
):
    for place in range(2):
        second_ends(
            size_x,
            size_y,
            size_z,
            count,
            entries,
            ends,
            middle,
            lambda rows, lanes: plane_solid(solid_far, solid_near, place, rows, lanes),
            (near, far),
            place,
            range(19),
            later,
            place,
        )


def last_kernel(size_x, size_y, size_z, count, ends, middle, advanced, held, done):
    walls = walls_of(count)
    copies = []
    for i in range(19):
        for x in range(size_x):
            if not 0 <= x - VEC[i][0] < size_x:
                continue
            for tile in range(size_y // 8):
                held[i, x, 8 * tile : 8 * tile + 8, :] = streamed(
                    ends, middle, None, i, x, tile, size_x, size_y, size_z, walls
                )
        low, high = max(0, VEC[i][0]), size_x + min(0, VEC[i][0])
        copy = pltpu.make_async_copy(
            held.at[i, low:high], advanced.at[i, low:high], done.at[i]
        )
        copy.start()
        copies.append(copy)
    for copy in copies:
        copy.wait()


def entering(size_x, size_y, size_z, count, ends, received, place, k, target):
    numbers = BACKWARD if place else FORWARD
    walls = walls_of(count)
    for tile in range(size_y // 8):
        target[k, 8 * tile : 8 * tile + 8, :] = streamed(
            ends, None, (received,), numbers[k], place * (size_x - 1), tile, size_x, size_y, size_z, walls
        )


def far_kernel(size_x, size_y, size_z, count, ends, received, held):
    def work(place, numbers):
        del numbers
        for k in range(5):
            entering(size_x, size_y, size_z, count, ends, received, place, k, held)

    by_plane(work, True)


def enter_kernel(size_x, size_y, size_z, count, ends, received, far, given, advanced, near, done):
    del given

    def write(place, held, base):
        numbers = BACKWARD if place else FORWARD
        for k, i in enumerate(numbers):
            copy = pltpu.make_async_copy(held.at[k], advanced.at[i, place * (size_x - 1)], done.at[base + k])
            copy.start()

    def work(place, numbers):
        del numbers
        write(1 - place, far, 0)
        for k in range(5):
            entering(size_x, size_y, size_z, count, ends, received, place, k, near)
        write(place, near, 5)

    by_plane(work, False)
    for k in range(5):
        pltpu.make_async_copy(far.at[k], advanced.at[FORWARD[k], 0], done.at[k]).wait()
        pltpu.make_async_copy(near.at[k], advanced.at[FORWARD[k], 0], done.at[5 + k]).wait()


def shape(*sizes):
    return jax.ShapeDtypeStruct(sizes, F32)


VMEM = pl.BlockSpec(memory_space=pltpu.VMEM)
SMEM = pl.BlockSpec(memory_space=pltpu.SMEM)
HBM = pl.BlockSpec(memory_space=pltpu.HBM)


def call(kernel, out_shape, limit, in_specs, out_specs=None, scratch=(), aliases=None):
    return pl.pallas_call(
        kernel,
        out_shape=out_shape,
        in_specs=in_specs,
        out_specs=jax.tree.map(lambda _: VMEM, out_shape) if out_specs is None else out_specs,
        scratch_shapes=scratch,
        input_output_aliases={} if aliases is None else aliases,
        compiler_params=pltpu.CompilerParams(vmem_limit_bytes=limit * 2**20),
    )


def in_hbm(value):
    return pltpu.with_memory_space_constraint(value, pltpu.HBM)


def around(value, axis, steps):
    count = lax.axis_size(axis)
    return lax.ppermute(value, axis, [(i, (i + steps) % count) for i in range(count)])


def paired_x(value, parity):
    count = lax.axis_size("gx")
    if count % 2:
        raise ValueError("odd ring")
    pairs = [(i, (i + 1 if i % 2 == parity else i - 1) % count) for i in range(count)]
    return lax.ppermute(value, "gx", pairs)


def paired_y(value, parity):
    count_x, count = lax.axis_size("gx"), lax.axis_size("gy")
    pairs = []
    for i in range(count_x):
        for j in range(count):
            other = j + 1 if j % 2 == parity else j - 1
            to = i * count + other if 0 <= other < count else (i ^ 1) * count + j
            pairs.append((i * count + j, to))
    return lax.ppermute(value, ("gx", "gy"), pairs)


def exchanged(near, far):
    far = paired_x(far, 1)
    return paired_x(near, 0), far


def local(populations, relax_rates, velocity, velocity_change, fractions, anchor, destination):
    _, size_x, size_y, size_z = populations.shape
    count = lax.axis_size("gy")
    rows = anchor.shape[0]
    sizes = (size_x, size_y, size_z)
    part = functools.partial
    packed = shape(8, 128)
    band = shape(19, size_x, 8, size_z)
    table, own, near, far, bottom, top = call(
        pack_kernel,
        (shape(32, rows), packed, packed, packed, band, band),
        8,
        [HBM] * 6,
        scratch=[
            pltpu.VMEM((3, rows), F32),
            pltpu.VMEM((3, rows), F32),
            pltpu.VMEM((27, rows), F32),
            pltpu.VMEM((1, rows), I32),
            pltpu.VMEM((1, rows), I32),
            pltpu.SemaphoreType.DMA((7,)),
        ],
    )(*map(in_hbm, (velocity, velocity_change, fractions, anchor[None, :], destination[None, :], populations)))
    near, far = exchanged(near, far)
    first = edge_rows(size_x)[-1]
    fold = size_z // 128
    message = shape(-(-(first + 8 // fold) // 8) * 8, size_z)
    entries = call(relax_kernel, shape(ENTRIES, 8, 128), 8, [SMEM])(relax_rates)
    one, two = call(
        part(edge_kernel, *sizes),
        (message, message),
        8,
        [VMEM] * 4,
        scratch=[pltpu.VMEM((19, 2 * size_x, size_z), F32)],
    )(bottom, top, table, entries)
    two = paired_y(two, 1)
    column, one = call(
        part(merge_kernel, first, fold),
        (shape(8, 128), message),
        8,
        [VMEM] * 4,
        aliases={3: 1},
    )(own, far, near, one)
    shifts = []
    for shift in (2, -2):
        if shift % count > 1 and all((shift - other) % count for other in shifts):
            shifts.append(shift)
    rest = [around(column, "gy", shift) for shift in shifts]
    one, column_two = paired_y(one, 0), paired_y(column, 1)
    unused = pl.BlockSpec(memory_space=pl.ANY)
    sums = call(part(stay_kernel, *sizes), shape(4, *sizes), 16, [VMEM, unused])(table, two)
    plane_pair = shape(19, 2, size_y, size_z)
    parts = call(
        part(fluid_kernel, *sizes), (plane_pair, plane_pair, shape(2, size_y, size_z)), 16, [VMEM] * 2
    )(entries, populations)
    width = -(-(3 + len(shifts)) * LANES // 128) * 128
    outside, inside = (0, size_x - 1), tuple(range(1, size_x - 1))

    def outer_shapes(planes):
        return tuple(shape(k, len(planes), 8, size_z) for k in (4, 19, 11))

    outer_sums, outer, second, migrants = call(
        part(outer_kernel, *sizes, count, shifts, outside),
        outer_shapes(outside) + (shape(40, width),),
        8,
        [VMEM] * (4 + len(shifts)),
    )(column, one, column_two, *rest, two)

    def padded(planes):
        return shape(19, planes, size_y + 24, size_z)

    def solid_shape(planes):
        return shape(4, planes, size_y + 8, size_z)

    sent = pltpu.VMEM((5, 1, size_y + 24, size_z), F32)
    wide_face = shape((5 * size_y + 10 + 7) // 8 * 8, size_z)
    face = shape(5 * size_y, size_z)

    def leaving(far, *given):
        return call(
            part(leaving_kernel, *sizes, far),
            (solid_shape(1), wide_face),
            16,
            [VMEM] * 9 + [unused] * (len(given) - 9),
            scratch=[sent],
        )(*given)

    known = (entries, sums, outer_sums, outer, second, migrants, *parts)
    solid_far, far = leaving(True, *known)
    solid_near, near = leaving(False, *known, solid_far)
    near, far = exchanged(near, far)
    inner = call(part(outer_kernel, *sizes, count, shifts, inside), outer_shapes(inside), 8, [VMEM] * 2)(
        two, one
    )
    middle, solid_middle = call(
        part(middle_kernel, *sizes, inside),
        (padded(len(inside)), solid_shape(len(inside))),
        16,
        [VMEM] * 7,
    )(entries, sums, *inner, migrants, populations)
    ends = call(part(ends_kernel, *sizes), padded(2), 16, [VMEM] * 8)(
        entries, outer, second, *parts, solid_far, solid_near
    )
    later_middle = call(part(second_kernel, *sizes, count), padded(len(inside)), 16, [VMEM] * 4)(
        entries, ends, middle, solid_middle
    )

    def second_leaving(far, *given):
        return call(
            part(second_leaving_kernel, *sizes, count, far),
            face,
            16,
            [VMEM] * 5 + [unused] * (len(given) - 5),
            scratch=[sent],
        )(*given)

    received = (far, near)
    far = second_leaving(True, entries, ends, middle, solid_far, far, later_middle)
    near = second_leaving(False, entries, ends, middle, solid_near, near, far)
    near, far = exchanged(near, far)
    later_ends = call(part(second_ends_kernel, *sizes, count), padded(2), 16, [VMEM] * 7)(
        entries, ends, middle, solid_far, solid_near, *received
    )
    advanced = call(
        part(last_kernel, *sizes, count),
        shape(19, *sizes),
        16,
        [VMEM] * 2,
        HBM,
        [pltpu.VMEM((19, *sizes), F32), pltpu.SemaphoreType.DMA((19,))],
    )(later_ends, later_middle)
    slabs = (5, size_y, size_z)
    far = call(part(far_kernel, *sizes, count), shape(*slabs), 16, [VMEM] * 2)(later_ends, far)
    return call(
        part(enter_kernel, *sizes, count),
        shape(19, *sizes),
        16,
        [VMEM] * 3 + [HBM],
        HBM,
        [pltpu.VMEM(slabs, F32), pltpu.SemaphoreType.DMA((10,))],
        {3: 0},
    )(later_ends, near, far, advanced)


def solution(mesh):
    placed = (
        P(None, "gx", "gy", None),
        P(),
        P(None, ("gx", "gy")),
        P(None, ("gx", "gy")),
        P(None, ("gx", "gy")),
        P(("gx", "gy")),
        P(("gx", "gy")),
    )
    return jax.shard_map(
        local, mesh=mesh, in_specs=placed, out_specs=P(None, "gx", "gy", None), check_vma=False
    )
```

```python
import functools

import jax
import jax.numpy as jnp
import numpy as np
from jax import lax
from jax.experimental import pallas as pl
from jax.experimental.pallas import tpu as pltpu
from jax.sharding import PartitionSpec as P

CAP = 4
STEPS = 2
LANES = 8 * CAP
F32 = jnp.float32
BF16 = jnp.bfloat16
I32 = jnp.int32


def lattice():
    vectors = [[0, 0, 0]]
    for axis_one in range(3):
        for orient in (1, -1):
            vector_one = [0, 0, 0]
            vector_one[axis_one] = orient
            vectors.append(vector_one)
    for axis_one, axis_two in ((0, 1), (0, 2), (1, 2)):
        for orient in (1, -1):
            for second in (1, -1):
                vector_one = [0, 0, 0]
                vector_one[axis_one] = orient
                vector_one[axis_two] = second
                vectors.append(vector_one)
    integral = np.array(vectors)
    speeds = integral * 1.0
    length = (speeds**2).sum(axis=1)
    weights = np.where(length == 0, 1.0 / 3.0, np.where(length == 1, 1.0 / 18.0, 1.0 / 36.0))
    opposite = [vectors.index([0 - component for component in vector_one]) for vector_one in vectors]
    along_x, along_y, along_z = (speeds[:, 0], speeds[:, 1], speeds[:, 2])
    rows_list = [
        np.ones(19),
        along_x,
        along_y,
        along_z,
        length,
        3 * along_x**2 - length,
        along_y**2 - along_z**2,
        along_x * along_y,
        along_y * along_z,
        along_x * along_z,
        along_x * length,
        along_y * length,
        along_z * length,
        along_x * (along_y**2 - along_z**2),
        along_y * (along_z**2 - along_x**2),
        along_z * (along_x**2 - along_y**2),
        length**2,
        (3 * along_x**2 - length) * length,
        (along_y**2 - along_z**2) * length,
    ]
    basis_rows = []
    for candidate in rows_list:
        for earlier in basis_rows:
            candidate = candidate - np.dot(candidate, earlier) * earlier
        basis_rows.append(candidate / np.sqrt(np.dot(candidate, candidate)))
    return [tuple(v) for v in vectors], weights, opposite, np.array(basis_rows)


VEC, WEIGHTS, OPP, BASIS = lattice()
FORWARD = [i for i in range(19) if VEC[i][0] == 1]
BACKWARD = [i for i in range(19) if VEC[i][0] == -1]
DOWNWARD = [i for i in range(19) if VEC[i][1] == -1]
UPWARD = [OPP[i] for i in DOWNWARD]


def symmetric_blocks():
    def vec(entries):
        out = np.zeros(19)
        for index, value in entries.items():
            out[index] = value
        return out

    def plane(base):
        s_one, d_one = vec({base: 1, base + 3: 1}), vec({base: 1, base + 3: -1})
        s_two, d_two = vec({base + 1: 1, base + 2: 1}), vec({base + 1: 1, base + 2: -1})
        return s_one + s_two, s_one - s_two, d_one + d_two, d_one - d_two

    rest = vec({0: 1})
    s_x, s_y, s_z = vec({1: 1, 2: 1}), vec({3: 1, 4: 1}), vec({5: 1, 6: 1})
    d_x, d_y, d_z = vec({1: 1, 2: -1}), vec({3: 1, 4: -1}), vec({5: 1, 6: -1})
    xy, q_xy, x_xy, y_xy = plane(7)
    xz, q_xz, x_xz, z_xz = plane(11)
    yz, q_yz, y_yz, z_yz = plane(15)
    blocks = [
        [rest, s_x + s_y + s_z, xy + xz + yz],
        [2 * s_x - s_y - s_z, xy + xz - 2 * yz],
        [s_y - s_z, xy - xz],
        [q_xy],
        [q_xz],
        [q_yz],
        [d_x, x_xy, x_xz],
        [d_y, y_xy, y_yz],
        [d_z, z_xz, z_yz],
    ]
    scales = [[1, 1 / 6, 1 / 12], [1 / 12, 1 / 24], [1 / 4, 1 / 8]]
    scales += [[1 / 4]] * 3 + [[1 / 2, 1 / 4, 1 / 4]] * 3
    forward = np.array([row for block in blocks for row in block])
    back = np.linalg.inv(forward)
    left = forward @ np.diag(1.0 / WEIGHTS) @ BASIS.T
    right = BASIS @ np.diag(WEIGHTS) @ back
    table = []
    start = 0
    for block, scale in zip(blocks, scales):
        size = len(block)
        rows = []
        for a in range(size):
            row = []
            for b in range(size):
                per_rate = -scale[a] * left[start + a, :] * right[:, start + b]
                row.append([(k, float(v)) for k, v in enumerate(per_rate) if abs(v) > 1e-12])
            rows.append(row)
        table.append(rows)
        start += size
    return table


RELAX = symmetric_blocks()


def relax_rows(rates, target):
    values = [rates[k] for k in range(19)]
    at = 0
    for block in RELAX:
        for row in block:
            for terms in row:
                total = None
                for k, factor in terms:
                    part = values[k] * np.float32(factor)
                    total = part if total is None else total + part
                target[at] = jnp.full((8, 128), total, F32)
                at += 1


def relax_blocks(table, lanes=128):
    blocks, at = [], 0
    for block in RELAX:
        rows = []
        for row in block:
            rows.append(
                [jnp.concatenate([table[at + k]] * (lanes // 128), axis=1) for k in range(len(row))]
            )
            at += len(row)
        blocks.append(rows)
    return blocks


ENTRIES = sum(len(row) for block in RELAX for row in block)


def apply_block(block, values):
    out = []
    for row in block:
        total = None
        for factor, value in zip(row, values):
            part = factor * value
            total = part if total is None else total + part
        out.append(total)
    return out


def collide(h, solid, s_x, s_y, s_z, blocks):
    def plane(base):
        s_one, d_one = h[base] + h[base + 3], h[base] - h[base + 3]
        s_two, d_two = h[base + 1] + h[base + 2], h[base + 1] - h[base + 2]
        return s_one + s_two, s_one - s_two, d_one + d_two, d_one - d_two

    sum_x, dif_x = h[1] + h[2], h[1] - h[2]
    sum_y, dif_y = h[3] + h[4], h[3] - h[4]
    sum_z, dif_z = h[5] + h[6], h[5] - h[6]
    xy, q_xy, x_xy, y_xy = plane(7)
    xz, q_xz, x_xz, z_xz = plane(11)
    yz, q_yz, y_yz, z_yz = plane(15)
    axes = sum_x + sum_y + sum_z
    edges = xy + xz + yz
    density = h[0] * (1.0 / 3.0) + axes * (1.0 / 18.0) + edges * (1.0 / 36.0)
    m_x = dif_x * (1.0 / 18.0) + (x_xy + x_xz) * (1.0 / 36.0)
    m_y = dif_y * (1.0 / 18.0) + (y_xy + y_yz) * (1.0 / 36.0)
    m_z = dif_z * (1.0 / 18.0) + (z_xz + z_yz) * (1.0 / 36.0)
    inverse = 1.0 / density
    u_x, u_y, u_z = m_x * inverse, m_y * inverse, m_z * inverse
    e_xx, e_yy, e_zz = m_x * u_x, m_y * u_y, m_z * u_z
    e_xy, e_xz, e_yz = m_x * u_y, m_x * u_z, m_y * u_z
    energy = e_xx + e_yy + e_zz
    turn = e_yy - e_zz
    lean = 3.0 * e_xx - energy
    rest_off = h[0] - density + 1.5 * energy
    axes_off = axes - 6.0 * density
    edges_off = edges - 12.0 * density - 18.0 * energy
    a_one = 3.0 * sum_x - axes - 9.0 * lean
    b_one = edges - 3.0 * yz - 18.0 * lean
    a_two = sum_y - sum_z - 9.0 * turn
    b_two = xy - xz - 18.0 * turn
    q_xy = q_xy - 36.0 * e_xy
    q_xz = q_xz - 36.0 * e_xz
    q_yz = q_yz - 36.0 * e_yz

    r_rest, r_axes, r_edges = apply_block(blocks[0], [rest_off, axes_off, edges_off])
    r_a_one, r_b_one = apply_block(blocks[1], [a_one, b_one])
    r_a_two, r_b_two = apply_block(blocks[2], [a_two, b_two])
    fluid = 1.0 - solid
    mixed = solid * density
    w_x, w_y, w_z = solid * m_x, solid * m_y, solid * m_z
    n_x, n_y, n_z = mixed * s_x, mixed * s_y, mixed * s_z
    p_x = n_x * s_x - solid * e_xx
    p_y = n_y * s_y - solid * e_yy
    p_z = n_z * s_z - solid * e_zz
    total = 1.5 * (p_x + p_y + p_z)
    lean_s = 2.25 * p_x - 0.5 * total
    turn_s = 2.25 * (p_y - p_z)
    rest = fluid * r_rest - total
    axes = fluid * r_axes
    edges = fluid * r_edges + total
    a_one = fluid * r_a_one + lean_s
    b_one = fluid * r_b_one + lean_s
    a_two = fluid * r_a_two + turn_s
    b_two = fluid * r_b_two + turn_s
    q_xy = fluid * apply_block(blocks[3], [q_xy])[0] + 9.0 * (n_x * s_y - solid * e_xy)
    q_xz = fluid * apply_block(blocks[4], [q_xz])[0] + 9.0 * (n_x * s_z - solid * e_xz)
    q_yz = fluid * apply_block(blocks[5], [q_yz])[0] + 9.0 * (n_y * s_z - solid * e_yz)

    def odd(block, axis, one, two, m, n, w):
        six = 6.0 * m
        axis = axis - six
        twelve = six + six
        one = one - twelve
        two = two - twelve
        r_axis, r_one, r_two = apply_block(block, [axis, one, two])
        push = 3.0 * (n - w)
        half = 0.5 * solid
        return (
            fluid * r_axis - solid * axis + push,
            fluid * r_one - half * one + push,
            fluid * r_two - half * two + push,
        )

    d_x, x_xy, x_xz = odd(blocks[6], dif_x, x_xy, x_xz, m_x, n_x, w_x)
    d_y, y_xy, y_yz = odd(blocks[7], dif_y, y_xy, y_yz, m_y, n_y, w_y)
    d_z, z_xz, z_yz = odd(blocks[8], dif_z, z_xz, z_yz, m_z, n_z, w_z)
    out = [None] * 19
    out[0] = h[0] + rest
    even = axes + 2.0 * a_one
    out[1], out[2] = h[1] + (even + d_x), h[2] + (even - d_x)
    base = axes - a_one
    even = base + a_two
    out[3], out[4] = h[3] + (even + d_y), h[4] + (even - d_y)
    even = base - a_two
    out[5], out[6] = h[5] + (even + d_z), h[6] + (even - d_z)

    def spread(start, even, twist, one, two):
        same, cross = even + twist, even - twist
        plus, minus = one + two, one - two
        out[start] = h[start] + (same + plus)
        out[start + 3] = h[start + 3] + (same - plus)
        out[start + 1] = h[start + 1] + (cross + minus)
        out[start + 2] = h[start + 2] + (cross - minus)

    base = edges + b_one
    spread(7, base + b_two, q_xy, x_xy, y_xy)
    spread(11, base - b_two, q_xz, x_xz, z_xz)
    spread(15, edges - 2.0 * b_one, q_yz, y_yz, z_yz)
    return out


def equilibrium(density, flow, numbers):
    v_x, v_y, v_z = flow
    rest = 1.0 - 1.5 * (v_x * v_x + v_y * v_y + v_z * v_z)
    out = {}
    for i in numbers:
        if i in out:
            continue
        along = None
        for sign, v in zip(VEC[i], flow):
            if sign:
                part = v if sign == 1 else -v
                along = part if along is None else along + part
        if along is None:
            out[i] = rest
        else:
            along = 3.0 * along
            even = rest + 0.5 * along * along
            out[i], out[OPP[i]] = even + along, even - along
    return out


def fluid_parts(h, blocks, numbers):
    zero = jnp.zeros_like(h[0])
    relaxed = collide(h, zero, zero, zero, zero, blocks)
    density, flow = zero, [zero, zero, zero]
    for i in range(19):
        part = np.float32(WEIGHTS[i]) * h[i]
        density = density + part
        for k in range(3):
            if VEC[i][k]:
                flow[k] = flow[k] + part if VEC[i][k] == 1 else flow[k] - part
    inverse = 1.0 / density
    still = equilibrium(density, [f * inverse for f in flow], numbers)
    bounced = [h[OPP[i]] - density * still[OPP[i]] for i in numbers]
    return [relaxed[i] for i in numbers], bounced, density


def blended(relaxed, bounced, density, share, still):
    return relaxed + share * ((bounced + density * still) - relaxed)


def iota(shape, dim):
    return lax.broadcasted_iota(I32, shape, dim)


def cells_of(anchor, size_y, size_z):
    plane = size_y * size_z
    a_x = lax.div(anchor, jnp.int32(plane))
    rest = anchor - a_x * plane
    a_y = lax.div(rest, jnp.int32(size_z))
    return a_x, a_y, rest - a_y * size_z


def halves(value):
    high = value.astype(BF16)
    return high, (value - high.astype(F32)).astype(BF16)


def dot_t(left, right):
    return lax.dot_general(left, right, (((1,), (1,)), ((), ())), preferred_element_type=F32)


def deposited(groups, shares, velocity, a_x, a_y, a_z, size_z, big):
    centre = a_x * big + a_y
    lanes = centre.shape[1]
    totals = None
    rows_z = iota((size_z, lanes), 0)
    for off_z in range(3):
        weights = []
        for rows_x, rows_y in groups:
            away = rows_x * big + rows_y - centre
            weight = jnp.zeros(away.shape, F32)
            for off in range(9):
                move = (off // 3 - 1) * big + off % 3 - 1
                row = 3 * off + off_z
                weight = jnp.where(away == move, shares[row : row + 1, :], weight)
            weights.append([weight] + [weight * velocity[k : k + 1, :] for k in range(3)])
        rows = jnp.concatenate([w for block in weights for w in block], axis=0)
        high, low = halves(rows)
        hot = jnp.where(rows_z == a_z + (off_z - 1), 1.0, 0.0).astype(BF16)
        part = dot_t(high, hot) + dot_t(low, hot)
        totals = part if totals is None else totals + part
    return totals


def even_x():
    return lax.rem(lax.axis_index("gx"), 2) == 0


def pack_kernel(
    velocity_in,
    change_in,
    fractions_in,
    anchor_in,
    destination_in,
    populations,
    table,
    own,
    near,
    far,
    bottom,
    top,
    velocity,
    change,
    fractions,
    anchor,
    destination,
    done,
):
    pairs = (
        (destination_in, destination),
        (velocity_in, velocity),
        (change_in, change),
        (fractions_in, fractions),
        (anchor_in, anchor),
        (populations.at[:, :, 0:8, :], bottom),
        (populations.at[:, :, populations.shape[2] - 8 :, :], top),
    )
    copies = [pltpu.make_async_copy(a, b, done.at[k]) for k, (a, b) in enumerate(pairs)]
    for copy in copies:
        copy.start()
    rows = destination.shape[1]
    order = jnp.where(iota((128, 128), 0) <= iota((128, 128), 1), 1.0, 0.0).astype(BF16)
    for copy in copies[:5]:
        copy.wait()
    dest = destination[...]
    kinds = iota((16, rows), 0)
    hot = jnp.where(dest == kinds, 1.0, 0.0)
    seen = jnp.zeros((16, 1), F32)
    ranks = []
    for start in range(0, rows, 128):
        counted = seen + lax.dot_general(
            hot[:, start : start + 128].astype(BF16),
            order,
            (((1,), (0,)), ((), ())),
            preferred_element_type=F32,
        )
        ranks.append(counted)
        seen = counted[:, 127:128]
    rank = jnp.concatenate(ranks, axis=1)
    kind = iota((16, 1), 0)
    begin = jnp.where(
        kind < 3,
        5 * CAP + CAP * kind,
        jnp.where(kind == 3, 0, jnp.where(kind == 5, CAP, 2 * CAP + CAP * (kind - 6))),
    ).astype(F32)
    leaving = (dest < 9) & (dest != 4)
    slot = jnp.sum(hot * (begin + rank - 1.0), axis=0, keepdims=True)
    slot = jnp.where(leaving, slot, -1.0).astype(I32)
    chosen = jnp.where(iota((128, rows), 0) == slot, 1.0, 0.0).astype(BF16)
    new_velocity = velocity[...] + change[...]
    payload = jnp.concatenate(
        [fractions[...], new_velocity, anchor[...].astype(F32), jnp.zeros((1, rows), F32)], axis=0
    )
    high = payload.astype(BF16)
    middle, low = halves(payload - high.astype(F32))
    packed = dot_t(high, chosen) + dot_t(middle, chosen) + dot_t(low, chosen)
    packed = folded(packed)
    lane = lax.rem(iota((8, 128), 1), jnp.int32(LANES))
    own[...] = jnp.where(lane < 2 * CAP, packed, 0.0)
    ahead = jnp.where((lane >= 2 * CAP) & (lane < 5 * CAP), packed, 0.0)
    behind = jnp.where(lane >= 5 * CAP, packed, 0.0)
    even = even_x()
    near[...] = jnp.where(even, ahead, behind)
    far[...] = jnp.where(even, behind, ahead)
    table[...] = jnp.where((iota((32, rows), 0) < 27) & (dest != 4), 0.0, payload)
    for copy in copies[5:]:
        copy.wait()


def edge_rows(size_x):
    starts = [0]
    for rows in (19 * size_x, 4 * 2 * size_x, 11 * size_x):
        starts.append(starts[-1] + rows)
    return starts


def edge_kernel(size_x, size_y, size_z, bottom, top, table, entries, one, two, held):
    a_x, a_y, a_z = cells_of(table[30:31, :].astype(I32), size_y, size_z)
    rows = 2 * size_x
    index = iota((rows, 1), 0)
    rows_x, low = lax.div(index, jnp.int32(2)), lax.rem(index, jnp.int32(2))
    sums = deposited(
        [(rows_x, low), (rows_x, low + (size_y - 2))],
        table[0:27, :],
        table[27:30, :],
        a_x,
        a_y,
        a_z,
        size_z,
        8 * size_y,
    )
    _, at_sums, at_second, _ = edge_rows(size_x)
    for i in range(19):
        for x in range(size_x):
            held[i, x : x + 1, :] = bottom[i, x, 1:2, :]
            held[i, size_x + x : size_x + x + 1, :] = top[i, x, 6:7, :]
    second = fluid_parts([held[i] for i in range(19)], relax_blocks(entries, size_z), DOWNWARD + UPWARD)
    relaxed, bounced, density = second

    def write(down, up):
        for i in range(19):
            for x in range(size_x):
                at = i * size_x + x
                down[at : at + 1, :] = bottom[i, x, 0:1, :]
                up[at : at + 1, :] = top[i, x, 7:8, :]
        down[at_sums : at_sums + 4 * rows, :] = sums[: 4 * rows]
        up[at_sums : at_sums + 4 * rows, :] = sums[4 * rows :]
        for target, own, at_row in ((down, 0, 0), (up, 5, size_x)):
            parts = relaxed[own : own + 5] + bounced[own : own + 5] + [density]
            for k, value in enumerate(parts):
                at = at_second + k * size_x
                target[at : at + size_x, :] = value[at_row : at_row + size_x]

    even = lax.rem(lax.axis_index("gy"), 2) == 0

    @pl.when(even)
    def _():
        write(two, one)

    @pl.when(jnp.logical_not(even))
    def _():
        write(one, two)


def folded(table):
    return sum(
        table[8 * k : 8 * k + 8] if k == 0 else pltpu.roll(table[8 * k : 8 * k + 8], LANES * k, 1)
        for k in range(4)
    )


def merge_kernel(first, fold, own, far, near, one_in, column, one):
    del one_in
    merged = own[...] + near[...] + far[...]
    column[...] = merged
    deep = 8 // fold
    for k in range(fold):
        one[first : first + deep, 128 * k : 128 * k + 128] = merged[deep * k : deep * k + deep]


def relax_kernel(rates, entries):
    relax_rows(rates, entries)


def fluid_kernel(size_x, size_y, size_z, entries, populations, relaxed, bounced, density):
    blocks = relax_blocks(entries)
    for p, x in enumerate((0, size_x - 1)):
        for tile in range(size_y // 8):
            rows = slice(8 * tile, 8 * tile + 8)
            for part in range(size_z // 128):
                lanes = slice(128 * part, 128 * part + 128)
                f, b, d = fluid_parts([populations[i, x, rows, lanes] for i in range(19)], blocks, range(19))
                for i in range(19):
                    relaxed[i, p, rows, lanes] = f[i]
                    bounced[i, p, rows, lanes] = b[i]
                density[p, rows, lanes] = d


def stay_kernel(size_x, size_y, size_z, planes, table, after, sums):
    del after
    a_x, a_y, a_z = cells_of(table[30:31, :].astype(I32), size_y, size_z)
    index = iota((len(planes) * size_y, 1), 0)
    number = lax.div(index, jnp.int32(size_y))
    rows_x = number * (size_x - 1) if planes[0] == 0 else number + planes[0]
    totals = deposited(
        [(rows_x, index - number * size_y)],
        table[0:27, :],
        table[27:30, :],
        a_x,
        a_y,
        a_z,
        size_z,
        8 * size_y,
    )
    cells = len(planes) * size_y
    for c in range(4):
        for p in range(len(planes)):
            at = c * cells + p * size_y
            sums[c, p, :, :] = totals[at : at + size_y]


def outer_kernel(size_x, size_y, size_z, count, shifts, planes, *refs):
    if planes[0] == 0:
        column, one, column_two, *rest = refs[: 3 + len(shifts)]
        two, sums, outer, second, migrants = refs[3 + len(shifts) :]
        arrivals(size_x, size_y, size_z, count, shifts, column, one, column_two, rest, migrants)
    else:
        two, one, sums, outer, second = refs
    blank = jnp.zeros((8, size_z), F32)
    ones = jnp.ones((8, size_z), F32)
    _, at_sums, at_second, _ = edge_rows(size_x)

    def write(above, below):
        for p, x in enumerate(planes):
            for c in range(4):
                at = at_sums + c * 2 * size_x + 2 * x
                sums[c, p, :, :] = blank
                sums[c, p, 0:2, :] = above[at : at + 2, :]
                sums[c, p, 6:8, :] = below[at : at + 2, :]
            for i in range(19):
                at = i * size_x + x
                outer[i, p, :, :] = ones
                outer[i, p, 0:1, :] = above[at : at + 1, :]
                outer[i, p, 7:8, :] = below[at : at + 1, :]
            for k in range(11):
                at = at_second + k * size_x + x
                second[k, p, :, :] = ones
                second[k, p, 1:2, :] = above[at : at + 1, :]
                second[k, p, 6:7, :] = below[at : at + 1, :]

    even = lax.rem(lax.axis_index("gy"), 2) == 0

    @pl.when(even)
    def _():
        write(one, two)

    @pl.when(jnp.logical_not(even))
    def _():
        write(two, one)


def pair_source(here, parity, count):
    other = jnp.where(lax.rem(here, 2) == parity, here + 1, here - 1)
    return jnp.where((other >= 0) & (other < count), other, here + 2 * count)


def arrivals(size_x, size_y, size_z, count, shifts, column, one, two, rest, migrants):
    first = edge_rows(size_x)[-1]
    here = lax.axis_index("gy")
    fold = size_z // 128
    deep = 8 // fold

    def gathered(message):
        return jnp.concatenate(
            [message[first : first + deep, 128 * k : 128 * k + 128] for k in range(fold)], axis=0
        )

    parts = [column[...], gathered(one), two[...]] + [r[...] for r in rest]
    sources = [here, pair_source(here, 0, count), pair_source(here, 1, count)]
    sources += [lax.rem(here - shift + 2 * count, count) for shift in shifts]
    lane = iota((1, 128), 1)
    spot = lax.rem(lane, jnp.int32(LANES))
    group = lax.div(spot, jnp.int32(CAP))
    across = jnp.where(
        (group == 0) | (group == 2) | (group == 5), -1, jnp.where((group == 3) | (group == 6), 0, 1)
    )
    per_group = 128 // LANES
    tables, offsets = [], []
    for start in range(0, len(parts), per_group):
        blocks = [jnp.zeros((8, 128), F32)] * 4
        offset = jnp.full((1, 128), 2 * count, I32)
        for k, part in enumerate(parts[start : start + per_group]):
            place = lax.div(lane, jnp.int32(LANES)) == k
            for q in range(4):
                turn = LANES * (k - q) % 128
                blocks[q] = jnp.where(place, part if turn == 0 else pltpu.roll(part, turn, 1), blocks[q])
            offset = jnp.where(lax.div(lane, jnp.int32(LANES)) == k, sources[start + k] - here, offset)
        tables.append(jnp.concatenate(blocks, axis=0))
        offsets.append((offset + across) * size_y)
    table = jnp.concatenate(tables, axis=1)
    a_x, a_y, a_z = cells_of(table[30:31, :].astype(I32), size_y, size_z)
    migrants[0:32, :] = table
    migrants[32:33, :] = a_x.astype(F32)
    migrants[33:34, :] = (a_y + jnp.concatenate(offsets, axis=1)).astype(F32)
    migrants[34:35, :] = a_z.astype(F32)


def store_padded(target, i, x, tile, part, value, tiles):
    lanes = slice(128 * part, 128 * part + 128)
    if tile == tiles:
        target[i, x, 0:8, lanes] = value
        target[i, x, 8 + 8 * tiles : 16 + 8 * tiles, lanes] = value
    else:
        target[i, x, 8 + 8 * tile : 16 + 8 * tile, lanes] = value
        if tile == 0:
            target[i, x, 16 + 8 * tiles : 24 + 8 * tiles, lanes] = value


def turned(value, shift, size_z):
    return value if shift == 0 else pltpu.roll(value, shift % size_z, 1)


def solids(size_x, size_y, size_z, planes, first, sums, outer_sums, migrants, solid):
    a_x, a_y, a_z = (migrants[k : k + 1, :].astype(I32) for k in (32, 33, 34))
    wide = size_y + 8
    index = iota((len(planes) * wide, 1), 0)
    number = lax.div(index, jnp.int32(wide))
    row = index - number * wide
    rows_y = jnp.where(row < size_y + 2, row, jnp.where(row >= size_y + 6, row - wide, -3 * size_y))
    big = 4 * size_y * (lax.axis_size("gy") + 2)
    totals = deposited(
        [(number + planes[0], rows_y)], migrants[0:27, :], migrants[27:30, :], a_x, a_y, a_z, size_z, big
    )
    cells = len(planes) * wide
    for p, x in enumerate(planes):
        parts = []
        for c in range(4):
            at = c * cells + p * wide
            solid_sum = jnp.concatenate([sums[c, first + p, :, :], outer_sums[c, first + p, :, :]], axis=0)
            parts.append(totals[at : at + wide] + solid_sum)
        scale = 1.0 / (parts[0] + 1e-06)
        solid[0, p, :, :] = jnp.minimum(parts[0], 1.0)
        for c in (1, 2, 3):
            solid[c, p, :, :] = parts[c] * scale


def outer_collision(solid, outer, second, blocks, p, lanes):
    share, *flow = solid
    out = collide([outer[i, p, :, lanes] for i in range(19)], share, *flow, blocks)
    line = iota((8, 128), 0)
    away = jnp.where(line < 4, 1.0, -1.0)
    still = equilibrium(None, [away * v for v in flow], DOWNWARD)
    density = second[10, p, :, lanes]
    for k, (i, j) in enumerate(zip(DOWNWARD, UPWARD)):
        value = blended(second[k, p, :, lanes], second[5 + k, p, :, lanes], density, share, still[i])
        out[i] = jnp.where(line == 1, value, out[i])
        out[j] = jnp.where(line == 6, value, out[j])
    return out


def prepared_collision(solid, relaxed, bounced, dense, p, rows, lanes, numbers):
    share, *flow = solid
    still = equilibrium(None, flow, numbers)
    density = dense[p, rows, lanes]
    return {
        i: blended(relaxed[i, p, rows, lanes], bounced[i, p, rows, lanes], density, share, still[i])
        for i in numbers
    }


def tile_parts(size_y, size_z):
    for tile in range(size_y // 8 + 1):
        for part in range(size_z // 128):
            yield tile, slice(8 * tile, 8 * tile + 8), part, slice(128 * part, 128 * part + 128)


def by_plane(work, far):
    even = even_x()

    @pl.when(even if far else jnp.logical_not(even))
    def _():
        work(0, BACKWARD)

    @pl.when(jnp.logical_not(even) if far else even)
    def _():
        work(1, FORWARD)


def leaving_kernel(
    size_x, size_y, size_z, far, entries, sums, outer_sums, outer, second, migrants, relaxed, bounced,
    dense, *refs
):
    solid, message, leaving = refs[-3:]
    tiles = size_y // 8

    def work(place, numbers):
        plane = place * (size_x - 1)
        solids(size_x, size_y, size_z, (plane,), place, sums, outer_sums, migrants, solid)
        blocks = relax_blocks(entries)
        for tile, rows, part, lanes in tile_parts(size_y, size_z):
            s = [solid[c, 0, rows, lanes] for c in range(4)]
            if tile == tiles:
                out = outer_collision(s, outer, second, blocks, place, lanes)
            else:
                out = prepared_collision(s, relaxed, bounced, dense, place, rows, lanes, numbers)
            for k, i in enumerate(numbers):
                store_padded(leaving, k, 0, tile, part, out[i], tiles)
        write_face(leaving, message, numbers, size_y, size_z, True)

    by_plane(work, far)


def plane_solid(far, near, place, rows, lanes):
    in_far = even_x() if place == 0 else jnp.logical_not(even_x())
    return [jnp.where(in_far, far[c, 0, rows, lanes], near[c, 0, rows, lanes]) for c in range(4)]


def ends_kernel(
    size_x, size_y, size_z, entries, outer, second, relaxed, bounced, dense, solid_far, solid_near, post
):
    tiles = size_y // 8
    blocks = relax_blocks(entries)
    for p in range(2):
        for tile, rows, part, lanes in tile_parts(size_y, size_z):
            s = plane_solid(solid_far, solid_near, p, rows, lanes)
            if tile == tiles:
                out = outer_collision(s, outer, second, blocks, p, lanes)
            else:
                out = prepared_collision(s, relaxed, bounced, dense, p, rows, lanes, range(19))
            for i in range(19):
                store_padded(post, i, p, tile, part, out[i], tiles)


def middle_kernel(
    size_x, size_y, size_z, planes, entries, sums, outer_sums, outer, second, migrants, populations,
    post, solid
):
    tiles = size_y // 8
    solids(size_x, size_y, size_z, planes, 0, sums, outer_sums, migrants, solid)
    blocks = relax_blocks(entries)
    for p, x in enumerate(planes):
        for tile, rows, part, lanes in tile_parts(size_y, size_z):
            share, *flow = (solid[c, p, rows, lanes] for c in range(4))
            if tile == tiles:
                out = outer_collision((share, *flow), outer, second, blocks, p, lanes)
            else:
                h = [populations[i, x, rows, lanes] for i in range(19)]
                out = collide(h, share, *flow, blocks)
            for i in range(19):
                store_padded(post, i, p, tile, part, out[i], tiles)


def write_face(post, message, numbers, size_y, size_z, outer):
    tiles = size_y // 8
    for k, i in enumerate(numbers):
        _, c_y, c_z = VEC[i]
        for tile in range(tiles):
            at = 8 + 8 * tile - c_y
            to = k * size_y + 8 * tile
            message[to : to + 8, :] = turned(post[k, 0, at : at + 8, :], c_z, size_z)
        if outer:
            at = 8 + size_y - c_y
            value = turned(post[k, 0, at : at + 8, :], c_z, size_z)
            to = 5 * size_y + 2 * k
            message[to : to + 1, :] = value[0:1]
            message[to + 1 : to + 2, :] = value[7:8]


def streamed(ends, middle, messages, i, x, tile, size_x, size_y, size_z, walls):
    tiles = size_y // 8
    row = iota((8, size_z), 0)
    c_x, c_y, c_z = VEC[i]

    def plane(x):
        if x == 0:
            return ends, 0
        if x == size_x - 1:
            return ends, 1
        return middle, x - 1

    from_x = x - c_x
    if 0 <= from_x < size_x:
        source, p = plane(from_x)
        at = 8 + 8 * tile - c_y
        value = turned(source[i, p, at : at + 8, :], c_z, size_z)
    else:
        numbers = FORWARD if from_x < 0 else BACKWARD
        k = numbers.index(i)

        def received(at, rows):
            if len(messages) == 1:
                return messages[0][at : at + rows, :]
            near, far = messages
            from_near = jnp.logical_not(even_x()) if from_x < 0 else even_x()
            return jnp.where(from_near, near[at : at + rows, :], far[at : at + rows, :])

        if tile < tiles:
            value = received(k * size_y + 8 * tile, 8)
        else:
            at = 5 * size_y + 2 * k
            value = jnp.where(row < 4, received(at, 1), received(at + 1, 1))
    source, p = plane(x)
    if c_y == 1 and tile == 0:
        value = jnp.where((row == 0) & walls[0], source[OPP[i], p, 8:16, :], value)
    if c_y == -1 and tile == tiles - 1:
        back = source[OPP[i], p, size_y : 8 + size_y, :]
        value = jnp.where((row == 7) & walls[1], back, value)
    return value


def walls_of(count):
    here = lax.axis_index("gy")
    return here == 0, here == count - 1


def second_kernel(size_x, size_y, size_z, count, entries, ends, middle, solid, later):
    walls = walls_of(count)
    blocks = relax_blocks(entries)
    for p in range(size_x - 2):
        for tile in range(size_y // 8 + 1):
            rows = slice(8 * tile, 8 * tile + 8)
            h = [
                streamed(ends, middle, None, i, p + 1, tile, size_x, size_y, size_z, walls)
                for i in range(19)
            ]
            for part in range(size_z // 128):
                lanes = slice(128 * part, 128 * part + 128)
                s = [solid[c, p, rows, lanes] for c in range(4)]
                out = collide([v[:, lanes] for v in h], *s, blocks)
                for i in range(19):
                    store_padded(later, i, p, tile, part, out[i], size_y // 8)


def second_ends(
    size_x, size_y, size_z, count, entries, ends, middle, solid, messages, place, numbers, later, p
):
    walls = walls_of(count)
    blocks = relax_blocks(entries)
    x = place * (size_x - 1)
    for tile in range(size_y // 8 + 1):
        rows = slice(8 * tile, 8 * tile + 8)
        h = [
            streamed(ends, middle, messages, i, x, tile, size_x, size_y, size_z, walls) for i in range(19)
        ]
        for part in range(size_z // 128):
            lanes = slice(128 * part, 128 * part + 128)
            s = solid(rows, lanes)
            out = collide([v[:, lanes] for v in h], *s, blocks)
            for k, i in enumerate(numbers):
                store_padded(later, k, p, tile, part, out[i], size_y // 8)


def second_leaving_kernel(size_x, size_y, size_z, count, far, entries, ends, middle, solid, received, *refs):
    message, leaving = refs[-2:]

    def work(place, numbers):
        second_ends(
            size_x,
            size_y,
            size_z,
            count,
            entries,
            ends,
            middle,
            lambda rows, lanes: [solid[c, 0, rows, lanes] for c in range(4)],
            (received,),
            place,
            numbers,
            leaving,
            0,
        )
        write_face(leaving, message, numbers, size_y, size_z, False)

    by_plane(work, far)


def second_ends_kernel(
    size_x, size_y, size_z, count, entries, ends, middle, solid_far, solid_near, far, near, later
):
    for place in range(2):
        second_ends(
            size_x,
            size_y,
            size_z,
            count,
            entries,
            ends,
            middle,
            lambda rows, lanes: plane_solid(solid_far, solid_near, place, rows, lanes),
            (near, far),
            place,
            range(19),
            later,
            place,
        )


def last_kernel(size_x, size_y, size_z, count, ends, middle, advanced, held, done):
    walls = walls_of(count)
    copies = []
    for i in range(19):
        for x in range(size_x):
            if not 0 <= x - VEC[i][0] < size_x:
                continue
            for tile in range(size_y // 8):
                held[i, x, 8 * tile : 8 * tile + 8, :] = streamed(
                    ends, middle, None, i, x, tile, size_x, size_y, size_z, walls
                )
        low, high = max(0, VEC[i][0]), size_x + min(0, VEC[i][0])
        copy = pltpu.make_async_copy(
            held.at[i, low:high], advanced.at[i, low:high], done.at[i]
        )
        copy.start()
        copies.append(copy)
    for copy in copies:
        copy.wait()


def entering(size_x, size_y, size_z, count, ends, received, place, k, target):
    numbers = BACKWARD if place else FORWARD
    walls = walls_of(count)
    for tile in range(size_y // 8):
        target[k, 8 * tile : 8 * tile + 8, :] = streamed(
            ends, None, (received,), numbers[k], place * (size_x - 1), tile, size_x, size_y, size_z, walls
        )


def far_kernel(size_x, size_y, size_z, count, ends, received, held):
    def work(place, numbers):
        del numbers
        for k in range(5):
            entering(size_x, size_y, size_z, count, ends, received, place, k, held)

    by_plane(work, True)


def enter_kernel(size_x, size_y, size_z, count, ends, received, far, given, advanced, near, done):
    del given

    def write(place, held, base):
        numbers = BACKWARD if place else FORWARD
        for k, i in enumerate(numbers):
            copy = pltpu.make_async_copy(held.at[k], advanced.at[i, place * (size_x - 1)], done.at[base + k])
            copy.start()

    def work(place, numbers):
        del numbers
        write(1 - place, far, 0)
        for k in range(5):
            entering(size_x, size_y, size_z, count, ends, received, place, k, near)
        write(place, near, 5)

    by_plane(work, False)
    for k in range(5):
        pltpu.make_async_copy(far.at[k], advanced.at[FORWARD[k], 0], done.at[k]).wait()
        pltpu.make_async_copy(near.at[k], advanced.at[FORWARD[k], 0], done.at[5 + k]).wait()


def shape(*sizes):
    return jax.ShapeDtypeStruct(sizes, F32)


VMEM = pl.BlockSpec(memory_space=pltpu.VMEM)
SMEM = pl.BlockSpec(memory_space=pltpu.SMEM)
HBM = pl.BlockSpec(memory_space=pltpu.HBM)


def call(kernel, out_shape, limit, in_specs, out_specs=None, scratch=(), aliases=None):
    return pl.pallas_call(
        kernel,
        out_shape=out_shape,
        in_specs=in_specs,
        out_specs=jax.tree.map(lambda _: VMEM, out_shape) if out_specs is None else out_specs,
        scratch_shapes=scratch,
        input_output_aliases={} if aliases is None else aliases,
        compiler_params=pltpu.CompilerParams(vmem_limit_bytes=limit * 2**20),
    )


def in_hbm(value):
    return pltpu.with_memory_space_constraint(value, pltpu.HBM)


def around(value, axis, steps):
    count = lax.axis_size(axis)
    return lax.ppermute(value, axis, [(i, (i + steps) % count) for i in range(count)])


def paired_x(value, parity):
    count = lax.axis_size("gx")
    if count % 2:
        raise ValueError("odd ring")
    pairs = [(i, (i + 1 if i % 2 == parity else i - 1) % count) for i in range(count)]
    return lax.ppermute(value, "gx", pairs)


def paired_y(value, parity):
    count_x, count = lax.axis_size("gx"), lax.axis_size("gy")
    pairs = []
    for i in range(count_x):
        for j in range(count):
            other = j + 1 if j % 2 == parity else j - 1
            to = i * count + other if 0 <= other < count else (i ^ 1) * count + j
            pairs.append((i * count + j, to))
    return lax.ppermute(value, ("gx", "gy"), pairs)


def exchanged(near, far):
    far = paired_x(far, 1)
    return paired_x(near, 0), far


def local(populations, relax_rates, velocity, velocity_change, fractions, anchor, destination):
    _, size_x, size_y, size_z = populations.shape
    count = lax.axis_size("gy")
    rows = anchor.shape[0]
    sizes = (size_x, size_y, size_z)
    part = functools.partial
    packed = shape(8, 128)
    band = shape(19, size_x, 8, size_z)
    table, own, near, far, bottom, top = call(
        pack_kernel,
        (shape(32, rows), packed, packed, packed, band, band),
        8,
        [HBM] * 6,
        scratch=[
            pltpu.VMEM((3, rows), F32),
            pltpu.VMEM((3, rows), F32),
            pltpu.VMEM((27, rows), F32),
            pltpu.VMEM((1, rows), I32),
            pltpu.VMEM((1, rows), I32),
            pltpu.SemaphoreType.DMA((7,)),
        ],
    )(*map(in_hbm, (velocity, velocity_change, fractions, anchor[None, :], destination[None, :], populations)))
    near, far = exchanged(near, far)
    first = edge_rows(size_x)[-1]
    fold = size_z // 128
    message = shape(-(-(first + 8 // fold) // 8) * 8, size_z)
    entries = call(relax_kernel, shape(ENTRIES, 8, 128), 8, [SMEM])(relax_rates)
    one, two = call(
        part(edge_kernel, *sizes),
        (message, message),
        8,
        [VMEM] * 4,
        scratch=[pltpu.VMEM((19, 2 * size_x, size_z), F32)],
    )(bottom, top, table, entries)
    two = paired_y(two, 1)
    column, one = call(
        part(merge_kernel, first, fold),
        (shape(8, 128), message),
        8,
        [VMEM] * 4,
        aliases={3: 1},
    )(own, far, near, one)
    shifts = []
    for shift in (2, -2):
        if shift % count > 1 and all((shift - other) % count for other in shifts):
            shifts.append(shift)
    rest = [around(column, "gy", shift) for shift in shifts]
    one, column_two = paired_y(one, 0), paired_y(column, 1)
    unused = pl.BlockSpec(memory_space=pl.ANY)
    outside, inside = (0, size_x - 1), tuple(range(1, size_x - 1))

    def staying(planes, after):
        return call(
            part(stay_kernel, *sizes, planes),
            shape(4, len(planes), size_y, size_z),
            16,
            [VMEM, unused],
        )(table, after)

    sums = staying(outside, two)
    plane_pair = shape(19, 2, size_y, size_z)
    parts = call(
        part(fluid_kernel, *sizes), (plane_pair, plane_pair, shape(2, size_y, size_z)), 16, [VMEM] * 2
    )(entries, populations)
    width = -(-(3 + len(shifts)) * LANES // 128) * 128
    def outer_shapes(planes):
        return tuple(shape(k, len(planes), 8, size_z) for k in (4, 19, 11))

    outer_sums, outer, second, migrants = call(
        part(outer_kernel, *sizes, count, shifts, outside),
        outer_shapes(outside) + (shape(40, width),),
        8,
        [VMEM] * (4 + len(shifts)),
    )(column, one, column_two, *rest, two)

    def padded(planes):
        return shape(19, planes, size_y + 24, size_z)

    def solid_shape(planes):
        return shape(4, planes, size_y + 8, size_z)

    sent = pltpu.VMEM((5, 1, size_y + 24, size_z), F32)
    wide_face = shape((5 * size_y + 10 + 7) // 8 * 8, size_z)
    face = shape(5 * size_y, size_z)

    def leaving(far, *given):
        return call(
            part(leaving_kernel, *sizes, far),
            (solid_shape(1), wide_face),
            16,
            [VMEM] * 9 + [unused] * (len(given) - 9),
            scratch=[sent],
        )(*given)

    known = (entries, sums, outer_sums, outer, second, migrants, *parts)
    solid_far, far = leaving(True, *known)
    solid_near, near = leaving(False, *known, solid_far)
    near, far = exchanged(near, far)
    inner = call(part(outer_kernel, *sizes, count, shifts, inside), outer_shapes(inside), 8, [VMEM] * 2)(
        two, one
    )
    middle, solid_middle = call(
        part(middle_kernel, *sizes, inside),
        (padded(len(inside)), solid_shape(len(inside))),
        16,
        [VMEM] * 7,
    )(entries, staying(inside, solid_near), *inner, migrants, populations)
    ends = call(part(ends_kernel, *sizes), padded(2), 16, [VMEM] * 8)(
        entries, outer, second, *parts, solid_far, solid_near
    )
    later_middle = call(part(second_kernel, *sizes, count), padded(len(inside)), 16, [VMEM] * 4)(
        entries, ends, middle, solid_middle
    )

    def second_leaving(far, *given):
        return call(
            part(second_leaving_kernel, *sizes, count, far),
            face,
            16,
            [VMEM] * 5 + [unused] * (len(given) - 5),
            scratch=[sent],
        )(*given)

    received = (far, near)
    far = second_leaving(True, entries, ends, middle, solid_far, far, later_middle)
    near = second_leaving(False, entries, ends, middle, solid_near, near, far)
    near, far = exchanged(near, far)
    later_ends = call(part(second_ends_kernel, *sizes, count), padded(2), 16, [VMEM] * 7)(
        entries, ends, middle, solid_far, solid_near, *received
    )
    advanced = call(
        part(last_kernel, *sizes, count),
        shape(19, *sizes),
        16,
        [VMEM] * 2,
        HBM,
        [pltpu.VMEM((19, *sizes), F32), pltpu.SemaphoreType.DMA((19,))],
    )(later_ends, later_middle)
    slabs = (5, size_y, size_z)
    far = call(part(far_kernel, *sizes, count), shape(*slabs), 16, [VMEM] * 2)(later_ends, far)
    return call(
        part(enter_kernel, *sizes, count),
        shape(19, *sizes),
        16,
        [VMEM] * 3 + [HBM],
        HBM,
        [pltpu.VMEM(slabs, F32), pltpu.SemaphoreType.DMA((10,))],
        {3: 0},
    )(later_ends, near, far, advanced)


def solution(mesh):
    placed = (
        P(None, "gx", "gy", None),
        P(),
        P(None, ("gx", "gy")),
        P(None, ("gx", "gy")),
        P(None, ("gx", "gy")),
        P(("gx", "gy")),
        P(("gx", "gy")),
    )
    return jax.shard_map(
        local, mesh=mesh, in_specs=placed, out_specs=P(None, "gx", "gy", None), check_vma=False
    )
```

```python
import functools

import jax
import jax.numpy as jnp
import numpy as np
from jax import lax
from jax.experimental import pallas as pl
from jax.experimental.pallas import tpu as pltpu
from jax.sharding import PartitionSpec as P

CAP = 4
STEPS = 2
LANES = 8 * CAP
F32 = jnp.float32
BF16 = jnp.bfloat16
I32 = jnp.int32


def lattice():
    vectors = [[0, 0, 0]]
    for axis_one in range(3):
        for orient in (1, -1):
            vector_one = [0, 0, 0]
            vector_one[axis_one] = orient
            vectors.append(vector_one)
    for axis_one, axis_two in ((0, 1), (0, 2), (1, 2)):
        for orient in (1, -1):
            for second in (1, -1):
                vector_one = [0, 0, 0]
                vector_one[axis_one] = orient
                vector_one[axis_two] = second
                vectors.append(vector_one)
    integral = np.array(vectors)
    speeds = integral * 1.0
    length = (speeds**2).sum(axis=1)
    weights = np.where(length == 0, 1.0 / 3.0, np.where(length == 1, 1.0 / 18.0, 1.0 / 36.0))
    opposite = [vectors.index([0 - component for component in vector_one]) for vector_one in vectors]
    along_x, along_y, along_z = (speeds[:, 0], speeds[:, 1], speeds[:, 2])
    rows_list = [
        np.ones(19),
        along_x,
        along_y,
        along_z,
        length,
        3 * along_x**2 - length,
        along_y**2 - along_z**2,
        along_x * along_y,
        along_y * along_z,
        along_x * along_z,
        along_x * length,
        along_y * length,
        along_z * length,
        along_x * (along_y**2 - along_z**2),
        along_y * (along_z**2 - along_x**2),
        along_z * (along_x**2 - along_y**2),
        length**2,
        (3 * along_x**2 - length) * length,
        (along_y**2 - along_z**2) * length,
    ]
    basis_rows = []
    for candidate in rows_list:
        for earlier in basis_rows:
            candidate = candidate - np.dot(candidate, earlier) * earlier
        basis_rows.append(candidate / np.sqrt(np.dot(candidate, candidate)))
    return [tuple(v) for v in vectors], weights, opposite, np.array(basis_rows)


VEC, WEIGHTS, OPP, BASIS = lattice()
FORWARD = [i for i in range(19) if VEC[i][0] == 1]
BACKWARD = [i for i in range(19) if VEC[i][0] == -1]
DOWNWARD = [i for i in range(19) if VEC[i][1] == -1]
UPWARD = [OPP[i] for i in DOWNWARD]


def symmetric_blocks():
    def vec(entries):
        out = np.zeros(19)
        for index, value in entries.items():
            out[index] = value
        return out

    def plane(base):
        s_one, d_one = vec({base: 1, base + 3: 1}), vec({base: 1, base + 3: -1})
        s_two, d_two = vec({base + 1: 1, base + 2: 1}), vec({base + 1: 1, base + 2: -1})
        return s_one + s_two, s_one - s_two, d_one + d_two, d_one - d_two

    rest = vec({0: 1})
    s_x, s_y, s_z = vec({1: 1, 2: 1}), vec({3: 1, 4: 1}), vec({5: 1, 6: 1})
    d_x, d_y, d_z = vec({1: 1, 2: -1}), vec({3: 1, 4: -1}), vec({5: 1, 6: -1})
    xy, q_xy, x_xy, y_xy = plane(7)
    xz, q_xz, x_xz, z_xz = plane(11)
    yz, q_yz, y_yz, z_yz = plane(15)
    blocks = [
        [rest, s_x + s_y + s_z, xy + xz + yz],
        [2 * s_x - s_y - s_z, xy + xz - 2 * yz],
        [s_y - s_z, xy - xz],
        [q_xy],
        [q_xz],
        [q_yz],
        [d_x, x_xy, x_xz],
        [d_y, y_xy, y_yz],
        [d_z, z_xz, z_yz],
    ]
    scales = [[1, 1 / 6, 1 / 12], [1 / 12, 1 / 24], [1 / 4, 1 / 8]]
    scales += [[1 / 4]] * 3 + [[1 / 2, 1 / 4, 1 / 4]] * 3
    forward = np.array([row for block in blocks for row in block])
    back = np.linalg.inv(forward)
    left = forward @ np.diag(1.0 / WEIGHTS) @ BASIS.T
    right = BASIS @ np.diag(WEIGHTS) @ back
    table = []
    start = 0
    for block, scale in zip(blocks, scales):
        size = len(block)
        rows = []
        for a in range(size):
            row = []
            for b in range(size):
                per_rate = -scale[a] * left[start + a, :] * right[:, start + b]
                row.append([(k, float(v)) for k, v in enumerate(per_rate) if abs(v) > 1e-12])
            rows.append(row)
        table.append(rows)
        start += size
    return table


RELAX = symmetric_blocks()


def relax_rows(rates, target):
    values = [jnp.broadcast_to(rates[0:1, k : k + 1], (8, 128)) for k in range(19)]
    at = 0
    for block in RELAX:
        for row in block:
            for terms in row:
                target[at] = sum(values[k] * np.float32(factor) for k, factor in terms)
                at += 1


def relax_blocks(table, lanes=128):
    blocks, at = [], 0
    for block in RELAX:
        rows = []
        for row in block:
            rows.append(
                [jnp.concatenate([table[at + k]] * (lanes // 128), axis=1) for k in range(len(row))]
            )
            at += len(row)
        blocks.append(rows)
    return blocks


ENTRIES = sum(len(row) for block in RELAX for row in block)


def apply_block(block, values):
    out = []
    for row in block:
        total = None
        for factor, value in zip(row, values):
            part = factor * value
            total = part if total is None else total + part
        out.append(total)
    return out


def collide(h, solid, s_x, s_y, s_z, blocks):
    def plane(base):
        s_one, d_one = h[base] + h[base + 3], h[base] - h[base + 3]
        s_two, d_two = h[base + 1] + h[base + 2], h[base + 1] - h[base + 2]
        return s_one + s_two, s_one - s_two, d_one + d_two, d_one - d_two

    sum_x, dif_x = h[1] + h[2], h[1] - h[2]
    sum_y, dif_y = h[3] + h[4], h[3] - h[4]
    sum_z, dif_z = h[5] + h[6], h[5] - h[6]
    xy, q_xy, x_xy, y_xy = plane(7)
    xz, q_xz, x_xz, z_xz = plane(11)
    yz, q_yz, y_yz, z_yz = plane(15)
    axes = sum_x + sum_y + sum_z
    edges = xy + xz + yz
    density = h[0] * (1.0 / 3.0) + axes * (1.0 / 18.0) + edges * (1.0 / 36.0)
    m_x = dif_x * (1.0 / 18.0) + (x_xy + x_xz) * (1.0 / 36.0)
    m_y = dif_y * (1.0 / 18.0) + (y_xy + y_yz) * (1.0 / 36.0)
    m_z = dif_z * (1.0 / 18.0) + (z_xz + z_yz) * (1.0 / 36.0)
    inverse = 1.0 / density
    u_x, u_y, u_z = m_x * inverse, m_y * inverse, m_z * inverse
    e_xx, e_yy, e_zz = m_x * u_x, m_y * u_y, m_z * u_z
    e_xy, e_xz, e_yz = m_x * u_y, m_x * u_z, m_y * u_z
    energy = e_xx + e_yy + e_zz
    turn = e_yy - e_zz
    lean = 3.0 * e_xx - energy
    rest_off = h[0] - density + 1.5 * energy
    axes_off = axes - 6.0 * density
    edges_off = edges - 12.0 * density - 18.0 * energy
    a_one = 3.0 * sum_x - axes - 9.0 * lean
    b_one = edges - 3.0 * yz - 18.0 * lean
    a_two = sum_y - sum_z - 9.0 * turn
    b_two = xy - xz - 18.0 * turn
    q_xy = q_xy - 36.0 * e_xy
    q_xz = q_xz - 36.0 * e_xz
    q_yz = q_yz - 36.0 * e_yz

    r_rest, r_axes, r_edges = apply_block(blocks[0], [rest_off, axes_off, edges_off])
    r_a_one, r_b_one = apply_block(blocks[1], [a_one, b_one])
    r_a_two, r_b_two = apply_block(blocks[2], [a_two, b_two])
    fluid = 1.0 - solid
    mixed = solid * density
    w_x, w_y, w_z = solid * m_x, solid * m_y, solid * m_z
    n_x, n_y, n_z = mixed * s_x, mixed * s_y, mixed * s_z
    p_x = n_x * s_x - solid * e_xx
    p_y = n_y * s_y - solid * e_yy
    p_z = n_z * s_z - solid * e_zz
    total = 1.5 * (p_x + p_y + p_z)
    lean_s = 2.25 * p_x - 0.5 * total
    turn_s = 2.25 * (p_y - p_z)
    rest = fluid * r_rest - total
    axes = fluid * r_axes
    edges = fluid * r_edges + total
    a_one = fluid * r_a_one + lean_s
    b_one = fluid * r_b_one + lean_s
    a_two = fluid * r_a_two + turn_s
    b_two = fluid * r_b_two + turn_s
    q_xy = fluid * apply_block(blocks[3], [q_xy])[0] + 9.0 * (n_x * s_y - solid * e_xy)
    q_xz = fluid * apply_block(blocks[4], [q_xz])[0] + 9.0 * (n_x * s_z - solid * e_xz)
    q_yz = fluid * apply_block(blocks[5], [q_yz])[0] + 9.0 * (n_y * s_z - solid * e_yz)

    def odd(block, axis, one, two, m, n, w):
        six = 6.0 * m
        axis = axis - six
        twelve = six + six
        one = one - twelve
        two = two - twelve
        r_axis, r_one, r_two = apply_block(block, [axis, one, two])
        push = 3.0 * (n - w)
        half = 0.5 * solid
        return (
            fluid * r_axis - solid * axis + push,
            fluid * r_one - half * one + push,
            fluid * r_two - half * two + push,
        )

    d_x, x_xy, x_xz = odd(blocks[6], dif_x, x_xy, x_xz, m_x, n_x, w_x)
    d_y, y_xy, y_yz = odd(blocks[7], dif_y, y_xy, y_yz, m_y, n_y, w_y)
    d_z, z_xz, z_yz = odd(blocks[8], dif_z, z_xz, z_yz, m_z, n_z, w_z)
    out = [None] * 19
    out[0] = h[0] + rest
    even = axes + 2.0 * a_one
    out[1], out[2] = h[1] + (even + d_x), h[2] + (even - d_x)
    base = axes - a_one
    even = base + a_two
    out[3], out[4] = h[3] + (even + d_y), h[4] + (even - d_y)
    even = base - a_two
    out[5], out[6] = h[5] + (even + d_z), h[6] + (even - d_z)

    def spread(start, even, twist, one, two):
        same, cross = even + twist, even - twist
        plus, minus = one + two, one - two
        out[start] = h[start] + (same + plus)
        out[start + 3] = h[start + 3] + (same - plus)
        out[start + 1] = h[start + 1] + (cross + minus)
        out[start + 2] = h[start + 2] + (cross - minus)

    base = edges + b_one
    spread(7, base + b_two, q_xy, x_xy, y_xy)
    spread(11, base - b_two, q_xz, x_xz, z_xz)
    spread(15, edges - 2.0 * b_one, q_yz, y_yz, z_yz)
    return out


def equilibrium(density, flow, numbers):
    v_x, v_y, v_z = flow
    rest = 1.0 - 1.5 * (v_x * v_x + v_y * v_y + v_z * v_z)
    out = {}
    for i in numbers:
        if i in out:
            continue
        along = None
        for sign, v in zip(VEC[i], flow):
            if sign:
                part = v if sign == 1 else -v
                along = part if along is None else along + part
        if along is None:
            out[i] = rest
        else:
            along = 3.0 * along
            even = rest + 0.5 * along * along
            out[i], out[OPP[i]] = even + along, even - along
    return out


def fluid_parts(h, blocks, numbers):
    zero = jnp.zeros_like(h[0])
    relaxed = collide(h, zero, zero, zero, zero, blocks)
    density, flow = zero, [zero, zero, zero]
    for i in range(19):
        part = np.float32(WEIGHTS[i]) * h[i]
        density = density + part
        for k in range(3):
            if VEC[i][k]:
                flow[k] = flow[k] + part if VEC[i][k] == 1 else flow[k] - part
    inverse = 1.0 / density
    still = equilibrium(density, [f * inverse for f in flow], numbers)
    bounced = [h[OPP[i]] - density * still[OPP[i]] for i in numbers]
    return [relaxed[i] for i in numbers], bounced, density


def blended(relaxed, bounced, density, share, still):
    return relaxed + share * ((bounced + density * still) - relaxed)


def iota(shape, dim):
    return lax.broadcasted_iota(I32, shape, dim)


def cells_of(anchor, size_y, size_z):
    plane = size_y * size_z
    a_x = lax.div(anchor, jnp.int32(plane))
    rest = anchor - a_x * plane
    a_y = lax.div(rest, jnp.int32(size_z))
    return a_x, a_y, rest - a_y * size_z


def halves(value):
    high = value.astype(BF16)
    return high, (value - high.astype(F32)).astype(BF16)


def dot_t(left, right):
    return lax.dot_general(left, right, (((1,), (1,)), ((), ())), preferred_element_type=F32)


def deposited(groups, shares, velocity, a_x, a_y, a_z, size_z, big):
    centre = a_x * big + a_y
    lanes = centre.shape[1]
    totals = None
    rows_z = iota((size_z, lanes), 0)
    for off_z in range(3):
        weights = []
        for rows_x, rows_y in groups:
            away = rows_x * big + rows_y - centre
            weight = jnp.zeros(away.shape, F32)
            for off in range(9):
                move = (off // 3 - 1) * big + off % 3 - 1
                row = 3 * off + off_z
                weight = jnp.where(away == move, shares[row : row + 1, :], weight)
            weights.append([weight] + [weight * velocity[k : k + 1, :] for k in range(3)])
        rows = jnp.concatenate([w for block in weights for w in block], axis=0)
        high, low = halves(rows)
        hot = jnp.where(rows_z == a_z + (off_z - 1), 1.0, 0.0).astype(BF16)
        part = dot_t(high, hot) + dot_t(low, hot)
        totals = part if totals is None else totals + part
    return totals


def even_x():
    return lax.rem(lax.axis_index("gx"), 2) == 0


def pack_kernel(
    velocity_in,
    change_in,
    fractions_in,
    anchor_in,
    destination_in,
    populations,
    table,
    own,
    near,
    far,
    bottom,
    top,
    velocity,
    change,
    fractions,
    anchor,
    destination,
    done,
):
    pairs = (
        (destination_in, destination),
        (velocity_in, velocity),
        (change_in, change),
        (fractions_in, fractions),
        (anchor_in, anchor),
        (populations.at[:, :, 0:8, :], bottom),
        (populations.at[:, :, populations.shape[2] - 8 :, :], top),
    )
    copies = [pltpu.make_async_copy(a, b, done.at[k]) for k, (a, b) in enumerate(pairs)]
    for copy in copies:
        copy.start()
    rows = destination.shape[1]
    order = jnp.where(iota((128, 128), 0) <= iota((128, 128), 1), 1.0, 0.0).astype(BF16)
    for copy in copies[:5]:
        copy.wait()
    dest = destination[...]
    kinds = iota((16, rows), 0)
    hot = jnp.where(dest == kinds, 1.0, 0.0)
    seen = jnp.zeros((16, 1), F32)
    ranks = []
    for start in range(0, rows, 128):
        counted = seen + lax.dot_general(
            hot[:, start : start + 128].astype(BF16),
            order,
            (((1,), (0,)), ((), ())),
            preferred_element_type=F32,
        )
        ranks.append(counted)
        seen = counted[:, 127:128]
    rank = jnp.concatenate(ranks, axis=1)
    kind = iota((16, 1), 0)
    begin = jnp.where(
        kind < 3,
        5 * CAP + CAP * kind,
        jnp.where(kind == 3, 0, jnp.where(kind == 5, CAP, 2 * CAP + CAP * (kind - 6))),
    ).astype(F32)
    leaving = (dest < 9) & (dest != 4)
    slot = jnp.sum(hot * (begin + rank - 1.0), axis=0, keepdims=True)
    slot = jnp.where(leaving, slot, -1.0).astype(I32)
    chosen = jnp.where(iota((128, rows), 0) == slot, 1.0, 0.0).astype(BF16)
    new_velocity = velocity[...] + change[...]
    payload = jnp.concatenate(
        [fractions[...], new_velocity, anchor[...].astype(F32), jnp.zeros((1, rows), F32)], axis=0
    )
    high = payload.astype(BF16)
    middle, low = halves(payload - high.astype(F32))
    packed = dot_t(high, chosen) + dot_t(middle, chosen) + dot_t(low, chosen)
    packed = folded(packed)
    lane = lax.rem(iota((8, 128), 1), jnp.int32(LANES))
    own[...] = jnp.where(lane < 2 * CAP, packed, 0.0)
    ahead = jnp.where((lane >= 2 * CAP) & (lane < 5 * CAP), packed, 0.0)
    behind = jnp.where(lane >= 5 * CAP, packed, 0.0)
    even = even_x()
    near[...] = jnp.where(even, ahead, behind)
    far[...] = jnp.where(even, behind, ahead)
    table[...] = jnp.where((iota((32, rows), 0) < 27) & (dest != 4), 0.0, payload)
    for copy in copies[5:]:
        copy.wait()


def edge_rows(size_x):
    starts = [0]
    for rows in (19 * size_x, 4 * 2 * size_x, 11 * size_x):
        starts.append(starts[-1] + rows)
    return starts


def edge_kernel(size_x, size_y, size_z, bottom, top, table, entries, one, two, held):
    a_x, a_y, a_z = cells_of(table[30:31, :].astype(I32), size_y, size_z)
    rows = 2 * size_x
    index = iota((rows, 1), 0)
    rows_x, low = lax.div(index, jnp.int32(2)), lax.rem(index, jnp.int32(2))
    sums = deposited(
        [(rows_x, low), (rows_x, low + (size_y - 2))],
        table[0:27, :],
        table[27:30, :],
        a_x,
        a_y,
        a_z,
        size_z,
        8 * size_y,
    )
    _, at_sums, at_second, _ = edge_rows(size_x)
    for i in range(19):
        for x in range(size_x):
            held[i, x : x + 1, :] = bottom[i, x, 1:2, :]
            held[i, size_x + x : size_x + x + 1, :] = top[i, x, 6:7, :]
    second = fluid_parts([held[i] for i in range(19)], relax_blocks(entries, size_z), DOWNWARD + UPWARD)
    relaxed, bounced, density = second

    def write(down, up):
        for i in range(19):
            for x in range(size_x):
                at = i * size_x + x
                down[at : at + 1, :] = bottom[i, x, 0:1, :]
                up[at : at + 1, :] = top[i, x, 7:8, :]
        down[at_sums : at_sums + 4 * rows, :] = sums[: 4 * rows]
        up[at_sums : at_sums + 4 * rows, :] = sums[4 * rows :]
        for target, own, at_row in ((down, 0, 0), (up, 5, size_x)):
            parts = relaxed[own : own + 5] + bounced[own : own + 5] + [density]
            for k, value in enumerate(parts):
                at = at_second + k * size_x
                target[at : at + size_x, :] = value[at_row : at_row + size_x]

    even = lax.rem(lax.axis_index("gy"), 2) == 0

    @pl.when(even)
    def _():
        write(two, one)

    @pl.when(jnp.logical_not(even))
    def _():
        write(one, two)


def folded(table):
    return sum(
        table[8 * k : 8 * k + 8] if k == 0 else pltpu.roll(table[8 * k : 8 * k + 8], LANES * k, 1)
        for k in range(4)
    )


def merge_kernel(first, fold, own, far, near, one_in, column, one):
    del one_in
    merged = own[...] + near[...] + far[...]
    column[...] = merged
    deep = 8 // fold
    for k in range(fold):
        one[first : first + deep, 128 * k : 128 * k + 128] = merged[deep * k : deep * k + deep]


def relax_kernel(rates, entries):
    relax_rows(rates, entries)


def fluid_kernel(size_x, size_y, size_z, entries, populations, relaxed, bounced, density):
    blocks = relax_blocks(entries)
    for p, x in enumerate((0, size_x - 1)):
        for tile in range(size_y // 8):
            rows = slice(8 * tile, 8 * tile + 8)
            for part in range(size_z // 128):
                lanes = slice(128 * part, 128 * part + 128)
                f, b, d = fluid_parts([populations[i, x, rows, lanes] for i in range(19)], blocks, range(19))
                for i in range(19):
                    relaxed[i, p, rows, lanes] = f[i]
                    bounced[i, p, rows, lanes] = b[i]
                density[p, rows, lanes] = d


def stay_kernel(size_x, size_y, size_z, planes, table, after, sums):
    del after
    a_x, a_y, a_z = cells_of(table[30:31, :].astype(I32), size_y, size_z)
    index = iota((len(planes) * size_y, 1), 0)
    number = lax.div(index, jnp.int32(size_y))
    rows_x = number * (size_x - 1) if planes[0] == 0 else number + planes[0]
    totals = deposited(
        [(rows_x, index - number * size_y)],
        table[0:27, :],
        table[27:30, :],
        a_x,
        a_y,
        a_z,
        size_z,
        8 * size_y,
    )
    cells = len(planes) * size_y
    for c in range(4):
        for p in range(len(planes)):
            at = c * cells + p * size_y
            sums[c, p, :, :] = totals[at : at + size_y]


def outer_kernel(size_x, size_y, size_z, count, shifts, planes, *refs):
    if planes[0] == 0:
        column, one, column_two, *rest = refs[: 3 + len(shifts)]
        two, sums, outer, second, migrants = refs[3 + len(shifts) :]
        arrivals(size_x, size_y, size_z, count, shifts, column, one, column_two, rest, migrants)
    else:
        two, one, sums, outer, second = refs
    blank = jnp.zeros((8, size_z), F32)
    ones = jnp.ones((8, size_z), F32)
    _, at_sums, at_second, _ = edge_rows(size_x)

    def write(above, below):
        for p, x in enumerate(planes):
            for c in range(4):
                at = at_sums + c * 2 * size_x + 2 * x
                sums[c, p, :, :] = blank
                sums[c, p, 0:2, :] = above[at : at + 2, :]
                sums[c, p, 6:8, :] = below[at : at + 2, :]
            for i in range(19):
                at = i * size_x + x
                outer[i, p, :, :] = ones
                outer[i, p, 0:1, :] = above[at : at + 1, :]
                outer[i, p, 7:8, :] = below[at : at + 1, :]
            for k in range(11):
                at = at_second + k * size_x + x
                second[k, p, :, :] = ones
                second[k, p, 1:2, :] = above[at : at + 1, :]
                second[k, p, 6:7, :] = below[at : at + 1, :]

    even = lax.rem(lax.axis_index("gy"), 2) == 0

    @pl.when(even)
    def _():
        write(one, two)

    @pl.when(jnp.logical_not(even))
    def _():
        write(two, one)


def pair_source(here, parity, count):
    other = jnp.where(lax.rem(here, 2) == parity, here + 1, here - 1)
    return jnp.where((other >= 0) & (other < count), other, here + 2 * count)


def arrivals(size_x, size_y, size_z, count, shifts, column, one, two, rest, migrants):
    first = edge_rows(size_x)[-1]
    here = lax.axis_index("gy")
    fold = size_z // 128
    deep = 8 // fold

    def gathered(message):
        return jnp.concatenate(
            [message[first : first + deep, 128 * k : 128 * k + 128] for k in range(fold)], axis=0
        )

    parts = [column[...], gathered(one), two[...]] + [r[...] for r in rest]
    sources = [here, pair_source(here, 0, count), pair_source(here, 1, count)]
    sources += [lax.rem(here - shift + 2 * count, count) for shift in shifts]
    lane = iota((1, 128), 1)
    spot = lax.rem(lane, jnp.int32(LANES))
    group = lax.div(spot, jnp.int32(CAP))
    across = jnp.where(
        (group == 0) | (group == 2) | (group == 5), -1, jnp.where((group == 3) | (group == 6), 0, 1)
    )
    per_group = 128 // LANES
    tables, offsets = [], []
    for start in range(0, len(parts), per_group):
        blocks = [jnp.zeros((8, 128), F32)] * 4
        offset = jnp.full((1, 128), 2 * count, I32)
        for k, part in enumerate(parts[start : start + per_group]):
            place = lax.div(lane, jnp.int32(LANES)) == k
            for q in range(4):
                turn = LANES * (k - q) % 128
                blocks[q] = jnp.where(place, part if turn == 0 else pltpu.roll(part, turn, 1), blocks[q])
            offset = jnp.where(lax.div(lane, jnp.int32(LANES)) == k, sources[start + k] - here, offset)
        tables.append(jnp.concatenate(blocks, axis=0))
        offsets.append((offset + across) * size_y)
    table = jnp.concatenate(tables, axis=1)
    a_x, a_y, a_z = cells_of(table[30:31, :].astype(I32), size_y, size_z)
    migrants[0:32, :] = table
    migrants[32:33, :] = a_x.astype(F32)
    migrants[33:34, :] = (a_y + jnp.concatenate(offsets, axis=1)).astype(F32)
    migrants[34:35, :] = a_z.astype(F32)


def store_padded(target, i, x, tile, part, value, tiles):
    lanes = slice(128 * part, 128 * part + 128)
    if tile == tiles:
        target[i, x, 0:8, lanes] = value
        target[i, x, 8 + 8 * tiles : 16 + 8 * tiles, lanes] = value
    else:
        target[i, x, 8 + 8 * tile : 16 + 8 * tile, lanes] = value
        if tile == 0:
            target[i, x, 16 + 8 * tiles : 24 + 8 * tiles, lanes] = value


def turned(value, shift, size_z):
    return value if shift == 0 else pltpu.roll(value, shift % size_z, 1)


def solids(size_x, size_y, size_z, planes, first, sums, outer_sums, migrants, solid):
    a_x, a_y, a_z = (migrants[k : k + 1, :].astype(I32) for k in (32, 33, 34))
    wide = size_y + 8
    index = iota((len(planes) * wide, 1), 0)
    number = lax.div(index, jnp.int32(wide))
    row = index - number * wide
    rows_y = jnp.where(row < size_y + 2, row, jnp.where(row >= size_y + 6, row - wide, -3 * size_y))
    big = 4 * size_y * (lax.axis_size("gy") + 2)
    totals = deposited(
        [(number + planes[0], rows_y)], migrants[0:27, :], migrants[27:30, :], a_x, a_y, a_z, size_z, big
    )
    cells = len(planes) * wide
    for p, x in enumerate(planes):
        parts = []
        for c in range(4):
            at = c * cells + p * wide
            solid_sum = jnp.concatenate([sums[c, first + p, :, :], outer_sums[c, first + p, :, :]], axis=0)
            parts.append(totals[at : at + wide] + solid_sum)
        scale = 1.0 / (parts[0] + 1e-06)
        solid[0, p, :, :] = jnp.minimum(parts[0], 1.0)
        for c in (1, 2, 3):
            solid[c, p, :, :] = parts[c] * scale


def outer_collision(solid, outer, second, blocks, p, lanes):
    share, *flow = solid
    out = collide([outer[i, p, :, lanes] for i in range(19)], share, *flow, blocks)
    line = iota((8, 128), 0)
    away = jnp.where(line < 4, 1.0, -1.0)
    still = equilibrium(None, [away * v for v in flow], DOWNWARD)
    density = second[10, p, :, lanes]
    for k, (i, j) in enumerate(zip(DOWNWARD, UPWARD)):
        value = blended(second[k, p, :, lanes], second[5 + k, p, :, lanes], density, share, still[i])
        out[i] = jnp.where(line == 1, value, out[i])
        out[j] = jnp.where(line == 6, value, out[j])
    return out


def prepared_collision(solid, relaxed, bounced, dense, p, rows, lanes, numbers):
    share, *flow = solid
    still = equilibrium(None, flow, numbers)
    density = dense[p, rows, lanes]
    return {
        i: blended(relaxed[i, p, rows, lanes], bounced[i, p, rows, lanes], density, share, still[i])
        for i in numbers
    }


def tile_parts(size_y, size_z):
    for tile in range(size_y // 8 + 1):
        for part in range(size_z // 128):
            yield tile, slice(8 * tile, 8 * tile + 8), part, slice(128 * part, 128 * part + 128)


def by_plane(work, far):
    even = even_x()

    @pl.when(even if far else jnp.logical_not(even))
    def _():
        work(0, BACKWARD)

    @pl.when(jnp.logical_not(even) if far else even)
    def _():
        work(1, FORWARD)


def leaving_kernel(
    size_x, size_y, size_z, far, entries, sums, outer_sums, outer, second, migrants, relaxed, bounced,
    dense, *refs
):
    solid, message, leaving = refs[-3:]
    tiles = size_y // 8

    def work(place, numbers):
        plane = place * (size_x - 1)
        solids(size_x, size_y, size_z, (plane,), place, sums, outer_sums, migrants, solid)
        blocks = relax_blocks(entries)
        for tile, rows, part, lanes in tile_parts(size_y, size_z):
            s = [solid[c, 0, rows, lanes] for c in range(4)]
            if tile == tiles:
                out = outer_collision(s, outer, second, blocks, place, lanes)
            else:
                out = prepared_collision(s, relaxed, bounced, dense, place, rows, lanes, numbers)
            for k, i in enumerate(numbers):
                store_padded(leaving, k, 0, tile, part, out[i], tiles)
        write_face(leaving, message, numbers, size_y, size_z, True)

    by_plane(work, far)


def plane_solid(far, near, place, rows, lanes):
    in_far = even_x() if place == 0 else jnp.logical_not(even_x())
    return [jnp.where(in_far, far[c, 0, rows, lanes], near[c, 0, rows, lanes]) for c in range(4)]


def ends_kernel(
    size_x, size_y, size_z, entries, outer, second, relaxed, bounced, dense, solid_far, solid_near, post
):
    tiles = size_y // 8
    blocks = relax_blocks(entries)
    for p in range(2):
        for tile, rows, part, lanes in tile_parts(size_y, size_z):
            s = plane_solid(solid_far, solid_near, p, rows, lanes)
            if tile == tiles:
                out = outer_collision(s, outer, second, blocks, p, lanes)
            else:
                out = prepared_collision(s, relaxed, bounced, dense, p, rows, lanes, range(19))
            for i in range(19):
                store_padded(post, i, p, tile, part, out[i], tiles)


def middle_kernel(
    size_x, size_y, size_z, planes, entries, sums, outer_sums, outer, second, migrants, populations,
    post, solid
):
    tiles = size_y // 8
    solids(size_x, size_y, size_z, planes, 0, sums, outer_sums, migrants, solid)
    blocks = relax_blocks(entries)
    for p, x in enumerate(planes):
        for tile, rows, part, lanes in tile_parts(size_y, size_z):
            share, *flow = (solid[c, p, rows, lanes] for c in range(4))
            if tile == tiles:
                out = outer_collision((share, *flow), outer, second, blocks, p, lanes)
            else:
                h = [populations[i, x, rows, lanes] for i in range(19)]
                out = collide(h, share, *flow, blocks)
            for i in range(19):
                store_padded(post, i, p, tile, part, out[i], tiles)


def write_face(post, message, numbers, size_y, size_z, outer):
    tiles = size_y // 8
    for k, i in enumerate(numbers):
        _, c_y, c_z = VEC[i]
        for tile in range(tiles):
            at = 8 + 8 * tile - c_y
            to = k * size_y + 8 * tile
            message[to : to + 8, :] = turned(post[k, 0, at : at + 8, :], c_z, size_z)
        if outer:
            at = 8 + size_y - c_y
            value = turned(post[k, 0, at : at + 8, :], c_z, size_z)
            to = 5 * size_y + 2 * k
            message[to : to + 1, :] = value[0:1]
            message[to + 1 : to + 2, :] = value[7:8]


def streamed(ends, middle, messages, i, x, tile, size_x, size_y, size_z, walls):
    tiles = size_y // 8
    row = iota((8, size_z), 0)
    c_x, c_y, c_z = VEC[i]

    def plane(x):
        if x == 0:
            return ends, 0
        if x == size_x - 1:
            return ends, 1
        return middle, x - 1

    from_x = x - c_x
    if 0 <= from_x < size_x:
        source, p = plane(from_x)
        at = 8 + 8 * tile - c_y
        value = turned(source[i, p, at : at + 8, :], c_z, size_z)
    else:
        numbers = FORWARD if from_x < 0 else BACKWARD
        k = numbers.index(i)

        def received(at, rows):
            if len(messages) == 1:
                return messages[0][at : at + rows, :]
            near, far = messages
            from_near = jnp.logical_not(even_x()) if from_x < 0 else even_x()
            return jnp.where(from_near, near[at : at + rows, :], far[at : at + rows, :])

        if tile < tiles:
            value = received(k * size_y + 8 * tile, 8)
        else:
            at = 5 * size_y + 2 * k
            value = jnp.where(row < 4, received(at, 1), received(at + 1, 1))
    source, p = plane(x)
    if c_y == 1 and tile == 0:
        value = jnp.where((row == 0) & walls[0], source[OPP[i], p, 8:16, :], value)
    if c_y == -1 and tile == tiles - 1:
        back = source[OPP[i], p, size_y : 8 + size_y, :]
        value = jnp.where((row == 7) & walls[1], back, value)
    return value


def walls_of(count):
    here = lax.axis_index("gy")
    return here == 0, here == count - 1


def second_kernel(size_x, size_y, size_z, count, entries, ends, middle, solid, later):
    walls = walls_of(count)
    blocks = relax_blocks(entries)
    for p in range(size_x - 2):
        for tile in range(size_y // 8 + 1):
            rows = slice(8 * tile, 8 * tile + 8)
            h = [
                streamed(ends, middle, None, i, p + 1, tile, size_x, size_y, size_z, walls)
                for i in range(19)
            ]
            for part in range(size_z // 128):
                lanes = slice(128 * part, 128 * part + 128)
                s = [solid[c, p, rows, lanes] for c in range(4)]
                out = collide([v[:, lanes] for v in h], *s, blocks)
                for i in range(19):
                    store_padded(later, i, p, tile, part, out[i], size_y // 8)


def second_ends(
    size_x, size_y, size_z, count, entries, ends, middle, solid, messages, place, numbers, later, p
):
    walls = walls_of(count)
    blocks = relax_blocks(entries)
    x = place * (size_x - 1)
    for tile in range(size_y // 8 + 1):
        rows = slice(8 * tile, 8 * tile + 8)
        h = [
            streamed(ends, middle, messages, i, x, tile, size_x, size_y, size_z, walls) for i in range(19)
        ]
        for part in range(size_z // 128):
            lanes = slice(128 * part, 128 * part + 128)
            s = solid(rows, lanes)
            out = collide([v[:, lanes] for v in h], *s, blocks)
            for k, i in enumerate(numbers):
                store_padded(later, k, p, tile, part, out[i], size_y // 8)


def second_leaving_kernel(size_x, size_y, size_z, count, far, entries, ends, middle, solid, received, *refs):
    message, leaving = refs[-2:]

    def work(place, numbers):
        second_ends(
            size_x,
            size_y,
            size_z,
            count,
            entries,
            ends,
            middle,
            lambda rows, lanes: [solid[c, 0, rows, lanes] for c in range(4)],
            (received,),
            place,
            numbers,
            leaving,
            0,
        )
        write_face(leaving, message, numbers, size_y, size_z, False)

    by_plane(work, far)


def second_ends_kernel(
    size_x, size_y, size_z, count, entries, ends, middle, solid_far, solid_near, far, near, later
):
    for place in range(2):
        second_ends(
            size_x,
            size_y,
            size_z,
            count,
            entries,
            ends,
            middle,
            lambda rows, lanes: plane_solid(solid_far, solid_near, place, rows, lanes),
            (near, far),
            place,
            range(19),
            later,
            place,
        )


def last_kernel(size_x, size_y, size_z, count, ends, middle, advanced, held, done):
    walls = walls_of(count)
    copies = []
    for i in range(19):
        for x in range(size_x):
            if not 0 <= x - VEC[i][0] < size_x:
                continue
            for tile in range(size_y // 8):
                held[i, x, 8 * tile : 8 * tile + 8, :] = streamed(
                    ends, middle, None, i, x, tile, size_x, size_y, size_z, walls
                )
        low, high = max(0, VEC[i][0]), size_x + min(0, VEC[i][0])
        copy = pltpu.make_async_copy(
            held.at[i, low:high], advanced.at[i, low:high], done.at[i]
        )
        copy.start()
        copies.append(copy)
    for copy in copies:
        copy.wait()


def entering(size_x, size_y, size_z, count, ends, received, place, k, target):
    numbers = BACKWARD if place else FORWARD
    walls = walls_of(count)
    for tile in range(size_y // 8):
        target[k, 8 * tile : 8 * tile + 8, :] = streamed(
            ends, None, (received,), numbers[k], place * (size_x - 1), tile, size_x, size_y, size_z, walls
        )


def far_kernel(size_x, size_y, size_z, count, ends, received, held):
    def work(place, numbers):
        del numbers
        for k in range(5):
            entering(size_x, size_y, size_z, count, ends, received, place, k, held)

    by_plane(work, True)


def enter_kernel(size_x, size_y, size_z, count, ends, received, far, given, advanced, near, done):
    del given

    def write(place, held, base):
        numbers = BACKWARD if place else FORWARD
        for k, i in enumerate(numbers):
            copy = pltpu.make_async_copy(held.at[k], advanced.at[i, place * (size_x - 1)], done.at[base + k])
            copy.start()

    def work(place, numbers):
        del numbers
        write(1 - place, far, 0)
        for k in range(5):
            entering(size_x, size_y, size_z, count, ends, received, place, k, near)
        write(place, near, 5)

    by_plane(work, False)
    for k in range(5):
        pltpu.make_async_copy(far.at[k], advanced.at[FORWARD[k], 0], done.at[k]).wait()
        pltpu.make_async_copy(near.at[k], advanced.at[FORWARD[k], 0], done.at[5 + k]).wait()


def shape(*sizes):
    return jax.ShapeDtypeStruct(sizes, F32)


VMEM = pl.BlockSpec(memory_space=pltpu.VMEM)
SMEM = pl.BlockSpec(memory_space=pltpu.SMEM)
HBM = pl.BlockSpec(memory_space=pltpu.HBM)


def call(kernel, out_shape, limit, in_specs, out_specs=None, scratch=(), aliases=None):
    return pl.pallas_call(
        kernel,
        out_shape=out_shape,
        in_specs=in_specs,
        out_specs=jax.tree.map(lambda _: VMEM, out_shape) if out_specs is None else out_specs,
        scratch_shapes=scratch,
        input_output_aliases={} if aliases is None else aliases,
        compiler_params=pltpu.CompilerParams(vmem_limit_bytes=limit * 2**20),
    )


def in_hbm(value):
    return pltpu.with_memory_space_constraint(value, pltpu.HBM)


def around(value, axis, steps):
    count = lax.axis_size(axis)
    return lax.ppermute(value, axis, [(i, (i + steps) % count) for i in range(count)])


def paired_x(value, parity):
    count = lax.axis_size("gx")
    if count % 2:
        raise ValueError("odd ring")
    pairs = [(i, (i + 1 if i % 2 == parity else i - 1) % count) for i in range(count)]
    return lax.ppermute(value, "gx", pairs)


def paired_y(value, parity):
    count_x, count = lax.axis_size("gx"), lax.axis_size("gy")
    pairs = []
    for i in range(count_x):
        for j in range(count):
            other = j + 1 if j % 2 == parity else j - 1
            to = i * count + other if 0 <= other < count else (i ^ 1) * count + j
            pairs.append((i * count + j, to))
    return lax.ppermute(value, ("gx", "gy"), pairs)


def exchanged(near, far):
    far = paired_x(far, 1)
    return paired_x(near, 0), far


def local(populations, relax_rates, velocity, velocity_change, fractions, anchor, destination):
    _, size_x, size_y, size_z = populations.shape
    count = lax.axis_size("gy")
    rows = anchor.shape[0]
    sizes = (size_x, size_y, size_z)
    part = functools.partial
    packed = shape(8, 128)
    band = shape(19, size_x, 8, size_z)
    table, own, near, far, bottom, top = call(
        pack_kernel,
        (shape(32, rows), packed, packed, packed, band, band),
        8,
        [HBM] * 6,
        scratch=[
            pltpu.VMEM((3, rows), F32),
            pltpu.VMEM((3, rows), F32),
            pltpu.VMEM((27, rows), F32),
            pltpu.VMEM((1, rows), I32),
            pltpu.VMEM((1, rows), I32),
            pltpu.SemaphoreType.DMA((7,)),
        ],
    )(*map(in_hbm, (velocity, velocity_change, fractions, anchor[None, :], destination[None, :], populations)))
    near, far = exchanged(near, far)
    first = edge_rows(size_x)[-1]
    fold = size_z // 128
    message = shape(-(-(first + 8 // fold) // 8) * 8, size_z)
    entries = call(relax_kernel, shape(ENTRIES, 8, 128), 8, [VMEM])(relax_rates[None, :])
    one, two = call(
        part(edge_kernel, *sizes),
        (message, message),
        8,
        [VMEM] * 4,
        scratch=[pltpu.VMEM((19, 2 * size_x, size_z), F32)],
    )(bottom, top, table, entries)
    two = paired_y(two, 1)
    column, one = call(
        part(merge_kernel, first, fold),
        (shape(8, 128), message),
        8,
        [VMEM] * 4,
        aliases={3: 1},
    )(own, far, near, one)
    shifts = []
    for shift in (2, -2):
        if shift % count > 1 and all((shift - other) % count for other in shifts):
            shifts.append(shift)
    rest = [around(column, "gy", shift) for shift in shifts]
    one, column_two = paired_y(one, 0), paired_y(column, 1)
    unused = pl.BlockSpec(memory_space=pl.ANY)
    outside, inside = (0, size_x - 1), tuple(range(1, size_x - 1))

    def staying(planes, after):
        return call(
            part(stay_kernel, *sizes, planes),
            shape(4, len(planes), size_y, size_z),
            16,
            [VMEM, unused],
        )(table, after)

    sums = staying(outside, two)
    plane_pair = shape(19, 2, size_y, size_z)
    parts = call(
        part(fluid_kernel, *sizes), (plane_pair, plane_pair, shape(2, size_y, size_z)), 16, [VMEM] * 2
    )(entries, populations)
    width = -(-(3 + len(shifts)) * LANES // 128) * 128
    def outer_shapes(planes):
        return tuple(shape(k, len(planes), 8, size_z) for k in (4, 19, 11))

    outer_sums, outer, second, migrants = call(
        part(outer_kernel, *sizes, count, shifts, outside),
        outer_shapes(outside) + (shape(40, width),),
        8,
        [VMEM] * (4 + len(shifts)),
    )(column, one, column_two, *rest, two)

    def padded(planes):
        return shape(19, planes, size_y + 24, size_z)

    def solid_shape(planes):
        return shape(4, planes, size_y + 8, size_z)

    sent = pltpu.VMEM((5, 1, size_y + 24, size_z), F32)
    wide_face = shape((5 * size_y + 10 + 7) // 8 * 8, size_z)
    face = shape(5 * size_y, size_z)

    def leaving(far, *given):
        return call(
            part(leaving_kernel, *sizes, far),
            (solid_shape(1), wide_face),
            16,
            [VMEM] * 9 + [unused] * (len(given) - 9),
            scratch=[sent],
        )(*given)

    known = (entries, sums, outer_sums, outer, second, migrants, *parts)
    solid_far, far = leaving(True, *known)
    solid_near, near = leaving(False, *known, solid_far)
    near, far = exchanged(near, far)
    inner = call(part(outer_kernel, *sizes, count, shifts, inside), outer_shapes(inside), 8, [VMEM] * 2)(
        two, one
    )
    middle, solid_middle = call(
        part(middle_kernel, *sizes, inside),
        (padded(len(inside)), solid_shape(len(inside))),
        16,
        [VMEM] * 7,
    )(entries, staying(inside, solid_near), *inner, migrants, populations)
    ends = call(part(ends_kernel, *sizes), padded(2), 16, [VMEM] * 8)(
        entries, outer, second, *parts, solid_far, solid_near
    )
    later_middle = call(part(second_kernel, *sizes, count), padded(len(inside)), 16, [VMEM] * 4)(
        entries, ends, middle, solid_middle
    )

    def second_leaving(far, *given):
        return call(
            part(second_leaving_kernel, *sizes, count, far),
            face,
            16,
            [VMEM] * 5 + [unused] * (len(given) - 5),
            scratch=[sent],
        )(*given)

    received = (far, near)
    far = second_leaving(True, entries, ends, middle, solid_far, far, later_middle)
    near = second_leaving(False, entries, ends, middle, solid_near, near, far)
    near, far = exchanged(near, far)
    later_ends = call(part(second_ends_kernel, *sizes, count), padded(2), 16, [VMEM] * 7)(
        entries, ends, middle, solid_far, solid_near, *received
    )
    advanced = call(
        part(last_kernel, *sizes, count),
        shape(19, *sizes),
        16,
        [VMEM] * 2,
        HBM,
        [pltpu.VMEM((19, *sizes), F32), pltpu.SemaphoreType.DMA((19,))],
    )(later_ends, later_middle)
    slabs = (5, size_y, size_z)
    far = call(part(far_kernel, *sizes, count), shape(*slabs), 16, [VMEM] * 2)(later_ends, far)
    return call(
        part(enter_kernel, *sizes, count),
        shape(19, *sizes),
        16,
        [VMEM] * 3 + [HBM],
        HBM,
        [pltpu.VMEM(slabs, F32), pltpu.SemaphoreType.DMA((10,))],
        {3: 0},
    )(later_ends, near, far, advanced)


def solution(mesh):
    placed = (
        P(None, "gx", "gy", None),
        P(),
        P(None, ("gx", "gy")),
        P(None, ("gx", "gy")),
        P(None, ("gx", "gy")),
        P(("gx", "gy")),
        P(("gx", "gy")),
    )
    return jax.shard_map(
        local, mesh=mesh, in_specs=placed, out_specs=P(None, "gx", "gy", None), check_vma=False
    )
```

```python
import functools

import jax
import jax.numpy as jnp
import numpy as np
from jax import lax
from jax.experimental import pallas as pl
from jax.experimental.pallas import tpu as pltpu
from jax.sharding import PartitionSpec as P

CAP = 4
STEPS = 2
LANES = 8 * CAP
F32 = jnp.float32
BF16 = jnp.bfloat16
I32 = jnp.int32


def lattice():
    vectors = [[0, 0, 0]]
    for axis_one in range(3):
        for orient in (1, -1):
            vector_one = [0, 0, 0]
            vector_one[axis_one] = orient
            vectors.append(vector_one)
    for axis_one, axis_two in ((0, 1), (0, 2), (1, 2)):
        for orient in (1, -1):
            for second in (1, -1):
                vector_one = [0, 0, 0]
                vector_one[axis_one] = orient
                vector_one[axis_two] = second
                vectors.append(vector_one)
    integral = np.array(vectors)
    speeds = integral * 1.0
    length = (speeds**2).sum(axis=1)
    weights = np.where(length == 0, 1.0 / 3.0, np.where(length == 1, 1.0 / 18.0, 1.0 / 36.0))
    opposite = [vectors.index([0 - component for component in vector_one]) for vector_one in vectors]
    along_x, along_y, along_z = (speeds[:, 0], speeds[:, 1], speeds[:, 2])
    rows_list = [
        np.ones(19),
        along_x,
        along_y,
        along_z,
        length,
        3 * along_x**2 - length,
        along_y**2 - along_z**2,
        along_x * along_y,
        along_y * along_z,
        along_x * along_z,
        along_x * length,
        along_y * length,
        along_z * length,
        along_x * (along_y**2 - along_z**2),
        along_y * (along_z**2 - along_x**2),
        along_z * (along_x**2 - along_y**2),
        length**2,
        (3 * along_x**2 - length) * length,
        (along_y**2 - along_z**2) * length,
    ]
    basis_rows = []
    for candidate in rows_list:
        for earlier in basis_rows:
            candidate = candidate - np.dot(candidate, earlier) * earlier
        basis_rows.append(candidate / np.sqrt(np.dot(candidate, candidate)))
    return [tuple(v) for v in vectors], weights, opposite, np.array(basis_rows)


VEC, WEIGHTS, OPP, BASIS = lattice()
FORWARD = [i for i in range(19) if VEC[i][0] == 1]
BACKWARD = [i for i in range(19) if VEC[i][0] == -1]
DOWNWARD = [i for i in range(19) if VEC[i][1] == -1]
UPWARD = [OPP[i] for i in DOWNWARD]


def symmetric_blocks():
    def vec(entries):
        out = np.zeros(19)
        for index, value in entries.items():
            out[index] = value
        return out

    def plane(base):
        s_one, d_one = vec({base: 1, base + 3: 1}), vec({base: 1, base + 3: -1})
        s_two, d_two = vec({base + 1: 1, base + 2: 1}), vec({base + 1: 1, base + 2: -1})
        return s_one + s_two, s_one - s_two, d_one + d_two, d_one - d_two

    rest = vec({0: 1})
    s_x, s_y, s_z = vec({1: 1, 2: 1}), vec({3: 1, 4: 1}), vec({5: 1, 6: 1})
    d_x, d_y, d_z = vec({1: 1, 2: -1}), vec({3: 1, 4: -1}), vec({5: 1, 6: -1})
    xy, q_xy, x_xy, y_xy = plane(7)
    xz, q_xz, x_xz, z_xz = plane(11)
    yz, q_yz, y_yz, z_yz = plane(15)
    blocks = [
        [rest, s_x + s_y + s_z, xy + xz + yz],
        [2 * s_x - s_y - s_z, xy + xz - 2 * yz],
        [s_y - s_z, xy - xz],
        [q_xy],
        [q_xz],
        [q_yz],
        [d_x, x_xy, x_xz],
        [d_y, y_xy, y_yz],
        [d_z, z_xz, z_yz],
    ]
    scales = [[1, 1 / 6, 1 / 12], [1 / 12, 1 / 24], [1 / 4, 1 / 8]]
    scales += [[1 / 4]] * 3 + [[1 / 2, 1 / 4, 1 / 4]] * 3
    forward = np.array([row for block in blocks for row in block])
    back = np.linalg.inv(forward)
    left = forward @ np.diag(1.0 / WEIGHTS) @ BASIS.T
    right = BASIS @ np.diag(WEIGHTS) @ back
    table = []
    start = 0
    for block, scale in zip(blocks, scales):
        size = len(block)
        rows = []
        for a in range(size):
            row = []
            for b in range(size):
                per_rate = -scale[a] * left[start + a, :] * right[:, start + b]
                row.append([(k, float(v)) for k, v in enumerate(per_rate) if abs(v) > 1e-12])
            rows.append(row)
        table.append(rows)
        start += size
    return table


RELAX = symmetric_blocks()


def relax_rows(rates, target):
    values = [rates[k] for k in range(19)]
    at = 0
    for block in RELAX:
        for row in block:
            for terms in row:
                total = None
                for k, factor in terms:
                    part = values[k] * np.float32(factor)
                    total = part if total is None else total + part
                target[at] = jnp.full((8, 128), total, F32)
                at += 1


def relax_blocks(table, lanes=128):
    blocks, at = [], 0
    for block in RELAX:
        rows = []
        for row in block:
            rows.append(
                [jnp.concatenate([table[at + k]] * (lanes // 128), axis=1) for k in range(len(row))]
            )
            at += len(row)
        blocks.append(rows)
    return blocks


ENTRIES = sum(len(row) for block in RELAX for row in block)


def apply_block(block, values):
    out = []
    for row in block:
        total = None
        for factor, value in zip(row, values):
            part = factor * value
            total = part if total is None else total + part
        out.append(total)
    return out


def collide(h, solid, s_x, s_y, s_z, blocks):
    def plane(base):
        s_one, d_one = h[base] + h[base + 3], h[base] - h[base + 3]
        s_two, d_two = h[base + 1] + h[base + 2], h[base + 1] - h[base + 2]
        return s_one + s_two, s_one - s_two, d_one + d_two, d_one - d_two

    sum_x, dif_x = h[1] + h[2], h[1] - h[2]
    sum_y, dif_y = h[3] + h[4], h[3] - h[4]
    sum_z, dif_z = h[5] + h[6], h[5] - h[6]
    xy, q_xy, x_xy, y_xy = plane(7)
    xz, q_xz, x_xz, z_xz = plane(11)
    yz, q_yz, y_yz, z_yz = plane(15)
    axes = sum_x + sum_y + sum_z
    edges = xy + xz + yz
    density = h[0] * (1.0 / 3.0) + axes * (1.0 / 18.0) + edges * (1.0 / 36.0)
    m_x = dif_x * (1.0 / 18.0) + (x_xy + x_xz) * (1.0 / 36.0)
    m_y = dif_y * (1.0 / 18.0) + (y_xy + y_yz) * (1.0 / 36.0)
    m_z = dif_z * (1.0 / 18.0) + (z_xz + z_yz) * (1.0 / 36.0)
    inverse = 1.0 / density
    u_x, u_y, u_z = m_x * inverse, m_y * inverse, m_z * inverse
    e_xx, e_yy, e_zz = m_x * u_x, m_y * u_y, m_z * u_z
    e_xy, e_xz, e_yz = m_x * u_y, m_x * u_z, m_y * u_z
    energy = e_xx + e_yy + e_zz
    turn = e_yy - e_zz
    lean = 3.0 * e_xx - energy
    rest_off = h[0] - density + 1.5 * energy
    axes_off = axes - 6.0 * density
    edges_off = edges - 12.0 * density - 18.0 * energy
    a_one = 3.0 * sum_x - axes - 9.0 * lean
    b_one = edges - 3.0 * yz - 18.0 * lean
    a_two = sum_y - sum_z - 9.0 * turn
    b_two = xy - xz - 18.0 * turn
    q_xy = q_xy - 36.0 * e_xy
    q_xz = q_xz - 36.0 * e_xz
    q_yz = q_yz - 36.0 * e_yz

    r_rest, r_axes, r_edges = apply_block(blocks[0], [rest_off, axes_off, edges_off])
    r_a_one, r_b_one = apply_block(blocks[1], [a_one, b_one])
    r_a_two, r_b_two = apply_block(blocks[2], [a_two, b_two])
    fluid = 1.0 - solid
    mixed = solid * density
    w_x, w_y, w_z = solid * m_x, solid * m_y, solid * m_z
    n_x, n_y, n_z = mixed * s_x, mixed * s_y, mixed * s_z
    p_x = n_x * s_x - solid * e_xx
    p_y = n_y * s_y - solid * e_yy
    p_z = n_z * s_z - solid * e_zz
    total = 1.5 * (p_x + p_y + p_z)
    lean_s = 2.25 * p_x - 0.5 * total
    turn_s = 2.25 * (p_y - p_z)
    rest = fluid * r_rest - total
    axes = fluid * r_axes
    edges = fluid * r_edges + total
    a_one = fluid * r_a_one + lean_s
    b_one = fluid * r_b_one + lean_s
    a_two = fluid * r_a_two + turn_s
    b_two = fluid * r_b_two + turn_s
    q_xy = fluid * apply_block(blocks[3], [q_xy])[0] + 9.0 * (n_x * s_y - solid * e_xy)
    q_xz = fluid * apply_block(blocks[4], [q_xz])[0] + 9.0 * (n_x * s_z - solid * e_xz)
    q_yz = fluid * apply_block(blocks[5], [q_yz])[0] + 9.0 * (n_y * s_z - solid * e_yz)

    def odd(block, axis, one, two, m, n, w):
        six = 6.0 * m
        axis = axis - six
        twelve = six + six
        one = one - twelve
        two = two - twelve
        r_axis, r_one, r_two = apply_block(block, [axis, one, two])
        push = 3.0 * (n - w)
        half = 0.5 * solid
        return (
            fluid * r_axis - solid * axis + push,
            fluid * r_one - half * one + push,
            fluid * r_two - half * two + push,
        )

    d_x, x_xy, x_xz = odd(blocks[6], dif_x, x_xy, x_xz, m_x, n_x, w_x)
    d_y, y_xy, y_yz = odd(blocks[7], dif_y, y_xy, y_yz, m_y, n_y, w_y)
    d_z, z_xz, z_yz = odd(blocks[8], dif_z, z_xz, z_yz, m_z, n_z, w_z)
    out = [None] * 19
    out[0] = h[0] + rest
    even = axes + 2.0 * a_one
    out[1], out[2] = h[1] + (even + d_x), h[2] + (even - d_x)
    base = axes - a_one
    even = base + a_two
    out[3], out[4] = h[3] + (even + d_y), h[4] + (even - d_y)
    even = base - a_two
    out[5], out[6] = h[5] + (even + d_z), h[6] + (even - d_z)

    def spread(start, even, twist, one, two):
        same, cross = even + twist, even - twist
        plus, minus = one + two, one - two
        out[start] = h[start] + (same + plus)
        out[start + 3] = h[start + 3] + (same - plus)
        out[start + 1] = h[start + 1] + (cross + minus)
        out[start + 2] = h[start + 2] + (cross - minus)

    base = edges + b_one
    spread(7, base + b_two, q_xy, x_xy, y_xy)
    spread(11, base - b_two, q_xz, x_xz, z_xz)
    spread(15, edges - 2.0 * b_one, q_yz, y_yz, z_yz)
    return out


def equilibrium(density, flow, numbers):
    v_x, v_y, v_z = flow
    rest = 1.0 - 1.5 * (v_x * v_x + v_y * v_y + v_z * v_z)
    out = {}
    for i in numbers:
        if i in out:
            continue
        along = None
        for sign, v in zip(VEC[i], flow):
            if sign:
                part = v if sign == 1 else -v
                along = part if along is None else along + part
        if along is None:
            out[i] = rest
        else:
            along = 3.0 * along
            even = rest + 0.5 * along * along
            out[i], out[OPP[i]] = even + along, even - along
    return out


def fluid_parts(h, blocks, numbers):
    zero = jnp.zeros_like(h[0])
    relaxed = collide(h, zero, zero, zero, zero, blocks)
    density, flow = zero, [zero, zero, zero]
    for i in range(19):
        part = np.float32(WEIGHTS[i]) * h[i]
        density = density + part
        for k in range(3):
            if VEC[i][k]:
                flow[k] = flow[k] + part if VEC[i][k] == 1 else flow[k] - part
    inverse = 1.0 / density
    still = equilibrium(density, [f * inverse for f in flow], numbers)
    bounced = [h[OPP[i]] - density * still[OPP[i]] for i in numbers]
    return [relaxed[i] for i in numbers], bounced, density


def blended(relaxed, bounced, density, share, still):
    return relaxed + share * ((bounced + density * still) - relaxed)


def iota(shape, dim):
    return lax.broadcasted_iota(I32, shape, dim)


def cells_of(anchor, size_y, size_z):
    plane = size_y * size_z
    a_x = lax.div(anchor, jnp.int32(plane))
    rest = anchor - a_x * plane
    a_y = lax.div(rest, jnp.int32(size_z))
    return a_x, a_y, rest - a_y * size_z


def halves(value):
    high = value.astype(BF16)
    return high, (value - high.astype(F32)).astype(BF16)


def dot_t(left, right):
    return lax.dot_general(left, right, (((1,), (1,)), ((), ())), preferred_element_type=F32)


def deposited(groups, shares, velocity, a_x, a_y, a_z, size_z, big):
    centre = a_x * big + a_y
    lanes = centre.shape[1]
    totals = None
    rows_z = iota((size_z, lanes), 0)
    for off_z in range(3):
        weights = []
        for rows_x, rows_y in groups:
            away = rows_x * big + rows_y - centre
            weight = jnp.zeros(away.shape, F32)
            for off in range(9):
                move = (off // 3 - 1) * big + off % 3 - 1
                row = 3 * off + off_z
                weight = jnp.where(away == move, shares[row : row + 1, :], weight)
            weights.append([weight] + [weight * velocity[k : k + 1, :] for k in range(3)])
        rows = jnp.concatenate([w for block in weights for w in block], axis=0)
        high, low = halves(rows)
        hot = jnp.where(rows_z == a_z + (off_z - 1), 1.0, 0.0).astype(BF16)
        both = dot_t(jnp.concatenate([high, low], axis=0), hot)
        part = both[: rows.shape[0]] + both[rows.shape[0] :]
        totals = part if totals is None else totals + part
    return totals


def even_x():
    return lax.rem(lax.axis_index("gx"), 2) == 0


def pack_kernel(
    velocity_in,
    change_in,
    fractions_in,
    anchor_in,
    destination_in,
    populations,
    table,
    own,
    near,
    far,
    bottom,
    top,
    velocity,
    change,
    fractions,
    anchor,
    destination,
    done,
):
    pairs = (
        (destination_in, destination),
        (velocity_in, velocity),
        (change_in, change),
        (fractions_in, fractions),
        (anchor_in, anchor),
        (populations.at[:, :, 0:8, :], bottom),
        (populations.at[:, :, populations.shape[2] - 8 :, :], top),
    )
    copies = [pltpu.make_async_copy(a, b, done.at[k]) for k, (a, b) in enumerate(pairs)]
    for copy in copies:
        copy.start()
    rows = destination.shape[1]
    order = jnp.where(iota((128, 128), 0) <= iota((128, 128), 1), 1.0, 0.0).astype(BF16)
    for copy in copies[:5]:
        copy.wait()
    dest = destination[...]
    kinds = iota((16, rows), 0)
    hot = jnp.where(dest == kinds, 1.0, 0.0)
    seen = jnp.zeros((16, 1), F32)
    ranks = []
    for start in range(0, rows, 128):
        counted = seen + lax.dot_general(
            hot[:, start : start + 128].astype(BF16),
            order,
            (((1,), (0,)), ((), ())),
            preferred_element_type=F32,
        )
        ranks.append(counted)
        seen = counted[:, 127:128]
    rank = jnp.concatenate(ranks, axis=1)
    kind = iota((16, 1), 0)
    begin = jnp.where(
        kind < 3,
        5 * CAP + CAP * kind,
        jnp.where(kind == 3, 0, jnp.where(kind == 5, CAP, 2 * CAP + CAP * (kind - 6))),
    ).astype(F32)
    leaving = (dest < 9) & (dest != 4)
    slot = jnp.sum(hot * (begin + rank - 1.0), axis=0, keepdims=True)
    slot = jnp.where(leaving, slot, -1.0).astype(I32)
    chosen = jnp.where(iota((LANES, rows), 0) == slot, 1.0, 0.0).astype(BF16)
    chosen = jnp.concatenate([chosen, jnp.zeros((128 - LANES, rows), BF16)], axis=0)
    new_velocity = velocity[...] + change[...]
    payload = jnp.concatenate(
        [fractions[...], new_velocity, anchor[...].astype(F32), jnp.zeros((1, rows), F32)], axis=0
    )
    high = payload.astype(BF16)
    middle, low = halves(payload - high.astype(F32))
    pieces = dot_t(jnp.concatenate([high, middle, low], axis=0), chosen)
    packed = pieces[0:32] + pieces[32:64] + pieces[64:96]
    packed = folded(packed)
    lane = lax.rem(iota((8, 128), 1), jnp.int32(LANES))
    own[...] = jnp.where(lane < 2 * CAP, packed, 0.0)
    ahead = jnp.where((lane >= 2 * CAP) & (lane < 5 * CAP), packed, 0.0)
    behind = jnp.where(lane >= 5 * CAP, packed, 0.0)
    even = even_x()
    near[...] = jnp.where(even, ahead, behind)
    far[...] = jnp.where(even, behind, ahead)
    table[...] = jnp.where((iota((32, rows), 0) < 27) & (dest != 4), 0.0, payload)
    for copy in copies[5:]:
        copy.wait()


def edge_rows(size_x):
    starts = [0]
    for rows in (19 * size_x, 4 * 2 * size_x, 11 * size_x):
        starts.append(starts[-1] + rows)
    return starts


def edge_kernel(size_x, size_y, size_z, bottom, top, table, entries, one, two, held):
    a_x, a_y, a_z = cells_of(table[30:31, :].astype(I32), size_y, size_z)
    rows = 2 * size_x
    index = iota((rows, 1), 0)
    rows_x, low = lax.div(index, jnp.int32(2)), lax.rem(index, jnp.int32(2))
    sums = deposited(
        [(rows_x, low), (rows_x, low + (size_y - 2))],
        table[0:27, :],
        table[27:30, :],
        a_x,
        a_y,
        a_z,
        size_z,
        8 * size_y,
    )
    _, at_sums, at_second, _ = edge_rows(size_x)
    for i in range(19):
        for x in range(size_x):
            held[i, x : x + 1, :] = bottom[i, x, 1:2, :]
            held[i, size_x + x : size_x + x + 1, :] = top[i, x, 6:7, :]
    second = fluid_parts([held[i] for i in range(19)], relax_blocks(entries, size_z), DOWNWARD + UPWARD)
    relaxed, bounced, density = second

    def write(down, up):
        for i in range(19):
            for x in range(size_x):
                at = i * size_x + x
                down[at : at + 1, :] = bottom[i, x, 0:1, :]
                up[at : at + 1, :] = top[i, x, 7:8, :]
        down[at_sums : at_sums + 4 * rows, :] = sums[: 4 * rows]
        up[at_sums : at_sums + 4 * rows, :] = sums[4 * rows :]
        for target, own, at_row in ((down, 0, 0), (up, 5, size_x)):
            parts = relaxed[own : own + 5] + bounced[own : own + 5] + [density]
            for k, value in enumerate(parts):
                at = at_second + k * size_x
                target[at : at + size_x, :] = value[at_row : at_row + size_x]

    even = lax.rem(lax.axis_index("gy"), 2) == 0

    @pl.when(even)
    def _():
        write(two, one)

    @pl.when(jnp.logical_not(even))
    def _():
        write(one, two)


def folded(table):
    return sum(
        table[8 * k : 8 * k + 8] if k == 0 else pltpu.roll(table[8 * k : 8 * k + 8], LANES * k, 1)
        for k in range(4)
    )


def merge_kernel(first, fold, own, far, near, one_in, column, one):
    del one_in
    merged = own[...] + near[...] + far[...]
    column[...] = merged
    deep = 8 // fold
    for k in range(fold):
        one[first : first + deep, 128 * k : 128 * k + 128] = merged[deep * k : deep * k + deep]


def relax_kernel(rates, entries):
    relax_rows(rates, entries)


def fluid_kernel(size_x, size_y, size_z, entries, populations, relaxed, bounced, density):
    blocks = relax_blocks(entries)
    for p, x in enumerate((0, size_x - 1)):
        for tile in range(size_y // 8):
            rows = slice(8 * tile, 8 * tile + 8)
            for part in range(size_z // 128):
                lanes = slice(128 * part, 128 * part + 128)
                f, b, d = fluid_parts([populations[i, x, rows, lanes] for i in range(19)], blocks, range(19))
                for i in range(19):
                    relaxed[i, p, rows, lanes] = f[i]
                    bounced[i, p, rows, lanes] = b[i]
                density[p, rows, lanes] = d


def stay_kernel(size_x, size_y, size_z, planes, table, after, sums):
    del after
    a_x, a_y, a_z = cells_of(table[30:31, :].astype(I32), size_y, size_z)
    index = iota((len(planes) * size_y, 1), 0)
    number = lax.div(index, jnp.int32(size_y))
    rows_x = number * (size_x - 1) if planes[0] == 0 else number + planes[0]
    totals = deposited(
        [(rows_x, index - number * size_y)],
        table[0:27, :],
        table[27:30, :],
        a_x,
        a_y,
        a_z,
        size_z,
        8 * size_y,
    )
    cells = len(planes) * size_y
    for c in range(4):
        for p in range(len(planes)):
            at = c * cells + p * size_y
            sums[c, p, :, :] = totals[at : at + size_y]


def outer_kernel(size_x, size_y, size_z, count, shifts, planes, *refs):
    if planes[0] == 0:
        column, one, column_two, *rest = refs[: 3 + len(shifts)]
        two, sums, outer, second, migrants = refs[3 + len(shifts) :]
        arrivals(size_x, size_y, size_z, count, shifts, column, one, column_two, rest, migrants)
    else:
        two, one, sums, outer, second = refs
    blank = jnp.zeros((8, size_z), F32)
    ones = jnp.ones((8, size_z), F32)
    _, at_sums, at_second, _ = edge_rows(size_x)

    def write(above, below):
        for p, x in enumerate(planes):
            for c in range(4):
                at = at_sums + c * 2 * size_x + 2 * x
                sums[c, p, :, :] = blank
                sums[c, p, 0:2, :] = above[at : at + 2, :]
                sums[c, p, 6:8, :] = below[at : at + 2, :]
            for i in range(19):
                at = i * size_x + x
                outer[i, p, :, :] = ones
                outer[i, p, 0:1, :] = above[at : at + 1, :]
                outer[i, p, 7:8, :] = below[at : at + 1, :]
            for k in range(11):
                at = at_second + k * size_x + x
                second[k, p, :, :] = ones
                second[k, p, 1:2, :] = above[at : at + 1, :]
                second[k, p, 6:7, :] = below[at : at + 1, :]

    even = lax.rem(lax.axis_index("gy"), 2) == 0

    @pl.when(even)
    def _():
        write(one, two)

    @pl.when(jnp.logical_not(even))
    def _():
        write(two, one)


def pair_source(here, parity, count):
    other = jnp.where(lax.rem(here, 2) == parity, here + 1, here - 1)
    return jnp.where((other >= 0) & (other < count), other, here + 2 * count)


def arrivals(size_x, size_y, size_z, count, shifts, column, one, two, rest, migrants):
    first = edge_rows(size_x)[-1]
    here = lax.axis_index("gy")
    fold = size_z // 128
    deep = 8 // fold

    def gathered(message):
        return jnp.concatenate(
            [message[first : first + deep, 128 * k : 128 * k + 128] for k in range(fold)], axis=0
        )

    parts = [column[...], gathered(one), two[...]] + [r[...] for r in rest]
    sources = [here, pair_source(here, 0, count), pair_source(here, 1, count)]
    sources += [lax.rem(here - shift + 2 * count, count) for shift in shifts]
    lane = iota((1, 128), 1)
    spot = lax.rem(lane, jnp.int32(LANES))
    group = lax.div(spot, jnp.int32(CAP))
    across = jnp.where(
        (group == 0) | (group == 2) | (group == 5), -1, jnp.where((group == 3) | (group == 6), 0, 1)
    )
    per_group = 128 // LANES
    tables, offsets = [], []
    for start in range(0, len(parts), per_group):
        blocks = [jnp.zeros((8, 128), F32)] * 4
        offset = jnp.full((1, 128), 2 * count, I32)
        for k, part in enumerate(parts[start : start + per_group]):
            place = lax.div(lane, jnp.int32(LANES)) == k
            for q in range(4):
                turn = LANES * (k - q) % 128
                blocks[q] = jnp.where(place, part if turn == 0 else pltpu.roll(part, turn, 1), blocks[q])
            offset = jnp.where(lax.div(lane, jnp.int32(LANES)) == k, sources[start + k] - here, offset)
        tables.append(jnp.concatenate(blocks, axis=0))
        offsets.append((offset + across) * size_y)
    table = jnp.concatenate(tables, axis=1)
    a_x, a_y, a_z = cells_of(table[30:31, :].astype(I32), size_y, size_z)
    migrants[0:32, :] = table
    migrants[32:33, :] = a_x.astype(F32)
    migrants[33:34, :] = (a_y + jnp.concatenate(offsets, axis=1)).astype(F32)
    migrants[34:35, :] = a_z.astype(F32)


def store_padded(target, i, x, tile, part, value, tiles):
    lanes = slice(128 * part, 128 * part + 128)
    if tile == tiles:
        target[i, x, 0:8, lanes] = value
        target[i, x, 8 + 8 * tiles : 16 + 8 * tiles, lanes] = value
    else:
        target[i, x, 8 + 8 * tile : 16 + 8 * tile, lanes] = value
        if tile == 0:
            target[i, x, 16 + 8 * tiles : 24 + 8 * tiles, lanes] = value


def turned(value, shift, size_z):
    return value if shift == 0 else pltpu.roll(value, shift % size_z, 1)


def solids(size_x, size_y, size_z, planes, first, sums, outer_sums, migrants, solid):
    a_x, a_y, a_z = (migrants[k : k + 1, :].astype(I32) for k in (32, 33, 34))
    wide = size_y + 8
    index = iota((len(planes) * wide, 1), 0)
    number = lax.div(index, jnp.int32(wide))
    row = index - number * wide
    rows_y = jnp.where(row < size_y + 2, row, jnp.where(row >= size_y + 6, row - wide, -3 * size_y))
    big = 4 * size_y * (lax.axis_size("gy") + 2)
    totals = deposited(
        [(number + planes[0], rows_y)], migrants[0:27, :], migrants[27:30, :], a_x, a_y, a_z, size_z, big
    )
    cells = len(planes) * wide
    for p, x in enumerate(planes):
        parts = []
        for c in range(4):
            at = c * cells + p * wide
            solid_sum = jnp.concatenate([sums[c, first + p, :, :], outer_sums[c, first + p, :, :]], axis=0)
            parts.append(totals[at : at + wide] + solid_sum)
        scale = 1.0 / (parts[0] + 1e-06)
        solid[0, p, :, :] = jnp.minimum(parts[0], 1.0)
        for c in (1, 2, 3):
            solid[c, p, :, :] = parts[c] * scale


def outer_collision(solid, outer, second, blocks, p, lanes):
    share, *flow = solid
    out = collide([outer[i, p, :, lanes] for i in range(19)], share, *flow, blocks)
    line = iota((8, 128), 0)
    away = jnp.where(line < 4, 1.0, -1.0)
    still = equilibrium(None, [away * v for v in flow], DOWNWARD)
    density = second[10, p, :, lanes]
    for k, (i, j) in enumerate(zip(DOWNWARD, UPWARD)):
        value = blended(second[k, p, :, lanes], second[5 + k, p, :, lanes], density, share, still[i])
        out[i] = jnp.where(line == 1, value, out[i])
        out[j] = jnp.where(line == 6, value, out[j])
    return out


def prepared_collision(solid, relaxed, bounced, dense, p, rows, lanes, numbers):
    share, *flow = solid
    still = equilibrium(None, flow, numbers)
    density = dense[p, rows, lanes]
    return {
        i: blended(relaxed[i, p, rows, lanes], bounced[i, p, rows, lanes], density, share, still[i])
        for i in numbers
    }


def tile_parts(size_y, size_z):
    for tile in range(size_y // 8 + 1):
        for part in range(size_z // 128):
            yield tile, slice(8 * tile, 8 * tile + 8), part, slice(128 * part, 128 * part + 128)


def by_plane(work, far):
    even = even_x()

    @pl.when(even if far else jnp.logical_not(even))
    def _():
        work(0, BACKWARD)

    @pl.when(jnp.logical_not(even) if far else even)
    def _():
        work(1, FORWARD)


def leaving_kernel(
    size_x, size_y, size_z, far, entries, sums, outer_sums, outer, second, migrants, relaxed, bounced,
    dense, *refs
):
    solid, message, leaving = refs[-3:]
    tiles = size_y // 8

    def work(place, numbers):
        plane = place * (size_x - 1)
        solids(size_x, size_y, size_z, (plane,), place, sums, outer_sums, migrants, solid)
        blocks = relax_blocks(entries)
        for tile, rows, part, lanes in tile_parts(size_y, size_z):
            s = [solid[c, 0, rows, lanes] for c in range(4)]
            if tile == tiles:
                out = outer_collision(s, outer, second, blocks, place, lanes)
            else:
                out = prepared_collision(s, relaxed, bounced, dense, place, rows, lanes, numbers)
            for k, i in enumerate(numbers):
                store_padded(leaving, k, 0, tile, part, out[i], tiles)
        write_face(leaving, message, numbers, size_y, size_z, True)

    by_plane(work, far)


def plane_solid(far, near, place, rows, lanes):
    in_far = even_x() if place == 0 else jnp.logical_not(even_x())
    return [jnp.where(in_far, far[c, 0, rows, lanes], near[c, 0, rows, lanes]) for c in range(4)]


def ends_kernel(
    size_x, size_y, size_z, entries, outer, second, relaxed, bounced, dense, solid_far, solid_near, post
):
    tiles = size_y // 8
    blocks = relax_blocks(entries)
    for p in range(2):
        for tile, rows, part, lanes in tile_parts(size_y, size_z):
            s = plane_solid(solid_far, solid_near, p, rows, lanes)
            if tile == tiles:
                out = outer_collision(s, outer, second, blocks, p, lanes)
            else:
                out = prepared_collision(s, relaxed, bounced, dense, p, rows, lanes, range(19))
            for i in range(19):
                store_padded(post, i, p, tile, part, out[i], tiles)


def middle_kernel(
    size_x, size_y, size_z, planes, entries, sums, outer_sums, outer, second, migrants, populations,
    post, solid
):
    tiles = size_y // 8
    solids(size_x, size_y, size_z, planes, 0, sums, outer_sums, migrants, solid)
    blocks = relax_blocks(entries)
    for p, x in enumerate(planes):
        for tile, rows, part, lanes in tile_parts(size_y, size_z):
            share, *flow = (solid[c, p, rows, lanes] for c in range(4))
            if tile == tiles:
                out = outer_collision((share, *flow), outer, second, blocks, p, lanes)
            else:
                h = [populations[i, x, rows, lanes] for i in range(19)]
                out = collide(h, share, *flow, blocks)
            for i in range(19):
                store_padded(post, i, p, tile, part, out[i], tiles)


def write_face(post, message, numbers, size_y, size_z, outer):
    tiles = size_y // 8
    for k, i in enumerate(numbers):
        _, c_y, c_z = VEC[i]
        for tile in range(tiles):
            at = 8 + 8 * tile - c_y
            to = k * size_y + 8 * tile
            message[to : to + 8, :] = turned(post[k, 0, at : at + 8, :], c_z, size_z)
        if outer:
            at = 8 + size_y - c_y
            value = turned(post[k, 0, at : at + 8, :], c_z, size_z)
            to = 5 * size_y + 2 * k
            message[to : to + 1, :] = value[0:1]
            message[to + 1 : to + 2, :] = value[7:8]


def streamed(ends, middle, messages, i, x, tile, size_x, size_y, size_z, walls):
    tiles = size_y // 8
    row = iota((8, size_z), 0)
    c_x, c_y, c_z = VEC[i]

    def plane(x):
        if x == 0:
            return ends, 0
        if x == size_x - 1:
            return ends, 1
        return middle, x - 1

    from_x = x - c_x
    if 0 <= from_x < size_x:
        source, p = plane(from_x)
        at = 8 + 8 * tile - c_y
        value = turned(source[i, p, at : at + 8, :], c_z, size_z)
    else:
        numbers = FORWARD if from_x < 0 else BACKWARD
        k = numbers.index(i)

        def received(at, rows):
            if len(messages) == 1:
                return messages[0][at : at + rows, :]
            near, far = messages
            from_near = jnp.logical_not(even_x()) if from_x < 0 else even_x()
            return jnp.where(from_near, near[at : at + rows, :], far[at : at + rows, :])

        if tile < tiles:
            value = received(k * size_y + 8 * tile, 8)
        else:
            at = 5 * size_y + 2 * k
            value = jnp.where(row < 4, received(at, 1), received(at + 1, 1))
    source, p = plane(x)
    if c_y == 1 and tile == 0:
        value = jnp.where((row == 0) & walls[0], source[OPP[i], p, 8:16, :], value)
    if c_y == -1 and tile == tiles - 1:
        back = source[OPP[i], p, size_y : 8 + size_y, :]
        value = jnp.where((row == 7) & walls[1], back, value)
    return value


def walls_of(count):
    here = lax.axis_index("gy")
    return here == 0, here == count - 1


def second_kernel(size_x, size_y, size_z, count, entries, ends, middle, solid, later):
    walls = walls_of(count)
    blocks = relax_blocks(entries)
    for p in range(size_x - 2):
        for tile in range(size_y // 8 + 1):
            rows = slice(8 * tile, 8 * tile + 8)
            h = [
                streamed(ends, middle, None, i, p + 1, tile, size_x, size_y, size_z, walls)
                for i in range(19)
            ]
            for part in range(size_z // 128):
                lanes = slice(128 * part, 128 * part + 128)
                s = [solid[c, p, rows, lanes] for c in range(4)]
                out = collide([v[:, lanes] for v in h], *s, blocks)
                for i in range(19):
                    store_padded(later, i, p, tile, part, out[i], size_y // 8)


def second_ends(
    size_x, size_y, size_z, count, entries, ends, middle, solid, messages, place, numbers, later, p
):
    walls = walls_of(count)
    blocks = relax_blocks(entries)
    x = place * (size_x - 1)
    for tile in range(size_y // 8 + 1):
        rows = slice(8 * tile, 8 * tile + 8)
        h = [
            streamed(ends, middle, messages, i, x, tile, size_x, size_y, size_z, walls) for i in range(19)
        ]
        for part in range(size_z // 128):
            lanes = slice(128 * part, 128 * part + 128)
            s = solid(rows, lanes)
            out = collide([v[:, lanes] for v in h], *s, blocks)
            for k, i in enumerate(numbers):
                store_padded(later, k, p, tile, part, out[i], size_y // 8)


def second_leaving_kernel(size_x, size_y, size_z, count, far, entries, ends, middle, solid, received, *refs):
    message, leaving = refs[-2:]

    def work(place, numbers):
        second_ends(
            size_x,
            size_y,
            size_z,
            count,
            entries,
            ends,
            middle,
            lambda rows, lanes: [solid[c, 0, rows, lanes] for c in range(4)],
            (received,),
            place,
            numbers,
            leaving,
            0,
        )
        write_face(leaving, message, numbers, size_y, size_z, False)

    by_plane(work, far)


def second_ends_kernel(
    size_x, size_y, size_z, count, entries, ends, middle, solid_far, solid_near, far, near, later
):
    for place in range(2):
        second_ends(
            size_x,
            size_y,
            size_z,
            count,
            entries,
            ends,
            middle,
            lambda rows, lanes: plane_solid(solid_far, solid_near, place, rows, lanes),
            (near, far),
            place,
            range(19),
            later,
            place,
        )


def last_kernel(size_x, size_y, size_z, count, ends, middle, advanced, held, done):
    walls = walls_of(count)
    copies = []
    for i in range(19):
        for x in range(size_x):
            if not 0 <= x - VEC[i][0] < size_x:
                continue
            for tile in range(size_y // 8):
                held[i, x, 8 * tile : 8 * tile + 8, :] = streamed(
                    ends, middle, None, i, x, tile, size_x, size_y, size_z, walls
                )
        low, high = max(0, VEC[i][0]), size_x + min(0, VEC[i][0])
        copy = pltpu.make_async_copy(
            held.at[i, low:high], advanced.at[i, low:high], done.at[i]
        )
        copy.start()
        copies.append(copy)
    for copy in copies:
        copy.wait()


def entering(size_x, size_y, size_z, count, ends, received, place, k, target):
    numbers = BACKWARD if place else FORWARD
    walls = walls_of(count)
    for tile in range(size_y // 8):
        target[k, 8 * tile : 8 * tile + 8, :] = streamed(
            ends, None, (received,), numbers[k], place * (size_x - 1), tile, size_x, size_y, size_z, walls
        )


def far_kernel(size_x, size_y, size_z, count, ends, received, held):
    def work(place, numbers):
        del numbers
        for k in range(5):
            entering(size_x, size_y, size_z, count, ends, received, place, k, held)

    by_plane(work, True)


def enter_kernel(size_x, size_y, size_z, count, ends, received, far, given, advanced, near, done):
    del given

    def write(place, held, base):
        numbers = BACKWARD if place else FORWARD
        for k, i in enumerate(numbers):
            copy = pltpu.make_async_copy(held.at[k], advanced.at[i, place * (size_x - 1)], done.at[base + k])
            copy.start()

    def work(place, numbers):
        del numbers
        write(1 - place, far, 0)
        for k in range(5):
            entering(size_x, size_y, size_z, count, ends, received, place, k, near)
        write(place, near, 5)

    by_plane(work, False)
    for k in range(5):
        pltpu.make_async_copy(far.at[k], advanced.at[FORWARD[k], 0], done.at[k]).wait()
        pltpu.make_async_copy(near.at[k], advanced.at[FORWARD[k], 0], done.at[5 + k]).wait()


def shape(*sizes):
    return jax.ShapeDtypeStruct(sizes, F32)


VMEM = pl.BlockSpec(memory_space=pltpu.VMEM)
SMEM = pl.BlockSpec(memory_space=pltpu.SMEM)
HBM = pl.BlockSpec(memory_space=pltpu.HBM)


def call(kernel, out_shape, limit, in_specs, out_specs=None, scratch=(), aliases=None):
    return pl.pallas_call(
        kernel,
        out_shape=out_shape,
        in_specs=in_specs,
        out_specs=jax.tree.map(lambda _: VMEM, out_shape) if out_specs is None else out_specs,
        scratch_shapes=scratch,
        input_output_aliases={} if aliases is None else aliases,
        compiler_params=pltpu.CompilerParams(vmem_limit_bytes=limit * 2**20),
    )


def in_hbm(value):
    return pltpu.with_memory_space_constraint(value, pltpu.HBM)


def around(value, axis, steps):
    count = lax.axis_size(axis)
    return lax.ppermute(value, axis, [(i, (i + steps) % count) for i in range(count)])


def paired_x(value, parity):
    count = lax.axis_size("gx")
    if count % 2:
        raise ValueError("odd ring")
    pairs = [(i, (i + 1 if i % 2 == parity else i - 1) % count) for i in range(count)]
    return lax.ppermute(value, "gx", pairs)


def paired_y(value, parity):
    count_x, count = lax.axis_size("gx"), lax.axis_size("gy")
    pairs = []
    for i in range(count_x):
        for j in range(count):
            other = j + 1 if j % 2 == parity else j - 1
            to = i * count + other if 0 <= other < count else (i ^ 1) * count + j
            pairs.append((i * count + j, to))
    return lax.ppermute(value, ("gx", "gy"), pairs)


def exchanged(near, far):
    far = paired_x(far, 1)
    return paired_x(near, 0), far


def local(populations, relax_rates, velocity, velocity_change, fractions, anchor, destination):
    _, size_x, size_y, size_z = populations.shape
    count = lax.axis_size("gy")
    rows = anchor.shape[0]
    sizes = (size_x, size_y, size_z)
    part = functools.partial
    packed = shape(8, 128)
    band = shape(19, size_x, 8, size_z)
    table, own, near, far, bottom, top = call(
        pack_kernel,
        (shape(32, rows), packed, packed, packed, band, band),
        8,
        [HBM] * 6,
        scratch=[
            pltpu.VMEM((3, rows), F32),
            pltpu.VMEM((3, rows), F32),
            pltpu.VMEM((27, rows), F32),
            pltpu.VMEM((1, rows), I32),
            pltpu.VMEM((1, rows), I32),
            pltpu.SemaphoreType.DMA((7,)),
        ],
    )(*map(in_hbm, (velocity, velocity_change, fractions, anchor[None, :], destination[None, :], populations)))
    near, far = exchanged(near, far)
    first = edge_rows(size_x)[-1]
    fold = size_z // 128
    message = shape(-(-(first + 8 // fold) // 8) * 8, size_z)
    entries = call(relax_kernel, shape(ENTRIES, 8, 128), 8, [SMEM])(relax_rates)
    one, two = call(
        part(edge_kernel, *sizes),
        (message, message),
        8,
        [VMEM] * 4,
        scratch=[pltpu.VMEM((19, 2 * size_x, size_z), F32)],
    )(bottom, top, table, entries)
    two = paired_y(two, 1)
    column, one = call(
        part(merge_kernel, first, fold),
        (shape(8, 128), message),
        8,
        [VMEM] * 4,
        aliases={3: 1},
    )(own, far, near, one)
    shifts = []
    for shift in (2, -2):
        if shift % count > 1 and all((shift - other) % count for other in shifts):
            shifts.append(shift)
    rest = [around(column, "gy", shift) for shift in shifts]
    one, column_two = paired_y(one, 0), paired_y(column, 1)
    unused = pl.BlockSpec(memory_space=pl.ANY)
    outside, inside = (0, size_x - 1), tuple(range(1, size_x - 1))

    def staying(planes, after):
        return call(
            part(stay_kernel, *sizes, planes),
            shape(4, len(planes), size_y, size_z),
            16,
            [VMEM, unused],
        )(table, after)

    sums = staying(outside, two)
    plane_pair = shape(19, 2, size_y, size_z)
    parts = call(
        part(fluid_kernel, *sizes), (plane_pair, plane_pair, shape(2, size_y, size_z)), 16, [VMEM] * 2
    )(entries, populations)
    width = -(-(3 + len(shifts)) * LANES // 128) * 128
    def outer_shapes(planes):
        return tuple(shape(k, len(planes), 8, size_z) for k in (4, 19, 11))

    outer_sums, outer, second, migrants = call(
        part(outer_kernel, *sizes, count, shifts, outside),
        outer_shapes(outside) + (shape(40, width),),
        8,
        [VMEM] * (4 + len(shifts)),
    )(column, one, column_two, *rest, two)

    def padded(planes):
        return shape(19, planes, size_y + 24, size_z)

    def solid_shape(planes):
        return shape(4, planes, size_y + 8, size_z)

    sent = pltpu.VMEM((5, 1, size_y + 24, size_z), F32)
    wide_face = shape((5 * size_y + 10 + 7) // 8 * 8, size_z)
    face = shape(5 * size_y, size_z)

    def leaving(far, *given):
        return call(
            part(leaving_kernel, *sizes, far),
            (solid_shape(1), wide_face),
            16,
            [VMEM] * 9 + [unused] * (len(given) - 9),
            scratch=[sent],
        )(*given)

    known = (entries, sums, outer_sums, outer, second, migrants, *parts)
    solid_far, far = leaving(True, *known)
    solid_near, near = leaving(False, *known, solid_far)
    near, far = exchanged(near, far)
    inner = call(part(outer_kernel, *sizes, count, shifts, inside), outer_shapes(inside), 8, [VMEM] * 2)(
        two, one
    )
    middle, solid_middle = call(
        part(middle_kernel, *sizes, inside),
        (padded(len(inside)), solid_shape(len(inside))),
        16,
        [VMEM] * 7,
    )(entries, staying(inside, solid_near), *inner, migrants, populations)
    ends = call(part(ends_kernel, *sizes), padded(2), 16, [VMEM] * 8)(
        entries, outer, second, *parts, solid_far, solid_near
    )
    later_middle = call(part(second_kernel, *sizes, count), padded(len(inside)), 16, [VMEM] * 4)(
        entries, ends, middle, solid_middle
    )

    def second_leaving(far, *given):
        return call(
            part(second_leaving_kernel, *sizes, count, far),
            face,
            16,
            [VMEM] * 5 + [unused] * (len(given) - 5),
            scratch=[sent],
        )(*given)

    received = (far, near)
    far = second_leaving(True, entries, ends, middle, solid_far, far, later_middle)
    near = second_leaving(False, entries, ends, middle, solid_near, near, far)
    near, far = exchanged(near, far)
    later_ends = call(part(second_ends_kernel, *sizes, count), padded(2), 16, [VMEM] * 7)(
        entries, ends, middle, solid_far, solid_near, *received
    )
    advanced = call(
        part(last_kernel, *sizes, count),
        shape(19, *sizes),
        16,
        [VMEM] * 2,
        HBM,
        [pltpu.VMEM((19, *sizes), F32), pltpu.SemaphoreType.DMA((19,))],
    )(later_ends, later_middle)
    slabs = (5, size_y, size_z)
    far = call(part(far_kernel, *sizes, count), shape(*slabs), 16, [VMEM] * 2)(later_ends, far)
    return call(
        part(enter_kernel, *sizes, count),
        shape(19, *sizes),
        16,
        [VMEM] * 3 + [HBM],
        HBM,
        [pltpu.VMEM(slabs, F32), pltpu.SemaphoreType.DMA((10,))],
        {3: 0},
    )(later_ends, near, far, advanced)


def solution(mesh):
    placed = (
        P(None, "gx", "gy", None),
        P(),
        P(None, ("gx", "gy")),
        P(None, ("gx", "gy")),
        P(None, ("gx", "gy")),
        P(("gx", "gy")),
        P(("gx", "gy")),
    )
    return jax.shard_map(
        local, mesh=mesh, in_specs=placed, out_specs=P(None, "gx", "gy", None), check_vma=False
    )
```
